32 devices in a mesh: tm: 16 (over z, y, core), plane: 2 (over x).
Axes of the slice: x: 2, y: 2, z: 4, core: 2. Of those that a mesh axis runs over, the one named last changes fastest.
Arguments:
- frames: bfloat16 [32, 2, 512, 1024], P('tm', 'plane'), may hold values from -6 to 6
- template: bfloat16 [32, 2, 128, 128], P('tm', 'plane'), may hold values from -6 to 6
- shift_codes: int32 [32, 2, 32], P('tm'), may hold values from -128 to 127
Outputs:
- correlation: float32 [32, 32, 256], P('tm', 'plane')
- new_template: float32 [32, 2, 128, 128], P('tm', 'plane')
The draws below stay inside these ranges and needn't reach their ends.
Inputs may be any that keep to these rules, and one draw needn't show every extreme that they name: shift_codes is 16 times the shift in pixels, its integer part at most 8 pixels either way; every plane of a volume shares it.
All inputs are finite; a program needn't handle non-finite values.
Results may differ from the reference program's by a relative error of at most 0.0065.
Values may be sent and summed in bfloat16 or wider, within the bound.
No kernel may reach another device: no remote copies, remote signals or barrier semaphores. Data moves between devices by JAX's collectives and lax.ppermute only.
A program may use at most 128 MiB of HBM per device.

```python
import math
import jax
import jax.numpy as jnp
from jax import lax

BLOCK = 128
IMG_W = 1024
IMG_H = 512
SHIFT = 8
WIN = 16
TAPS = 8
SUB = 16
VOLS = 32
PLANES = 2
BX = 8
BY = 4
BLOCKS = 32


def touch_ends(entries, stream_key, smallest, top_value):
    extent = entries.shape
    index_at = [jax.random.randint(jax.random.fold_in(stream_key, axis), (), 0, extent[axis]) for axis in range(len(extent))]
    entries = entries.at[tuple(index_at)].set(smallest)
    longest = extent.index(max(extent))
    index_at[longest] = (index_at[longest] + 1) % extent[longest]
    return entries.at[tuple(index_at)].set(top_value)


def levels(stream_key, shape, cuts, smallest, high):
    def one(axis_at, blocks):
        steps = jax.random.uniform(jax.random.fold_in(jax.random.fold_in(stream_key, 6), axis_at), (blocks,), jnp.float32, smallest / len(cuts), high / len(cuts))
        return jnp.repeat(jnp.exp(steps), shape[axis_at] // blocks).reshape((-1,) + (1,) * (len(shape) - axis_at - 1))

    level = one(*cuts[0])
    for cut in cuts[1:]:
        level = level * one(*cut)
    return level


def gaussian(stream_key, extent, spread, reach, cuts=(), kind=jnp.bfloat16):
    values = jax.random.normal(stream_key, extent, jnp.float32) * spread
    if len(cuts) > 0:
        values = levels(stream_key, extent, cuts, -0.22, 0.18) * values
    return jnp.clip(values, min=-reach, max=reach).astype(kind)


def setup_inputs(seed: int = 0) -> dict:
    key_of = jax.random.split(jax.random.key(seed), 4)
    return {
        "frames": gaussian(key_of[0], (VOLS, PLANES, IMG_H, IMG_W), 1.0, 6.0, ((0, 16), (1, 2))),
        "template": gaussian(key_of[1], (BLOCKS, PLANES, BLOCK, BLOCK), 1.0, 6.0, ((0, 16), (1, 2))),
        "shift_codes": touch_ends(jax.random.randint(key_of[2], (VOLS, 2, BLOCKS), -SHIFT * SUB, SHIFT * SUB), jax.random.fold_in(key_of[2], 1), -SHIFT * SUB, (SHIFT * SUB) - 1).astype(jnp.int32),
    }


full_turn = 2.0 * math.pi

def dft_tables(block_size):
    positions = jnp.arange(block_size, dtype=jnp.int32)
    product = jnp.mod(positions[:, None] * positions[None, :], block_size)
    angles = product.astype(jnp.float32) * (full_turn / block_size)
    return (jnp.cos(angles).astype(jnp.bfloat16), (-jnp.sin(angles)).astype(jnp.bfloat16))

def spectrum(blocks, cosine_table, sine_table):
    highest = lax.Precision.HIGHEST
    blocks_wide = blocks.astype(jnp.float32)
    cos_wide = cosine_table.astype(jnp.float32)
    sin_wide = sine_table.astype(jnp.float32)
    row_real = jnp.einsum('...rc,ck->...rk', blocks_wide, cos_wide, precision=highest)
    row_imag = jnp.einsum('...rc,ck->...rk', blocks_wide, sin_wide, precision=highest)
    row_real = lax.optimization_barrier(row_real.astype(jnp.bfloat16)).astype(jnp.float32)
    row_imag = lax.optimization_barrier(row_imag.astype(jnp.bfloat16)).astype(jnp.float32)
    real_part = jnp.einsum('kr,...rl->...kl', cos_wide, row_real, precision=highest) - jnp.einsum('kr,...rl->...kl', sin_wide, row_imag, precision=highest)
    imag_part = jnp.einsum('kr,...rl->...kl', cos_wide, row_imag, precision=highest) + jnp.einsum('kr,...rl->...kl', sin_wide, row_real, precision=highest)
    return (real_part, imag_part)

def normalized_cross(frame_real, frame_imag, temp_real, temp_imag):
    temp_real = temp_real.astype(jnp.float32)
    temp_imag = temp_imag.astype(jnp.float32)
    cross_real = frame_real * temp_real + frame_imag * temp_imag
    cross_imag = frame_imag * temp_real - frame_real * temp_imag
    magnitude = jnp.sqrt(cross_real * cross_real + cross_imag * cross_imag)
    mean_mag = lax.optimization_barrier(jnp.mean(magnitude, axis=(-2, -1), keepdims=True)) + 1e-06
    return (cross_real / (magnitude + mean_mag), cross_imag / (magnitude + mean_mag))

def window_tables(shifts, block_size, window):
    offsets = jnp.arange(window, dtype=jnp.int32) - window // 2
    lags = jnp.mod(shifts[:, None] + offsets[None, :], block_size)
    positions = jnp.arange(block_size, dtype=jnp.int32)
    product = jnp.mod(positions[None, :, None] * lags[:, None, :], block_size)
    angles = product.astype(jnp.float32) * (full_turn / block_size)
    return (jnp.cos(angles), jnp.sin(angles))

def windows(norm_real, norm_imag, shift_rows, shift_cols, block_size, window):
    highest = lax.Precision.HIGHEST
    row_cos, row_sin = window_tables(shift_rows, block_size, window)
    col_cos, col_sin = window_tables(shift_cols, block_size, window)
    prod_real = jnp.einsum('nkl,nlc->nkc', norm_real, col_cos, precision=highest) - jnp.einsum('nkl,nlc->nkc', norm_imag, col_sin, precision=highest)
    prod_imag = jnp.einsum('nkl,nlc->nkc', norm_real, col_sin, precision=highest) + jnp.einsum('nkl,nlc->nkc', norm_imag, col_cos, precision=highest)
    result = jnp.einsum('nka,nkc->nac', row_cos, prod_real, precision=highest) - jnp.einsum('nka,nkc->nac', row_sin, prod_imag, precision=highest)
    result = result * (1.0 / block_size)
    return result.reshape(result.shape[0], window * window)

def tap_table(fractions, taps, steps):
    offsets = jnp.arange(taps, dtype=jnp.float32) - (taps // 2 - 1)
    spots = offsets - fractions[..., None].astype(jnp.float32) / steps
    raw_taps = jnp.sinc(spots) * jnp.sinc(spots / (taps // 2))
    return raw_taps / lax.optimization_barrier(jnp.sum(raw_taps, axis=-1, keepdims=True))

def warp_block(padded, row_start, col_start, tap_rows, tap_cols, block_size, taps):
    span = block_size + taps - 1
    region = lax.dynamic_slice(padded, (row_start, col_start), (span, span)).astype(jnp.float32)
    across = jnp.zeros((span, block_size), jnp.float32)
    for tap_index in range(taps):
        across = across + tap_cols[tap_index] * region[:, tap_index:tap_index + block_size]
    result = jnp.zeros((block_size, block_size), jnp.float32)
    for tap_index in range(taps):
        result = result + tap_rows[tap_index] * across[tap_index:tap_index + block_size, :]
    return result

def reference(frames, template, shift_codes):
    cosine_table, sine_table = dft_tables(BLOCK)
    temp_real, temp_imag = spectrum(template, cosine_table, sine_table)
    temp_real = lax.optimization_barrier(temp_real.astype(jnp.bfloat16))
    temp_imag = lax.optimization_barrier(temp_imag.astype(jnp.bfloat16))
    shifts = jnp.floor_divide(shift_codes, SUB).astype(jnp.int32)
    fractions = jnp.mod(shift_codes, SUB).astype(jnp.int32)
    margin = SHIFT + TAPS
    block_ids = jnp.arange(BLOCKS, dtype=jnp.int32)
    block_rows = block_ids // BX * BLOCK
    block_cols = block_ids % BX * BLOCK
    warper = jax.vmap(jax.vmap(partial_warp(BLOCK, TAPS), in_axes=(None, 0, 0, 0, 0)), in_axes=(0, None, None, None, None))

    def one_volume(summed, inputs):
        volume, vol_shift, vol_frac = inputs
        blocks = volume.reshape(PLANES, BY, BLOCK, BX, BLOCK).transpose(1, 3, 0, 2, 4)
        blocks = blocks.reshape(BLOCKS, PLANES, BLOCK, BLOCK)
        frame_real, frame_imag = spectrum(blocks, cosine_table, sine_table)
        norm_real, norm_imag = normalized_cross(frame_real, frame_imag, temp_real, temp_imag)
        shift_rows = jnp.broadcast_to(vol_shift[0][:, None], (BLOCKS, PLANES)).reshape(-1)
        shift_cols = jnp.broadcast_to(vol_shift[1][:, None], (BLOCKS, PLANES)).reshape(-1)
        window_out = windows(norm_real.reshape(-1, BLOCK, BLOCK), norm_imag.reshape(-1, BLOCK, BLOCK), shift_rows, shift_cols, BLOCK, WIN)
        window_out = lax.optimization_barrier(jnp.sum(window_out.reshape(BLOCKS, PLANES, WIN * WIN), axis=1))
        tap_rows = tap_table(vol_frac[0], TAPS, SUB)
        tap_cols = tap_table(vol_frac[1], TAPS, SUB)
        padded = jnp.pad(volume, ((0, 0), (margin, margin), (margin, margin)))
        row_start = (block_rows + margin + vol_shift[0] - (TAPS // 2 - 1)).astype(jnp.int32)
        col_start = (block_cols + margin + vol_shift[1] - (TAPS // 2 - 1)).astype(jnp.int32)
        warped = warper(padded, row_start, col_start, tap_rows, tap_cols)
        return (summed + jnp.transpose(warped, (1, 0, 2, 3)), window_out)
    initial = jnp.zeros((BLOCKS, PLANES, BLOCK, BLOCK), jnp.float32)
    summed, correlation = lax.scan(one_volume, initial, (frames, shifts, fractions))
    return (correlation, summed * (1.0 / VOLS))

def partial_warp(block_size, taps):

    def warp_one(padded, row_start, col_start, tap_rows, tap_cols):
        return warp_block(padded, row_start, col_start, tap_rows, tap_cols, block_size, taps)
    return warp_one
```

```python
import functools
import math

import jax
import jax.numpy as jnp
import numpy as np
from jax import lax
from jax.experimental import pallas as pl
from jax.experimental.pallas import tpu as pltpu
from jax.sharding import PartitionSpec as P

SHIFT = 8
WIN = 16
TAPS = 8
SUB = 16
EDGE = 16
LANES = 128
MIB = 1024 * 1024

full_turn = 2.0 * math.pi


def dft_constants(block_size):
    positions = np.arange(block_size)
    angles = full_turn * (np.outer(positions, positions) % block_size) / block_size
    cosine = np.cos(angles)
    sine = -np.sin(angles)
    half = block_size // 2 + 1
    rows = -(-half // 8) * 8
    row_table = np.concatenate([cosine, sine], axis=1)
    col_table = np.zeros((2 * rows, 2 * block_size))
    col_table[:half] = np.concatenate([cosine[:half], -sine[:half]], axis=1)
    col_table[rows : rows + half] = np.concatenate([sine[:half], cosine[:half]], axis=1)
    weights = np.zeros((rows,))
    weights[:half] = 2.0
    weights[0] = weights[half - 1] = 1.0
    starts = 2 * SHIFT
    lag_table = np.zeros((starts, 2 * WIN, 2 * rows))
    for start in range(starts):
        lags = start - SHIFT - WIN // 2 + np.arange(WIN)
        turns = full_turn * (np.outer(lags, positions[:half]) % block_size) / block_size
        lag_cos = np.cos(turns) * weights[:half]
        lag_sin = np.sin(turns) * weights[:half]
        lag_table[start, :WIN, :half] = lag_cos
        lag_table[start, :WIN, rows : rows + half] = -lag_sin
        lag_table[start, WIN:, :half] = lag_sin
        lag_table[start, WIN:, rows : rows + half] = lag_cos
    span = starts + WIN
    lags = np.arange(span) - SHIFT - WIN // 2
    turns = full_turn * (np.outer(positions, lags) % block_size) / block_size
    span_table = np.zeros((2 * block_size, LANES))
    span_table[:block_size, :span] = np.cos(turns)
    span_table[block_size:, :span] = -np.sin(turns)
    return tuple(
        jnp.asarray(table, jnp.bfloat16) for table in (row_table, col_table, lag_table, span_table)
    ) + (jnp.asarray(np.broadcast_to(weights[:, None], (rows, LANES)), jnp.float32),)


def tap_constants(width):
    offsets = np.arange(TAPS) - (TAPS // 2 - 1)
    spots = offsets[None, :] - np.arange(SUB)[:, None] / SUB
    raw_taps = np.sinc(spots) * np.sinc(spots / (TAPS // 2))
    taps = raw_taps / raw_taps.sum(axis=-1, keepdims=True)
    table = np.zeros((SUB, EDGE, width))
    for row in range(EDGE):
        table[:, row, row : row + TAPS] = taps
    return jnp.asarray(table, jnp.float32)


def band_matrix(head, start, size):
    width = head.shape[1]
    head = pltpu.roll(head, start, 1).astype(jnp.bfloat16)
    groups = [head]
    for step in range(EDGE, size, EDGE):
        groups.append(jnp.concatenate([head[:, width - step :], head[:, : width - step]], axis=1))
    return jnp.concatenate(groups, axis=0)


def warp_kernel(vols, down, across, block, codes_ref, taps_ref, frames_ref, out_ref, padded, sems):
    rows, cols = down * block, across * block
    copies = [
        pltpu.make_async_copy(
            frames_ref.at[v],
            padded.at[v, pl.ds(EDGE, rows), pl.ds(block, cols)],
            sems.at[v],
        )
        for v in range(vols)
    ]
    for copy in copies:
        copy.start()
    zero_rows = jnp.zeros((EDGE, cols + 2 * block), jnp.bfloat16)
    zero_cols = jnp.zeros((rows, block), jnp.bfloat16)
    for v in range(vols):
        padded[v, :EDGE, :] = zero_rows
        padded[v, EDGE + rows :, :] = zero_rows
        padded[v, EDGE : EDGE + rows, :block] = zero_cols
        padded[v, EDGE : EDGE + rows, block + cols :] = zero_cols
    for copy in copies:
        copy.wait()
    tall = block + 2 * EDGE
    lane = lax.broadcasted_iota(jnp.int32, (tall, block), 1)
    width = 2 * block
    before = TAPS // 2 - 1

    def one_block(index, _):
        row = pl.multiple_of((index // across) * block, block)
        col = pl.multiple_of((index % across) * block, block)
        total = jnp.zeros((block, block), jnp.float32)
        for v in range(vols):
            row_code = codes_ref[v, 0, index]
            col_code = codes_ref[v, 1, index]
            row_start = (row_code >> 4) + (EDGE - before)
            col_start = (col_code >> 4) + (width - before)
            row_band = band_matrix(taps_ref[row_code & (SUB - 1)], row_start, block)
            col_band = band_matrix(taps_ref[col_code & (SUB - 1)], col_start, block)
            left = padded[v, pl.ds(row, tall), pl.ds(col, block)]
            middle = padded[v, pl.ds(row, tall), pl.ds(col + block, block)]
            right = padded[v, pl.ds(row, tall), pl.ds(col + 2 * block, block)]
            sides = jnp.where(lane < block // 2, right, left)
            region = jnp.concatenate([middle, sides], axis=1)
            partial = lax.dot_general(
                region,
                col_band,
                (((1,), (1,)), ((), ())),
                preferred_element_type=jnp.float32,
            ).astype(jnp.bfloat16)
            total += jnp.dot(row_band[:, :tall], partial, preferred_element_type=jnp.float32)
        out_ref[index] = total.astype(jnp.bfloat16)
        return 0

    lax.fori_loop(0, down * across, one_block, 0, unroll=2)


def warp_sums(frames, codes, block):
    vols, rows, cols = frames.shape
    down, across = rows // block, cols // block
    taps = tap_constants(2 * block)
    return pl.pallas_call(
        functools.partial(warp_kernel, vols, down, across, block),
        out_shape=jax.ShapeDtypeStruct((down * across, block, block), jnp.bfloat16),
        in_specs=[
            pl.BlockSpec(memory_space=pltpu.SMEM),
            pl.BlockSpec(memory_space=pltpu.VMEM),
            pl.BlockSpec(memory_space=pl.ANY),
        ],
        out_specs=pl.BlockSpec(memory_space=pltpu.VMEM),
        scratch_shapes=[
            pltpu.VMEM((vols, rows + 2 * EDGE, cols + 2 * block), jnp.bfloat16),
            pltpu.SemaphoreType.DMA((vols,)),
        ],
        compiler_params=pltpu.CompilerParams(vmem_limit_bytes=32 * MIB),
        cost_estimate=pl.CostEstimate(
            flops=2 * vols * rows * cols * block * 4,
            bytes_accessed=vols * rows * cols * 2 + rows * cols * 2,
            transcendentals=0,
        ),
        name="warp",
    )(codes, taps, frames)


def spectrum_kernel(
    vols,
    across,
    block,
    codes_ref,
    row_ref,
    col_ref,
    lag_ref,
    span_ref,
    weight_ref,
    frames_ref,
    template_ref,
    out_ref,
    found,
):
    band = pl.program_id(0)
    half = weight_ref.shape[0]
    row_table = row_ref[...]
    col_table = col_ref[...]
    span_table = span_ref[...]
    weights = weight_ref[...]
    count = vols + 1

    def one_pair(pair, _):
        col = pl.multiple_of(pair * 2 * block, 2 * block)
        parts = [template_ref[2 * pair], template_ref[2 * pair + 1]]
        for v in range(vols):
            both = frames_ref[v, :, pl.ds(col, 2 * block)]
            parts += [both[:, :block], both[:, block:]]
        rows = jnp.dot(
            jnp.concatenate(parts, axis=0), row_table, preferred_element_type=jnp.float32
        ).astype(jnp.bfloat16)
        spectra = []
        for at in range(count):
            stacks = []
            for side in range(2):
                one = rows[(2 * at + side) * block : (2 * at + side + 1) * block]
                stacks.append(jnp.concatenate([one[:, :block], one[:, block:]], axis=0))
            spectra.append(
                jnp.dot(
                    col_table,
                    jnp.concatenate(stacks, axis=1),
                    preferred_element_type=jnp.float32,
                )
            )
        temp = spectra[0].astype(jnp.bfloat16).astype(jnp.float32)
        lag_sums = []
        for v in range(vols):
            for side in range(2):
                lanes = slice(side * block, (side + 1) * block)
                temp_real, temp_imag = temp[:half, lanes], temp[half:, lanes]
                real, imag = spectra[v + 1][:half, lanes], spectra[v + 1][half:, lanes]
                cross_real = real * temp_real + imag * temp_imag
                cross_imag = imag * temp_real - real * temp_imag
                power = cross_real * cross_real + cross_imag * cross_imag
                magnitude = power * lax.rsqrt(jnp.maximum(power, 1e-36))
                mean = jnp.sum(magnitude * weights) * (1.0 / (block * block)) + 1e-06
                scale = 1.0 / (magnitude + mean)
                norm = jnp.concatenate(
                    [
                        (cross_real * scale).astype(jnp.bfloat16),
                        (cross_imag * scale).astype(jnp.bfloat16),
                    ],
                    axis=0,
                )
                index = band * across + 2 * pair + side
                row_shift = codes_ref[v, 0, index] >> 4
                lag_rows = jnp.dot(
                    lag_ref[row_shift + SHIFT], norm, preferred_element_type=jnp.float32
                ).astype(jnp.bfloat16)
                lag_sums.append(jnp.concatenate([lag_rows[:WIN], lag_rows[WIN:]], axis=1))
        lags = jnp.dot(
            jnp.concatenate(lag_sums, axis=0), span_table, preferred_element_type=jnp.float32
        )
        for v in range(vols):
            for side in range(2):
                index = band * across + 2 * pair + side
                col_shift = codes_ref[v, 1, index] >> 4
                at = 2 * v + side
                one = lags[at * WIN : (at + 1) * WIN]
                one = pltpu.roll(one, LANES - SHIFT - col_shift, 1)
                start = pl.multiple_of((2 * pair + side) * WIN, WIN)
                found[v, pl.ds(start, WIN), :] = one
        return 0

    lax.fori_loop(0, across // 2, one_pair, 0)

    per_tile = LANES // WIN
    lane = lax.broadcasted_iota(jnp.int32, (across, LANES), 1) // WIN
    for v in range(vols):
        for tile in range(WIN // per_tile):
            total = jnp.zeros((across, LANES), jnp.float32)
            for part in range(per_tile):
                one = found[v, pl.ds(tile * per_tile + part, across, stride=WIN), :]
                if part:
                    one = pltpu.roll(one, part * WIN, 1)
                total = jnp.where(lane == part, one, total)
            out_ref[v, :, tile * LANES : (tile + 1) * LANES] = total * (1.0 / block)


def lag_windows(frames, template, codes):
    vols, rows, cols = frames.shape
    block = template.shape[-1]
    down, across = rows // block, cols // block
    tables = dft_constants(block)
    whole = [
        pl.BlockSpec(table.shape, functools.partial(lambda dims, band: (0,) * dims, table.ndim))
        for table in tables
    ]
    return pl.pallas_call(
        functools.partial(spectrum_kernel, vols, across, block),
        grid=(down,),
        out_shape=jax.ShapeDtypeStruct((vols, down * across, WIN * WIN), jnp.float32),
        in_specs=[
            pl.BlockSpec(memory_space=pltpu.SMEM),
            *whole,
            pl.BlockSpec((vols, block, cols), lambda band: (0, band, 0)),
            pl.BlockSpec((across, block, block), lambda band: (band, 0, 0)),
        ],
        out_specs=pl.BlockSpec((vols, across, WIN * WIN), lambda band: (0, band, 0)),
        scratch_shapes=[pltpu.VMEM((vols, across * WIN, LANES), jnp.float32)],
        compiler_params=pltpu.CompilerParams(vmem_limit_bytes=32 * MIB),
        cost_estimate=pl.CostEstimate(
            flops=2 * 3 * rows * cols * block * 4,
            bytes_accessed=vols * rows * cols * 2 + rows * cols * 2,
            transcendentals=0,
        ),
        name="lag_windows",
    )(codes, *tables, frames, template)


def on_device(frames, template, shift_codes):
    vol_dev, pl_dev, img_rows, img_cols = frames.shape
    block = template.shape[-1]
    tm_size = lax.axis_size("tm")
    plane_size = lax.axis_size("plane")
    own = template.shape[0]
    total = own * tm_size
    gathered = lax.all_gather(template, "tm", axis=0, tiled=True)
    warped = jnp.stack(
        [warp_sums(frames[:, p], shift_codes, block) for p in range(pl_dev)], axis=1
    )
    moved = lax.all_to_all(
        warped.reshape(tm_size, own, pl_dev, block, block), "tm", 0, 0, tiled=True
    )
    window = lag_windows(frames[:, 0], gathered[:, 0], shift_codes)
    for p in range(1, pl_dev):
        window = window + lag_windows(frames[:, p], gathered[:, p], shift_codes)
    me = lax.axis_index("plane")
    share = total // plane_size
    pieces = window.reshape(vol_dev, plane_size, share, WIN * WIN)
    correlation = lax.dynamic_index_in_dim(pieces, me, 1, keepdims=False)
    for step in range(1, plane_size):
        there = lax.rem(me + step, plane_size)
        sent = lax.dynamic_index_in_dim(pieces, there, 1, keepdims=False)
        correlation = correlation + lax.ppermute(
            sent, "plane", [(j, (j + step) % plane_size) for j in range(plane_size)]
        )
    volumes = vol_dev * tm_size
    new_template = jnp.sum(moved.astype(jnp.float32), axis=0) * (1.0 / volumes)
    return (correlation, new_template)


def solution(mesh):
    in_specs = (P("tm", "plane", None, None), P("tm", "plane", None, None), P("tm", None, None))
    out_specs = (P("tm", "plane", None), P("tm", "plane", None, None))
    return jax.shard_map(
        on_device, mesh=mesh, in_specs=in_specs, out_specs=out_specs, check_vma=False
    )
```

```python
import functools
import math

import jax
import jax.numpy as jnp
import numpy as np
from jax import lax
from jax.experimental import pallas as pl
from jax.experimental.pallas import tpu as pltpu
from jax.sharding import PartitionSpec as P

SHIFT = 8
WIN = 16
TAPS = 8
SUB = 16
EDGE = 16
LANES = 128
VMEM_LIMIT = 56 * 1024 * 1024

full_turn = 2.0 * math.pi


def dft_constants(block_size):
    positions = np.arange(block_size)
    angles = full_turn * (np.outer(positions, positions) % block_size) / block_size
    cosine = np.cos(angles)
    sine = -np.sin(angles)
    half = block_size // 2 + 1
    rows = -(-half // 8) * 8
    row_table = np.concatenate([cosine, sine], axis=1)
    col_table = np.zeros((2 * rows, 2 * block_size))
    col_table[:half] = np.concatenate([cosine[:half], -sine[:half]], axis=1)
    col_table[rows : rows + half] = np.concatenate([sine[:half], cosine[:half]], axis=1)
    weights = np.zeros((rows,))
    weights[:half] = 2.0
    weights[0] = weights[half - 1] = 1.0
    starts = 2 * SHIFT
    lag_table = np.zeros((starts, 2 * WIN, 2 * rows))
    for start in range(starts):
        lags = start - SHIFT - WIN // 2 + np.arange(WIN)
        turns = full_turn * (np.outer(lags, positions[:half]) % block_size) / block_size
        lag_cos = np.cos(turns) * weights[:half]
        lag_sin = np.sin(turns) * weights[:half]
        lag_table[start, :WIN, :half] = lag_cos
        lag_table[start, :WIN, rows : rows + half] = -lag_sin
        lag_table[start, WIN:, :half] = lag_sin
        lag_table[start, WIN:, rows : rows + half] = lag_cos
    span = starts + WIN
    lags = np.arange(span) - SHIFT - WIN // 2
    turns = full_turn * (np.outer(positions, lags) % block_size) / block_size
    span_table = np.zeros((2 * block_size, LANES))
    span_table[:block_size, :span] = np.cos(turns)
    span_table[block_size:, :span] = -np.sin(turns)
    return tuple(
        jnp.asarray(table, jnp.bfloat16) for table in (row_table, col_table, lag_table, span_table)
    )


def tap_constants():
    offsets = np.arange(TAPS) - (TAPS // 2 - 1)
    spots = offsets[None, :] - np.arange(SUB)[:, None] / SUB
    raw_taps = np.sinc(spots) * np.sinc(spots / (TAPS // 2))
    taps = raw_taps / raw_taps.sum(axis=-1, keepdims=True)
    table = np.zeros((SUB, EDGE, LANES))
    for row in range(EDGE):
        table[:, row, row : row + TAPS] = taps
    return jnp.asarray(table, jnp.float32)


def band_groups(head, shift, lane):
    start = shift + (LANES - (TAPS // 2 - 1))
    head = pltpu.roll(head, start, 1).astype(jnp.bfloat16)
    groups = [head] + [pltpu.roll(head, step, 1) for step in range(EDGE, LANES, EDGE)]
    zero = jnp.zeros_like(head)
    low = lane < LANES // 2
    before, after = jnp.where(low, zero, groups[0]), jnp.where(low, groups[-1], zero)
    middle = [jnp.where(low, groups[0], zero), *groups[1:-1], jnp.where(low, zero, groups[-1])]
    return middle, before, after


def warp_kernel(vols, down, across, block, codes_ref, taps_ref, mid_ref, above_ref, below_ref, out_ref):
    band = pl.program_id(0)
    lane = lax.broadcasted_iota(jnp.int32, (EDGE, LANES), 1)
    tall_lane = lax.broadcasted_iota(jnp.int32, (block + 2 * EDGE, LANES), 1)
    zero = jnp.zeros((EDGE, LANES), jnp.bfloat16)
    no_tile = jnp.zeros((block + 2 * EDGE, block), jnp.bfloat16)

    def tile(v, at):
        if at < 0 or at >= across:
            return no_tile
        lanes = slice(at * block, (at + 1) * block)
        above = jnp.where(band > 0, above_ref[v, :, lanes], zero)
        below = jnp.where(band < down - 1, below_ref[v, :, lanes], zero)
        return jnp.concatenate([mid_ref[v, :, lanes], below, above], axis=0)

    for at in range(across):
        index = band * across + at
        row_tiles, first_edge, last_edge = [], [], []
        partials, edges = [], []
        for v in range(vols):
            row_code = codes_ref[v, 0, index]
            col_code = codes_ref[v, 1, index]
            middle, before, after = band_groups(taps_ref[col_code & (SUB - 1)], col_code >> 4, lane)
            col_band = jnp.concatenate(
                [
                    jnp.concatenate(middle, axis=0),
                    jnp.concatenate([before] + [zero] * (block // EDGE - 2) + [after], axis=0),
                ],
                axis=1,
            )
            sides = jnp.where(tall_lane < LANES // 2, tile(v, at + 1), tile(v, at - 1))
            partial = lax.dot_general(
                jnp.concatenate([tile(v, at), sides], axis=1),
                col_band,
                (((1,), (1,)), ((), ())),
                preferred_element_type=jnp.float32,
            ).astype(jnp.bfloat16)
            partials.append(partial[:block])
            edges.append(partial[block:])
            middle, before, after = band_groups(taps_ref[row_code & (SUB - 1)], row_code >> 4, lane)
            row_tiles.append(jnp.concatenate(middle, axis=0))
            place = 2 * EDGE * v % LANES
            first_edge.append(pltpu.roll(before, (place + 2 * EDGE) % LANES, 1))
            last_edge.append(pltpu.roll(after, place, 1) if place else after)
        per_tile = LANES // (2 * EDGE)
        for v in range(0, vols, per_tile):
            first, last = first_edge[v], last_edge[v]
            for more in range(v + 1, min(v + per_tile, vols)):
                first, last = first + first_edge[more], last + last_edge[more]
            row_tiles.append(
                jnp.concatenate([first] + [zero] * (block // EDGE - 2) + [last], axis=0)
            )
        depth = vols * (block + 2 * EDGE)
        total = jnp.dot(
            jnp.concatenate(row_tiles, axis=1)[:, :depth],
            jnp.concatenate(partials + edges, axis=0),
            preferred_element_type=jnp.float32,
        )
        out_ref[at] = total.astype(jnp.bfloat16)


def warp_sums(frames, codes, block):
    vols, rows, cols = frames.shape
    down, across = rows // block, cols // block
    steps = block // EDGE
    taps = tap_constants()
    return pl.pallas_call(
        functools.partial(warp_kernel, vols, down, across, block),
        grid=(down,),
        out_shape=jax.ShapeDtypeStruct((down * across, block, block), jnp.bfloat16),
        in_specs=[
            pl.BlockSpec(memory_space=pltpu.SMEM),
            pl.BlockSpec(taps.shape, lambda band: (0, 0, 0)),
            pl.BlockSpec((vols, block, cols), lambda band: (0, band, 0)),
            pl.BlockSpec((vols, EDGE, cols), lambda band: (0, jnp.maximum(band * steps - 1, 0), 0)),
            pl.BlockSpec(
                (vols, EDGE, cols),
                lambda band: (0, jnp.minimum((band + 1) * steps, down * steps - 1), 0),
            ),
        ],
        out_specs=pl.BlockSpec((across, block, block), lambda band: (band, 0, 0)),
        compiler_params=pltpu.CompilerParams(vmem_limit_bytes=VMEM_LIMIT),
        cost_estimate=pl.CostEstimate(
            flops=2 * vols * rows * cols * block * 4,
            bytes_accessed=vols * rows * cols * 2 + rows * cols * 2,
            transcendentals=0,
        ),
        name="warp",
    )(codes, taps, frames, frames, frames)


def spectrum_kernel(
    vols,
    across,
    block,
    codes_ref,
    here_ref,
    row_ref,
    col_ref,
    lag_ref,
    span_ref,
    frames_ref,
    template_ref,
    out_ref,
    cross,
    sums,
    found,
):
    band = pl.program_id(0)
    own = template_ref.shape[1]
    row_table = row_ref[...]
    col_table = col_ref[...]
    half = col_table.shape[0] // 2
    top = lax.broadcasted_iota(jnp.int32, (8, LANES), 0) == 0

    for pair in range(across // 2):
        parts = []
        for side in range(2):
            index = band * across + 2 * pair + side
            parts.append(template_ref[(index // own) ^ here_ref[0], index % own])
        for v in range(vols):
            for side in range(2):
                at = 2 * pair + side
                parts.append(frames_ref[v, :, at * block : (at + 1) * block])
        rows = jnp.dot(
            jnp.concatenate(parts, axis=0), row_table, preferred_element_type=jnp.float32
        ).astype(jnp.bfloat16)
        spectra = []
        for source in range(vols + 1):
            stacks = []
            for side in range(2):
                at = (2 * source + side) * block
                one = rows[at : at + block]
                stacks.append(jnp.concatenate([one[:, :block], one[:, block:]], axis=0))
            spectra.append(
                jnp.dot(
                    col_table, jnp.concatenate(stacks, axis=1), preferred_element_type=jnp.float32
                )
            )
        temp = spectra[0].astype(jnp.bfloat16).astype(jnp.float32)
        for v in range(vols):
            for side in range(2):
                lanes = slice(side * block, (side + 1) * block)
                one = (2 * pair + side) * vols + v
                total = jnp.zeros((8, LANES), jnp.float32)
                for row in range(0, half, 8):
                    temp_real = temp[row : row + 8, lanes]
                    temp_imag = temp[half + row : half + row + 8, lanes]
                    real = spectra[v + 1][row : row + 8, lanes]
                    imag = spectra[v + 1][half + row : half + row + 8, lanes]
                    cross_real = real * temp_real + imag * temp_imag
                    cross_imag = imag * temp_real - real * temp_imag
                    power = cross_real * cross_real + cross_imag * cross_imag
                    magnitude = power * lax.rsqrt(jnp.maximum(power, 1e-36))
                    cross[one, row : row + 8, :] = cross_real
                    cross[one, half + row : half + row + 8, :] = cross_imag
                    cross[one, 2 * half + row : 2 * half + row + 8, :] = magnitude
                    if row == 0:
                        total = jnp.where(top, magnitude, 2.0 * magnitude)
                    elif row == block // 2:
                        total += magnitude
                    else:
                        total += 2.0 * magnitude
                sums[one] = jnp.sum(total, axis=0, keepdims=True)

    means = jnp.sum(sums[...], axis=2, keepdims=True) * (1.0 / (block * block)) + 1e-06
    lag_sums = []
    for one in range(across * vols):
        at, v = one // vols, one % vols
        mean = means[one]
        norms = []
        scales = []
        for row in range(0, half, 16):
            size = min(16, half - row)
            magnitude = cross[one, 2 * half + row : 2 * half + row + size, :]
            scales.append(pl.reciprocal(magnitude + mean, approx=True))
        scale = jnp.concatenate(scales, axis=0)
        norm = jnp.concatenate(
            [
                (cross[one, :half, :] * scale).astype(jnp.bfloat16),
                (cross[one, half : 2 * half, :] * scale).astype(jnp.bfloat16),
            ],
            axis=0,
        )
        row_shift = codes_ref[v, 0, band * across + at] >> 4
        lag_rows = jnp.dot(
            lag_ref[row_shift + SHIFT], norm, preferred_element_type=jnp.float32
        ).astype(jnp.bfloat16)
        lag_sums.append(jnp.concatenate([lag_rows[:WIN], lag_rows[WIN:]], axis=1))
    lags = jnp.dot(
        jnp.concatenate(lag_sums, axis=0), span_ref[...], preferred_element_type=jnp.float32
    )
    for one in range(across * vols):
        at, v = one // vols, one % vols
        col_shift = codes_ref[v, 1, band * across + at] >> 4
        found[v, at * WIN : (at + 1) * WIN, :] = pltpu.roll(
            lags[one * WIN : (one + 1) * WIN], LANES - SHIFT - col_shift, 1
        )

    per_tile = LANES // WIN
    lane = lax.broadcasted_iota(jnp.int32, (across, LANES), 1) // WIN
    for v in range(vols):
        for tile in range(WIN // per_tile):
            total = jnp.zeros((across, LANES), jnp.float32)
            for part in range(per_tile):
                one = found[v, pl.ds(tile * per_tile + part, across, stride=WIN), :]
                if part:
                    one = pltpu.roll(one, part * WIN, 1)
                total = jnp.where(lane == part, one, total)
            out_ref[v, :, tile * LANES : (tile + 1) * LANES] = total * (1.0 / block)


def lag_windows(frames, template, codes, here):
    vols, rows, cols = frames.shape
    block = template.shape[-1]
    down, across = rows // block, cols // block
    tables = dft_constants(block)
    half = tables[1].shape[0] // 2
    whole = [
        pl.BlockSpec(table.shape, functools.partial(lambda dims, band: (0,) * dims, table.ndim))
        for table in tables
    ]
    return pl.pallas_call(
        functools.partial(spectrum_kernel, vols, across, block),
        grid=(down,),
        out_shape=jax.ShapeDtypeStruct((vols, down * across, WIN * WIN), jnp.float32),
        in_specs=[
            pl.BlockSpec(memory_space=pltpu.SMEM),
            pl.BlockSpec(memory_space=pltpu.SMEM),
            *whole,
            pl.BlockSpec((vols, block, cols), lambda band: (0, band, 0)),
            pl.BlockSpec(template.shape, lambda band: (0, 0, 0, 0)),
        ],
        out_specs=pl.BlockSpec((vols, across, WIN * WIN), lambda band: (0, band, 0)),
        scratch_shapes=[
            pltpu.VMEM((vols * across, 3 * half, LANES), jnp.float32),
            pltpu.VMEM((vols * across, 1, LANES), jnp.float32),
            pltpu.VMEM((vols, across * WIN, LANES), jnp.float32),
        ],
        compiler_params=pltpu.CompilerParams(vmem_limit_bytes=VMEM_LIMIT),
        cost_estimate=pl.CostEstimate(
            flops=2 * 3 * rows * cols * block * 4,
            bytes_accessed=vols * rows * cols * 2 + rows * cols * 2,
            transcendentals=0,
        ),
        name="lag_windows",
    )(codes, here.reshape(1), *tables, frames, template)


def on_device(frames, template, shift_codes):
    vol_dev, pl_dev, img_rows, img_cols = frames.shape
    block = template.shape[-1]
    tm_size = lax.axis_size("tm")
    plane_size = lax.axis_size("plane")
    own = template.shape[0]
    total = own * tm_size
    here = lax.axis_index("tm")
    everyone = range(tm_size)
    same = [template[:, 0]]
    for step in range(2, tm_size, 2):
        same.append(lax.ppermute(template[:, 0], "tm", [(t, t ^ step) for t in everyone]))
    same = jnp.stack(same)
    other = lax.ppermute(same, "tm", [(t, t ^ 1) for t in everyone])
    gathered = jnp.stack([same, other], axis=1).reshape(tm_size, own, block, block)
    warped = jnp.stack(
        [warp_sums(frames[:, p], shift_codes, block) for p in range(pl_dev)], axis=1
    )
    moved = lax.all_to_all(
        warped.reshape(tm_size, own, pl_dev, block, block), "tm", 0, 0, tiled=True
    )
    window = lag_windows(frames[:, 0], gathered, shift_codes, here)
    me = lax.axis_index("plane")
    share = total // plane_size
    pieces = window.reshape(vol_dev, plane_size, share, WIN * WIN)
    correlation = lax.dynamic_index_in_dim(pieces, me, 1, keepdims=False)
    for step in range(1, plane_size):
        there = lax.rem(me + step, plane_size)
        sent = lax.dynamic_index_in_dim(pieces, there, 1, keepdims=False)
        correlation = correlation + lax.ppermute(
            sent, "plane", [(j, (j + step) % plane_size) for j in range(plane_size)]
        )
    volumes = vol_dev * tm_size
    new_template = jnp.sum(moved.astype(jnp.float32), axis=0) * (1.0 / volumes)
    return (correlation, new_template)


def solution(mesh):
    in_specs = (P("tm", "plane", None, None), P("tm", "plane", None, None), P("tm", None, None))
    out_specs = (P("tm", "plane", None), P("tm", "plane", None, None))
    return jax.shard_map(
        on_device, mesh=mesh, in_specs=in_specs, out_specs=out_specs, check_vma=False
    )
```

```python
import functools
import math

import jax
import jax.numpy as jnp
import numpy as np
from jax import lax
from jax.experimental import pallas as pl
from jax.experimental.pallas import tpu as pltpu
from jax.sharding import PartitionSpec as P

SHIFT = 8
WIN = 16
TAPS = 8
SUB = 16
EDGE = 16
LANES = 128
VMEM_LIMIT = 56 * 1024 * 1024

full_turn = 2.0 * math.pi


def dft_constants(block_size):
    positions = np.arange(block_size)
    angles = full_turn * (np.outer(positions, positions) % block_size) / block_size
    cosine = np.cos(angles)
    sine = -np.sin(angles)
    half = block_size // 2 + 1
    rows = -(-half // 8) * 8
    row_table = np.concatenate([cosine, sine], axis=1)
    col_table = np.zeros((2 * rows, 2 * block_size))
    col_table[:half] = np.concatenate([cosine[:half], -sine[:half]], axis=1)
    col_table[rows : rows + half] = np.concatenate([sine[:half], cosine[:half]], axis=1)
    weights = np.zeros((rows,))
    weights[:half] = 2.0
    weights[0] = weights[half - 1] = 1.0
    starts = 2 * SHIFT
    lag_table = np.zeros((starts, 2 * WIN, 2 * rows))
    for start in range(starts):
        lags = start - SHIFT - WIN // 2 + np.arange(WIN)
        turns = full_turn * (np.outer(lags, positions[:half]) % block_size) / block_size
        lag_cos = np.cos(turns) * weights[:half]
        lag_sin = np.sin(turns) * weights[:half]
        lag_table[start, :WIN, :half] = lag_cos
        lag_table[start, :WIN, rows : rows + half] = -lag_sin
        lag_table[start, WIN:, :half] = lag_sin
        lag_table[start, WIN:, rows : rows + half] = lag_cos
    span = starts + WIN
    lags = np.arange(span) - SHIFT - WIN // 2
    turns = full_turn * (np.outer(positions, lags) % block_size) / block_size
    span_table = np.zeros((2 * block_size, LANES))
    span_table[:block_size, :span] = np.cos(turns)
    span_table[block_size:, :span] = -np.sin(turns)
    return tuple(
        jnp.asarray(table, jnp.bfloat16) for table in (row_table, col_table, lag_table, span_table)
    )


def tap_constants():
    offsets = np.arange(TAPS) - (TAPS // 2 - 1)
    spots = offsets[None, :] - np.arange(SUB)[:, None] / SUB
    raw_taps = np.sinc(spots) * np.sinc(spots / (TAPS // 2))
    taps = raw_taps / raw_taps.sum(axis=-1, keepdims=True)
    table = np.zeros((SUB, EDGE, LANES))
    for row in range(EDGE):
        table[:, row, row : row + TAPS] = taps
    return jnp.asarray(table, jnp.float32)


def band_groups(head, shift, lane):
    start = shift + (LANES - (TAPS // 2 - 1))
    head = pltpu.roll(head, start, 1).astype(jnp.bfloat16)
    groups = [head] + [pltpu.roll(head, step, 1) for step in range(EDGE, LANES, EDGE)]
    zero = jnp.zeros_like(head)
    low = lane < LANES // 2
    before, after = jnp.where(low, zero, groups[0]), jnp.where(low, groups[-1], zero)
    middle = [jnp.where(low, groups[0], zero), *groups[1:-1], jnp.where(low, zero, groups[-1])]
    return middle, before, after


def warp_kernel(
    vols,
    down,
    across,
    block,
    own,
    core_ref,
    codes_ref,
    other_codes_ref,
    taps_ref,
    mid_ref,
    above_ref,
    below_ref,
    other_mid_ref,
    other_above_ref,
    other_below_ref,
    out_ref,
):
    band = pl.program_id(0)
    lane = lax.broadcasted_iota(jnp.int32, (EDGE, LANES), 1)
    tall_lane = lax.broadcasted_iota(jnp.int32, (block + 2 * EDGE, LANES), 1)
    zero = jnp.zeros((EDGE, LANES), jnp.bfloat16)
    no_tile = jnp.zeros((block + 2 * EDGE, block), jnp.bfloat16)
    volumes = [(codes_ref, mid_ref, above_ref, below_ref, v) for v in range(vols)]
    volumes += [
        (other_codes_ref, other_mid_ref, other_above_ref, other_below_ref, v) for v in range(vols)
    ]

    def tile(volume, at):
        _, mid, above, below, v = volume
        lanes = pl.ds(pl.multiple_of(at * block, block), block)
        above = jnp.where(band > 0, above[v, :, lanes], zero)
        below = jnp.where(band < down - 1, below[v, :, lanes], zero)
        return jnp.concatenate([mid[v, :, lanes], below, above], axis=0)

    for count in range(across // 2):
        at = (2 * (count // own) + core_ref[0]) * own + count % own
        index = band * across + at
        row_tiles, first_edge, last_edge = [], [], []
        partials, edges = [], []
        for order, volume in enumerate(volumes):
            codes, v = volume[0], volume[-1]
            row_code = codes[v, 0, index]
            col_code = codes[v, 1, index]
            middle, before, after = band_groups(taps_ref[col_code & (SUB - 1)], col_code >> 4, lane)
            col_band = jnp.concatenate(
                [
                    jnp.concatenate(middle, axis=0),
                    jnp.concatenate([before] + [zero] * (block // EDGE - 2) + [after], axis=0),
                ],
                axis=1,
            )
            left = jnp.where(at > 0, tile(volume, jnp.maximum(at - 1, 0)), no_tile)
            right = jnp.where(
                at < across - 1, tile(volume, jnp.minimum(at + 1, across - 1)), no_tile
            )
            sides = jnp.where(tall_lane < LANES // 2, right, left)
            partial = lax.dot_general(
                jnp.concatenate([tile(volume, at), sides], axis=1),
                col_band,
                (((1,), (1,)), ((), ())),
                preferred_element_type=jnp.float32,
            ).astype(jnp.bfloat16)
            partials.append(partial[:block])
            edges.append(partial[block:])
            middle, before, after = band_groups(taps_ref[row_code & (SUB - 1)], row_code >> 4, lane)
            row_tiles.append(jnp.concatenate(middle, axis=0))
            place = 2 * EDGE * order % LANES
            first_edge.append(pltpu.roll(before, (place + 2 * EDGE) % LANES, 1))
            last_edge.append(pltpu.roll(after, place, 1) if place else after)
        per_tile = LANES // (2 * EDGE)
        for first_order in range(0, 2 * vols, per_tile):
            first, last = first_edge[first_order], last_edge[first_order]
            for more in range(first_order + 1, min(first_order + per_tile, 2 * vols)):
                first, last = first + first_edge[more], last + last_edge[more]
            row_tiles.append(
                jnp.concatenate([first] + [zero] * (block // EDGE - 2) + [last], axis=0)
            )
        depth = 2 * vols * (block + 2 * EDGE)
        total = jnp.dot(
            jnp.concatenate(row_tiles, axis=1)[:, :depth],
            jnp.concatenate(partials + edges, axis=0),
            preferred_element_type=jnp.float32,
        )
        out_ref[count] = total.astype(jnp.bfloat16)


def warp_sums(core, codes, other_codes, frames, other_frames, block, own):
    vols, rows, cols = frames.shape
    down, across = rows // block, cols // block
    steps = block // EDGE
    taps = tap_constants()
    smem = pl.BlockSpec(memory_space=pltpu.SMEM)
    frame_specs = [
        pl.BlockSpec((vols, block, cols), lambda band: (0, band, 0)),
        pl.BlockSpec((vols, EDGE, cols), lambda band: (0, jnp.maximum(band * steps - 1, 0), 0)),
        pl.BlockSpec(
            (vols, EDGE, cols),
            lambda band: (0, jnp.minimum((band + 1) * steps, down * steps - 1), 0),
        ),
    ]
    return pl.pallas_call(
        functools.partial(warp_kernel, vols, down, across, block, own),
        grid=(down,),
        out_shape=jax.ShapeDtypeStruct((down * across // 2, block, block), jnp.bfloat16),
        in_specs=[
            smem,
            smem,
            smem,
            pl.BlockSpec(taps.shape, lambda band: (0, 0, 0)),
            *frame_specs,
            *frame_specs,
        ],
        out_specs=pl.BlockSpec((across // 2, block, block), lambda band: (band, 0, 0)),
        compiler_params=pltpu.CompilerParams(vmem_limit_bytes=VMEM_LIMIT),
        cost_estimate=pl.CostEstimate(
            flops=2 * vols * rows * cols * block * 4,
            bytes_accessed=vols * rows * cols * 4 + rows * cols,
            transcendentals=0,
        ),
        name="warp",
    )(core, codes, other_codes, taps, *([frames] * 3), *([other_frames] * 3))


def spectrum_kernel(
    vols,
    down,
    across,
    block,
    own,
    planes,
    core_ref,
    codes_ref,
    other_codes_ref,
    row_ref,
    col_ref,
    lag_ref,
    span_ref,
    frames_ref,
    other_frames_ref,
    template_ref,
    out_ref,
    cross,
    sums,
    found,
):
    band = pl.program_id(0)
    core = core_ref[0]
    row_table = row_ref[...]
    col_table = col_ref[...]
    half = col_table.shape[0] // 2
    top = lax.broadcasted_iota(jnp.int32, (8, LANES), 0) == 0
    volumes = [(codes_ref, frames_ref, v) for v in range(vols)]
    volumes += [(other_codes_ref, other_frames_ref, v) for v in range(vols)]
    many = len(volumes)
    local = across // 2
    places = [(2 * (count // own) + core) * own + count % own for count in range(local)]

    for pair in range(local // 2):
        pair_places = places[2 * pair : 2 * pair + 2]
        parts = [template_ref[2 * pair], template_ref[2 * pair + 1]]
        for _, frames, v in volumes:
            for at in pair_places:
                parts.append(frames[v, :, pl.ds(pl.multiple_of(at * block, block), block)])
        rows = jnp.dot(
            jnp.concatenate(parts, axis=0), row_table, preferred_element_type=jnp.float32
        ).astype(jnp.bfloat16)
        spectra = []
        for source in range(many + 1):
            stacks = []
            for side in range(2):
                at = (2 * source + side) * block
                one = rows[at : at + block]
                stacks.append(jnp.concatenate([one[:, :block], one[:, block:]], axis=0))
            spectra.append(
                jnp.dot(
                    col_table, jnp.concatenate(stacks, axis=1), preferred_element_type=jnp.float32
                )
            )
        temp = spectra[0].astype(jnp.bfloat16).astype(jnp.float32)
        for order in range(many):
            for side in range(2):
                lanes = slice(side * block, (side + 1) * block)
                one = (2 * pair + side) * many + order
                total = jnp.zeros((8, LANES), jnp.float32)
                for row in range(0, half, 8):
                    temp_real = temp[row : row + 8, lanes]
                    temp_imag = temp[half + row : half + row + 8, lanes]
                    real = spectra[order + 1][row : row + 8, lanes]
                    imag = spectra[order + 1][half + row : half + row + 8, lanes]
                    cross_real = real * temp_real + imag * temp_imag
                    cross_imag = imag * temp_real - real * temp_imag
                    power = cross_real * cross_real + cross_imag * cross_imag
                    magnitude = power * lax.rsqrt(jnp.maximum(power, 1e-36))
                    cross[one, row : row + 8, :] = cross_real
                    cross[one, half + row : half + row + 8, :] = cross_imag
                    cross[one, 2 * half + row : 2 * half + row + 8, :] = magnitude
                    if row == 0:
                        total = jnp.where(top, magnitude, 2.0 * magnitude)
                    elif row == block // 2:
                        total += magnitude
                    else:
                        total += 2.0 * magnitude
                sums[one] = jnp.sum(total, axis=0, keepdims=True)

    means = jnp.sum(sums[...], axis=2, keepdims=True) * (1.0 / (block * block)) + 1e-06
    lag_sums = []
    for one in range(local * many):
        codes, _, v = volumes[one % many]
        index = band * across + places[one // many]
        scale = pl.reciprocal(cross[one, 2 * half :, :] + means[one], approx=True)
        norm = jnp.concatenate(
            [
                (cross[one, :half, :] * scale).astype(jnp.bfloat16),
                (cross[one, half : 2 * half, :] * scale).astype(jnp.bfloat16),
            ],
            axis=0,
        )
        row_shift = codes[v, 0, index] >> 4
        lag_rows = jnp.dot(
            lag_ref[row_shift + SHIFT], norm, preferred_element_type=jnp.float32
        ).astype(jnp.bfloat16)
        lag_sums.append(jnp.concatenate([lag_rows[:WIN], lag_rows[WIN:]], axis=1))
    lags = jnp.dot(
        jnp.concatenate(lag_sums, axis=0), span_ref[...], preferred_element_type=jnp.float32
    )
    for one in range(local * many):
        codes, _, v = volumes[one % many]
        index = band * across + places[one // many]
        col_shift = codes[v, 1, index] >> 4
        start = pl.multiple_of((band * local + one // many) * WIN, WIN)
        found[one % many, pl.ds(start, WIN), :] = pltpu.roll(
            lags[one * WIN : (one + 1) * WIN], LANES - SHIFT - col_shift, 1
        )

    @pl.when(band == down - 1)
    def _():
        share = down * local // planes
        per_tile = LANES // WIN
        lane = lax.broadcasted_iota(jnp.int32, (share, LANES), 1) // WIN
        for order in range(many):
            owner = core if order < vols else 1 - core
            for plane in range(planes):
                for tile in range(WIN // per_tile):
                    total = jnp.zeros((share, LANES), jnp.float32)
                    for part in range(per_tile):
                        start = plane * share * WIN + tile * per_tile + part
                        one = found[order, pl.ds(start, share, stride=WIN), :]
                        if part:
                            one = pltpu.roll(one, part * WIN, 1)
                        total = jnp.where(lane == part, one, total)
                    lanes = slice(tile * LANES, (tile + 1) * LANES)
                    out_ref[owner * planes + plane, order % vols, :, lanes] = total * (1.0 / block)


def lag_windows(core, codes, other_codes, frames, other_frames, template, planes, own):
    vols, rows, cols = frames.shape
    block = template.shape[-1]
    down, across = rows // block, cols // block
    tables = dft_constants(block)
    half = tables[1].shape[0] // 2
    whole = [
        pl.BlockSpec(table.shape, functools.partial(lambda dims, band: (0,) * dims, table.ndim))
        for table in tables
    ]
    smem = pl.BlockSpec(memory_space=pltpu.SMEM)
    frame_spec = pl.BlockSpec((vols, block, cols), lambda band: (0, band, 0))
    local = down * across // 2
    out_dims = (2 * planes, vols, local // planes, WIN * WIN)
    return pl.pallas_call(
        functools.partial(spectrum_kernel, vols, down, across, block, own, planes),
        grid=(down,),
        out_shape=jax.ShapeDtypeStruct(out_dims, jnp.float32),
        in_specs=[
            smem,
            smem,
            smem,
            *whole,
            frame_spec,
            frame_spec,
            pl.BlockSpec((across // 2, block, block), lambda band: (band, 0, 0)),
        ],
        out_specs=pl.BlockSpec(out_dims, lambda band: (0, 0, 0, 0)),
        scratch_shapes=[
            pltpu.VMEM((vols * across, 3 * half, LANES), jnp.float32),
            pltpu.VMEM((vols * across, 1, LANES), jnp.float32),
            pltpu.VMEM((2 * vols, local * WIN, LANES), jnp.float32),
        ],
        compiler_params=pltpu.CompilerParams(vmem_limit_bytes=VMEM_LIMIT),
        cost_estimate=pl.CostEstimate(
            flops=2 * 3 * rows * cols * block * 4,
            bytes_accessed=vols * rows * cols * 4 + rows * cols,
            transcendentals=0,
        ),
        name="lag_windows",
    )(core, codes, other_codes, *tables, frames, other_frames, template)


def on_device(frames, template, shift_codes):
    vol_dev, pl_dev, img_rows, img_cols = frames.shape
    own, block = template.shape[0], template.shape[-1]
    chips = lax.axis_size("chip")
    planes = lax.axis_size("plane")
    share = 2 * chips * own // planes
    core = lax.axis_index("core").reshape(1)
    swap = [(0, 1), (1, 0)]
    other_frames = lax.ppermute(frames, "core", swap)
    other_codes = lax.ppermute(shift_codes, "core", swap)
    copies = jnp.broadcast_to(template[None], (chips, *template.shape))
    gathered = lax.all_to_all(copies, "chip", 0, 0, tiled=True)
    gathered = gathered.reshape(chips * own, pl_dev, block, block)
    moved, window = [], 0.0
    for p in range(pl_dev):
        work = (core, shift_codes, other_codes, frames[:, p], other_frames[:, p])
        warped = warp_sums(*work, block, own).reshape(chips, own, block, block)
        moved.append(lax.all_to_all(warped, "chip", 0, 0, tiled=True))
        window = window + lag_windows(*work, gathered[:, p], planes, own)
    window = lax.all_to_all(window, ("core", "plane"), 0, 0, tiled=True)
    window = window.reshape(2, planes, vol_dev, share // (2 * own), own, WIN * WIN)
    window = jnp.sum(window, axis=1)
    correlation = window.transpose(1, 2, 0, 3, 4).reshape(vol_dev, share, WIN * WIN)
    volumes = vol_dev * chips * 2
    sums = [jnp.sum(one.astype(jnp.float32), axis=0) for one in moved]
    new_template = jnp.stack(sums, axis=1) * (1.0 / volumes)
    return (correlation, new_template)


def solution(mesh):
    devices = mesh.devices.reshape(-1, 2, mesh.shape["plane"])
    split = jax.sharding.Mesh(devices, ("chip", "core", "plane"))
    vols = ("chip", "core")
    in_specs = (P(vols, "plane", None, None), P(vols, "plane", None, None), P(vols, None, None))
    out_specs = (P(vols, "plane", None), P(vols, "plane", None, None))
    return jax.shard_map(
        on_device, mesh=split, in_specs=in_specs, out_specs=out_specs, check_vma=False
    )
```

```python
import functools
import math

import jax
import jax.numpy as jnp
import numpy as np
from jax import lax
from jax.experimental import pallas as pl
from jax.experimental.pallas import tpu as pltpu
from jax.sharding import PartitionSpec as P

SHIFT = 8
WIN = 16
TAPS = 8
SUB = 16
EDGE = 16
LANES = 128
VMEM_LIMIT = 56 * 1024 * 1024

full_turn = 2.0 * math.pi


def dft_constants(block_size):
    positions = np.arange(block_size)
    angles = full_turn * (np.outer(positions, positions) % block_size) / block_size
    cosine = np.cos(angles)
    sine = -np.sin(angles)
    half = block_size // 2 + 1
    rows = -(-half // 8) * 8
    row_table = np.concatenate([cosine, sine], axis=1)
    col_table = np.zeros((2 * rows, 2 * block_size))
    col_table[:half] = np.concatenate([cosine[:half], -sine[:half]], axis=1)
    col_table[rows : rows + half] = np.concatenate([sine[:half], cosine[:half]], axis=1)
    weights = np.zeros((rows,))
    weights[:half] = 2.0
    weights[0] = weights[half - 1] = 1.0
    starts = 2 * SHIFT
    lag_table = np.zeros((starts, 2 * WIN, 2 * rows))
    for start in range(starts):
        lags = start - SHIFT - WIN // 2 + np.arange(WIN)
        turns = full_turn * (np.outer(lags, positions[:half]) % block_size) / block_size
        lag_cos = np.cos(turns) * weights[:half]
        lag_sin = np.sin(turns) * weights[:half]
        lag_table[start, :WIN, :half] = lag_cos
        lag_table[start, :WIN, rows : rows + half] = -lag_sin
        lag_table[start, WIN:, :half] = lag_sin
        lag_table[start, WIN:, rows : rows + half] = lag_cos
    span = starts + WIN
    lags = np.arange(span) - SHIFT - WIN // 2
    turns = full_turn * (np.outer(positions, lags) % block_size) / block_size
    span_table = np.zeros((2 * block_size, LANES))
    span_table[:block_size, :span] = np.cos(turns)
    span_table[block_size:, :span] = -np.sin(turns)
    return tuple(
        jnp.asarray(table, jnp.bfloat16) for table in (row_table, col_table, lag_table, span_table)
    )


def tap_constants():
    offsets = np.arange(TAPS) - (TAPS // 2 - 1)
    spots = offsets[None, :] - np.arange(SUB)[:, None] / SUB
    raw_taps = np.sinc(spots) * np.sinc(spots / (TAPS // 2))
    taps = raw_taps / raw_taps.sum(axis=-1, keepdims=True)
    table = np.zeros((SUB, EDGE, LANES))
    for row in range(EDGE):
        table[:, row, row : row + TAPS] = taps
    return jnp.asarray(table, jnp.float32)


def band_groups(head, shift, lane):
    start = shift + (LANES - (TAPS // 2 - 1))
    head = pltpu.roll(head, start, 1).astype(jnp.bfloat16)
    groups = [head] + [pltpu.roll(head, step, 1) for step in range(EDGE, LANES, EDGE)]
    zero = jnp.zeros_like(head)
    low = lane < LANES // 2
    before, after = jnp.where(low, zero, groups[0]), jnp.where(low, groups[-1], zero)
    middle = [jnp.where(low, groups[0], zero), *groups[1:-1], jnp.where(low, zero, groups[-1])]
    return middle, before, after


def local_places(band, across, own, core, row):
    return [
        (2 * (2 * group + row) + core) * own + one
        for group in range(across // (4 * own))
        for one in range(own)
    ]


def warp_kernel(
    vols,
    down,
    across,
    block,
    own,
    place_ref,
    codes_ref,
    other_codes_ref,
    taps_ref,
    mid_ref,
    above_ref,
    below_ref,
    other_mid_ref,
    other_above_ref,
    other_below_ref,
    after_ref,
    out_ref,
):
    band = pl.program_id(0)
    lane = lax.broadcasted_iota(jnp.int32, (EDGE, LANES), 1)
    tall_lane = lax.broadcasted_iota(jnp.int32, (block + 2 * EDGE, LANES), 1)
    zero = jnp.zeros((EDGE, LANES), jnp.bfloat16)
    no_tile = jnp.zeros((block + 2 * EDGE, block), jnp.bfloat16)
    volumes = [(codes_ref, mid_ref, above_ref, below_ref, v) for v in range(vols)]
    volumes += [
        (other_codes_ref, other_mid_ref, other_above_ref, other_below_ref, v) for v in range(vols)
    ]

    def tile(volume, at):
        _, mid, above, below, v = volume
        lanes = pl.ds(pl.multiple_of(at * block, block), block)
        above = jnp.where(band > 0, above[v, :, lanes], zero)
        below = jnp.where(band < down - 1, below[v, :, lanes], zero)
        return jnp.concatenate([mid[v, :, lanes], below, above], axis=0)

    for count, at in enumerate(local_places(band, across, own, place_ref[0], place_ref[1])):
        index = band * across + at
        row_tiles, first_edge, last_edge = [], [], []
        partials, edges = [], []
        for order, volume in enumerate(volumes):
            codes, v = volume[0], volume[-1]
            row_code = codes[v, 0, index]
            col_code = codes[v, 1, index]
            middle, before, after = band_groups(taps_ref[col_code & (SUB - 1)], col_code >> 4, lane)
            col_band = jnp.concatenate(
                [
                    jnp.concatenate(middle, axis=0),
                    jnp.concatenate([before] + [zero] * (block // EDGE - 2) + [after], axis=0),
                ],
                axis=1,
            )
            left = jnp.where(at > 0, tile(volume, jnp.maximum(at - 1, 0)), no_tile)
            right = jnp.where(
                at < across - 1, tile(volume, jnp.minimum(at + 1, across - 1)), no_tile
            )
            sides = jnp.where(tall_lane < LANES // 2, right, left)
            partial = lax.dot_general(
                jnp.concatenate([tile(volume, at), sides], axis=1),
                col_band,
                (((1,), (1,)), ((), ())),
                preferred_element_type=jnp.float32,
            ).astype(jnp.bfloat16)
            partials.append(partial[:block])
            edges.append(partial[block:])
            middle, before, after = band_groups(taps_ref[row_code & (SUB - 1)], row_code >> 4, lane)
            row_tiles.append(jnp.concatenate(middle, axis=0))
            place = 2 * EDGE * order % LANES
            first_edge.append(pltpu.roll(before, (place + 2 * EDGE) % LANES, 1))
            last_edge.append(pltpu.roll(after, place, 1) if place else after)
        per_tile = LANES // (2 * EDGE)
        for first_order in range(0, 2 * vols, per_tile):
            first, last = first_edge[first_order], last_edge[first_order]
            for more in range(first_order + 1, min(first_order + per_tile, 2 * vols)):
                first, last = first + first_edge[more], last + last_edge[more]
            row_tiles.append(
                jnp.concatenate([first] + [zero] * (block // EDGE - 2) + [last], axis=0)
            )
        depth = 2 * vols * (block + 2 * EDGE)
        total = jnp.dot(
            jnp.concatenate(row_tiles, axis=1)[:, :depth],
            jnp.concatenate(partials + edges, axis=0),
            preferred_element_type=jnp.float32,
        )
        out_ref[count] = total.astype(jnp.bfloat16)


def warp_sums(place, codes, other_codes, frames, other_frames, after, block, own):
    vols, rows, cols = frames.shape
    down, across = rows // block, cols // block
    steps = block // EDGE
    taps = tap_constants()
    smem = pl.BlockSpec(memory_space=pltpu.SMEM)
    frame_specs = [
        pl.BlockSpec((vols, block, cols), lambda band: (0, band, 0)),
        pl.BlockSpec((vols, EDGE, cols), lambda band: (0, jnp.maximum(band * steps - 1, 0), 0)),
        pl.BlockSpec(
            (vols, EDGE, cols),
            lambda band: (0, jnp.minimum((band + 1) * steps, down * steps - 1), 0),
        ),
    ]
    return pl.pallas_call(
        functools.partial(warp_kernel, vols, down, across, block, own),
        grid=(down,),
        out_shape=jax.ShapeDtypeStruct((down * across // 4, block, block), jnp.bfloat16),
        in_specs=[
            smem,
            smem,
            smem,
            pl.BlockSpec(taps.shape, lambda band: (0, 0, 0)),
            *frame_specs,
            *frame_specs,
            pl.BlockSpec(memory_space=pl.ANY),
        ],
        out_specs=pl.BlockSpec((across // 4, block, block), lambda band: (band, 0, 0)),
        compiler_params=pltpu.CompilerParams(vmem_limit_bytes=VMEM_LIMIT),
        cost_estimate=pl.CostEstimate(
            flops=2 * vols * rows * cols * block * 2,
            bytes_accessed=vols * rows * cols * 4 + rows * cols // 2,
            transcendentals=0,
        ),
        name="warp",
    )(place, codes, other_codes, taps, *([frames] * 3), *([other_frames] * 3), after)


def spectrum_kernel(
    vols,
    down,
    across,
    block,
    own,
    planes,
    place_ref,
    codes_ref,
    other_codes_ref,
    row_ref,
    col_ref,
    lag_ref,
    span_ref,
    frames_ref,
    other_frames_ref,
    template_ref,
    after_ref,
    out_ref,
    cross,
    sums,
    found,
):
    band = pl.program_id(0)
    core = place_ref[0]
    row_table = row_ref[...]
    col_table = col_ref[...]
    half = col_table.shape[0] // 2
    top = lax.broadcasted_iota(jnp.int32, (8, LANES), 0) == 0
    volumes = [(codes_ref, frames_ref, v) for v in range(vols)]
    volumes += [(other_codes_ref, other_frames_ref, v) for v in range(vols)]
    many = len(volumes)
    local = across // 4
    places = local_places(band, across, own, core, place_ref[1])

    for pair in range(local // 2):
        pair_places = places[2 * pair : 2 * pair + 2]
        parts = [template_ref[2 * pair], template_ref[2 * pair + 1]]
        for _, frames, v in volumes:
            for at in pair_places:
                parts.append(frames[v, :, pl.ds(pl.multiple_of(at * block, block), block)])
        rows = jnp.dot(
            jnp.concatenate(parts, axis=0), row_table, preferred_element_type=jnp.float32
        ).astype(jnp.bfloat16)
        spectra = []
        for source in range(many + 1):
            stacks = []
            for side in range(2):
                at = (2 * source + side) * block
                one = rows[at : at + block]
                stacks.append(jnp.concatenate([one[:, :block], one[:, block:]], axis=0))
            spectra.append(
                jnp.dot(
                    col_table, jnp.concatenate(stacks, axis=1), preferred_element_type=jnp.float32
                )
            )
        temp = spectra[0].astype(jnp.bfloat16).astype(jnp.float32)
        for order in range(many):
            for side in range(2):
                lanes = slice(side * block, (side + 1) * block)
                one = (2 * pair + side) * many + order
                total = jnp.zeros((8, LANES), jnp.float32)
                for row in range(0, half, 8):
                    temp_real = temp[row : row + 8, lanes]
                    temp_imag = temp[half + row : half + row + 8, lanes]
                    real = spectra[order + 1][row : row + 8, lanes]
                    imag = spectra[order + 1][half + row : half + row + 8, lanes]
                    cross_real = real * temp_real + imag * temp_imag
                    cross_imag = imag * temp_real - real * temp_imag
                    power = cross_real * cross_real + cross_imag * cross_imag
                    magnitude = power * lax.rsqrt(jnp.maximum(power, 1e-36))
                    cross[one, row : row + 8, :] = cross_real
                    cross[one, half + row : half + row + 8, :] = cross_imag
                    cross[one, 2 * half + row : 2 * half + row + 8, :] = magnitude
                    if row == 0:
                        total = jnp.where(top, magnitude, 2.0 * magnitude)
                    elif row == block // 2:
                        total += magnitude
                    else:
                        total += 2.0 * magnitude
                sums[one] = jnp.sum(total, axis=0, keepdims=True)

    means = jnp.sum(sums[...], axis=2, keepdims=True) * (1.0 / (block * block)) + 1e-06
    lag_sums = []
    for one in range(local * many):
        codes, _, v = volumes[one % many]
        index = band * across + places[one // many]
        scale = pl.reciprocal(cross[one, 2 * half :, :] + means[one], approx=True)
        norm = jnp.concatenate(
            [
                (cross[one, :half, :] * scale).astype(jnp.bfloat16),
                (cross[one, half : 2 * half, :] * scale).astype(jnp.bfloat16),
            ],
            axis=0,
        )
        row_shift = codes[v, 0, index] >> 4
        lag_rows = jnp.dot(
            lag_ref[row_shift + SHIFT], norm, preferred_element_type=jnp.float32
        ).astype(jnp.bfloat16)
        lag_sums.append(jnp.concatenate([lag_rows[:WIN], lag_rows[WIN:]], axis=1))
    lags = jnp.dot(
        jnp.concatenate(lag_sums, axis=0), span_ref[...], preferred_element_type=jnp.float32
    )
    for one in range(local * many):
        codes, _, v = volumes[one % many]
        index = band * across + places[one // many]
        col_shift = codes[v, 1, index] >> 4
        start = pl.multiple_of((band * local + one // many) * WIN, WIN)
        found[one % many, pl.ds(start, WIN), :] = pltpu.roll(
            lags[one * WIN : (one + 1) * WIN], LANES - SHIFT - col_shift, 1
        )

    @pl.when(band == down - 1)
    def _():
        share = down * local // planes
        per_tile = LANES // WIN
        lane = lax.broadcasted_iota(jnp.int32, (share, LANES), 1) // WIN
        for order in range(many):
            owner = core if order < vols else 1 - core
            for plane in range(planes):
                for tile in range(WIN // per_tile):
                    total = jnp.zeros((share, LANES), jnp.float32)
                    for part in range(per_tile):
                        start = plane * share * WIN + tile * per_tile + part
                        one = found[order, pl.ds(start, share, stride=WIN), :]
                        if part:
                            one = pltpu.roll(one, part * WIN, 1)
                        total = jnp.where(lane == part, one, total)
                    lanes = slice(tile * LANES, (tile + 1) * LANES)
                    out_ref[owner * planes + plane, order % vols, :, lanes] = total * (1.0 / block)


def lag_windows(place, codes, other_codes, frames, other_frames, template, after, planes, own):
    vols, rows, cols = frames.shape
    block = template.shape[-1]
    down, across = rows // block, cols // block
    tables = dft_constants(block)
    half = tables[1].shape[0] // 2
    whole = [
        pl.BlockSpec(table.shape, functools.partial(lambda dims, band: (0,) * dims, table.ndim))
        for table in tables
    ]
    smem = pl.BlockSpec(memory_space=pltpu.SMEM)
    frame_spec = pl.BlockSpec((vols, block, cols), lambda band: (0, band, 0))
    local = down * across // 4
    out_dims = (2 * planes, vols, local // planes, WIN * WIN)
    return pl.pallas_call(
        functools.partial(spectrum_kernel, vols, down, across, block, own, planes),
        grid=(down,),
        out_shape=jax.ShapeDtypeStruct(out_dims, jnp.float32),
        in_specs=[
            smem,
            smem,
            smem,
            *whole,
            frame_spec,
            frame_spec,
            pl.BlockSpec((across // 4, block, block), lambda band: (band, 0, 0)),
            pl.BlockSpec(memory_space=pl.ANY),
        ],
        out_specs=pl.BlockSpec(out_dims, lambda band: (0, 0, 0, 0)),
        scratch_shapes=[
            pltpu.VMEM((vols * across // 2, 3 * half, LANES), jnp.float32),
            pltpu.VMEM((vols * across // 2, 1, LANES), jnp.float32),
            pltpu.VMEM((2 * vols, local * WIN, LANES), jnp.float32),
        ],
        compiler_params=pltpu.CompilerParams(vmem_limit_bytes=VMEM_LIMIT),
        cost_estimate=pl.CostEstimate(
            flops=2 * 3 * rows * cols * block * 4,
            bytes_accessed=vols * rows * cols * 4 + rows * cols,
            transcendentals=0,
        ),
        name="lag_windows",
    )(place, codes, other_codes, *tables, frames, other_frames, template, after)


def on_device(frames, template, shift_codes):
    vol_dev, pl_dev, img_rows, img_cols = frames.shape
    own, block = template.shape[0], template.shape[-1]
    depth = lax.axis_size("z")
    planes = lax.axis_size("plane")
    share = 4 * depth * own // planes
    core, row = lax.axis_index("core"), lax.axis_index("y")
    here, there = jnp.stack([core, row]), jnp.stack([core, 1 - row])
    swap = [(0, 1), (1, 0)]
    other_frames = lax.ppermute(frames, "core", swap)
    other_codes = lax.ppermute(shift_codes, "core", swap)
    copies = jnp.broadcast_to(template[None], (depth, *template.shape))
    near = lax.all_to_all(copies, "z", 0, 0, tiled=True)
    far = lax.ppermute(near, "y", swap)
    near = near.reshape(depth * own, pl_dev, block, block)
    far = far.reshape(depth * own, pl_dev, block, block)
    moved, window = [], 0.0
    for p in range(pl_dev):
        work = (shift_codes, other_codes, frames[:, p], other_frames[:, p])
        far_sums = warp_sums(there, *work, template, block, own)
        taken = lax.ppermute(far_sums, "y", swap)
        near_sums = warp_sums(here, *work, far_sums, block, own)
        sums = near_sums.astype(jnp.float32) + taken.astype(jnp.float32)
        sums = sums.astype(jnp.bfloat16).reshape(depth, own, block, block)
        moved.append(lax.all_to_all(sums, "z", 0, 0, tiled=True))
        near_window = lag_windows(here, *work, near[:, p], sums, planes, own)
        far_window = lag_windows(there, *work, far[:, p], near_window, planes, own)
        window = window + jnp.stack([near_window, far_window], axis=1)
    window = lax.all_to_all(window, ("core", "plane"), 0, 0, tiled=True)
    window = window.reshape(2, planes, 2, vol_dev, depth // planes, own, WIN * WIN)
    window = jnp.sum(window, axis=1)
    window = jnp.where(row == 0, window, window[:, ::-1])
    correlation = window.transpose(2, 3, 1, 0, 4, 5).reshape(vol_dev, share, WIN * WIN)
    volumes = vol_dev * depth * 4
    sums = [jnp.sum(one.astype(jnp.float32), axis=0) for one in moved]
    new_template = jnp.stack(sums, axis=1) * (1.0 / volumes)
    return (correlation, new_template)


def solution(mesh):
    devices = mesh.devices.reshape(-1, 2, 2, mesh.shape["plane"])
    split = jax.sharding.Mesh(devices, ("z", "y", "core", "plane"))
    vols = ("z", "y", "core")
    in_specs = (P(vols, "plane", None, None), P(vols, "plane", None, None), P(vols, None, None))
    out_specs = (P(vols, "plane", None), P(vols, "plane", None, None))
    return jax.shard_map(
        on_device, mesh=split, in_specs=in_specs, out_specs=out_specs, check_vma=False
    )
```

```python
import functools
import math

import jax
import jax.numpy as jnp
import numpy as np
from jax import lax
from jax.experimental import pallas as pl
from jax.experimental.pallas import tpu as pltpu
from jax.sharding import PartitionSpec as P

SHIFT = 8
WIN = 16
TAPS = 8
SUB = 16
EDGE = 16
LANES = 128
VMEM_LIMIT = 24 * 1024 * 1024

full_turn = 2.0 * math.pi


def dft_constants(block_size):
    positions = np.arange(block_size)
    angles = full_turn * (np.outer(positions, positions) % block_size) / block_size
    cosine = np.cos(angles)
    sine = -np.sin(angles)
    half = block_size // 2 + 1
    rows = -(-half // 8) * 8
    row_table = np.concatenate([cosine, sine], axis=1)
    col_table = np.zeros((2 * rows, 2 * block_size))
    col_table[:half] = np.concatenate([cosine[:half], -sine[:half]], axis=1)
    col_table[rows : rows + half] = np.concatenate([sine[:half], cosine[:half]], axis=1)
    weights = np.zeros((rows,))
    weights[:half] = 2.0
    weights[0] = weights[half - 1] = 1.0
    starts = 2 * SHIFT
    lag_table = np.zeros((starts, 2 * WIN, 2 * rows))
    for start in range(starts):
        lags = start - SHIFT - WIN // 2 + np.arange(WIN)
        turns = full_turn * (np.outer(lags, positions[:half]) % block_size) / block_size
        lag_cos = np.cos(turns) * weights[:half]
        lag_sin = np.sin(turns) * weights[:half]
        lag_table[start, :WIN, :half] = lag_cos
        lag_table[start, :WIN, rows : rows + half] = -lag_sin
        lag_table[start, WIN:, :half] = lag_sin
        lag_table[start, WIN:, rows : rows + half] = lag_cos
    span = starts + WIN
    lags = np.arange(span) - SHIFT - WIN // 2
    turns = full_turn * (np.outer(positions, lags) % block_size) / block_size
    span_table = np.zeros((2 * block_size, LANES))
    span_table[:block_size, :span] = np.cos(turns)
    span_table[block_size:, :span] = -np.sin(turns)
    return tuple(
        jnp.asarray(table, jnp.bfloat16) for table in (row_table, col_table, lag_table, span_table)
    )


def tap_constants():
    offsets = np.arange(TAPS) - (TAPS // 2 - 1)
    spots = offsets[None, :] - np.arange(SUB)[:, None] / SUB
    raw_taps = np.sinc(spots) * np.sinc(spots / (TAPS // 2))
    taps = raw_taps / raw_taps.sum(axis=-1, keepdims=True)
    table = np.zeros((SUB, EDGE, LANES))
    for row in range(EDGE):
        table[:, row, row : row + TAPS] = taps
    return jnp.asarray(table, jnp.float32)


def band_groups(head, shift, lane):
    start = shift + (LANES - (TAPS // 2 - 1))
    head = pltpu.roll(head, start, 1).astype(jnp.bfloat16)
    groups = [head] + [pltpu.roll(head, step, 1) for step in range(EDGE, LANES, EDGE)]
    zero = jnp.zeros_like(head)
    low = lane < LANES // 2
    before, after = jnp.where(low, zero, groups[0]), jnp.where(low, groups[-1], zero)
    middle = [jnp.where(low, groups[0], zero), *groups[1:-1], jnp.where(low, zero, groups[-1])]
    return middle, before, after


def step_places(place_ref, across, own):
    z = place_ref[0] ^ pl.program_id(0)
    places = []
    for other in range(2):
        for one in range(own):
            index = ((2 * z + (place_ref[1] ^ other)) * 2 + place_ref[2]) * own + one
            places.append((index, index % across))
    return places


def step_band(place_ref, step, across, own):
    return (place_ref[0] ^ step) * (4 * own) // across


def warp_kernel(
    vols,
    down,
    across,
    block,
    own,
    place_ref,
    codes_ref,
    other_codes_ref,
    taps_ref,
    mid_ref,
    above_ref,
    below_ref,
    other_mid_ref,
    other_above_ref,
    other_below_ref,
    *out_refs,
):
    step = pl.program_id(0)
    band = step_band(place_ref, step, across, own)
    lane = lax.broadcasted_iota(jnp.int32, (EDGE, LANES), 1)
    tall_lane = lax.broadcasted_iota(jnp.int32, (block + 2 * EDGE, LANES), 1)
    zero = jnp.zeros((EDGE, LANES), jnp.bfloat16)
    no_tile = jnp.zeros((block + 2 * EDGE, block), jnp.bfloat16)
    *out_refs, sums = out_refs
    volumes = [(codes_ref, mid_ref, above_ref, below_ref, v) for v in range(vols)]
    volumes += [
        (other_codes_ref, other_mid_ref, other_above_ref, other_below_ref, v) for v in range(vols)
    ]

    def tile(volume, at):
        _, mid, above, below, v = volume
        lanes = pl.ds(pl.multiple_of(at * block, block), block)
        above = jnp.where(band > 0, above[v, :, lanes], zero)
        below = jnp.where(band < down - 1, below[v, :, lanes], zero)
        return jnp.concatenate([mid[v, :, lanes], below, above], axis=0)

    for count, (index, at) in enumerate(step_places(place_ref, across, own)):
        row_tiles, first_edge, last_edge = [], [], []
        partials, edges = [], []
        for order, volume in enumerate(volumes):
            codes, v = volume[0], volume[-1]
            row_code = codes[v, 0, index]
            col_code = codes[v, 1, index]
            middle, before, after = band_groups(taps_ref[col_code & (SUB - 1)], col_code >> 4, lane)
            col_band = jnp.concatenate(
                [
                    jnp.concatenate(middle, axis=0),
                    jnp.concatenate([before] + [zero] * (block // EDGE - 2) + [after], axis=0),
                ],
                axis=1,
            )
            left = jnp.where(at > 0, tile(volume, jnp.maximum(at - 1, 0)), no_tile)
            right = jnp.where(
                at < across - 1, tile(volume, jnp.minimum(at + 1, across - 1)), no_tile
            )
            sides = jnp.where(tall_lane < LANES // 2, right, left)
            partial = lax.dot_general(
                jnp.concatenate([tile(volume, at), sides], axis=1),
                col_band,
                (((1,), (1,)), ((), ())),
                preferred_element_type=jnp.float32,
            ).astype(jnp.bfloat16)
            partials.append(partial[:block])
            edges.append(partial[block:])
            middle, before, after = band_groups(taps_ref[row_code & (SUB - 1)], row_code >> 4, lane)
            row_tiles.append(jnp.concatenate(middle, axis=0))
            place = 2 * EDGE * order % LANES
            first_edge.append(pltpu.roll(before, (place + 2 * EDGE) % LANES, 1))
            last_edge.append(pltpu.roll(after, place, 1) if place else after)
        per_tile = LANES // (2 * EDGE)
        for first_order in range(0, 2 * vols, per_tile):
            first, last = first_edge[first_order], last_edge[first_order]
            for more in range(first_order + 1, min(first_order + per_tile, 2 * vols)):
                first, last = first + first_edge[more], last + last_edge[more]
            row_tiles.append(
                jnp.concatenate([first] + [zero] * (block // EDGE - 2) + [last], axis=0)
            )
        depth = 2 * vols * (block + 2 * EDGE)
        total = jnp.dot(
            jnp.concatenate(row_tiles, axis=1)[:, :depth],
            jnp.concatenate(partials + edges, axis=0),
            preferred_element_type=jnp.float32,
        )
        sums[count] = total.astype(jnp.bfloat16)
    for at_step, out_ref in enumerate(out_refs):

        @pl.when(step == at_step)
        def _():
            out_ref[...] = sums[...]


def warp_sums(place, codes, other_codes, frames, other_frames, depth, block, own):
    vols, rows, cols = frames.shape
    down, across = rows // block, cols // block
    steps = block // EDGE
    taps = tap_constants()
    smem = pl.BlockSpec(memory_space=pltpu.SMEM)

    def above(step, place):
        return (0, jnp.maximum(step_band(place, step, across, own) * steps - 1, 0), 0)

    def below(step, place):
        last = down * steps - 1
        return (0, jnp.minimum((step_band(place, step, across, own) + 1) * steps, last), 0)

    frame_specs = [
        pl.BlockSpec(
            (vols, block, cols), lambda step, place: (0, step_band(place, step, across, own), 0)
        ),
        pl.BlockSpec((vols, EDGE, cols), above),
        pl.BlockSpec((vols, EDGE, cols), below),
    ]
    out = (2 * own, block, block)
    return pl.pallas_call(
        functools.partial(warp_kernel, vols, down, across, block, own),
        grid_spec=pltpu.PrefetchScalarGridSpec(
            num_scalar_prefetch=1,
            grid=(depth,),
            in_specs=[
                smem,
                smem,
                pl.BlockSpec(taps.shape, lambda step, place: (0, 0, 0)),
                *frame_specs,
                *frame_specs,
            ],
            out_specs=[pl.BlockSpec(out, lambda step, place: (0, 0, 0))] * depth,
            scratch_shapes=[pltpu.VMEM(out, jnp.bfloat16)],
        ),
        out_shape=[jax.ShapeDtypeStruct(out, jnp.bfloat16)] * depth,
        compiler_params=pltpu.CompilerParams(vmem_limit_bytes=VMEM_LIMIT),
        cost_estimate=pl.CostEstimate(
            flops=2 * vols * rows * cols * block * 4,
            bytes_accessed=vols * rows * cols * 4 + rows * cols,
            transcendentals=0,
        ),
        name="warp",
    )(place, codes, other_codes, taps, *([frames] * 3), *([other_frames] * 3))


def spectrum_kernel(
    vols,
    across,
    block,
    own,
    planes,
    depth,
    place_ref,
    codes_ref,
    other_codes_ref,
    row_ref,
    col_ref,
    lag_ref,
    span_ref,
    frames_ref,
    other_frames_ref,
    *refs,
):
    template_refs, out_refs = refs[:depth], refs[depth + 1 : depth + 1 + 2 * planes]
    templates, cross, sums, found, sems = refs[depth + 1 + 2 * planes :]
    step = pl.program_id(0)

    @pl.when(step == 0)
    def _():
        copies = [
            pltpu.make_async_copy(template_ref, templates.at[at], sems.at[at])
            for at, template_ref in enumerate(template_refs)
        ]
        for copy in copies:
            copy.start()
        for copy in copies:
            copy.wait()

    row_table = row_ref[...]
    col_table = col_ref[...]
    half = col_table.shape[0] // 2
    top = lax.broadcasted_iota(jnp.int32, (8, LANES), 0) == 0
    volumes = [(codes_ref, frames_ref, v) for v in range(vols)]
    volumes += [(other_codes_ref, other_frames_ref, v) for v in range(vols)]
    many = len(volumes)
    places = step_places(place_ref, across, own)
    local = len(places)

    for pair in range(local // 2):
        pair_places = places[2 * pair : 2 * pair + 2]
        parts = [templates[step, 2 * pair], templates[step, 2 * pair + 1]]
        for _, frames, v in volumes:
            for _, at in pair_places:
                parts.append(frames[v, :, pl.ds(pl.multiple_of(at * block, block), block)])
        rows = jnp.dot(
            jnp.concatenate(parts, axis=0), row_table, preferred_element_type=jnp.float32
        ).astype(jnp.bfloat16)
        spectra = []
        for source in range(many + 1):
            stacks = []
            for side in range(2):
                at = (2 * source + side) * block
                one = rows[at : at + block]
                stacks.append(jnp.concatenate([one[:, :block], one[:, block:]], axis=0))
            spectra.append(
                jnp.dot(
                    col_table, jnp.concatenate(stacks, axis=1), preferred_element_type=jnp.float32
                )
            )
        temp = spectra[0].astype(jnp.bfloat16).astype(jnp.float32)
        for order in range(many):
            for side in range(2):
                lanes = slice(side * block, (side + 1) * block)
                one = (2 * pair + side) * many + order
                total = jnp.zeros((8, LANES), jnp.float32)
                for row in range(0, half, 8):
                    temp_real = temp[row : row + 8, lanes]
                    temp_imag = temp[half + row : half + row + 8, lanes]
                    real = spectra[order + 1][row : row + 8, lanes]
                    imag = spectra[order + 1][half + row : half + row + 8, lanes]
                    cross_real = real * temp_real + imag * temp_imag
                    cross_imag = imag * temp_real - real * temp_imag
                    power = cross_real * cross_real + cross_imag * cross_imag
                    magnitude = power * lax.rsqrt(jnp.maximum(power, 1e-36))
                    cross[one, row : row + 8, :] = cross_real
                    cross[one, half + row : half + row + 8, :] = cross_imag
                    cross[one, 2 * half + row : 2 * half + row + 8, :] = magnitude
                    if row == 0:
                        total = jnp.where(top, magnitude, 2.0 * magnitude)
                    elif row == block // 2:
                        total += magnitude
                    else:
                        total += 2.0 * magnitude
                sums[one] = jnp.sum(total, axis=0, keepdims=True)

    means = jnp.sum(sums[...], axis=2, keepdims=True) * (1.0 / (block * block)) + 1e-06
    lag_sums = []
    for one in range(local * many):
        codes, _, v = volumes[one % many]
        index, _ = places[one // many]
        scale = pl.reciprocal(cross[one, 2 * half :, :] + means[one], approx=True)
        norm = jnp.concatenate(
            [
                (cross[one, :half, :] * scale).astype(jnp.bfloat16),
                (cross[one, half : 2 * half, :] * scale).astype(jnp.bfloat16),
            ],
            axis=0,
        )
        row_shift = codes[v, 0, index] >> 4
        lag_rows = jnp.dot(
            lag_ref[row_shift + SHIFT], norm, preferred_element_type=jnp.float32
        ).astype(jnp.bfloat16)
        lag_sums.append(jnp.concatenate([lag_rows[:WIN], lag_rows[WIN:]], axis=1))
    lags = jnp.dot(
        jnp.concatenate(lag_sums, axis=0), span_ref[...], preferred_element_type=jnp.float32
    )
    for one in range(local * many):
        codes, _, v = volumes[one % many]
        index, _ = places[one // many]
        col_shift = codes[v, 1, index] >> 4
        order = index // (2 * own) * own + one // many % own
        found[one % many, pl.ds(pl.multiple_of(order * WIN, WIN), WIN), :] = pltpu.roll(
            lags[one * WIN : (one + 1) * WIN], LANES - SHIFT - col_shift, 1
        )

    @pl.when(step == depth - 1)
    def _():
        share = depth * local // planes
        per_tile = LANES // WIN
        lane = lax.broadcasted_iota(jnp.int32, (share, LANES), 1) // WIN
        for turn, out_ref in enumerate(out_refs):
            plane = place_ref[3] ^ (turn % planes)
            for v in range(vols):
                order = turn // planes * vols + v
                for tile in range(WIN // per_tile):
                    total = jnp.zeros((share, LANES), jnp.float32)
                    for part in range(per_tile):
                        start = plane * share * WIN + tile * per_tile + part
                        one = found[order, pl.ds(start, share, stride=WIN), :]
                        if part:
                            one = pltpu.roll(one, part * WIN, 1)
                        total = jnp.where(lane == part, one, total)
                    out_ref[v, :, tile * LANES : (tile + 1) * LANES] = total * (1.0 / block)


def lag_windows(place, codes, other_codes, frames, other_frames, templates, after, planes, own):
    vols, rows, cols = frames.shape
    block = templates[0].shape[-1]
    down, across = rows // block, cols // block
    depth = len(templates)
    tables = dft_constants(block)
    half = tables[1].shape[0] // 2
    whole = [
        pl.BlockSpec(
            table.shape, functools.partial(lambda dims, step, place: (0,) * dims, table.ndim)
        )
        for table in tables
    ]
    smem = pl.BlockSpec(memory_space=pltpu.SMEM)
    frame_spec = pl.BlockSpec(
        (vols, block, cols), lambda step, place: (0, step_band(place, step, across, own), 0)
    )
    local = depth * 2 * own
    many = 2 * vols * 2 * own
    out = (vols, local // planes, WIN * WIN)
    return pl.pallas_call(
        functools.partial(spectrum_kernel, vols, across, block, own, planes, depth),
        grid_spec=pltpu.PrefetchScalarGridSpec(
            num_scalar_prefetch=1,
            grid=(depth,),
            in_specs=[smem, smem, *whole, frame_spec, frame_spec]
            + [pl.BlockSpec(memory_space=pl.ANY)] * (depth + 1),
            out_specs=[pl.BlockSpec(out, lambda step, place: (0, 0, 0))] * (2 * planes),
            scratch_shapes=[
                pltpu.VMEM((depth, 2 * own, block, block), jnp.bfloat16),
                pltpu.VMEM((many, 3 * half, LANES), jnp.float32),
                pltpu.VMEM((many, 1, LANES), jnp.float32),
                pltpu.VMEM((2 * vols, local * WIN, LANES), jnp.float32),
                pltpu.SemaphoreType.DMA((depth,)),
            ],
        ),
        out_shape=[jax.ShapeDtypeStruct(out, jnp.float32)] * (2 * planes),
        compiler_params=pltpu.CompilerParams(vmem_limit_bytes=VMEM_LIMIT),
        cost_estimate=pl.CostEstimate(
            flops=2 * 3 * rows * cols * block * 4,
            bytes_accessed=vols * rows * cols * 4 + rows * cols,
            transcendentals=0,
        ),
        name="lag_windows",
    )(place, codes, other_codes, *tables, frames, other_frames, *templates, after)


def exchange(value, axes, size, turn):
    return lax.ppermute(value, axes, [(at, at ^ turn) for at in range(size)])


def on_device(frames, template, shift_codes):
    vol_dev, pl_dev, img_rows, img_cols = frames.shape
    own, block = template.shape[0], template.shape[-1]
    depth = lax.axis_size("z")
    planes = lax.axis_size("plane")
    share = 4 * depth * own // planes
    place = jnp.stack([lax.axis_index(axis) for axis in ("z", "y", "core", "plane")])
    other_frames = exchange(frames, "core", 2, 1)
    other_codes = exchange(shift_codes, "core", 2, 1)
    templates = [jnp.concatenate([template, exchange(template, "y", 2, 1)], axis=0)]
    for turn in range(1, depth):
        templates.append(exchange(templates[0], "z", depth, turn))
    averages, window = [], [0.0, 0.0]
    volumes = vol_dev * depth * 4
    for p in range(pl_dev):
        work = (place, shift_codes, other_codes, frames[:, p], other_frames[:, p])
        warped = warp_sums(*work, depth, block, own)
        chosen = [one[:, p] for one in templates]
        found = lag_windows(*work, chosen, warped[0], planes, own)
        warped = [warped[0]] + [
            exchange(warped[turn], "z", depth, turn) for turn in range(1, depth)
        ]
        sums = [sum(one[at : at + own].astype(jnp.float32) for one in warped) for at in (0, own)]
        taken = exchange(sums[1].astype(jnp.bfloat16), "y", 2, 1)
        averages.append((sums[0] + taken.astype(jnp.float32)) * (1.0 / volumes))
        for turn, one in enumerate(found):
            if turn:
                one = exchange(one, ("core", "plane"), 2 * planes, turn)
            window[turn // planes] += one
    core = place[2]
    window = [jnp.where(core == 0, *window), jnp.where(core == 0, *window[::-1])]
    window = [one.reshape(vol_dev, share // (2 * own), 1, own, WIN * WIN) for one in window]
    correlation = jnp.concatenate(window, axis=2).reshape(vol_dev, share, WIN * WIN)
    return (correlation, jnp.stack(averages, axis=1))


def solution(mesh):
    devices = mesh.devices.reshape(-1, 2, 2, mesh.shape["plane"])
    split = jax.sharding.Mesh(devices, ("z", "y", "core", "plane"))
    vols = ("z", "y", "core")
    in_specs = (P(vols, "plane", None, None), P(vols, "plane", None, None), P(vols, None, None))
    out_specs = (P(vols, "plane", None), P(vols, "plane", None, None))
    return jax.shard_map(
        on_device, mesh=split, in_specs=in_specs, out_specs=out_specs, check_vma=False
    )
```

```python
import functools
import math

import jax
import jax.numpy as jnp
import numpy as np
from jax import lax
from jax.experimental import pallas as pl
from jax.experimental.pallas import tpu as pltpu
from jax.sharding import PartitionSpec as P

SHIFT = 8
WIN = 16
TAPS = 8
SUB = 16
EDGE = 16
LANES = 128
VMEM_LIMIT = 24 * 1024 * 1024

full_turn = 2.0 * math.pi


def dft_constants(block_size):
    positions = np.arange(block_size)
    angles = full_turn * (np.outer(positions, positions) % block_size) / block_size
    cosine = np.cos(angles)
    sine = -np.sin(angles)
    half = block_size // 2 + 1
    rows = -(-half // 8) * 8
    row_table = np.concatenate([cosine, sine], axis=1)
    col_table = np.zeros((2 * rows, 2 * block_size))
    col_table[:half] = np.concatenate([cosine[:half], -sine[:half]], axis=1)
    col_table[rows : rows + half] = np.concatenate([sine[:half], cosine[:half]], axis=1)
    weights = np.zeros((rows,))
    weights[:half] = 2.0
    weights[0] = weights[half - 1] = 1.0
    starts = 2 * SHIFT
    lag_table = np.zeros((starts, 2 * WIN, 2 * rows))
    for start in range(starts):
        lags = start - SHIFT - WIN // 2 + np.arange(WIN)
        turns = full_turn * (np.outer(lags, positions[:half]) % block_size) / block_size
        lag_cos = np.cos(turns) * weights[:half]
        lag_sin = np.sin(turns) * weights[:half]
        lag_table[start, :WIN, :half] = lag_cos
        lag_table[start, :WIN, rows : rows + half] = -lag_sin
        lag_table[start, WIN:, :half] = lag_sin
        lag_table[start, WIN:, rows : rows + half] = lag_cos
    span = starts + WIN
    lags = np.arange(span) - SHIFT - WIN // 2
    turns = full_turn * (np.outer(positions, lags) % block_size) / block_size
    span_table = np.zeros((2 * block_size, LANES))
    span_table[:block_size, :span] = np.cos(turns)
    span_table[block_size:, :span] = -np.sin(turns)
    return tuple(
        jnp.asarray(table, jnp.bfloat16) for table in (row_table, col_table, lag_table, span_table)
    )


def tap_constants():
    offsets = np.arange(TAPS) - (TAPS // 2 - 1)
    spots = offsets[None, :] - np.arange(SUB)[:, None] / SUB
    raw_taps = np.sinc(spots) * np.sinc(spots / (TAPS // 2))
    taps = raw_taps / raw_taps.sum(axis=-1, keepdims=True)
    table = np.zeros((2, SUB, EDGE, LANES))
    for row in range(EDGE):
        table[0, :, row, row : row + TAPS] = taps
        table[1, :, row, row : row + TAPS] = taps[:, ::-1]
    return jnp.asarray(table, jnp.float32)


def band_groups(head, start, lane):
    head = pltpu.roll(head, start + LANES, 1).astype(jnp.bfloat16)
    groups = [head] + [pltpu.roll(head, step, 1) for step in range(EDGE, LANES, EDGE)]
    zero = jnp.zeros_like(head)
    low = lane < LANES // 2
    before, after = jnp.where(low, zero, groups[0]), jnp.where(low, groups[-1], zero)
    middle = [jnp.where(low, groups[0], zero), *groups[1:-1], jnp.where(low, zero, groups[-1])]
    return middle, before, after


def step_places(place_ref, step, across, own):
    z = place_ref[0] ^ step
    places = []
    for other in range(2):
        for one in range(own):
            index = ((2 * z + (place_ref[1] ^ other)) * 2 + place_ref[2]) * own + one
            places.append((index, index % across))
    return places


def step_band(place_ref, step, across, own):
    return (place_ref[0] ^ step) * (4 * own) // across


def warp_kernel(vols, down, across, block, own, depth, *refs):
    place_ref, codes_hbm, other_codes_hbm, taps_hbm, frames_hbm, other_frames_ref = refs[:6]
    out_refs = refs[6 : 6 + depth]
    codes_ref, other_codes_ref, taps_ref, frames_ref, sums, sems = refs[6 + depth :]
    moves = [
        (frames_hbm, frames_ref),
        (codes_hbm, codes_ref),
        (other_codes_hbm, other_codes_ref),
        (taps_hbm, taps_ref),
    ]
    copies = [
        pltpu.make_async_copy(source, target, sems.at[at])
        for at, (source, target) in enumerate(moves)
    ]
    for copy in copies:
        copy.start()
    for copy in copies:
        copy.wait()
    lane = lax.broadcasted_iota(jnp.int32, (EDGE, LANES), 1)
    tall_lane = lax.broadcasted_iota(jnp.int32, (block + 2 * EDGE, LANES), 1)
    zero = jnp.zeros((EDGE, LANES), jnp.bfloat16)
    gap = jnp.zeros((block - 2 * EDGE, LANES), jnp.bfloat16)
    no_tile = jnp.zeros((block + 2 * EDGE, block), jnp.bfloat16)
    volumes = [(codes_ref, frames_ref, v) for v in range(vols)]
    volumes += [(other_codes_ref, other_frames_ref, v) for v in range(vols)]
    before_taps = TAPS // 2 - 1
    after_taps = TAPS // 2

    def one_step(step, _):
        band = step_band(place_ref, step, across, own)
        row = pl.multiple_of(band * block, block)
        row_above = pl.multiple_of(jnp.maximum(row - EDGE, 0), EDGE)
        row_below = pl.multiple_of(jnp.minimum(row + block, down * block - EDGE), EDGE)

        def tile(volume, at):
            _, frames, v = volume
            lanes = pl.ds(pl.multiple_of(at * block, block), block)
            above = jnp.where(band > 0, frames[v, pl.ds(row_above, EDGE), lanes], zero)
            below = jnp.where(band < down - 1, frames[v, pl.ds(row_below, EDGE), lanes], zero)
            return jnp.concatenate([frames[v, pl.ds(row, block), lanes], below, above], axis=0)

        for count, (index, at) in enumerate(step_places(place_ref, step, across, own)):
            row_tiles, first_edge, last_edge = [], [], []
            partials, edges = [], []
            for order, volume in enumerate(volumes):
                codes, _, v = volume
                row_code = codes[v, 0, index]
                col_code = codes[v, 1, index]
                middle, before, after = band_groups(
                    taps_ref[1, col_code & (SUB - 1)], -after_taps - (col_code >> 4), lane
                )
                left = jnp.where(at > 0, tile(volume, jnp.maximum(at - 1, 0)), no_tile)
                right = jnp.where(
                    at < across - 1, tile(volume, jnp.minimum(at + 1, across - 1)), no_tile
                )
                sides = jnp.where(tall_lane < LANES // 2, right, left)
                partial = jnp.dot(
                    jnp.concatenate([tile(volume, at), sides], axis=1),
                    jnp.concatenate([*middle, before, gap, after], axis=0),
                    preferred_element_type=jnp.float32,
                ).astype(jnp.bfloat16)
                partials.append(partial[:block])
                edges.append(partial[block:])
                middle, before, after = band_groups(
                    taps_ref[0, row_code & (SUB - 1)], (row_code >> 4) - before_taps, lane
                )
                row_tiles.append(jnp.concatenate(middle, axis=0))
                place = 2 * EDGE * order % LANES
                first_edge.append(pltpu.roll(before, (place + 2 * EDGE) % LANES, 1))
                last_edge.append(pltpu.roll(after, place, 1) if place else after)
            per_tile = LANES // (2 * EDGE)
            for start in range(0, 2 * vols, per_tile):
                first, last = first_edge[start], last_edge[start]
                for more in range(start + 1, min(start + per_tile, 2 * vols)):
                    first, last = first + first_edge[more], last + last_edge[more]
                row_tiles.append(jnp.concatenate([first, gap, last], axis=0))
            deep = 2 * vols * (block + 2 * EDGE)
            total = jnp.dot(
                jnp.concatenate(row_tiles, axis=1)[:, :deep],
                jnp.concatenate(partials + edges, axis=0),
                preferred_element_type=jnp.float32,
            )
            sums[count] = total.astype(jnp.bfloat16)
        for at_step, out_ref in enumerate(out_refs):

            @pl.when(step == at_step)
            def _():
                out_ref[...] = sums[...]

        return 0

    lax.fori_loop(0, depth, one_step, 0)


def warp_sums(place, codes, other_codes, frames, other_frames, depth, block, own):
    vols, rows, cols = frames.shape
    down, across = rows // block, cols // block
    taps = tap_constants()
    out = (2 * own, block, block)
    hbm = pl.BlockSpec(memory_space=pltpu.HBM)
    kept = [
        pltpu.with_memory_space_constraint(one, pltpu.HBM)
        for one in (codes, other_codes, taps, frames)
    ]
    vmem = pl.BlockSpec(memory_space=pltpu.VMEM)
    return pl.pallas_call(
        functools.partial(warp_kernel, vols, down, across, block, own, depth),
        out_shape=[jax.ShapeDtypeStruct(out, jnp.bfloat16)] * depth,
        in_specs=[pl.BlockSpec(memory_space=pltpu.SMEM), hbm, hbm, hbm, hbm, vmem],
        out_specs=[vmem] * depth,
        scratch_shapes=[
            pltpu.SMEM(codes.shape, jnp.int32),
            pltpu.SMEM(codes.shape, jnp.int32),
            pltpu.VMEM(taps.shape, jnp.float32),
            pltpu.VMEM(frames.shape, jnp.bfloat16),
            pltpu.VMEM(out, jnp.bfloat16),
            pltpu.SemaphoreType.DMA((4,)),
        ],
        compiler_params=pltpu.CompilerParams(vmem_limit_bytes=VMEM_LIMIT),
        cost_estimate=pl.CostEstimate(
            flops=2 * vols * rows * cols * block * 16,
            bytes_accessed=vols * rows * cols * 4 + rows * cols,
            transcendentals=0,
        ),
        name="warp",
    )(place, *kept, other_frames)


def spectrum_kernel(vols, across, block, own, planes, depth, *refs):
    place_ref, codes_ref, other_codes_ref, row_ref, col_ref, lag_ref, span_ref = refs[:7]
    frames_ref, other_frames_ref = refs[7:9]
    template_refs, out_refs = refs[9 : 9 + depth], refs[10 + depth : 10 + depth + 2 * planes]
    templates, cross, sums, found = refs[10 + depth + 2 * planes :]
    for at, template_ref in enumerate(template_refs):
        templates[at] = template_ref[...]

    row_table = row_ref[...]
    col_table = col_ref[...]
    half = col_table.shape[0] // 2
    top = lax.broadcasted_iota(jnp.int32, (8, LANES), 0) == 0
    volumes = [(codes_ref, frames_ref, v) for v in range(vols)]
    volumes += [(other_codes_ref, other_frames_ref, v) for v in range(vols)]
    many = len(volumes)
    local = 2 * own
    def one_step(step, _):
        places = step_places(place_ref, step, across, own)
        band = step_band(place_ref, step, across, own)
        band_rows = pl.ds(pl.multiple_of(band * block, block), block)

        for pair in range(local // 2):
            pair_places = places[2 * pair : 2 * pair + 2]
            parts = [templates[step, 2 * pair], templates[step, 2 * pair + 1]]
            for _, frames, v in volumes:
                for _, at in pair_places:
                    parts.append(frames[v, band_rows, pl.ds(pl.multiple_of(at * block, block), block)])
            rows = jnp.dot(
                jnp.concatenate(parts, axis=0), row_table, preferred_element_type=jnp.float32
            ).astype(jnp.bfloat16)
            spectra = []
            for source in range(many + 1):
                stacks = []
                for side in range(2):
                    at = (2 * source + side) * block
                    one = rows[at : at + block]
                    stacks.append(jnp.concatenate([one[:, :block], one[:, block:]], axis=0))
                spectra.append(
                    jnp.dot(
                        col_table, jnp.concatenate(stacks, axis=1), preferred_element_type=jnp.float32
                    )
                )
            temp = spectra[0].astype(jnp.bfloat16).astype(jnp.float32)
            for order in range(many):
                for side in range(2):
                    lanes = slice(side * block, (side + 1) * block)
                    one = (2 * pair + side) * many + order
                    total = jnp.zeros((8, LANES), jnp.float32)
                    for row in range(0, half, 8):
                        temp_real = temp[row : row + 8, lanes]
                        temp_imag = temp[half + row : half + row + 8, lanes]
                        real = spectra[order + 1][row : row + 8, lanes]
                        imag = spectra[order + 1][half + row : half + row + 8, lanes]
                        cross_real = real * temp_real + imag * temp_imag
                        cross_imag = imag * temp_real - real * temp_imag
                        power = cross_real * cross_real + cross_imag * cross_imag
                        magnitude = power * lax.rsqrt(jnp.maximum(power, 1e-36))
                        cross[one, row : row + 8, :] = cross_real
                        cross[one, half + row : half + row + 8, :] = cross_imag
                        cross[one, 2 * half + row : 2 * half + row + 8, :] = magnitude
                        if row == 0:
                            total = jnp.where(top, magnitude, 2.0 * magnitude)
                        elif row == block // 2:
                            total += magnitude
                        else:
                            total += 2.0 * magnitude
                    sums[one] = jnp.sum(total, axis=0, keepdims=True)

        means = jnp.sum(sums[...], axis=2, keepdims=True) * (1.0 / (block * block)) + 1e-06
        lag_sums = []
        for one in range(local * many):
            codes, _, v = volumes[one % many]
            index, _ = places[one // many]
            scale = pl.reciprocal(cross[one, 2 * half :, :] + means[one], approx=True)
            norm = jnp.concatenate(
                [
                    (cross[one, :half, :] * scale).astype(jnp.bfloat16),
                    (cross[one, half : 2 * half, :] * scale).astype(jnp.bfloat16),
                ],
                axis=0,
            )
            row_shift = codes[v, 0, index] >> 4
            lag_rows = jnp.dot(
                lag_ref[row_shift + SHIFT], norm, preferred_element_type=jnp.float32
            ).astype(jnp.bfloat16)
            lag_sums.append(jnp.concatenate([lag_rows[:WIN], lag_rows[WIN:]], axis=1))
        lags = jnp.dot(
            jnp.concatenate(lag_sums, axis=0), span_ref[...], preferred_element_type=jnp.float32
        )
        for one in range(local * many):
            codes, _, v = volumes[one % many]
            index, _ = places[one // many]
            col_shift = codes[v, 1, index] >> 4
            order = index // (2 * own) * own + one // many % own
            found[one % many, pl.ds(pl.multiple_of(order * WIN, WIN), WIN), :] = pltpu.roll(
                lags[one * WIN : (one + 1) * WIN], LANES - SHIFT - col_shift, 1
            )
        return 0

    lax.fori_loop(0, depth, one_step, 0)

    share = depth * local // planes
    per_tile = LANES // WIN
    lane = lax.broadcasted_iota(jnp.int32, (share, LANES), 1) // WIN
    for turn, out_ref in enumerate(out_refs):
        plane = place_ref[3] ^ (turn % planes)
        for v in range(vols):
            order = turn // planes * vols + v
            for tile in range(WIN // per_tile):
                total = jnp.zeros((share, LANES), jnp.float32)
                for part in range(per_tile):
                    start = plane * share * WIN + tile * per_tile + part
                    one = found[order, pl.ds(start, share, stride=WIN), :]
                    if part:
                        one = pltpu.roll(one, part * WIN, 1)
                    total = jnp.where(lane == part, one, total)
                out_ref[v, :, tile * LANES : (tile + 1) * LANES] = total * (1.0 / block)


def lag_windows(place, codes, other_codes, frames, other_frames, templates, after, planes, own):
    vols, rows, cols = frames.shape
    block = templates[0].shape[-1]
    down, across = rows // block, cols // block
    depth = len(templates)
    tables = dft_constants(block)
    half = tables[1].shape[0] // 2
    smem = pl.BlockSpec(memory_space=pltpu.SMEM)
    vmem = pl.BlockSpec(memory_space=pltpu.VMEM)
    local = depth * 2 * own
    many = 2 * vols * 2 * own
    out = (vols, local // planes, WIN * WIN)
    return pl.pallas_call(
        functools.partial(spectrum_kernel, vols, across, block, own, planes, depth),
        out_shape=[jax.ShapeDtypeStruct(out, jnp.float32)] * (2 * planes),
        in_specs=[smem] * 3
        + [vmem] * (len(tables) + 2 + depth)
        + [pl.BlockSpec(memory_space=pl.ANY)],
        out_specs=[vmem] * (2 * planes),
        scratch_shapes=[
            pltpu.VMEM((depth, 2 * own, block, block), jnp.bfloat16),
            pltpu.VMEM((many, 3 * half, LANES), jnp.float32),
            pltpu.VMEM((many, 1, LANES), jnp.float32),
            pltpu.VMEM((2 * vols, local * WIN, LANES), jnp.float32),
        ],
        compiler_params=pltpu.CompilerParams(vmem_limit_bytes=VMEM_LIMIT),
        cost_estimate=pl.CostEstimate(
            flops=2 * 3 * rows * cols * block * 16,
            bytes_accessed=vols * rows * cols * 4 + rows * cols,
            transcendentals=0,
        ),
        name="lag_windows",
    )(place, codes, other_codes, *tables, frames, other_frames, *templates, after)


def exchange(value, axes, size, turn):
    return lax.ppermute(value, axes, [(at, at ^ turn) for at in range(size)])


def on_device(frames, template, shift_codes):
    vol_dev, pl_dev, img_rows, img_cols = frames.shape
    own, block = template.shape[0], template.shape[-1]
    depth = lax.axis_size("z")
    planes = lax.axis_size("plane")
    share = 4 * depth * own // planes
    place = jnp.stack([lax.axis_index(axis) for axis in ("z", "y", "core", "plane")])
    other_codes = exchange(shift_codes, "core", 2, 1)
    other_template = exchange(template, "y", 2, 1)
    later_frames, other_template = lax.optimization_barrier((frames, other_template))
    other_frames = exchange(later_frames, "core", 2, 1)
    templates = [jnp.concatenate([template, other_template], axis=0)]
    for turn in range(1, depth):
        templates.append(exchange(templates[0], "z", depth, turn))
    averages, window = [], [0.0, 0.0]
    volumes = vol_dev * depth * 4
    for p in range(pl_dev):
        work = (place, shift_codes, other_codes, frames[:, p], other_frames[:, p])
        warped = warp_sums(*work, depth, block, own)
        chosen = [one[:, p] for one in templates]
        found = lag_windows(*work, chosen, warped[0], planes, own)
        warped = [warped[0]] + [
            exchange(warped[turn], "z", depth, turn) for turn in range(1, depth)
        ]
        sums = [sum(one[at : at + own].astype(jnp.float32) for one in warped) for at in (0, own)]
        found, sums = lax.optimization_barrier((found, sums))
        taken = exchange(sums[1].astype(jnp.bfloat16), "y", 2, 1)
        averages.append((sums[0] + taken.astype(jnp.float32)) * (1.0 / volumes))
        for turn, one in enumerate(found):
            if turn:
                one = exchange(one, ("core", "plane"), 2 * planes, turn)
            window[turn // planes] += one
    core = place[2]
    window = [jnp.where(core == 0, *window), jnp.where(core == 0, *window[::-1])]
    window = [one.reshape(vol_dev, share // (2 * own), 1, own, WIN * WIN) for one in window]
    correlation = jnp.concatenate(window, axis=2).reshape(vol_dev, share, WIN * WIN)
    return (correlation, jnp.stack(averages, axis=1))


def solution(mesh):
    devices = mesh.devices.reshape(-1, 2, 2, mesh.shape["plane"])
    split = jax.sharding.Mesh(devices, ("z", "y", "core", "plane"))
    vols = ("z", "y", "core")
    in_specs = (P(vols, "plane", None, None), P(vols, "plane", None, None), P(vols, None, None))
    out_specs = (P(vols, "plane", None), P(vols, "plane", None, None))
    return jax.shard_map(
        on_device, mesh=split, in_specs=in_specs, out_specs=out_specs, check_vma=False
    )
```

```python
import functools
import math

import jax
import jax.numpy as jnp
import numpy as np
from jax import lax
from jax.experimental import pallas as pl
from jax.experimental.pallas import tpu as pltpu
from jax.sharding import PartitionSpec as P

SHIFT = 8
WIN = 16
TAPS = 8
SUB = 16
EDGE = 16
LANES = 128
VMEM_LIMIT = 24 * 1024 * 1024

full_turn = 2.0 * math.pi


def dft_constants(block_size):
    positions = np.arange(block_size)
    angles = full_turn * (np.outer(positions, positions) % block_size) / block_size
    cosine = np.cos(angles)
    sine = -np.sin(angles)
    half = block_size // 2 + 1
    rows = -(-half // 16) * 16
    row_table = np.zeros((2 * rows, block_size))
    row_table[:half] = cosine[:half]
    row_table[rows : rows + half] = sine[:half]
    col_table = np.block([[cosine, sine], [-sine, cosine]])
    weights = np.full((half,), 2.0)
    weights[0] = weights[half - 1] = 1.0
    span = 2 * SHIFT + WIN
    lags = np.arange(span) - SHIFT - WIN // 2
    turns = full_turn * (np.outer(lags, positions) % block_size) / block_size
    lag_cos, lag_sin = np.cos(turns), np.sin(turns)
    lag_table = np.zeros((2 * span, 2 * rows))
    lag_table[:span, :half] = lag_cos[:, :half] * weights
    lag_table[:span, rows : rows + half] = -lag_sin[:, :half] * weights
    lag_table[span:, :half] = lag_sin[:, :half] * weights
    lag_table[span:, rows : rows + half] = lag_cos[:, :half] * weights
    span_table = np.zeros((2 * block_size, LANES))
    span_table[:block_size, :span] = lag_cos.T
    span_table[block_size:, :span] = -lag_sin.T
    return tuple(
        jnp.asarray(table, jnp.bfloat16) for table in (row_table, col_table, lag_table, span_table)
    )


def tap_constants():
    offsets = np.arange(TAPS) - (TAPS // 2 - 1)
    spots = offsets[None, :] - np.arange(SUB)[:, None] / SUB
    raw_taps = np.sinc(spots) * np.sinc(spots / (TAPS // 2))
    taps = raw_taps / raw_taps.sum(axis=-1, keepdims=True)
    heads = np.zeros((SUB, EDGE, LANES))
    for row in range(EDGE):
        heads[:, row, row : row + TAPS] = taps[:, ::-1]
    return jnp.asarray(taps, jnp.float32), jnp.asarray(heads, jnp.float32)


def band_groups(head, start, lane):
    head = pltpu.roll(head, start + LANES, 1).astype(jnp.bfloat16)
    groups = [head] + [pltpu.roll(head, step, 1) for step in range(EDGE, LANES, EDGE)]
    zero = jnp.zeros_like(head)
    low = lane < LANES // 2
    before, after = jnp.where(low, zero, groups[0]), jnp.where(low, groups[-1], zero)
    middle = [jnp.where(low, groups[0], zero), *groups[1:-1], jnp.where(low, zero, groups[-1])]
    return middle, before, after


def step_places(place_ref, step, across, own):
    z = place_ref[0] ^ step
    places = []
    for other in range(2):
        for one in range(own):
            index = ((2 * z + (place_ref[1] ^ other)) * 2 + place_ref[2]) * own + one
            places.append((index, index % across))
    return places


def step_band(place_ref, step, across, own):
    return (place_ref[0] ^ step) * (4 * own) // across


def warp_kernel(vols, down, across, block, own, depth, *refs):
    place_ref, codes_hbm, other_codes_hbm, taps_hbm, heads_hbm, frames_hbm = refs[:6]
    other_frames_ref, out_refs = refs[6], refs[7 : 7 + depth]
    codes_ref, other_codes_ref, taps_ref, heads_ref, frames_ref, columns, sums, sems = refs[7 + depth :]
    moves = [
        (frames_hbm, frames_ref),
        (codes_hbm, codes_ref),
        (other_codes_hbm, other_codes_ref),
        (taps_hbm, taps_ref),
        (heads_hbm, heads_ref),
    ]
    copies = [
        pltpu.make_async_copy(source, target, sems.at[at])
        for at, (source, target) in enumerate(moves)
    ]
    for copy in copies:
        copy.start()
    for copy in copies:
        copy.wait()
    lane = lax.broadcasted_iota(jnp.int32, (EDGE, LANES), 1)
    tall_lane = lax.broadcasted_iota(jnp.int32, (block + 2 * EDGE, LANES), 1)
    zero = jnp.zeros((EDGE, LANES), jnp.bfloat16)
    gap = jnp.zeros((block - 2 * EDGE, LANES), jnp.bfloat16)
    no_tile = jnp.zeros((block + 2 * EDGE, block), jnp.bfloat16)
    volumes = [(codes_ref, frames_ref, v) for v in range(vols)]
    volumes += [(other_codes_ref, other_frames_ref, v) for v in range(vols)]
    before_taps = TAPS // 2 - 1
    after_taps = TAPS // 2

    def one_step(step, _):
        band = step_band(place_ref, step, across, own)
        row = pl.multiple_of(band * block, block)
        row_above = pl.multiple_of(jnp.maximum(row - EDGE, 0), EDGE)
        row_below = pl.multiple_of(jnp.minimum(row + block, down * block - EDGE), EDGE)

        def tile(volume, at):
            _, frames, v = volume
            lanes = pl.ds(pl.multiple_of(at * block, block), block)
            above = jnp.where(band > 0, frames[v, pl.ds(row_above, EDGE), lanes], zero)
            below = jnp.where(band < down - 1, frames[v, pl.ds(row_below, EDGE), lanes], zero)
            return jnp.concatenate([above, frames[v, pl.ds(row, block), lanes], below], axis=0)

        places = step_places(place_ref, step, across, own)
        for count, (index, at) in enumerate(places):
            for order, volume in enumerate(volumes):
                codes, _, v = volume
                col_code = codes[v, 1, index]
                middle, before, after = band_groups(
                    heads_ref[col_code & (SUB - 1)], -after_taps - (col_code >> 4), lane
                )
                left = jnp.where(at > 0, tile(volume, jnp.maximum(at - 1, 0)), no_tile)
                right = jnp.where(
                    at < across - 1, tile(volume, jnp.minimum(at + 1, across - 1)), no_tile
                )
                sides = jnp.where(tall_lane < LANES // 2, right, left)
                columns[count * 2 * vols + order] = jnp.dot(
                    jnp.concatenate([tile(volume, at), sides], axis=1),
                    jnp.concatenate([*middle, before, gap, after], axis=0),
                    preferred_element_type=jnp.float32,
                )
        for count, (index, _) in enumerate(places):
            total = jnp.zeros((block, block), jnp.float32)
            for order, (codes, _, v) in enumerate(volumes):
                row_code = codes[v, 0, index]
                start = EDGE - before_taps + (row_code >> 4)
                for tap in range(TAPS):
                    part = columns[count * 2 * vols + order, pl.ds(start + tap, block), :]
                    total += taps_ref[row_code & (SUB - 1), tap] * part
            sums[count] = total.astype(jnp.bfloat16)
        for at_step, out_ref in enumerate(out_refs):

            @pl.when(step == at_step)
            def _():
                out_ref[...] = sums[...]

        return 0

    lax.fori_loop(0, depth, one_step, 0)


def warp_sums(place, codes, other_codes, frames, other_frames, depth, block, own):
    vols, rows, cols = frames.shape
    down, across = rows // block, cols // block
    taps, heads = tap_constants()
    out = (2 * own, block, block)
    hbm = pl.BlockSpec(memory_space=pltpu.HBM)
    kept = [
        pltpu.with_memory_space_constraint(one, pltpu.HBM)
        for one in (codes, other_codes, taps, heads, frames)
    ]
    vmem = pl.BlockSpec(memory_space=pltpu.VMEM)
    return pl.pallas_call(
        functools.partial(warp_kernel, vols, down, across, block, own, depth),
        out_shape=[jax.ShapeDtypeStruct(out, jnp.bfloat16)] * depth,
        in_specs=[pl.BlockSpec(memory_space=pltpu.SMEM)] + [hbm] * 5 + [vmem],
        out_specs=[vmem] * depth,
        scratch_shapes=[
            pltpu.SMEM(codes.shape, jnp.int32),
            pltpu.SMEM(codes.shape, jnp.int32),
            pltpu.SMEM(taps.shape, jnp.float32),
            pltpu.VMEM(heads.shape, jnp.float32),
            pltpu.VMEM(frames.shape, jnp.bfloat16),
            pltpu.VMEM((2 * vols * 2 * own, block + 2 * EDGE, block), jnp.float32),
            pltpu.VMEM(out, jnp.bfloat16),
            pltpu.SemaphoreType.DMA((5,)),
        ],
        compiler_params=pltpu.CompilerParams(vmem_limit_bytes=VMEM_LIMIT),
        cost_estimate=pl.CostEstimate(
            flops=2 * vols * rows * cols * block * 16,
            bytes_accessed=vols * rows * cols * 4 + rows * cols,
            transcendentals=0,
        ),
        name="warp",
    )(place, *kept, other_frames)


def spectrum_kernel(vols, across, block, own, planes, depth, *refs):
    place_ref, codes_ref, other_codes_ref, row_ref, col_ref, lag_ref, span_ref = refs[:7]
    frames_ref, other_frames_ref = refs[7:9]
    template_refs, out_refs = refs[9 : 9 + depth], refs[10 + depth : 10 + depth + 2 * planes]
    templates, cross, sums, found = refs[10 + depth + 2 * planes :]
    for at, template_ref in enumerate(template_refs):
        templates[at] = template_ref[...]

    row_table = row_ref[...]
    col_table = col_ref[...]
    lag_table = lag_ref[...]
    half = row_table.shape[0] // 2
    kept = -(-(block // 2 + 1) // 8) * 8
    span = lag_table.shape[0] // 2
    top = lax.broadcasted_iota(jnp.int32, (8, LANES), 0) == 0
    volumes = [(codes_ref, frames_ref, v) for v in range(vols)]
    volumes += [(other_codes_ref, other_frames_ref, v) for v in range(vols)]
    many = len(volumes)
    local = 2 * own
    no_rows = jnp.zeros((half - kept, LANES), jnp.float32)

    def one_step(step, _):
        places = step_places(place_ref, step, across, own)
        band = step_band(place_ref, step, across, own)
        band_rows = pl.ds(pl.multiple_of(band * block, block), block)

        for pair in range(local // 2):
            pair_places = places[2 * pair : 2 * pair + 2]
            sources = [[templates[step, 2 * pair], templates[step, 2 * pair + 1]]]
            for _, frames, v in volumes:
                sources.append(
                    [
                        frames[v, band_rows, pl.ds(pl.multiple_of(at * block, block), block)]
                        for _, at in pair_places
                    ]
                )
            parts = []
            for source in sources:
                rows = jnp.dot(
                    row_table,
                    jnp.concatenate(source, axis=1),
                    preferred_element_type=jnp.float32,
                ).astype(jnp.bfloat16)
                for side in range(2):
                    lanes = slice(side * block, (side + 1) * block)
                    parts.append(jnp.concatenate([rows[:half, lanes], rows[half:, lanes]], axis=1))
            spectra = jnp.dot(
                jnp.concatenate(parts, axis=0), col_table, preferred_element_type=jnp.float32
            )
            temp = spectra[: 2 * half].astype(jnp.bfloat16).astype(jnp.float32)
            for order in range(many):
                for side in range(2):
                    one = (2 * pair + side) * many + order
                    base = (2 * (order + 1) + side) * half
                    total = jnp.zeros((8, LANES), jnp.float32)
                    for row in range(0, kept, 8):
                        at = side * half + row
                        temp_real = temp[at : at + 8, :block]
                        temp_imag = temp[at : at + 8, block:]
                        real = spectra[base + row : base + row + 8, :block]
                        imag = spectra[base + row : base + row + 8, block:]
                        cross_real = real * temp_real + imag * temp_imag
                        cross_imag = imag * temp_real - real * temp_imag
                        power = cross_real * cross_real + cross_imag * cross_imag
                        magnitude = power * lax.rsqrt(jnp.maximum(power, 1e-36))
                        cross[one, row : row + 8, :] = cross_real
                        cross[one, kept + row : kept + row + 8, :] = cross_imag
                        cross[one, 2 * kept + row : 2 * kept + row + 8, :] = magnitude
                        if row == 0:
                            total = jnp.where(top, magnitude, 2.0 * magnitude)
                        elif row == block // 2:
                            total += magnitude
                        else:
                            total += 2.0 * magnitude
                    sums[one] = jnp.sum(total, axis=0, keepdims=True)

        means = jnp.sum(sums[...], axis=2, keepdims=True) * (1.0 / (block * block)) + 1e-06
        lag_sums = []
        for pair in range(local // 2):
            for order in range(many):
                norms = []
                for side in range(2):
                    one = (2 * pair + side) * many + order
                    scale = pl.reciprocal(cross[one, 2 * kept :, :] + means[one], approx=True)
                    norms.append(
                        jnp.concatenate(
                            [
                                cross[one, :kept, :] * scale,
                                no_rows,
                                cross[one, kept : 2 * kept, :] * scale,
                                no_rows,
                            ],
                            axis=0,
                        ).astype(jnp.bfloat16)
                    )
                lag_rows = jnp.dot(
                    lag_table, jnp.concatenate(norms, axis=1), preferred_element_type=jnp.float32
                ).astype(jnp.bfloat16)
                for side in range(2):
                    lanes = slice(side * block, (side + 1) * block)
                    lag_sums.append(
                        jnp.concatenate([lag_rows[:span, lanes], lag_rows[span:, lanes]], axis=1)
                    )
        lags = jnp.dot(
            jnp.concatenate(lag_sums, axis=0), span_ref[...], preferred_element_type=jnp.float32
        )
        for pair in range(local // 2):
            for order, (codes, _, v) in enumerate(volumes):
                for side in range(2):
                    index, _ = places[2 * pair + side]
                    row_shift = codes[v, 0, index] >> 4
                    col_shift = codes[v, 1, index] >> 4
                    at = (pair * many + order) * 2 + side
                    one = lags[at * span : (at + 1) * span]
                    one = pltpu.roll(one, span - SHIFT - row_shift, 0)[:WIN]
                    place = index // (2 * own) * own + (2 * pair + side) % own
                    found[order, pl.ds(pl.multiple_of(place * WIN, WIN), WIN), :] = pltpu.roll(
                        one, LANES - SHIFT - col_shift, 1
                    )
        return 0

    lax.fori_loop(0, depth, one_step, 0)

    share = depth * local // planes
    per_tile = LANES // WIN
    lane = lax.broadcasted_iota(jnp.int32, (share, LANES), 1) // WIN
    for turn, out_ref in enumerate(out_refs):
        plane = place_ref[3] ^ (turn % planes)
        for v in range(vols):
            order = turn // planes * vols + v
            for tile in range(WIN // per_tile):
                total = jnp.zeros((share, LANES), jnp.float32)
                for part in range(per_tile):
                    start = plane * share * WIN + tile * per_tile + part
                    one = found[order, pl.ds(start, share, stride=WIN), :]
                    if part:
                        one = pltpu.roll(one, part * WIN, 1)
                    total = jnp.where(lane == part, one, total)
                out_ref[v, :, tile * LANES : (tile + 1) * LANES] = total * (1.0 / block)


def lag_windows(place, codes, other_codes, frames, other_frames, templates, after, planes, own):
    vols, rows, cols = frames.shape
    block = templates[0].shape[-1]
    down, across = rows // block, cols // block
    depth = len(templates)
    tables = dft_constants(block)
    kept = -(-(block // 2 + 1) // 8) * 8
    smem = pl.BlockSpec(memory_space=pltpu.SMEM)
    vmem = pl.BlockSpec(memory_space=pltpu.VMEM)
    local = depth * 2 * own
    many = 2 * vols * 2 * own
    out = (vols, local // planes, WIN * WIN)
    return pl.pallas_call(
        functools.partial(spectrum_kernel, vols, across, block, own, planes, depth),
        out_shape=[jax.ShapeDtypeStruct(out, jnp.float32)] * (2 * planes),
        in_specs=[smem] * 3
        + [vmem] * (len(tables) + 2 + depth)
        + [pl.BlockSpec(memory_space=pl.ANY)],
        out_specs=[vmem] * (2 * planes),
        scratch_shapes=[
            pltpu.VMEM((depth, 2 * own, block, block), jnp.bfloat16),
            pltpu.VMEM((many, 3 * kept, LANES), jnp.float32),
            pltpu.VMEM((many, 1, LANES), jnp.float32),
            pltpu.VMEM((2 * vols, local * WIN, LANES), jnp.float32),
        ],
        compiler_params=pltpu.CompilerParams(vmem_limit_bytes=VMEM_LIMIT),
        cost_estimate=pl.CostEstimate(
            flops=2 * 3 * rows * cols * block * 16,
            bytes_accessed=vols * rows * cols * 4 + rows * cols,
            transcendentals=0,
        ),
        name="lag_windows",
    )(place, codes, other_codes, *tables, frames, other_frames, *templates, after)


def exchange(value, axes, size, turn):
    return lax.ppermute(value, axes, [(at, at ^ turn) for at in range(size)])


def on_device(frames, template, shift_codes):
    vol_dev, pl_dev, img_rows, img_cols = frames.shape
    own, block = template.shape[0], template.shape[-1]
    depth = lax.axis_size("z")
    planes = lax.axis_size("plane")
    share = 4 * depth * own // planes
    place = jnp.stack([lax.axis_index(axis) for axis in ("z", "y", "core", "plane")])
    other_codes = exchange(shift_codes, "core", 2, 1)
    other_template = exchange(template, "y", 2, 1)
    later_frames, other_template = lax.optimization_barrier((frames, other_template))
    other_frames = exchange(later_frames, "core", 2, 1)
    templates = [jnp.concatenate([template, other_template], axis=0)]
    for turn in range(1, depth):
        templates.append(exchange(templates[0], "z", depth, turn))
    averages, window = [], [0.0, 0.0]
    volumes = vol_dev * depth * 4
    for p in range(pl_dev):
        work = (place, shift_codes, other_codes, frames[:, p], other_frames[:, p])
        warped = warp_sums(*work, depth, block, own)
        chosen = [one[:, p] for one in templates]
        found = lag_windows(*work, chosen, warped[0], planes, own)
        warped = [warped[0]] + [
            exchange(warped[turn], "z", depth, turn) for turn in range(1, depth)
        ]
        sums = [sum(one[at : at + own].astype(jnp.float32) for one in warped) for at in (0, own)]
        found, sums = lax.optimization_barrier((found, sums))
        taken = exchange(sums[1].astype(jnp.bfloat16), "y", 2, 1)
        averages.append((sums[0] + taken.astype(jnp.float32)) * (1.0 / volumes))
        for turn, one in enumerate(found):
            if turn:
                one = exchange(one, ("core", "plane"), 2 * planes, turn)
            window[turn // planes] += one
    core = place[2]
    window = [jnp.where(core == 0, *window), jnp.where(core == 0, *window[::-1])]
    window = [one.reshape(vol_dev, share // (2 * own), 1, own, WIN * WIN) for one in window]
    correlation = jnp.concatenate(window, axis=2).reshape(vol_dev, share, WIN * WIN)
    return (correlation, jnp.stack(averages, axis=1))


def solution(mesh):
    devices = mesh.devices.reshape(-1, 2, 2, mesh.shape["plane"])
    split = jax.sharding.Mesh(devices, ("z", "y", "core", "plane"))
    vols = ("z", "y", "core")
    in_specs = (P(vols, "plane", None, None), P(vols, "plane", None, None), P(vols, None, None))
    out_specs = (P(vols, "plane", None), P(vols, "plane", None, None))
    return jax.shard_map(
        on_device, mesh=split, in_specs=in_specs, out_specs=out_specs, check_vma=False
    )
```

```python
import functools
import math

import jax
import jax.numpy as jnp
import numpy as np
from jax import lax
from jax.experimental import pallas as pl
from jax.experimental.pallas import tpu as pltpu
from jax.sharding import PartitionSpec as P

SHIFT = 8
WIN = 16
TAPS = 8
SUB = 16
EDGE = 16
LANES = 128
VMEM_LIMIT = 24 * 1024 * 1024

full_turn = 2.0 * math.pi


def dft_constants(block_size):
    positions = np.arange(block_size)
    angles = full_turn * (np.outer(positions, positions) % block_size) / block_size
    cosine = np.cos(angles)
    sine = -np.sin(angles)
    half = block_size // 2 + 1
    rows = -(-half // 16) * 16
    row_table = np.zeros((2 * rows, block_size))
    row_table[:half] = cosine[:half]
    row_table[rows : rows + half] = sine[:half]
    col_table = np.block([[cosine, sine], [-sine, cosine]])
    weights = np.full((half,), 2.0)
    weights[0] = weights[half - 1] = 1.0
    span = 2 * SHIFT + WIN
    lags = np.arange(span) - SHIFT - WIN // 2
    turns = full_turn * (np.outer(lags, positions) % block_size) / block_size
    lag_cos, lag_sin = np.cos(turns), np.sin(turns)
    lag_table = np.zeros((2 * span, 2 * rows))
    lag_table[:span, :half] = lag_cos[:, :half] * weights
    lag_table[:span, rows : rows + half] = -lag_sin[:, :half] * weights
    lag_table[span:, :half] = lag_sin[:, :half] * weights
    lag_table[span:, rows : rows + half] = lag_cos[:, :half] * weights
    span_table = np.zeros((2 * block_size, LANES))
    span_table[:block_size, :span] = lag_cos.T
    span_table[block_size:, :span] = -lag_sin.T
    return tuple(
        jnp.asarray(table, jnp.bfloat16) for table in (row_table, col_table, lag_table, span_table)
    )


def tap_constants():
    offsets = np.arange(TAPS) - (TAPS // 2 - 1)
    spots = offsets[None, :] - np.arange(SUB)[:, None] / SUB
    raw_taps = np.sinc(spots) * np.sinc(spots / (TAPS // 2))
    taps = raw_taps / raw_taps.sum(axis=-1, keepdims=True)
    table = np.zeros((2, SUB, EDGE, LANES))
    for row in range(EDGE):
        table[0, :, row, row : row + TAPS] = taps
        table[1, :, row, row : row + TAPS] = taps[:, ::-1]
    return jnp.asarray(table, jnp.float32)


def band_groups(head, start, lane):
    head = pltpu.roll(head, start + LANES, 1).astype(jnp.bfloat16)
    groups = [head] + [pltpu.roll(head, step, 1) for step in range(EDGE, LANES, EDGE)]
    zero = jnp.zeros_like(head)
    low = lane < LANES // 2
    before, after = jnp.where(low, zero, groups[0]), jnp.where(low, groups[-1], zero)
    middle = [jnp.where(low, groups[0], zero), *groups[1:-1], jnp.where(low, zero, groups[-1])]
    return middle, before, after


def step_places(place_ref, step, across, own):
    z = place_ref[0] ^ step
    places = []
    for other in range(2):
        for one in range(own):
            index = ((2 * z + (place_ref[1] ^ other)) * 2 + place_ref[2]) * own + one
            places.append((index, index % across))
    return places


def step_band(place_ref, step, across, own):
    return (place_ref[0] ^ step) * (4 * own) // across


def band_kernel(
    vols, across, own, depth, place_ref, codes_ref, other_codes_ref, heads_ref, *out_refs
):
    cols_ref, rows_ref, edges_ref = out_refs
    lane = lax.broadcasted_iota(jnp.int32, (EDGE, LANES), 1)
    volumes = [(codes_ref, v) for v in range(vols)] + [(other_codes_ref, v) for v in range(vols)]
    many = len(volumes)
    per_tile = LANES // (2 * EDGE)

    def one_step(step, _):
        for count, (index, _) in enumerate(step_places(place_ref, step, across, own)):
            block_at = step * (2 * own) + count
            edges = []
            for order, (codes, v) in enumerate(volumes):
                row_code = codes[v, 0, index]
                col_code = codes[v, 1, index]
                middle, before, after = band_groups(
                    heads_ref[1, col_code & (SUB - 1)], -(TAPS // 2) - (col_code >> 4), lane
                )
                one = block_at * many + order
                cols_ref[one] = jnp.concatenate([*middle, before, after], axis=0)
                middle, before, after = band_groups(
                    heads_ref[0, row_code & (SUB - 1)], (row_code >> 4) - (TAPS // 2 - 1), lane
                )
                rows_ref[one] = jnp.concatenate(middle, axis=0)
                place = 2 * EDGE * order % LANES
                first = pltpu.roll(before, (place + 2 * EDGE) % LANES, 1)
                last = pltpu.roll(after, place, 1) if place else after
                if order % per_tile:
                    first, last = edges[-1][0] + first, edges[-1][1] + last
                    edges.pop()
                edges.append((first, last))
            for at, (first, last) in enumerate(edges):
                edges_ref[block_at * len(edges) + at] = jnp.concatenate([first, last], axis=0)
        return 0

    lax.fori_loop(0, depth, one_step, 0)


def warp_bands(place, codes, other_codes, across, depth, block, own):
    vols = codes.shape[0]
    heads = tap_constants()
    smem = pl.BlockSpec(memory_space=pltpu.SMEM)
    vmem = pl.BlockSpec(memory_space=pltpu.VMEM)
    blocks = depth * 2 * own
    tiles = -(-2 * vols * 2 * EDGE // LANES)
    shapes = [
        (blocks * 2 * vols, block + 2 * EDGE, block),
        (blocks * 2 * vols, block, block),
        (blocks * tiles, 2 * EDGE, LANES),
    ]
    return pl.pallas_call(
        functools.partial(band_kernel, vols, across, own, depth),
        out_shape=[jax.ShapeDtypeStruct(shape, jnp.bfloat16) for shape in shapes],
        in_specs=[smem] * 3 + [vmem],
        out_specs=[vmem] * 3,
        compiler_params=pltpu.CompilerParams(vmem_limit_bytes=VMEM_LIMIT),
        cost_estimate=pl.CostEstimate(
            flops=blocks * vols * block * block * 128, bytes_accessed=0, transcendentals=0
        ),
        name="bands",
    )(place, codes, other_codes, heads)


def warp_step(place_ref, step, frame_refs, band_refs, down, across, block, own):
    cols_ref, rows_ref, edges_ref = band_refs
    band = step_band(place_ref, step, across, own)
    row = pl.multiple_of(band * block, block)
    row_above = pl.multiple_of(jnp.maximum(row - EDGE, 0), EDGE)
    row_below = pl.multiple_of(jnp.minimum(row + block, down * block - EDGE), EDGE)
    zero = jnp.zeros((EDGE, LANES), jnp.bfloat16)
    gap = jnp.zeros((block - 2 * EDGE, LANES), jnp.bfloat16)
    no_tile = jnp.zeros((block + 2 * EDGE, block), jnp.bfloat16)
    volumes = [(frames, v) for frames in frame_refs for v in range(frames.shape[0])]
    many = len(volumes)
    tiles = -(-many * 2 * EDGE // LANES)

    def tile(frames, v, at):
        lanes = pl.ds(pl.multiple_of(at * block, block), block)
        above = jnp.where(band > 0, frames[v, pl.ds(row_above, EDGE), lanes], zero)
        below = jnp.where(band < down - 1, frames[v, pl.ds(row_below, EDGE), lanes], zero)
        return jnp.concatenate([frames[v, pl.ds(row, block), lanes], below, above], axis=0)

    totals = []
    for count, (_, at) in enumerate(step_places(place_ref, step, across, own)):
        block_at = step * (2 * own) + count
        row_tiles, partials, edges = [], [], []
        for order, (frames, v) in enumerate(volumes):
            one = block_at * many + order
            left = jnp.where(at > 0, tile(frames, v, jnp.maximum(at - 1, 0)), no_tile)
            right = jnp.where(
                at < across - 1, tile(frames, v, jnp.minimum(at + 1, across - 1)), no_tile
            )
            sides = jnp.concatenate([right[:, : block // 2], left[:, block // 2 :]], axis=1)
            cols = cols_ref[one]
            partial = jnp.dot(
                jnp.concatenate([tile(frames, v, at), sides], axis=1),
                jnp.concatenate([cols[: block + EDGE], gap, cols[block + EDGE :]], axis=0),
                preferred_element_type=jnp.float32,
            ).astype(jnp.bfloat16)
            partials.append(partial[:block])
            edges.append(partial[block:])
            row_tiles.append(rows_ref[one])
        for at_tile in range(tiles):
            both = edges_ref[block_at * tiles + at_tile]
            row_tiles.append(jnp.concatenate([both[:EDGE], gap, both[EDGE:]], axis=0))
        deep = many * (block + 2 * EDGE)
        total = jnp.dot(
            jnp.concatenate(row_tiles, axis=1)[:, :deep],
            jnp.concatenate(partials + edges, axis=0),
            preferred_element_type=jnp.float32,
        )
        totals.append(total.astype(jnp.bfloat16))
    return totals


def warp_kernel(down, across, block, own, depth, *refs):
    place_ref, frames_hbm, other_frames_ref, *band_refs = refs[:6]
    out_refs = refs[6 : 5 + depth]
    frames_ref, sums, sem = refs[5 + depth :]
    copy = pltpu.make_async_copy(frames_hbm, frames_ref, sem)
    copy.start()
    copy.wait()
    frame_refs = (frames_ref, other_frames_ref)

    def one_step(step, _):
        totals = warp_step(place_ref, step, frame_refs, band_refs, down, across, block, own)
        for count, total in enumerate(totals):
            sums[count] = total
        for at, out_ref in enumerate(out_refs):

            @pl.when(step == at + 1)
            def _():
                out_ref[...] = sums[...]

        return 0

    lax.fori_loop(1, depth, one_step, 0)


def warp_sums(place, frames, other_frames, bands, depth, block, own):
    vols, rows, cols = frames.shape
    down, across = rows // block, cols // block
    out = (2 * own, block, block)
    hbm = pl.BlockSpec(memory_space=pltpu.HBM)
    vmem = pl.BlockSpec(memory_space=pltpu.VMEM)
    return pl.pallas_call(
        functools.partial(warp_kernel, down, across, block, own, depth),
        out_shape=[jax.ShapeDtypeStruct(out, jnp.bfloat16)] * (depth - 1),
        in_specs=[pl.BlockSpec(memory_space=pltpu.SMEM), hbm] + [vmem] * 4,
        out_specs=[vmem] * (depth - 1),
        scratch_shapes=[
            pltpu.VMEM(frames.shape, jnp.bfloat16),
            pltpu.VMEM(out, jnp.bfloat16),
            pltpu.SemaphoreType.DMA,
        ],
        compiler_params=pltpu.CompilerParams(vmem_limit_bytes=VMEM_LIMIT),
        cost_estimate=pl.CostEstimate(
            flops=2 * vols * rows * cols * block * 16,
            bytes_accessed=vols * rows * cols * 4 + rows * cols,
            transcendentals=0,
        ),
        name="warp",
    )(place, pltpu.with_memory_space_constraint(frames, pltpu.HBM), other_frames, *bands)


def spectrum_kernel(vols, down, across, block, own, planes, depth, *refs):
    place_ref, codes_ref, other_codes_ref, row_ref, col_ref, lag_ref, span_ref = refs[:7]
    frames_ref, other_frames_ref, near_ref, far_ref, *band_refs = refs[7:14]
    out_refs, sums_ref = refs[15 : 15 + 2 * planes], refs[15 + 2 * planes]
    cross, sums, found = refs[16 + 2 * planes :]
    frame_refs = (frames_ref, other_frames_ref)
    totals = warp_step(place_ref, 0, frame_refs, band_refs, down, across, block, own)
    for count, total in enumerate(totals):
        sums_ref[count] = total

    row_table = row_ref[...]
    col_table = col_ref[...]
    lag_table = lag_ref[...]
    half = row_table.shape[0] // 2
    kept = -(-(block // 2 + 1) // 8) * 8
    span = lag_table.shape[0] // 2
    top = lax.broadcasted_iota(jnp.int32, (8, LANES), 0) == 0
    volumes = [(codes_ref, frames_ref, v) for v in range(vols)]
    volumes += [(other_codes_ref, other_frames_ref, v) for v in range(vols)]
    many = len(volumes)
    local = 2 * own
    no_rows = jnp.zeros((half - kept, LANES), jnp.float32)

    def one_step(step, _):
        places = step_places(place_ref, step, across, own)
        band = step_band(place_ref, step, across, own)
        band_rows = pl.ds(pl.multiple_of(band * block, block), block)

        for pair in range(local // 2):
            pair_places = places[2 * pair : 2 * pair + 2]
            counts = (2 * pair, 2 * pair + 1)
            sources = [
                [(far_ref if count // own else near_ref)[step * own + count % own] for count in counts]
            ]
            for _, frames, v in volumes:
                sources.append(
                    [
                        frames[v, band_rows, pl.ds(pl.multiple_of(at * block, block), block)]
                        for _, at in pair_places
                    ]
                )
            parts = []
            for source in sources:
                rows = jnp.dot(
                    row_table,
                    jnp.concatenate(source, axis=1),
                    preferred_element_type=jnp.float32,
                ).astype(jnp.bfloat16)
                for side in range(2):
                    lanes = slice(side * block, (side + 1) * block)
                    parts.append(jnp.concatenate([rows[:half, lanes], rows[half:, lanes]], axis=1))
            spectra = jnp.dot(
                jnp.concatenate(parts, axis=0), col_table, preferred_element_type=jnp.float32
            )
            temp = spectra[: 2 * half].astype(jnp.bfloat16).astype(jnp.float32)
            for order in range(many):
                for side in range(2):
                    one = (2 * pair + side) * many + order
                    base = (2 * (order + 1) + side) * half
                    total = jnp.zeros((8, LANES), jnp.float32)
                    for row in range(0, kept, 8):
                        at = side * half + row
                        temp_real = temp[at : at + 8, :block]
                        temp_imag = temp[at : at + 8, block:]
                        real = spectra[base + row : base + row + 8, :block]
                        imag = spectra[base + row : base + row + 8, block:]
                        cross_real = real * temp_real + imag * temp_imag
                        cross_imag = imag * temp_real - real * temp_imag
                        power = cross_real * cross_real + cross_imag * cross_imag
                        magnitude = power * lax.rsqrt(jnp.maximum(power, 1e-36))
                        cross[one, row : row + 8, :] = cross_real
                        cross[one, kept + row : kept + row + 8, :] = cross_imag
                        cross[one, 2 * kept + row : 2 * kept + row + 8, :] = magnitude
                        if row == 0:
                            total = jnp.where(top, magnitude, 2.0 * magnitude)
                        elif row == block // 2:
                            total += magnitude
                        else:
                            total += 2.0 * magnitude
                    sums[one] = jnp.sum(total, axis=0, keepdims=True)

        means = jnp.sum(sums[...], axis=2, keepdims=True) * (1.0 / (block * block)) + 1e-06
        lag_sums = []
        for pair in range(local // 2):
            for order in range(many):
                norms = []
                for side in range(2):
                    one = (2 * pair + side) * many + order
                    scale = pl.reciprocal(cross[one, 2 * kept :, :] + means[one], approx=True)
                    norms.append(
                        jnp.concatenate(
                            [
                                cross[one, :kept, :] * scale,
                                no_rows,
                                cross[one, kept : 2 * kept, :] * scale,
                                no_rows,
                            ],
                            axis=0,
                        ).astype(jnp.bfloat16)
                    )
                lag_rows = jnp.dot(
                    lag_table, jnp.concatenate(norms, axis=1), preferred_element_type=jnp.float32
                ).astype(jnp.bfloat16)
                for side in range(2):
                    lanes = slice(side * block, (side + 1) * block)
                    lag_sums.append(
                        jnp.concatenate([lag_rows[:span, lanes], lag_rows[span:, lanes]], axis=1)
                    )
        lags = jnp.dot(
            jnp.concatenate(lag_sums, axis=0), span_ref[...], preferred_element_type=jnp.float32
        )
        for pair in range(local // 2):
            for order, (codes, _, v) in enumerate(volumes):
                for side in range(2):
                    index, _ = places[2 * pair + side]
                    row_shift = codes[v, 0, index] >> 4
                    col_shift = codes[v, 1, index] >> 4
                    at = (pair * many + order) * 2 + side
                    one = lags[at * span : (at + 1) * span]
                    one = pltpu.roll(one, span - SHIFT - row_shift, 0)[:WIN]
                    place = index // (2 * own) * own + (2 * pair + side) % own
                    found[order, pl.ds(pl.multiple_of(place * WIN, WIN), WIN), :] = pltpu.roll(
                        one, LANES - SHIFT - col_shift, 1
                    )
        return 0

    lax.fori_loop(0, depth, one_step, 0)

    share = depth * local // planes
    per_tile = LANES // WIN
    lane = lax.broadcasted_iota(jnp.int32, (share, LANES), 1) // WIN
    for turn, out_ref in enumerate(out_refs):
        plane = place_ref[3] ^ (turn % planes)
        for v in range(vols):
            order = turn // planes * vols + v
            for tile in range(WIN // per_tile):
                total = jnp.zeros((share, LANES), jnp.float32)
                for part in range(per_tile):
                    start = plane * share * WIN + tile * per_tile + part
                    one = found[order, pl.ds(start, share, stride=WIN), :]
                    if part:
                        one = pltpu.roll(one, part * WIN, 1)
                    total = jnp.where(lane == part, one, total)
                out_ref[v, :, tile * LANES : (tile + 1) * LANES] = total * (1.0 / block)


def lag_windows(
    place, codes, other_codes, frames, other_frames, templates, bands, after, planes, depth, own
):
    vols, rows, cols = frames.shape
    block = templates[0].shape[-1]
    down, across = rows // block, cols // block
    tables = dft_constants(block)
    kept = -(-(block // 2 + 1) // 8) * 8
    smem = pl.BlockSpec(memory_space=pltpu.SMEM)
    vmem = pl.BlockSpec(memory_space=pltpu.VMEM)
    local = depth * 2 * own
    many = 2 * vols * 2 * own
    out = (vols, local // planes, WIN * WIN)
    kept_sums = (2 * own, block, block)
    return pl.pallas_call(
        functools.partial(spectrum_kernel, vols, down, across, block, own, planes, depth),
        out_shape=[jax.ShapeDtypeStruct(out, jnp.float32)] * (2 * planes)
        + [jax.ShapeDtypeStruct(kept_sums, jnp.bfloat16)],
        in_specs=[smem] * 3
        + [vmem] * (len(tables) + 4 + len(bands))
        + [pl.BlockSpec(memory_space=pl.ANY)],
        out_specs=[vmem] * (2 * planes + 1),
        scratch_shapes=[
            pltpu.VMEM((many, 3 * kept, LANES), jnp.float32),
            pltpu.VMEM((many, 1, LANES), jnp.float32),
            pltpu.VMEM((2 * vols, local * WIN, LANES), jnp.float32),
        ],
        compiler_params=pltpu.CompilerParams(vmem_limit_bytes=VMEM_LIMIT),
        cost_estimate=pl.CostEstimate(
            flops=2 * 3 * rows * cols * block * 16,
            bytes_accessed=vols * rows * cols * 4 + rows * cols,
            transcendentals=0,
        ),
        name="lag_windows",
    )(place, codes, other_codes, *tables, frames, other_frames, *templates, *bands, after)


def exchange(value, axes, size, turn):
    return lax.ppermute(value, axes, [(at, at ^ turn) for at in range(size)])


def on_device(frames, template, shift_codes):
    vol_dev, pl_dev, img_rows, img_cols = frames.shape
    own, block = template.shape[0], template.shape[-1]
    depth = lax.axis_size("z")
    planes = lax.axis_size("plane")
    share = 4 * depth * own // planes
    place = jnp.stack([lax.axis_index(axis) for axis in ("z", "y", "core", "plane")])
    other_codes = exchange(shift_codes, "core", 2, 1)
    other_frames = exchange(frames, "core", 2, 1)
    near = jnp.concatenate(
        [template] + [exchange(template, "z", depth, turn) for turn in range(1, depth)], axis=0
    )
    far = exchange(near, "y", 2, 1)
    bands = warp_bands(place, shift_codes, other_codes, img_cols // block, depth, block, own)
    averages, window = [], [0.0, 0.0]
    volumes = vol_dev * depth * 4
    for p in range(pl_dev):
        work = (frames[:, p], other_frames[:, p])
        warped = warp_sums(place, *work, bands, depth, block, own)
        templates = (near[:, p], far[:, p])
        *found, kept = lag_windows(
            place, shift_codes, other_codes, *work, templates, bands, warped[0], planes, depth, own
        )
        warped = [exchange(one, "z", depth, turn + 1) for turn, one in enumerate(warped)]
        found, warped[0] = lax.optimization_barrier((found, warped[0]))
        warped.append(kept)
        sums = [sum(one[at : at + own].astype(jnp.float32) for one in warped) for at in (0, own)]
        taken = exchange(sums[1].astype(jnp.bfloat16), "y", 2, 1)
        averages.append((sums[0] + taken.astype(jnp.float32)) * (1.0 / volumes))
        for turn, one in enumerate(found):
            if turn:
                one = exchange(one, ("core", "plane"), 2 * planes, turn)
            window[turn // planes] += one
    core = place[2]
    window = [jnp.where(core == 0, *window), jnp.where(core == 0, *window[::-1])]
    window = [one.reshape(vol_dev, share // (2 * own), 1, own, WIN * WIN) for one in window]
    correlation = jnp.concatenate(window, axis=2).reshape(vol_dev, share, WIN * WIN)
    return (correlation, jnp.stack(averages, axis=1))


def solution(mesh):
    devices = mesh.devices.reshape(-1, 2, 2, mesh.shape["plane"])
    split = jax.sharding.Mesh(devices, ("z", "y", "core", "plane"))
    vols = ("z", "y", "core")
    in_specs = (P(vols, "plane", None, None), P(vols, "plane", None, None), P(vols, None, None))
    out_specs = (P(vols, "plane", None), P(vols, "plane", None, None))
    return jax.shard_map(
        on_device, mesh=split, in_specs=in_specs, out_specs=out_specs, check_vma=False
    )
```

```python
import functools
import math

import jax
import jax.numpy as jnp
import numpy as np
from jax import lax
from jax.experimental import pallas as pl
from jax.experimental.pallas import tpu as pltpu
from jax.sharding import PartitionSpec as P

SHIFT = 8
WIN = 16
TAPS = 8
SUB = 16
EDGE = 16
LANES = 128
VMEM_LIMIT = 24 * 1024 * 1024

full_turn = 2.0 * math.pi


def dft_constants(block_size):
    positions = np.arange(block_size)
    angles = full_turn * (np.outer(positions, positions) % block_size) / block_size
    cosine = np.cos(angles)
    sine = -np.sin(angles)
    half = block_size // 2 + 1
    rows = -(-half // 16) * 16
    row_table = np.zeros((2 * rows, block_size))
    row_table[:half] = cosine[:half]
    row_table[rows : rows + half] = sine[:half]
    col_table = np.block([[cosine, sine], [-sine, cosine]])
    weights = np.full((half,), 2.0)
    weights[0] = weights[half - 1] = 1.0
    span = 2 * SHIFT + WIN
    lags = np.arange(span) - SHIFT - WIN // 2
    turns = full_turn * (np.outer(lags, positions) % block_size) / block_size
    lag_cos, lag_sin = np.cos(turns), np.sin(turns)
    lag_table = np.zeros((2 * span, 2 * rows))
    lag_table[:span, :half] = lag_cos[:, :half] * weights
    lag_table[:span, rows : rows + half] = -lag_sin[:, :half] * weights
    lag_table[span:, :half] = lag_sin[:, :half] * weights
    lag_table[span:, rows : rows + half] = lag_cos[:, :half] * weights
    span_table = np.zeros((2 * block_size, LANES))
    span_table[:block_size, :span] = lag_cos.T
    span_table[block_size:, :span] = -lag_sin.T
    return tuple(
        jnp.asarray(table, jnp.bfloat16) for table in (row_table, col_table, lag_table, span_table)
    )


def tap_constants(block_size):
    offsets = np.arange(TAPS) - (TAPS // 2 - 1)
    spots = offsets[None, :] - np.arange(SUB)[:, None] / SUB
    raw_taps = np.sinc(spots) * np.sinc(spots / (TAPS // 2))
    taps = raw_taps / raw_taps.sum(axis=-1, keepdims=True)

    def band(inputs, outputs):
        at = inputs - outputs + TAPS // 2 - 1
        return np.where((at >= 0) & (at < TAPS), taps[:, np.clip(at, 0, TAPS - 1)], 0.0)

    lanes = np.arange(block_size)[None, :]
    inputs = np.arange(block_size + 3 * EDGE)[:, None] - EDGE - SHIFT
    outputs = np.arange(block_size + EDGE)[:, None] - SHIFT
    spare = np.arange(LANES)[None, :] % (2 * EDGE)
    first = band(spare - 2 * EDGE, outputs[: 2 * EDGE]) * (spare >= EDGE)
    last = band(spare + EDGE, outputs[: 2 * EDGE]) * (spare < EDGE)
    tables = band(inputs, lanes), band(lanes, outputs), np.stack([first, last], axis=1)
    return [jnp.asarray(table, jnp.float32) for table in tables]


def step_places(place_ref, step, across, own):
    z = place_ref[0] ^ step
    places = []
    for other in range(2):
        for one in range(own):
            index = ((2 * z + (place_ref[1] ^ other)) * 2 + place_ref[2]) * own + one
            places.append((index, index % across))
    return places


def step_band(place_ref, step, across, own):
    return (place_ref[0] ^ step) * (4 * own) // across


def stage_kernel(count, *refs):
    sources, targets, sems = refs[:count], refs[count + 1 : 2 * count + 1], refs[-1]
    copies = [
        pltpu.make_async_copy(source, target, sems.at[at])
        for at, (source, target) in enumerate(zip(sources, targets))
    ]
    for copy in copies:
        copy.start()
    for copy in copies:
        copy.wait()


def stage(arrays, after):
    kept = [pltpu.with_memory_space_constraint(one, pltpu.HBM) for one in arrays]
    count = len(arrays)
    return pl.pallas_call(
        functools.partial(stage_kernel, count),
        out_shape=[jax.ShapeDtypeStruct(one.shape, one.dtype) for one in arrays],
        in_specs=[pl.BlockSpec(memory_space=pltpu.HBM)] * count
        + [pl.BlockSpec(memory_space=pl.ANY)],
        out_specs=[pl.BlockSpec(memory_space=pltpu.VMEM)] * count,
        scratch_shapes=[pltpu.SemaphoreType.DMA((count,))],
        compiler_params=pltpu.CompilerParams(vmem_limit_bytes=VMEM_LIMIT),
        name="stage",
    )(*kept, after)


def warp_step(place_ref, step, code_refs, frame_refs, band_refs, down, across, block, own):
    cols_ref, rows_ref, edges_ref = band_refs
    band = step_band(place_ref, step, across, own)
    row = pl.multiple_of(band * block, block)
    row_above = pl.multiple_of(jnp.maximum(row - EDGE, 0), EDGE)
    row_below = pl.multiple_of(jnp.minimum(row + block, down * block - EDGE), EDGE)
    zero = jnp.zeros((EDGE, LANES), jnp.bfloat16)
    gap = jnp.zeros((block - 2 * EDGE, LANES), jnp.bfloat16)
    no_tile = jnp.zeros((block + 2 * EDGE, block), jnp.bfloat16)
    volumes = [
        (codes, frames, v)
        for codes, frames in zip(code_refs, frame_refs)
        for v in range(frames.shape[0])
    ]
    many = len(volumes)
    per_tile = LANES // (2 * EDGE)
    lane = lax.broadcasted_iota(jnp.int32, (EDGE, LANES), 1) // (2 * EDGE)

    def tile(frames, v, at):
        lanes = pl.ds(pl.multiple_of(at * block, block), block)
        above = jnp.where(band > 0, frames[v, pl.ds(row_above, EDGE), lanes], zero)
        below = jnp.where(band < down - 1, frames[v, pl.ds(row_below, EDGE), lanes], zero)
        return jnp.concatenate([frames[v, pl.ds(row, block), lanes], below, above], axis=0)

    places = step_places(place_ref, step, across, own)
    totals = []
    for group in range(0, len(places), own):
        start = places[group][1]
        tiles = []
        for _, frames, v in volumes:
            left = jnp.where(start > 0, tile(frames, v, jnp.maximum(start - 1, 0)), no_tile)
            right = jnp.where(
                start + own < across,
                tile(frames, v, jnp.minimum(start + own, across - 1)),
                no_tile,
            )
            tiles.append([left] + [tile(frames, v, start + one) for one in range(own)] + [right])
        for one in range(own):
            index = places[group + one][0]
            row_tiles, partials, edges = [], [], []
            firsts, lasts = [], []
            for order, (codes, _, v) in enumerate(volumes):
                row_code, col_code = codes[v, 0, index], codes[v, 1, index]
                left, middle, right = tiles[order][one : one + 3]
                sides = jnp.concatenate([right[:, : block // 2], left[:, block // 2 :]], axis=1)
                col_start = SHIFT - (col_code >> 4)
                cols = cols_ref[col_code & (SUB - 1), pl.ds(col_start, block + 2 * EDGE), :]
                cols = cols.astype(jnp.bfloat16)
                partial = jnp.dot(
                    jnp.concatenate([middle, sides], axis=1),
                    jnp.concatenate([cols[EDGE:], gap, cols[:EDGE]], axis=0),
                    preferred_element_type=jnp.float32,
                ).astype(jnp.bfloat16)
                partials.append(partial[:block])
                edges.append(partial[block:])
                row_start = SHIFT + (row_code >> 4)
                step_at = row_code & (SUB - 1)
                row_tiles.append(rows_ref[step_at, pl.ds(row_start, block), :].astype(jnp.bfloat16))
                first = edges_ref[step_at, 0, pl.ds(row_start, EDGE), :]
                last = edges_ref[step_at, 1, pl.ds(row_start, EDGE), :]
                if order % per_tile:
                    first = jnp.where(lane == order % per_tile, first, firsts.pop())
                    last = jnp.where(lane == order % per_tile, last, lasts.pop())
                firsts.append(first)
                lasts.append(last)
            for first, last in zip(firsts, lasts):
                both = [first.astype(jnp.bfloat16), gap, last.astype(jnp.bfloat16)]
                row_tiles.append(jnp.concatenate(both, axis=0))
            deep = many * (block + 2 * EDGE)
            total = jnp.dot(
                jnp.concatenate(row_tiles, axis=1)[:, :deep],
                jnp.concatenate(partials + edges, axis=0),
                preferred_element_type=jnp.float32,
            )
            totals.append(total.astype(jnp.bfloat16))
    return totals


def warp_kernel(down, across, block, own, depth, *refs):
    place_ref, *code_refs = refs[:3]
    frame_refs, band_refs = refs[3:5], refs[5:8]
    out_refs, sums = refs[8 : 7 + depth], refs[7 + depth]

    def one_step(step, _):
        totals = warp_step(
            place_ref, step, code_refs, frame_refs, band_refs, down, across, block, own
        )
        for count, total in enumerate(totals):
            sums[count] = total
        for at, out_ref in enumerate(out_refs):

            @pl.when(step == at + 1)
            def _():
                out_ref[...] = sums[...]

        return 0

    lax.fori_loop(1, depth, one_step, 0)


def warp_sums(place, codes, other_codes, frames, other_frames, bands, depth, block, own):
    vols, rows, cols = frames.shape
    down, across = rows // block, cols // block
    out = (2 * own, block, block)
    smem = pl.BlockSpec(memory_space=pltpu.SMEM)
    vmem = pl.BlockSpec(memory_space=pltpu.VMEM)
    return pl.pallas_call(
        functools.partial(warp_kernel, down, across, block, own, depth),
        out_shape=[jax.ShapeDtypeStruct(out, jnp.bfloat16)] * (depth - 1),
        in_specs=[smem] * 3 + [vmem] * 5,
        out_specs=[vmem] * (depth - 1),
        scratch_shapes=[pltpu.VMEM(out, jnp.bfloat16)],
        compiler_params=pltpu.CompilerParams(vmem_limit_bytes=VMEM_LIMIT),
        cost_estimate=pl.CostEstimate(
            flops=2 * vols * rows * cols * block * 16,
            bytes_accessed=vols * rows * cols * 4 + rows * cols,
            transcendentals=0,
        ),
        name="warp",
    )(place, codes, other_codes, frames, other_frames, *bands)


def spectrum_kernel(vols, down, across, block, own, planes, depth, *refs):
    place_ref, codes_ref, other_codes_ref, row_ref, col_ref, lag_ref, span_ref = refs[:7]
    frames_ref, other_frames_ref, near_ref, far_ref, *band_refs = refs[7:14]
    out_refs, sums_ref = refs[15 : 15 + 2 * planes], refs[15 + 2 * planes]
    cross, sums, found = refs[16 + 2 * planes :]
    frame_refs = (frames_ref, other_frames_ref)
    code_refs = (codes_ref, other_codes_ref)
    totals = warp_step(place_ref, 0, code_refs, frame_refs, band_refs, down, across, block, own)
    for count, total in enumerate(totals):
        sums_ref[count] = total

    row_table = row_ref[...]
    col_table = col_ref[...]
    lag_table = lag_ref[...]
    half = row_table.shape[0] // 2
    kept = -(-(block // 2 + 1) // 8) * 8
    span = lag_table.shape[0] // 2
    top = lax.broadcasted_iota(jnp.int32, (8, LANES), 0) == 0
    volumes = [(codes_ref, frames_ref, v) for v in range(vols)]
    volumes += [(other_codes_ref, other_frames_ref, v) for v in range(vols)]
    many = len(volumes)
    local = 2 * own
    no_rows = jnp.zeros((half - kept, LANES), jnp.float32)

    def one_step(step, _):
        places = step_places(place_ref, step, across, own)
        band = step_band(place_ref, step, across, own)
        band_rows = pl.ds(pl.multiple_of(band * block, block), block)

        for pair in range(local // 2):
            pair_places = places[2 * pair : 2 * pair + 2]
            counts = (2 * pair, 2 * pair + 1)
            sources = [
                [(far_ref if count // own else near_ref)[step * own + count % own] for count in counts]
            ]
            for _, frames, v in volumes:
                sources.append(
                    [
                        frames[v, band_rows, pl.ds(pl.multiple_of(at * block, block), block)]
                        for _, at in pair_places
                    ]
                )
            parts = []
            for source in sources:
                rows = jnp.dot(
                    row_table,
                    jnp.concatenate(source, axis=1),
                    preferred_element_type=jnp.float32,
                ).astype(jnp.bfloat16)
                for side in range(2):
                    lanes = slice(side * block, (side + 1) * block)
                    parts.append(jnp.concatenate([rows[:half, lanes], rows[half:, lanes]], axis=1))
            spectra = jnp.dot(
                jnp.concatenate(parts, axis=0), col_table, preferred_element_type=jnp.float32
            )
            temp = spectra[: 2 * half].astype(jnp.bfloat16).astype(jnp.float32)
            for order in range(many):
                for side in range(2):
                    one = (2 * pair + side) * many + order
                    base = (2 * (order + 1) + side) * half
                    total = jnp.zeros((8, LANES), jnp.float32)
                    for row in range(0, kept, 8):
                        at = side * half + row
                        temp_real = temp[at : at + 8, :block]
                        temp_imag = temp[at : at + 8, block:]
                        real = spectra[base + row : base + row + 8, :block]
                        imag = spectra[base + row : base + row + 8, block:]
                        cross_real = real * temp_real + imag * temp_imag
                        cross_imag = imag * temp_real - real * temp_imag
                        power = cross_real * cross_real + cross_imag * cross_imag
                        magnitude = power * lax.rsqrt(jnp.maximum(power, 1e-36))
                        cross[one, row : row + 8, :] = cross_real
                        cross[one, kept + row : kept + row + 8, :] = cross_imag
                        cross[one, 2 * kept + row : 2 * kept + row + 8, :] = magnitude
                        if row == 0:
                            total = jnp.where(top, magnitude, 2.0 * magnitude)
                        elif row == block // 2:
                            total += magnitude
                        else:
                            total += 2.0 * magnitude
                    sums[one] = jnp.sum(total, axis=0, keepdims=True)

        means = jnp.sum(sums[...], axis=2, keepdims=True) * (1.0 / (block * block)) + 1e-06
        lag_sums = []
        for pair in range(local // 2):
            for order in range(many):
                norms = []
                for side in range(2):
                    one = (2 * pair + side) * many + order
                    scale = pl.reciprocal(cross[one, 2 * kept :, :] + means[one], approx=True)
                    norms.append(
                        jnp.concatenate(
                            [
                                cross[one, :kept, :] * scale,
                                no_rows,
                                cross[one, kept : 2 * kept, :] * scale,
                                no_rows,
                            ],
                            axis=0,
                        ).astype(jnp.bfloat16)
                    )
                lag_rows = jnp.dot(
                    lag_table, jnp.concatenate(norms, axis=1), preferred_element_type=jnp.float32
                ).astype(jnp.bfloat16)
                for side in range(2):
                    lanes = slice(side * block, (side + 1) * block)
                    lag_sums.append(
                        jnp.concatenate([lag_rows[:span, lanes], lag_rows[span:, lanes]], axis=1)
                    )
        lags = jnp.dot(
            jnp.concatenate(lag_sums, axis=0), span_ref[...], preferred_element_type=jnp.float32
        )
        for pair in range(local // 2):
            for order, (codes, _, v) in enumerate(volumes):
                for side in range(2):
                    index, _ = places[2 * pair + side]
                    row_shift = codes[v, 0, index] >> 4
                    col_shift = codes[v, 1, index] >> 4
                    at = (pair * many + order) * 2 + side
                    one = lags[at * span : (at + 1) * span]
                    one = pltpu.roll(one, span - SHIFT - row_shift, 0)[:WIN]
                    place = index // (2 * own) * own + (2 * pair + side) % own
                    found[order, pl.ds(pl.multiple_of(place * WIN, WIN), WIN), :] = pltpu.roll(
                        one, LANES - SHIFT - col_shift, 1
                    )
        return 0

    lax.fori_loop(0, depth, one_step, 0)

    share = depth * local // planes
    per_tile = LANES // WIN
    lane = lax.broadcasted_iota(jnp.int32, (share, LANES), 1) // WIN
    for turn, out_ref in enumerate(out_refs):
        plane = place_ref[3] ^ (turn % planes)
        for v in range(vols):
            order = turn // planes * vols + v
            for tile in range(WIN // per_tile):
                total = jnp.zeros((share, LANES), jnp.float32)
                for part in range(per_tile):
                    start = plane * share * WIN + tile * per_tile + part
                    one = found[order, pl.ds(start, share, stride=WIN), :]
                    if part:
                        one = pltpu.roll(one, part * WIN, 1)
                    total = jnp.where(lane == part, one, total)
                out_ref[v, :, tile * LANES : (tile + 1) * LANES] = total * (1.0 / block)


def lag_windows(
    place, codes, other_codes, frames, other_frames, templates, bands, after, planes, depth, own
):
    vols, rows, cols = frames.shape
    block = templates[0].shape[-1]
    down, across = rows // block, cols // block
    tables = dft_constants(block)
    kept = -(-(block // 2 + 1) // 8) * 8
    smem = pl.BlockSpec(memory_space=pltpu.SMEM)
    vmem = pl.BlockSpec(memory_space=pltpu.VMEM)
    local = depth * 2 * own
    many = 2 * vols * 2 * own
    out = (vols, local // planes, WIN * WIN)
    kept_sums = (2 * own, block, block)
    return pl.pallas_call(
        functools.partial(spectrum_kernel, vols, down, across, block, own, planes, depth),
        out_shape=[jax.ShapeDtypeStruct(out, jnp.float32)] * (2 * planes)
        + [jax.ShapeDtypeStruct(kept_sums, jnp.bfloat16)],
        in_specs=[smem] * 3
        + [vmem] * (len(tables) + 4 + len(bands))
        + [pl.BlockSpec(memory_space=pl.ANY)],
        out_specs=[vmem] * (2 * planes + 1),
        scratch_shapes=[
            pltpu.VMEM((many, 3 * kept, LANES), jnp.float32),
            pltpu.VMEM((many, 1, LANES), jnp.float32),
            pltpu.VMEM((2 * vols, local * WIN, LANES), jnp.float32),
        ],
        compiler_params=pltpu.CompilerParams(vmem_limit_bytes=VMEM_LIMIT),
        cost_estimate=pl.CostEstimate(
            flops=2 * 3 * rows * cols * block * 16,
            bytes_accessed=vols * rows * cols * 4 + rows * cols,
            transcendentals=0,
        ),
        name="lag_windows",
    )(place, codes, other_codes, *tables, frames, other_frames, *templates, *bands, after)


def exchange(value, axes, size, turn):
    return lax.ppermute(value, axes, [(at, at ^ turn) for at in range(size)])


def on_device(frames, template, shift_codes):
    vol_dev, pl_dev, img_rows, img_cols = frames.shape
    own, block = template.shape[0], template.shape[-1]
    depth = lax.axis_size("z")
    planes = lax.axis_size("plane")
    share = 4 * depth * own // planes
    place = jnp.stack([lax.axis_index(axis) for axis in ("z", "y", "core", "plane")])
    other_codes = exchange(shift_codes, "core", 2, 1)
    other_frames = exchange(frames, "core", 2, 1)
    near = jnp.concatenate(
        [template] + [exchange(template, "z", depth, turn) for turn in range(1, depth)], axis=0
    )
    far = exchange(near, "y", 2, 1)
    staged, *bands = stage([frames, *tap_constants(block)], other_codes)
    averages, window = [], [0.0, 0.0]
    volumes = vol_dev * depth * 4
    for p in range(pl_dev):
        work = (place, shift_codes, other_codes, staged[:, p], other_frames[:, p])
        warped = warp_sums(*work, bands, depth, block, own)
        templates = (near[:, p], far[:, p])
        *found, kept = lag_windows(*work, templates, bands, warped[0], planes, depth, own)
        warped = [exchange(one, "z", depth, turn + 1) for turn, one in enumerate(warped)]
        found, warped[0] = lax.optimization_barrier((found, warped[0]))
        warped.append(kept)
        sums = [sum(one[at : at + own].astype(jnp.float32) for one in warped) for at in (0, own)]
        taken = exchange(sums[1].astype(jnp.bfloat16), "y", 2, 1)
        averages.append((sums[0] + taken.astype(jnp.float32)) * (1.0 / volumes))
        for turn, one in enumerate(found):
            if turn:
                one = exchange(one, ("core", "plane"), 2 * planes, turn)
            window[turn // planes] += one
    core = place[2]
    window = [jnp.where(core == 0, *window), jnp.where(core == 0, *window[::-1])]
    window = [one.reshape(vol_dev, share // (2 * own), 1, own, WIN * WIN) for one in window]
    correlation = jnp.concatenate(window, axis=2).reshape(vol_dev, share, WIN * WIN)
    return (correlation, jnp.stack(averages, axis=1))


def solution(mesh):
    devices = mesh.devices.reshape(-1, 2, 2, mesh.shape["plane"])
    split = jax.sharding.Mesh(devices, ("z", "y", "core", "plane"))
    vols = ("z", "y", "core")
    in_specs = (P(vols, "plane", None, None), P(vols, "plane", None, None), P(vols, None, None))
    out_specs = (P(vols, "plane", None), P(vols, "plane", None, None))
    return jax.shard_map(
        on_device, mesh=split, in_specs=in_specs, out_specs=out_specs, check_vma=False
    )
```

```python
import functools
import math

import jax
import jax.numpy as jnp
import numpy as np
from jax import lax
from jax.experimental import pallas as pl
from jax.experimental.pallas import tpu as pltpu
from jax.sharding import PartitionSpec as P

SHIFT = 8
WIN = 16
TAPS = 8
SUB = 16
EDGE = 16
LANES = 128
VMEM_LIMIT = 24 * 1024 * 1024

full_turn = 2.0 * math.pi


def dft_constants(block_size):
    positions = np.arange(block_size)
    angles = full_turn * (np.outer(positions, positions) % block_size) / block_size
    cosine = np.cos(angles)
    sine = -np.sin(angles)
    half = block_size // 2 + 1
    rows = -(-half // 16) * 16
    row_table = np.zeros((2 * rows, block_size))
    row_table[:half] = cosine[:half]
    row_table[rows : rows + half] = sine[:half]
    col_table = np.block([[cosine, sine], [-sine, cosine]])
    weights = np.full((half,), 2.0)
    weights[0] = weights[half - 1] = 1.0
    span = 2 * SHIFT + WIN
    lags = np.arange(span) - SHIFT - WIN // 2
    turns = full_turn * (np.outer(lags, positions) % block_size) / block_size
    lag_cos, lag_sin = np.cos(turns), np.sin(turns)
    lag_table = np.zeros((2 * span, 2 * rows))
    lag_table[:span, :half] = lag_cos[:, :half] * weights
    lag_table[:span, rows : rows + half] = -lag_sin[:, :half] * weights
    lag_table[span:, :half] = lag_sin[:, :half] * weights
    lag_table[span:, rows : rows + half] = lag_cos[:, :half] * weights
    span_table = np.zeros((2 * block_size, LANES))
    span_table[:block_size, :span] = lag_cos.T
    span_table[block_size:, :span] = -lag_sin.T
    return tuple(
        jnp.asarray(table, jnp.bfloat16) for table in (row_table, col_table, lag_table, span_table)
    )


def tap_constants(block_size):
    offsets = np.arange(TAPS) - (TAPS // 2 - 1)
    spots = offsets[None, :] - np.arange(SUB)[:, None] / SUB
    raw_taps = np.sinc(spots) * np.sinc(spots / (TAPS // 2))
    taps = raw_taps / raw_taps.sum(axis=-1, keepdims=True)

    def band(inputs, outputs):
        at = inputs - outputs + TAPS // 2 - 1
        return np.where((at >= 0) & (at < TAPS), taps[:, np.clip(at, 0, TAPS - 1)], 0.0)

    lanes = np.arange(block_size)[None, :]
    inputs = np.arange(block_size + 3 * EDGE)[:, None] - EDGE - SHIFT
    outputs = np.arange(block_size + EDGE)[:, None] - SHIFT
    spare = np.arange(LANES)[None, :] % (2 * EDGE)
    first = band(spare - 2 * EDGE, outputs[: 2 * EDGE]) * (spare >= EDGE)
    last = band(spare + EDGE, outputs[: 2 * EDGE]) * (spare < EDGE)
    tables = band(inputs, lanes), band(lanes, outputs), np.stack([first, last], axis=1)
    return [jnp.asarray(table, jnp.float32) for table in tables]


def step_places(place_ref, step, across, own):
    z = place_ref[0] ^ step
    places = []
    for other in range(2):
        for one in range(own):
            index = ((2 * z + (place_ref[1] ^ other)) * 2 + place_ref[2]) * own + one
            places.append((index, index % across))
    return places


def step_band(place_ref, step, across, own):
    return (place_ref[0] ^ step) * (4 * own) // across


def stage_kernel(count, *refs):
    sources, targets, sems = refs[:count], refs[count + 1 : 2 * count + 1], refs[-1]
    copies = [
        pltpu.make_async_copy(source, target, sems.at[at])
        for at, (source, target) in enumerate(zip(sources, targets))
    ]
    for copy in copies:
        copy.start()
    for copy in copies:
        copy.wait()


def stage(arrays, after):
    kept = [pltpu.with_memory_space_constraint(one, pltpu.HBM) for one in arrays]
    count = len(arrays)
    return pl.pallas_call(
        functools.partial(stage_kernel, count),
        out_shape=[jax.ShapeDtypeStruct(one.shape, one.dtype) for one in arrays],
        in_specs=[pl.BlockSpec(memory_space=pltpu.HBM)] * count
        + [pl.BlockSpec(memory_space=pl.ANY)],
        out_specs=[pl.BlockSpec(memory_space=pltpu.VMEM)] * count,
        scratch_shapes=[pltpu.SemaphoreType.DMA((count,))],
        compiler_params=pltpu.CompilerParams(vmem_limit_bytes=VMEM_LIMIT),
        name="stage",
    )(*kept, pltpu.with_memory_space_constraint(after, pltpu.HBM))


def warp_step(place_ref, step, code_refs, frame_refs, band_refs, down, across, block, own):
    cols_ref, rows_ref, edges_ref = band_refs
    band = step_band(place_ref, step, across, own)
    row = pl.multiple_of(band * block, block)
    row_above = pl.multiple_of(jnp.maximum(row - EDGE, 0), EDGE)
    row_below = pl.multiple_of(jnp.minimum(row + block, down * block - EDGE), EDGE)
    zero = jnp.zeros((EDGE, LANES), jnp.bfloat16)
    gap = jnp.zeros((block - 2 * EDGE, LANES), jnp.bfloat16)
    no_tile = jnp.zeros((block + 2 * EDGE, block), jnp.bfloat16)
    volumes = [
        (codes, frames, v)
        for codes, frames in zip(code_refs, frame_refs)
        for v in range(frames.shape[0])
    ]
    many = len(volumes)
    per_tile = LANES // (2 * EDGE)
    lane = lax.broadcasted_iota(jnp.int32, (EDGE, LANES), 1) // (2 * EDGE)

    def tile(frames, v, at):
        lanes = pl.ds(pl.multiple_of(at * block, block), block)
        above = jnp.where(band > 0, frames[v, pl.ds(row_above, EDGE), lanes], zero)
        below = jnp.where(band < down - 1, frames[v, pl.ds(row_below, EDGE), lanes], zero)
        return jnp.concatenate([frames[v, pl.ds(row, block), lanes], below, above], axis=0)

    places = step_places(place_ref, step, across, own)
    totals = []
    for group in range(0, len(places), own):
        start = places[group][1]
        tiles = []
        for _, frames, v in volumes:
            left = jnp.where(start > 0, tile(frames, v, jnp.maximum(start - 1, 0)), no_tile)
            right = jnp.where(
                start + own < across,
                tile(frames, v, jnp.minimum(start + own, across - 1)),
                no_tile,
            )
            tiles.append([left] + [tile(frames, v, start + one) for one in range(own)] + [right])
        for one in range(own):
            index = places[group + one][0]
            row_tiles, partials, edges = [], [], []
            firsts, lasts = [], []
            for order, (codes, _, v) in enumerate(volumes):
                row_code, col_code = codes[v, 0, index], codes[v, 1, index]
                left, middle, right = tiles[order][one : one + 3]
                sides = jnp.concatenate([right[:, : block // 2], left[:, block // 2 :]], axis=1)
                col_start = SHIFT - (col_code >> 4)
                cols = cols_ref[col_code & (SUB - 1), pl.ds(col_start, block + 2 * EDGE), :]
                cols = cols.astype(jnp.bfloat16)
                partial = jnp.dot(
                    jnp.concatenate([middle, sides], axis=1),
                    jnp.concatenate([cols[EDGE:], gap, cols[:EDGE]], axis=0),
                    preferred_element_type=jnp.float32,
                ).astype(jnp.bfloat16)
                partials.append(partial[:block])
                edges.append(partial[block:])
                row_start = SHIFT + (row_code >> 4)
                step_at = row_code & (SUB - 1)
                row_tiles.append(rows_ref[step_at, pl.ds(row_start, block), :].astype(jnp.bfloat16))
                first = edges_ref[step_at, 0, pl.ds(row_start, EDGE), :]
                last = edges_ref[step_at, 1, pl.ds(row_start, EDGE), :]
                if order % per_tile:
                    first = jnp.where(lane == order % per_tile, first, firsts.pop())
                    last = jnp.where(lane == order % per_tile, last, lasts.pop())
                firsts.append(first)
                lasts.append(last)
            for first, last in zip(firsts, lasts):
                both = [first.astype(jnp.bfloat16), gap, last.astype(jnp.bfloat16)]
                row_tiles.append(jnp.concatenate(both, axis=0))
            deep = many * (block + 2 * EDGE)
            total = jnp.dot(
                jnp.concatenate(row_tiles, axis=1)[:, :deep],
                jnp.concatenate(partials + edges, axis=0),
                preferred_element_type=jnp.float32,
            )
            totals.append(total.astype(jnp.bfloat16))
    return totals


def warp_kernel(down, across, block, own, depth, *refs):
    place_ref, *code_refs = refs[:3]
    frame_refs, band_refs = refs[3:5], refs[5:8]
    out_refs, sums = refs[8 : 7 + depth], refs[7 + depth]

    def one_step(step, _):
        totals = warp_step(
            place_ref, step, code_refs, frame_refs, band_refs, down, across, block, own
        )
        for count, total in enumerate(totals):
            sums[count] = total
        for at, out_ref in enumerate(out_refs):

            @pl.when(step == at + 1)
            def _():
                out_ref[...] = sums[...]

        return 0

    lax.fori_loop(1, depth, one_step, 0)


def warp_sums(place, codes, other_codes, frames, other_frames, bands, depth, block, own):
    vols, rows, cols = frames.shape
    down, across = rows // block, cols // block
    out = (2 * own, block, block)
    smem = pl.BlockSpec(memory_space=pltpu.SMEM)
    vmem = pl.BlockSpec(memory_space=pltpu.VMEM)
    return pl.pallas_call(
        functools.partial(warp_kernel, down, across, block, own, depth),
        out_shape=[jax.ShapeDtypeStruct(out, jnp.bfloat16)] * (depth - 1),
        in_specs=[smem] * 3 + [vmem] * 5,
        out_specs=[vmem] * (depth - 1),
        scratch_shapes=[pltpu.VMEM(out, jnp.bfloat16)],
        compiler_params=pltpu.CompilerParams(vmem_limit_bytes=VMEM_LIMIT),
        cost_estimate=pl.CostEstimate(
            flops=2 * vols * rows * cols * block * 16,
            bytes_accessed=vols * rows * cols * 4 + rows * cols,
            transcendentals=0,
        ),
        name="warp",
    )(place, codes, other_codes, frames, other_frames, *bands)


def spectrum_kernel(vols, down, across, block, own, planes, depth, other, *refs):
    place_ref, codes_ref, other_codes_ref, row_ref, col_ref, lag_ref, span_ref = refs[:7]
    frames_ref, other_frames_ref, template_ref = refs[7:10]
    cross, sums = refs[-2:]
    if other:
        found_ref, out_refs, found = refs[10], refs[11:-3], refs[-3]
        found[...] = found_ref[...]
    else:
        band_refs, found, sums_ref = refs[10:13], refs[14], refs[15]
        code_refs, frame_refs = (codes_ref, other_codes_ref), (frames_ref, other_frames_ref)
        totals = warp_step(
            place_ref, 0, code_refs, frame_refs, band_refs, down, across, block, own
        )
        for count, total in enumerate(totals):
            sums_ref[count] = total

    row_table = row_ref[...]
    col_table = col_ref[...]
    lag_table = lag_ref[...]
    half = row_table.shape[0] // 2
    kept = -(-(block // 2 + 1) // 8) * 8
    span = lag_table.shape[0] // 2
    top = lax.broadcasted_iota(jnp.int32, (8, LANES), 0) == 0
    volumes = [(codes_ref, frames_ref, v) for v in range(vols)]
    volumes += [(other_codes_ref, other_frames_ref, v) for v in range(vols)]
    many = len(volumes)
    local = 2 * own
    no_rows = jnp.zeros((half - kept, LANES), jnp.float32)

    def two_steps(half_step, _):
        places = []
        for step in (2 * half_step, 2 * half_step + 1):
            band = step_band(place_ref, step, across, own)
            band_rows = pl.ds(pl.multiple_of(band * block, block), block)
            chosen = step_places(place_ref, step, across, own)[other * own : (other + 1) * own]
            for one, (index, at) in enumerate(chosen):
                lanes = pl.ds(pl.multiple_of(at * block, block), block)
                places.append((index, band_rows, lanes, step * own + one))

        for pair in range(local // 2):
            pair_places = places[2 * pair : 2 * pair + 2]
            sources = [[template_ref[at] for _, _, _, at in pair_places]]
            for _, frames, v in volumes:
                sources.append([frames[v, rows, lanes] for _, rows, lanes, _ in pair_places])
            parts = []
            for source in sources:
                rows = jnp.dot(
                    row_table,
                    jnp.concatenate(source, axis=1),
                    preferred_element_type=jnp.float32,
                ).astype(jnp.bfloat16)
                for side in range(2):
                    lanes = slice(side * block, (side + 1) * block)
                    parts.append(jnp.concatenate([rows[:half, lanes], rows[half:, lanes]], axis=1))
            spectra = jnp.dot(
                jnp.concatenate(parts, axis=0), col_table, preferred_element_type=jnp.float32
            )
            temp = spectra[: 2 * half].astype(jnp.bfloat16).astype(jnp.float32)
            for order in range(many):
                for side in range(2):
                    one = (2 * pair + side) * many + order
                    base = (2 * (order + 1) + side) * half
                    total = jnp.zeros((8, LANES), jnp.float32)
                    for row in range(0, kept, 8):
                        at = side * half + row
                        temp_real = temp[at : at + 8, :block]
                        temp_imag = temp[at : at + 8, block:]
                        real = spectra[base + row : base + row + 8, :block]
                        imag = spectra[base + row : base + row + 8, block:]
                        cross_real = real * temp_real + imag * temp_imag
                        cross_imag = imag * temp_real - real * temp_imag
                        power = cross_real * cross_real + cross_imag * cross_imag
                        magnitude = power * lax.rsqrt(jnp.maximum(power, 1e-36))
                        cross[one, row : row + 8, :] = cross_real
                        cross[one, kept + row : kept + row + 8, :] = cross_imag
                        cross[one, 2 * kept + row : 2 * kept + row + 8, :] = magnitude
                        if row == 0:
                            total = jnp.where(top, magnitude, 2.0 * magnitude)
                        elif row == block // 2:
                            total += magnitude
                        else:
                            total += 2.0 * magnitude
                    sums[one] = jnp.sum(total, axis=0, keepdims=True)

        means = jnp.sum(sums[...], axis=2, keepdims=True) * (1.0 / (block * block)) + 1e-06
        lag_sums = []
        for pair in range(local // 2):
            for order in range(many):
                norms = []
                for side in range(2):
                    one = (2 * pair + side) * many + order
                    scale = pl.reciprocal(cross[one, 2 * kept :, :] + means[one], approx=True)
                    norms.append(
                        jnp.concatenate(
                            [
                                cross[one, :kept, :] * scale,
                                no_rows,
                                cross[one, kept : 2 * kept, :] * scale,
                                no_rows,
                            ],
                            axis=0,
                        ).astype(jnp.bfloat16)
                    )
                lag_rows = jnp.dot(
                    lag_table, jnp.concatenate(norms, axis=1), preferred_element_type=jnp.float32
                ).astype(jnp.bfloat16)
                for side in range(2):
                    lanes = slice(side * block, (side + 1) * block)
                    lag_sums.append(
                        jnp.concatenate([lag_rows[:span, lanes], lag_rows[span:, lanes]], axis=1)
                    )
        lags = jnp.dot(
            jnp.concatenate(lag_sums, axis=0), span_ref[...], preferred_element_type=jnp.float32
        )
        for pair in range(local // 2):
            for order, (codes, _, v) in enumerate(volumes):
                for side in range(2):
                    index = places[2 * pair + side][0]
                    row_shift = codes[v, 0, index] >> 4
                    col_shift = codes[v, 1, index] >> 4
                    at = (pair * many + order) * 2 + side
                    one = lags[at * span : (at + 1) * span]
                    one = pltpu.roll(one, span - SHIFT - row_shift, 0)[:WIN]
                    place = index // (2 * own) * own + (2 * pair + side) % own
                    found[order, pl.ds(pl.multiple_of(place * WIN, WIN), WIN), :] = pltpu.roll(
                        one, LANES - SHIFT - col_shift, 1
                    )
        return 0

    lax.fori_loop(0, depth // 2, two_steps, 0)
    if not other:
        return

    share = depth * local // planes
    per_tile = LANES // WIN
    lane = lax.broadcasted_iota(jnp.int32, (share, LANES), 1) // WIN
    for turn, out_ref in enumerate(out_refs):
        plane = place_ref[3] ^ (turn % planes)
        for v in range(vols):
            order = turn // planes * vols + v
            for tile in range(WIN // per_tile):
                total = jnp.zeros((share, LANES), jnp.float32)
                for part in range(per_tile):
                    start = plane * share * WIN + tile * per_tile + part
                    one = found[order, pl.ds(start, share, stride=WIN), :]
                    if part:
                        one = pltpu.roll(one, part * WIN, 1)
                    total = jnp.where(lane == part, one, total)
                out_ref[v, :, tile * LANES : (tile + 1) * LANES] = total * (1.0 / block)


def lag_windows(
    place, codes, other_codes, frames, other_frames, template, bands, other, planes, depth, own, more
):
    vols, rows, cols = frames.shape
    block = template.shape[-1]
    down, across = rows // block, cols // block
    tables = dft_constants(block)
    kept = -(-(block // 2 + 1) // 8) * 8
    smem = pl.BlockSpec(memory_space=pltpu.SMEM)
    vmem = pl.BlockSpec(memory_space=pltpu.VMEM)
    local = depth * 2 * own
    many = 2 * vols * 2 * own
    found = jax.ShapeDtypeStruct((2 * vols, local * WIN, LANES), jnp.float32)
    if other:
        out = (vols, local // planes, WIN * WIN)
        out_shape = [jax.ShapeDtypeStruct(out, jnp.float32)] * (2 * planes)
        scratch_shapes = [pltpu.VMEM(found.shape, found.dtype)]
        bands, last = [], vmem
    else:
        out_shape = [found, jax.ShapeDtypeStruct((2 * own, block, block), jnp.bfloat16)]
        scratch_shapes = []
        last = pl.BlockSpec(memory_space=pl.ANY)
    return pl.pallas_call(
        functools.partial(spectrum_kernel, vols, down, across, block, own, planes, depth, other),
        out_shape=out_shape,
        in_specs=[smem] * 3 + [vmem] * (len(tables) + 3 + len(bands)) + [last],
        out_specs=[vmem] * len(out_shape),
        scratch_shapes=scratch_shapes
        + [
            pltpu.VMEM((many, 3 * kept, LANES), jnp.float32),
            pltpu.VMEM((many, 1, LANES), jnp.float32),
        ],
        compiler_params=pltpu.CompilerParams(vmem_limit_bytes=VMEM_LIMIT),
        cost_estimate=pl.CostEstimate(
            flops=2 * 3 * rows * cols * block * 8,
            bytes_accessed=vols * rows * cols * 4 + rows * cols,
            transcendentals=0,
        ),
        name="lag_windows",
    )(place, codes, other_codes, *tables, frames, other_frames, template, *bands, more)


def exchange(value, axes, size, turn):
    return lax.ppermute(value, axes, [(at, at ^ turn) for at in range(size)])


def on_device(frames, template, shift_codes):
    vol_dev, pl_dev, img_rows, img_cols = frames.shape
    own, block = template.shape[0], template.shape[-1]
    depth = lax.axis_size("z")
    planes = lax.axis_size("plane")
    share = 4 * depth * own // planes
    place = jnp.stack([lax.axis_index(axis) for axis in ("z", "y", "core", "plane")])
    other_codes = exchange(shift_codes, "core", 2, 1)
    other_frames = exchange(frames, "core", 2, 1)
    pieces = [template] + [exchange(template, "z", depth, turn) for turn in range(1, depth)]
    staged, *bands = stage([frames, *tap_constants(block)], template)
    averages, window = [], [0.0, 0.0]
    volumes = vol_dev * depth * 4
    for p in range(pl_dev):
        work = (place, shift_codes, other_codes, staged[:, p], other_frames[:, p])
        warped = list(warp_sums(*work, bands, depth, block, own))
        pieces, warped[0] = lax.optimization_barrier((pieces, warped[0]))
        near = jnp.concatenate([piece[:, p] for piece in pieces], axis=0)
        far = exchange(near, "y", 2, 1)
        sizes = (planes, depth, own)
        part, kept = lag_windows(*work, near, bands, 0, *sizes, warped[0])
        found = lag_windows(*work, far, bands, 1, *sizes, part)
        warped = [exchange(one, "z", depth, turn + 1) for turn, one in enumerate(warped)]
        found, warped = lax.optimization_barrier((found, warped))
        warped.append(kept)
        sums = [sum(one[at : at + own].astype(jnp.float32) for one in warped) for at in (0, own)]
        taken = exchange(sums[1].astype(jnp.bfloat16), "y", 2, 1)
        averages.append((sums[0] + taken.astype(jnp.float32)) * (1.0 / volumes))
        for turn, one in enumerate(found):
            if turn:
                one = exchange(one, ("core", "plane"), 2 * planes, turn)
            window[turn // planes] += one
    core = place[2]
    window = [jnp.where(core == 0, *window), jnp.where(core == 0, *window[::-1])]
    window = [one.reshape(vol_dev, share // (2 * own), 1, own, WIN * WIN) for one in window]
    correlation = jnp.concatenate(window, axis=2).reshape(vol_dev, share, WIN * WIN)
    return (correlation, jnp.stack(averages, axis=1))


def solution(mesh):
    devices = mesh.devices.reshape(-1, 2, 2, mesh.shape["plane"])
    split = jax.sharding.Mesh(devices, ("z", "y", "core", "plane"))
    vols = ("z", "y", "core")
    in_specs = (P(vols, "plane", None, None), P(vols, "plane", None, None), P(vols, None, None))
    out_specs = (P(vols, "plane", None), P(vols, "plane", None, None))
    return jax.shard_map(
        on_device, mesh=split, in_specs=in_specs, out_specs=out_specs, check_vma=False
    )
```

```python
import functools
import math

import jax
import jax.numpy as jnp
import numpy as np
from jax import lax
from jax.experimental import pallas as pl
from jax.experimental.pallas import tpu as pltpu
from jax.sharding import PartitionSpec as P

SHIFT = 8
WIN = 16
TAPS = 8
SUB = 16
EDGE = 16
LANES = 128
VMEM_LIMIT = 24 * 1024 * 1024

full_turn = 2.0 * math.pi


def dft_constants(block_size):
    positions = np.arange(block_size)
    angles = full_turn * (np.outer(positions, positions) % block_size) / block_size
    cosine = np.cos(angles)
    sine = -np.sin(angles)
    half = block_size // 2 + 1
    rows = -(-half // 16) * 16
    row_table = np.zeros((2 * rows, block_size))
    row_table[:half] = cosine[:half]
    row_table[rows : rows + half] = sine[:half]
    col_table = np.block([[cosine, sine], [-sine, cosine]])
    weights = np.full((half,), 2.0)
    weights[0] = weights[half - 1] = 1.0
    span = 2 * SHIFT + WIN
    lags = np.arange(span) - SHIFT - WIN // 2
    turns = full_turn * (np.outer(lags, positions) % block_size) / block_size
    lag_cos, lag_sin = np.cos(turns), np.sin(turns)
    lag_table = np.zeros((2 * span, 2 * rows))
    lag_table[:span, :half] = lag_cos[:, :half] * weights
    lag_table[:span, rows : rows + half] = -lag_sin[:, :half] * weights
    lag_table[span:, :half] = lag_sin[:, :half] * weights
    lag_table[span:, rows : rows + half] = lag_cos[:, :half] * weights
    span_table = np.zeros((2 * block_size, LANES))
    span_table[:block_size, :span] = lag_cos.T
    span_table[block_size:, :span] = -lag_sin.T
    return tuple(
        jnp.asarray(table, jnp.bfloat16) for table in (row_table, col_table, lag_table, span_table)
    )


def tap_constants(block_size):
    offsets = np.arange(TAPS) - (TAPS // 2 - 1)
    spots = offsets[None, :] - np.arange(SUB)[:, None] / SUB
    raw_taps = np.sinc(spots) * np.sinc(spots / (TAPS // 2))
    taps = raw_taps / raw_taps.sum(axis=-1, keepdims=True)

    def band(inputs, outputs):
        at = inputs - outputs + TAPS // 2 - 1
        return np.where((at >= 0) & (at < TAPS), taps[:, np.clip(at, 0, TAPS - 1)], 0.0)

    lanes = np.arange(block_size)[None, :]
    inputs = np.arange(block_size + 3 * EDGE)[:, None] - EDGE - SHIFT
    outputs = np.arange(block_size + EDGE)[:, None] - SHIFT
    spare = np.arange(LANES)[None, :] % (2 * EDGE)
    first = band(spare - 2 * EDGE, outputs[: 2 * EDGE]) * (spare >= EDGE)
    last = band(spare + EDGE, outputs[: 2 * EDGE]) * (spare < EDGE)
    tables = band(inputs, lanes), band(lanes, outputs), np.stack([first, last], axis=1)
    return [jnp.asarray(table, jnp.float32) for table in tables]


def step_places(place_ref, step, across, own):
    z = place_ref[0] ^ step
    places = []
    for other in range(2):
        for one in range(own):
            index = ((2 * z + (place_ref[1] ^ other)) * 2 + place_ref[2]) * own + one
            places.append((index, index % across))
    return places


def step_band(place_ref, step, across, own):
    return (place_ref[0] ^ step) * (4 * own) // across


def stage_kernel(count, *refs):
    sources, targets, sems = refs[:count], refs[count + 1 : 2 * count + 1], refs[-1]
    copies = [
        pltpu.make_async_copy(source, target, sems.at[at])
        for at, (source, target) in enumerate(zip(sources, targets))
    ]
    for copy in copies:
        copy.start()
    for copy in copies:
        copy.wait()


def stage(arrays, after):
    kept = [pltpu.with_memory_space_constraint(one, pltpu.HBM) for one in arrays]
    count = len(arrays)
    return pl.pallas_call(
        functools.partial(stage_kernel, count),
        out_shape=[jax.ShapeDtypeStruct(one.shape, one.dtype) for one in arrays],
        in_specs=[pl.BlockSpec(memory_space=pltpu.HBM)] * count
        + [pl.BlockSpec(memory_space=pl.ANY)],
        out_specs=[pl.BlockSpec(memory_space=pltpu.VMEM)] * count,
        scratch_shapes=[pltpu.SemaphoreType.DMA((count,))],
        compiler_params=pltpu.CompilerParams(vmem_limit_bytes=VMEM_LIMIT),
        name="stage",
    )(*kept, pltpu.with_memory_space_constraint(after, pltpu.HBM))


def warp_step(place_ref, step, code_refs, frame_refs, band_refs, down, across, block, own):
    cols_ref, rows_ref, edges_ref = band_refs
    band = step_band(place_ref, step, across, own)
    row = pl.multiple_of(band * block, block)
    row_above = pl.multiple_of(jnp.maximum(row - EDGE, 0), EDGE)
    row_below = pl.multiple_of(jnp.minimum(row + block, down * block - EDGE), EDGE)
    zero = jnp.zeros((EDGE, LANES), jnp.bfloat16)
    gap = jnp.zeros((block - 2 * EDGE, LANES), jnp.bfloat16)
    no_tile = jnp.zeros((block + 2 * EDGE, block), jnp.bfloat16)
    volumes = [
        (codes, frames, v)
        for codes, frames in zip(code_refs, frame_refs)
        for v in range(frames.shape[0])
    ]
    many = len(volumes)
    per_tile = LANES // (2 * EDGE)
    lane = lax.broadcasted_iota(jnp.int32, (EDGE, LANES), 1) // (2 * EDGE)

    def tile(frames, v, at):
        lanes = pl.ds(pl.multiple_of(at * block, block), block)
        above = jnp.where(band > 0, frames[v, pl.ds(row_above, EDGE), lanes], zero)
        below = jnp.where(band < down - 1, frames[v, pl.ds(row_below, EDGE), lanes], zero)
        return jnp.concatenate([frames[v, pl.ds(row, block), lanes], below, above], axis=0)

    places = step_places(place_ref, step, across, own)
    totals = []
    for group in range(0, len(places), own):
        start = places[group][1]
        tiles = []
        for _, frames, v in volumes:
            left = jnp.where(start > 0, tile(frames, v, jnp.maximum(start - 1, 0)), no_tile)
            right = jnp.where(
                start + own < across,
                tile(frames, v, jnp.minimum(start + own, across - 1)),
                no_tile,
            )
            tiles.append([left] + [tile(frames, v, start + one) for one in range(own)] + [right])
        for one in range(own):
            index = places[group + one][0]
            row_tiles, partials, edges = [], [], []
            firsts, lasts = [], []
            for order, (codes, _, v) in enumerate(volumes):
                row_code, col_code = codes[v, 0, index], codes[v, 1, index]
                left, middle, right = tiles[order][one : one + 3]
                sides = jnp.concatenate([right[:, : block // 2], left[:, block // 2 :]], axis=1)
                col_start = SHIFT - (col_code >> 4)
                cols = cols_ref[col_code & (SUB - 1), pl.ds(col_start, block + 2 * EDGE), :]
                cols = cols.astype(jnp.bfloat16)
                partial = jnp.dot(
                    jnp.concatenate([middle, sides], axis=1),
                    jnp.concatenate([cols[EDGE:], gap, cols[:EDGE]], axis=0),
                    preferred_element_type=jnp.float32,
                ).astype(jnp.bfloat16)
                partials.append(partial[:block])
                edges.append(partial[block:])
                row_start = SHIFT + (row_code >> 4)
                step_at = row_code & (SUB - 1)
                row_tiles.append(rows_ref[step_at, pl.ds(row_start, block), :].astype(jnp.bfloat16))
                first = edges_ref[step_at, 0, pl.ds(row_start, EDGE), :]
                last = edges_ref[step_at, 1, pl.ds(row_start, EDGE), :]
                if order % per_tile:
                    first = jnp.where(lane == order % per_tile, first, firsts.pop())
                    last = jnp.where(lane == order % per_tile, last, lasts.pop())
                firsts.append(first)
                lasts.append(last)
            for first, last in zip(firsts, lasts):
                both = [first.astype(jnp.bfloat16), gap, last.astype(jnp.bfloat16)]
                row_tiles.append(jnp.concatenate(both, axis=0))
            deep = many * (block + 2 * EDGE)
            total = jnp.dot(
                jnp.concatenate(row_tiles, axis=1)[:, :deep],
                jnp.concatenate(partials + edges, axis=0),
                preferred_element_type=jnp.float32,
            )
            totals.append(total.astype(jnp.bfloat16))
    return totals


def warp_kernel(down, across, block, own, depth, *refs):
    place_ref, *code_refs = refs[:3]
    frame_refs, band_refs = refs[3:5], refs[5:8]
    out_refs = refs[8:]

    for at, out_ref in enumerate(out_refs):
        totals = warp_step(
            place_ref, at + 1, code_refs, frame_refs, band_refs, down, across, block, own
        )
        for count, total in enumerate(totals):
            out_ref[count] = total


def warp_sums(place, codes, other_codes, frames, other_frames, bands, depth, block, own):
    vols, rows, cols = frames.shape
    down, across = rows // block, cols // block
    out = (2 * own, block, block)
    smem = pl.BlockSpec(memory_space=pltpu.SMEM)
    vmem = pl.BlockSpec(memory_space=pltpu.VMEM)
    return pl.pallas_call(
        functools.partial(warp_kernel, down, across, block, own, depth),
        out_shape=[jax.ShapeDtypeStruct(out, jnp.bfloat16)] * (depth - 1),
        in_specs=[smem] * 3 + [vmem] * 5,
        out_specs=[vmem] * (depth - 1),
        compiler_params=pltpu.CompilerParams(vmem_limit_bytes=VMEM_LIMIT),
        cost_estimate=pl.CostEstimate(
            flops=2 * vols * rows * cols * block * 16,
            bytes_accessed=vols * rows * cols * 4 + rows * cols,
            transcendentals=0,
        ),
        name="warp",
    )(place, codes, other_codes, frames, other_frames, *bands)


def spectrum_kernel(vols, down, across, block, own, planes, depth, other, *refs):
    place_ref, codes_ref, other_codes_ref, row_ref, col_ref, lag_ref, span_ref = refs[:7]
    frames_ref, other_frames_ref, template_ref = refs[7:10]
    all_cross, all_sums = refs[-2:]
    if other:
        found_ref, out_refs, found = refs[10], refs[11:-3], refs[-3]
        found[...] = found_ref[...]
    else:
        band_refs, found, sums_ref = refs[10:13], refs[14], refs[15]
        code_refs, frame_refs = (codes_ref, other_codes_ref), (frames_ref, other_frames_ref)
        totals = warp_step(
            place_ref, 0, code_refs, frame_refs, band_refs, down, across, block, own
        )
        for count, total in enumerate(totals):
            sums_ref[count] = total
        found[...] = jnp.zeros(found.shape, jnp.float32)

    row_table = row_ref[...]
    col_table = col_ref[...]
    lag_table = lag_ref[...]
    half = row_table.shape[0] // 2
    kept = -(-(block // 2 + 1) // 8) * 8
    span = lag_table.shape[0] // 2
    top = lax.broadcasted_iota(jnp.int32, (8, LANES), 0) == 0
    volumes = [(codes_ref, frames_ref, v) for v in range(vols)]
    volumes += [(other_codes_ref, other_frames_ref, v) for v in range(vols)]
    many = len(volumes)
    local = 2 * own
    no_rows = jnp.zeros((half - kept, LANES), jnp.float32)

    for half_step in range(depth // 2):
        cross, sums = all_cross.at[half_step], all_sums.at[half_step]
        places = []
        for step in (2 * half_step, 2 * half_step + 1):
            band = step_band(place_ref, step, across, own)
            band_rows = pl.ds(pl.multiple_of(band * block, block), block)
            chosen = step_places(place_ref, step, across, own)[other * own : (other + 1) * own]
            for one, (index, at) in enumerate(chosen):
                lanes = pl.ds(pl.multiple_of(at * block, block), block)
                places.append((index, band_rows, lanes, step * own + one))

        for pair in range(local // 2):
            pair_places = places[2 * pair : 2 * pair + 2]
            sources = [[template_ref[at] for _, _, _, at in pair_places]]
            for _, frames, v in volumes:
                sources.append([frames[v, rows, lanes] for _, rows, lanes, _ in pair_places])
            parts = []
            for source in sources:
                rows = jnp.dot(
                    row_table,
                    jnp.concatenate(source, axis=1),
                    preferred_element_type=jnp.float32,
                ).astype(jnp.bfloat16)
                for side in range(2):
                    lanes = slice(side * block, (side + 1) * block)
                    parts.append(jnp.concatenate([rows[:half, lanes], rows[half:, lanes]], axis=1))
            spectra = jnp.dot(
                jnp.concatenate(parts, axis=0), col_table, preferred_element_type=jnp.float32
            )
            temp = spectra[: 2 * half].astype(jnp.bfloat16).astype(jnp.float32)
            for order in range(many):
                for side in range(2):
                    one = (2 * pair + side) * many + order
                    base = (2 * (order + 1) + side) * half
                    total = jnp.zeros((8, LANES), jnp.float32)
                    for row in range(0, kept, 8):
                        at = side * half + row
                        temp_real = temp[at : at + 8, :block]
                        temp_imag = temp[at : at + 8, block:]
                        real = spectra[base + row : base + row + 8, :block]
                        imag = spectra[base + row : base + row + 8, block:]
                        cross_real = real * temp_real + imag * temp_imag
                        cross_imag = imag * temp_real - real * temp_imag
                        power = cross_real * cross_real + cross_imag * cross_imag
                        magnitude = power * lax.rsqrt(jnp.maximum(power, 1e-36))
                        cross[one, row : row + 8, :] = cross_real
                        cross[one, kept + row : kept + row + 8, :] = cross_imag
                        cross[one, 2 * kept + row : 2 * kept + row + 8, :] = magnitude
                        if row == 0:
                            total = jnp.where(top, magnitude, 2.0 * magnitude)
                        elif row == block // 2:
                            total += magnitude
                        else:
                            total += 2.0 * magnitude
                    sums[one] = jnp.sum(total, axis=0, keepdims=True)

        means = jnp.sum(sums[...], axis=2, keepdims=True) * (1.0 / (block * block)) + 1e-06
        lag_sums = []
        for pair in range(local // 2):
            for order in range(many):
                norms = []
                for side in range(2):
                    one = (2 * pair + side) * many + order
                    scale = pl.reciprocal(cross[one, 2 * kept :, :] + means[one], approx=True)
                    norms.append(
                        jnp.concatenate(
                            [
                                cross[one, :kept, :] * scale,
                                no_rows,
                                cross[one, kept : 2 * kept, :] * scale,
                                no_rows,
                            ],
                            axis=0,
                        ).astype(jnp.bfloat16)
                    )
                lag_rows = jnp.dot(
                    lag_table, jnp.concatenate(norms, axis=1), preferred_element_type=jnp.float32
                ).astype(jnp.bfloat16)
                for side in range(2):
                    lanes = slice(side * block, (side + 1) * block)
                    lag_sums.append(
                        jnp.concatenate([lag_rows[:span, lanes], lag_rows[span:, lanes]], axis=1)
                    )
        lags = jnp.dot(
            jnp.concatenate(lag_sums, axis=0), span_ref[...], preferred_element_type=jnp.float32
        )
        for pair in range(local // 2):
            for order, (codes, _, v) in enumerate(volumes):
                for side in range(2):
                    index = places[2 * pair + side][0]
                    row_shift = codes[v, 0, index] >> 4
                    col_shift = codes[v, 1, index] >> 4
                    at = (pair * many + order) * 2 + side
                    one = lags[at * span : (at + 1) * span]
                    one = pltpu.roll(one, span - SHIFT - row_shift, 0)[:WIN]
                    found[order, pl.ds(pl.multiple_of(index * WIN, WIN), WIN), :] = pltpu.roll(
                        one, LANES - SHIFT - col_shift, 1
                    )

    if not other:
        return

    keep_refs, give_ref = out_refs[:-1], out_refs[-1]
    share = found.shape[1] // WIN // planes
    per_tile = LANES // WIN
    lane = lax.broadcasted_iota(jnp.int32, (share, LANES), 1) // WIN
    for turn, keep_ref in enumerate(keep_refs):
        plane = place_ref[3] ^ turn
        for order in range(many):
            for tile in range(WIN // per_tile):
                total = jnp.zeros((share, LANES), jnp.float32)
                for part in range(per_tile):
                    start = plane * share * WIN + tile * per_tile + part
                    one = found[order, pl.ds(start, share, stride=WIN), :]
                    if part:
                        one = pltpu.roll(one, part * WIN, 1)
                    total = jnp.where(lane == part, one, total)
                lanes = slice(tile * LANES, (tile + 1) * LANES)
                total = total * (1.0 / block)
                if order < vols:
                    keep_ref[order, :, lanes] = total
                else:
                    give_ref[turn, order - vols, :, lanes] = total


def lag_windows(
    place, codes, other_codes, frames, other_frames, template, bands, other, planes, depth, own, more
):
    vols, rows, cols = frames.shape
    block = template.shape[-1]
    down, across = rows // block, cols // block
    tables = dft_constants(block)
    kept = -(-(block // 2 + 1) // 8) * 8
    smem = pl.BlockSpec(memory_space=pltpu.SMEM)
    vmem = pl.BlockSpec(memory_space=pltpu.VMEM)
    blocks = down * across
    many = 2 * vols * 2 * own
    found = jax.ShapeDtypeStruct((2 * vols, blocks * WIN, LANES), jnp.float32)
    if other:
        out = (vols, blocks // planes, WIN * WIN)
        out_shape = [jax.ShapeDtypeStruct(out, jnp.float32)] * planes
        out_shape.append(jax.ShapeDtypeStruct((planes, *out), jnp.float32))
        scratch_shapes = [pltpu.VMEM(found.shape, found.dtype)]
        bands, last = [], vmem
    else:
        out_shape = [found, jax.ShapeDtypeStruct((2 * own, block, block), jnp.bfloat16)]
        scratch_shapes = []
        last = pl.BlockSpec(memory_space=pl.ANY)
    return pl.pallas_call(
        functools.partial(spectrum_kernel, vols, down, across, block, own, planes, depth, other),
        out_shape=out_shape,
        in_specs=[smem] * 3 + [vmem] * (len(tables) + 3 + len(bands)) + [last],
        out_specs=[vmem] * len(out_shape),
        scratch_shapes=scratch_shapes
        + [
            pltpu.VMEM((depth // 2, many, 3 * kept, LANES), jnp.float32),
            pltpu.VMEM((depth // 2, many, 1, LANES), jnp.float32),
        ],
        compiler_params=pltpu.CompilerParams(vmem_limit_bytes=VMEM_LIMIT),
        cost_estimate=pl.CostEstimate(
            flops=2 * 3 * rows * cols * block * 8,
            bytes_accessed=vols * rows * cols * 4 + rows * cols,
            transcendentals=0,
        ),
        name="lag_windows",
    )(place, codes, other_codes, *tables, frames, other_frames, template, *bands, more)


def exchange(value, axes, size, turn):
    return lax.ppermute(value, axes, [(at, at ^ turn) for at in range(size)])


def on_device(frames, template, shift_codes):
    vol_dev, pl_dev, img_rows, img_cols = frames.shape
    own, block = template.shape[0], template.shape[-1]
    depth = lax.axis_size("z")
    planes = lax.axis_size("plane")
    place = jnp.stack([lax.axis_index(axis) for axis in ("z", "y", "core", "plane")])
    other_codes = exchange(shift_codes, "core", 2, 1)
    other_frames = exchange(frames, "core", 2, 1)
    staged, *bands = stage([frames, *tap_constants(block)], template)
    later, staged = lax.optimization_barrier((template, staged))
    pieces = [template] + [exchange(later, "z", depth, turn) for turn in range(1, depth)]
    averages, correlation = [], 0.0
    volumes = vol_dev * depth * 4
    for p in range(pl_dev):
        work = (place, shift_codes, other_codes, staged[:, p], other_frames[:, p])
        warped = list(warp_sums(*work, bands, depth, block, own))
        pieces, warped[0] = lax.optimization_barrier((pieces, warped[0]))
        near = jnp.concatenate([piece[:, p] for piece in pieces], axis=0)
        far = exchange(near, "y", 2, 1)
        sizes = (planes, depth, own)
        part, kept = lag_windows(*work, near, bands, 0, *sizes, warped[0])
        found = lag_windows(*work, far, bands, 1, *sizes, part)
        warped = [exchange(one, "z", depth, turn + 1) for turn, one in enumerate(warped)]
        found, warped = lax.optimization_barrier((found, warped))
        warped.append(kept)
        sums = [sum(one[at : at + own].astype(jnp.float32) for one in warped) for at in (0, own)]
        taken = exchange(sums[1].astype(jnp.bfloat16), "y", 2, 1)
        averages.append((sums[0] + taken.astype(jnp.float32)) * (1.0 / volumes))
        got = exchange(found[-1], "core", 2, 1)
        for turn, one in enumerate(found[:-1]):
            one = one + got[turn]
            correlation += exchange(one, "plane", planes, turn) if turn else one
    return (correlation, jnp.stack(averages, axis=1))


def solution(mesh):
    devices = mesh.devices.reshape(-1, 2, 2, mesh.shape["plane"])
    split = jax.sharding.Mesh(devices, ("z", "y", "core", "plane"))
    vols = ("z", "y", "core")
    in_specs = (P(vols, "plane", None, None), P(vols, "plane", None, None), P(vols, None, None))
    out_specs = (P(vols, "plane", None), P(vols, "plane", None, None))
    return jax.shard_map(
        on_device, mesh=split, in_specs=in_specs, out_specs=out_specs, check_vma=False
    )
```

```python
import functools
import math

import jax
import jax.numpy as jnp
import numpy as np
from jax import lax
from jax.experimental import pallas as pl
from jax.experimental.pallas import tpu as pltpu
from jax.sharding import PartitionSpec as P

SHIFT = 8
WIN = 16
TAPS = 8
SUB = 16
EDGE = 16
LANES = 128
VMEM_LIMIT = 24 * 1024 * 1024

full_turn = 2.0 * math.pi


def dft_constants(block_size):
    positions = np.arange(block_size)
    angles = full_turn * (np.outer(positions, positions) % block_size) / block_size
    cosine = np.cos(angles)
    sine = -np.sin(angles)
    half = block_size // 2 + 1
    rows = -(-half // 16) * 16
    row_table = np.zeros((2 * rows, block_size))
    row_table[:half] = cosine[:half]
    row_table[rows : rows + half] = sine[:half]
    col_table = np.block([[cosine, sine], [-sine, cosine]])
    weights = np.full((half,), 2.0)
    weights[0] = weights[half - 1] = 1.0
    span = 2 * SHIFT + WIN
    lags = np.arange(span) - SHIFT - WIN // 2
    turns = full_turn * (np.outer(lags, positions) % block_size) / block_size
    lag_cos, lag_sin = np.cos(turns), np.sin(turns)
    lag_table = np.zeros((2 * span, 2 * rows))
    lag_table[:span, :half] = lag_cos[:, :half] * weights
    lag_table[:span, rows : rows + half] = -lag_sin[:, :half] * weights
    lag_table[span:, :half] = lag_sin[:, :half] * weights
    lag_table[span:, rows : rows + half] = lag_cos[:, :half] * weights
    span_table = np.zeros((2 * block_size, LANES))
    span_table[:block_size, :span] = lag_cos.T
    span_table[block_size:, :span] = -lag_sin.T
    return tuple(
        jnp.asarray(table, jnp.bfloat16) for table in (row_table, col_table, lag_table, span_table)
    )


def tap_constants(block_size):
    offsets = np.arange(TAPS) - (TAPS // 2 - 1)
    spots = offsets[None, :] - np.arange(SUB)[:, None] / SUB
    raw_taps = np.sinc(spots) * np.sinc(spots / (TAPS // 2))
    taps = raw_taps / raw_taps.sum(axis=-1, keepdims=True)

    def band(inputs, outputs):
        at = inputs - outputs + TAPS // 2 - 1
        return np.where((at >= 0) & (at < TAPS), taps[:, np.clip(at, 0, TAPS - 1)], 0.0)

    lanes = np.arange(block_size)[None, :]
    inputs = np.arange(block_size + 3 * EDGE)[:, None] - EDGE - SHIFT
    outputs = np.arange(2 * EDGE)[:, None] - SHIFT
    spare = np.arange(LANES)[None, :] % (2 * EDGE)
    first = band(spare - 2 * EDGE, outputs) * (spare >= EDGE)
    last = band(spare + EDGE, outputs) * (spare < EDGE)
    tables = band(inputs, lanes), np.stack([first, last], axis=1)
    return [jnp.asarray(table, jnp.float32) for table in tables]


def step_places(place_ref, step, across, own):
    z = place_ref[0] ^ step
    places = []
    for other in range(2):
        for one in range(own):
            index = ((2 * z + (place_ref[1] ^ other)) * 2 + place_ref[2]) * own + one
            places.append((index, index % across))
    return places


def step_band(place_ref, step, across, own):
    return (place_ref[0] ^ step) * (4 * own) // across


def stage_kernel(count, *refs):
    sources, targets, sems = refs[:count], refs[count + 1 : 2 * count + 1], refs[-1]
    copies = [
        pltpu.make_async_copy(source, target, sems.at[at])
        for at, (source, target) in enumerate(zip(sources, targets))
    ]
    for copy in copies:
        copy.start()
    for copy in copies:
        copy.wait()


def stage(arrays, after):
    kept = [pltpu.with_memory_space_constraint(one, pltpu.HBM) for one in arrays]
    count = len(arrays)
    return pl.pallas_call(
        functools.partial(stage_kernel, count),
        out_shape=[jax.ShapeDtypeStruct(one.shape, one.dtype) for one in arrays],
        in_specs=[pl.BlockSpec(memory_space=pltpu.HBM)] * count
        + [pl.BlockSpec(memory_space=pl.ANY)],
        out_specs=[pl.BlockSpec(memory_space=pltpu.VMEM)] * count,
        scratch_shapes=[pltpu.SemaphoreType.DMA((count,))],
        compiler_params=pltpu.CompilerParams(vmem_limit_bytes=VMEM_LIMIT),
        name="stage",
    )(*kept, pltpu.with_memory_space_constraint(after, pltpu.HBM))


def warp_step(place_ref, step, other, code_refs, frame_refs, band_refs, down, across, block, own):
    cols_ref, edges_ref = band_refs
    band = step_band(place_ref, step, across, own)
    row = pl.multiple_of(band * block, block)
    row_above = pl.multiple_of(jnp.maximum(row - EDGE, 0), EDGE)
    row_below = pl.multiple_of(jnp.minimum(row + block, down * block - EDGE), EDGE)
    zero = jnp.zeros((EDGE, LANES), jnp.bfloat16)
    gap = jnp.zeros((block - 2 * EDGE, LANES), jnp.bfloat16)
    no_tile = jnp.zeros((block + 2 * EDGE, block), jnp.bfloat16)
    volumes = [
        (codes, frames, v)
        for codes, frames in zip(code_refs, frame_refs)
        for v in range(frames.shape[0])
    ]
    many = len(volumes)
    per_tile = LANES // (2 * EDGE)
    lane = lax.broadcasted_iota(jnp.int32, (EDGE, LANES), 1) // (2 * EDGE)

    def tile(frames, v, at):
        lanes = pl.ds(pl.multiple_of(at * block, block), block)
        above = jnp.where(band > 0, frames[v, pl.ds(row_above, EDGE), lanes], zero)
        below = jnp.where(band < down - 1, frames[v, pl.ds(row_below, EDGE), lanes], zero)
        return jnp.concatenate([frames[v, pl.ds(row, block), lanes], below, above], axis=0)

    places = step_places(place_ref, step, across, own)[other * own : (other + 1) * own]
    start = places[0][1]
    tiles = []
    for _, frames, v in volumes:
        left = jnp.where(start > 0, tile(frames, v, jnp.maximum(start - 1, 0)), no_tile)
        right = jnp.where(
            start + own < across, tile(frames, v, jnp.minimum(start + own, across - 1)), no_tile
        )
        tiles.append([left] + [tile(frames, v, start + one) for one in range(own)] + [right])
    totals = []
    for one, (index, _) in enumerate(places):
        row_tiles, partials, edges = [], [], []
        firsts, lasts = [], []
        for order, (codes, _, v) in enumerate(volumes):
            row_code, col_code = codes[v, 0, index], codes[v, 1, index]
            left, middle, right = tiles[order][one : one + 3]
            sides = jnp.concatenate([right[:, : block // 2], left[:, block // 2 :]], axis=1)
            col_start = SHIFT - (col_code >> 4)
            cols = cols_ref[col_code & (SUB - 1), pl.ds(col_start, block + 2 * EDGE), :]
            cols = cols.astype(jnp.bfloat16)
            partial = jnp.dot(
                jnp.concatenate([middle, sides], axis=1),
                jnp.concatenate([cols[EDGE:], gap, cols[:EDGE]], axis=0),
                preferred_element_type=jnp.float32,
            ).astype(jnp.bfloat16)
            partials.append(partial[:block])
            edges.append(partial[block:])
            back = -row_code
            back_start = SHIFT + EDGE - (back >> 4)
            rows = cols_ref[back & (SUB - 1), pl.ds(back_start, block), :]
            row_tiles.append(rows.astype(jnp.bfloat16))
            row_start, step_at = SHIFT + (row_code >> 4), row_code & (SUB - 1)
            first = edges_ref[step_at, 0, pl.ds(row_start, EDGE), :]
            last = edges_ref[step_at, 1, pl.ds(row_start, EDGE), :]
            if order % per_tile:
                first = jnp.where(lane == order % per_tile, first, firsts.pop())
                last = jnp.where(lane == order % per_tile, last, lasts.pop())
            firsts.append(first)
            lasts.append(last)
        for first, last in zip(firsts, lasts):
            both = [first.astype(jnp.bfloat16), gap, last.astype(jnp.bfloat16)]
            row_tiles.append(jnp.concatenate(both, axis=0))
        deep = many * (block + 2 * EDGE)
        total = jnp.dot(
            jnp.concatenate(row_tiles, axis=1)[:, :deep],
            jnp.concatenate(partials + edges, axis=0),
            preferred_element_type=jnp.float32,
        )
        totals.append(total.astype(jnp.bfloat16))
    return totals


def warp_kernel(down, across, block, own, other, *refs):
    place_ref, *code_refs = refs[:3]
    frame_refs, band_refs, out_refs = refs[3:5], refs[5:7], refs[8:]
    depth = out_refs[0].shape[0] // own if other else len(out_refs)
    for step in range(depth):
        totals = warp_step(
            place_ref, step, other, code_refs, frame_refs, band_refs, down, across, block, own
        )
        for one, total in enumerate(totals):
            if other:
                out_refs[0][step * own + one] = total
            else:
                out_refs[step][one] = total


def warp_sums(
    place, codes, other_codes, frames, other_frames, bands, after, other, depth, block, own
):
    vols, rows, cols = frames.shape
    down, across = rows // block, cols // block
    smem = pl.BlockSpec(memory_space=pltpu.SMEM)
    vmem = pl.BlockSpec(memory_space=pltpu.VMEM)
    if other:
        out_shape = [jax.ShapeDtypeStruct((depth * own, block, block), jnp.bfloat16)]
    else:
        out_shape = [jax.ShapeDtypeStruct((own, block, block), jnp.bfloat16)] * depth
    return pl.pallas_call(
        functools.partial(warp_kernel, down, across, block, own, other),
        out_shape=out_shape,
        in_specs=[smem] * 3
        + [vmem] * (2 + len(bands))
        + [pl.BlockSpec(memory_space=pl.ANY)],
        out_specs=[vmem] * len(out_shape),
        compiler_params=pltpu.CompilerParams(vmem_limit_bytes=VMEM_LIMIT),
        cost_estimate=pl.CostEstimate(
            flops=2 * vols * rows * cols * block * 8,
            bytes_accessed=vols * rows * cols * 4 + rows * cols,
            transcendentals=0,
        ),
        name="warp",
    )(place, codes, other_codes, frames, other_frames, *bands, after)


def spectrum_kernel(vols, across, block, own, planes, depth, other, *refs):
    place_ref, codes_ref, other_codes_ref, row_ref, col_ref, lag_ref, span_ref = refs[:7]
    frames_ref, other_frames_ref, template_ref = refs[7:10]
    all_cross, all_sums = refs[-2:]
    if other:
        found_ref, out_refs, found = refs[10], refs[11:-3], refs[-3]
        found[...] = found_ref[...]
    else:
        found = refs[11]
        found[...] = jnp.zeros(found.shape, jnp.float32)

    row_table = row_ref[...]
    col_table = col_ref[...]
    lag_table = lag_ref[...]
    half = row_table.shape[0] // 2
    kept = -(-(block // 2 + 1) // 8) * 8
    span = lag_table.shape[0] // 2
    top = lax.broadcasted_iota(jnp.int32, (8, LANES), 0) == 0
    volumes = [(codes_ref, frames_ref, v) for v in range(vols)]
    volumes += [(other_codes_ref, other_frames_ref, v) for v in range(vols)]
    many = len(volumes)
    local = 2 * own
    no_rows = jnp.zeros((half - kept, LANES), jnp.float32)

    for half_step in range(depth // 2):
        cross, sums = all_cross.at[half_step], all_sums.at[half_step]
        places = []
        for step in (2 * half_step, 2 * half_step + 1):
            band = step_band(place_ref, step, across, own)
            band_rows = pl.ds(pl.multiple_of(band * block, block), block)
            chosen = step_places(place_ref, step, across, own)[other * own : (other + 1) * own]
            for one, (index, at) in enumerate(chosen):
                lanes = pl.ds(pl.multiple_of(at * block, block), block)
                places.append((index, band_rows, lanes, step * own + one))

        for pair in range(local // 2):
            pair_places = places[2 * pair : 2 * pair + 2]
            sources = [[template_ref[at] for _, _, _, at in pair_places]]
            for _, frames, v in volumes:
                sources.append([frames[v, rows, lanes] for _, rows, lanes, _ in pair_places])
            parts = []
            for source in sources:
                rows = jnp.dot(
                    row_table,
                    jnp.concatenate(source, axis=1),
                    preferred_element_type=jnp.float32,
                ).astype(jnp.bfloat16)
                for side in range(2):
                    lanes = slice(side * block, (side + 1) * block)
                    parts.append(jnp.concatenate([rows[:half, lanes], rows[half:, lanes]], axis=1))
            spectra = jnp.dot(
                jnp.concatenate(parts, axis=0), col_table, preferred_element_type=jnp.float32
            )
            temp = spectra[: 2 * half].astype(jnp.bfloat16).astype(jnp.float32)
            for order in range(many):
                for side in range(2):
                    one = (2 * pair + side) * many + order
                    base = (2 * (order + 1) + side) * half
                    total = jnp.zeros((8, LANES), jnp.float32)
                    for row in range(0, kept, 8):
                        at = side * half + row
                        temp_real = temp[at : at + 8, :block]
                        temp_imag = temp[at : at + 8, block:]
                        real = spectra[base + row : base + row + 8, :block]
                        imag = spectra[base + row : base + row + 8, block:]
                        cross_real = real * temp_real + imag * temp_imag
                        cross_imag = imag * temp_real - real * temp_imag
                        power = cross_real * cross_real + cross_imag * cross_imag
                        magnitude = power * lax.rsqrt(jnp.maximum(power, 1e-36))
                        cross[one, row : row + 8, :] = cross_real
                        cross[one, kept + row : kept + row + 8, :] = cross_imag
                        cross[one, 2 * kept + row : 2 * kept + row + 8, :] = magnitude
                        if row == 0:
                            total = jnp.where(top, magnitude, 2.0 * magnitude)
                        elif row == block // 2:
                            total += magnitude
                        else:
                            total += 2.0 * magnitude
                    sums[one] = jnp.sum(total, axis=0, keepdims=True)

        means = jnp.sum(sums[...], axis=2, keepdims=True) * (1.0 / (block * block)) + 1e-06
        lag_sums = []
        for pair in range(local // 2):
            for order in range(many):
                norms = []
                for side in range(2):
                    one = (2 * pair + side) * many + order
                    scale = pl.reciprocal(cross[one, 2 * kept :, :] + means[one], approx=True)
                    norms.append(
                        jnp.concatenate(
                            [
                                cross[one, :kept, :] * scale,
                                no_rows,
                                cross[one, kept : 2 * kept, :] * scale,
                                no_rows,
                            ],
                            axis=0,
                        ).astype(jnp.bfloat16)
                    )
                lag_rows = jnp.dot(
                    lag_table, jnp.concatenate(norms, axis=1), preferred_element_type=jnp.float32
                ).astype(jnp.bfloat16)
                for side in range(2):
                    lanes = slice(side * block, (side + 1) * block)
                    lag_sums.append(
                        jnp.concatenate([lag_rows[:span, lanes], lag_rows[span:, lanes]], axis=1)
                    )
        lags = jnp.dot(
            jnp.concatenate(lag_sums, axis=0), span_ref[...], preferred_element_type=jnp.float32
        )
        for pair in range(local // 2):
            for order, (codes, _, v) in enumerate(volumes):
                for side in range(2):
                    index = places[2 * pair + side][0]
                    row_shift = codes[v, 0, index] >> 4
                    col_shift = codes[v, 1, index] >> 4
                    at = (pair * many + order) * 2 + side
                    one = lags[at * span : (at + 1) * span]
                    one = pltpu.roll(one, span - SHIFT - row_shift, 0)[:WIN]
                    found[order, pl.ds(pl.multiple_of(index * WIN, WIN), WIN), :] = pltpu.roll(
                        one, LANES - SHIFT - col_shift, 1
                    )

    if not other:
        return

    keep_refs, give_ref = out_refs[:-1], out_refs[-1]
    share = found.shape[1] // WIN // planes
    per_tile = LANES // WIN
    lane = lax.broadcasted_iota(jnp.int32, (share, LANES), 1) // WIN
    for turn, keep_ref in enumerate(keep_refs):
        plane = place_ref[3] ^ turn
        for order in range(many):
            for tile in range(WIN // per_tile):
                total = jnp.zeros((share, LANES), jnp.float32)
                for part in range(per_tile):
                    start = plane * share * WIN + tile * per_tile + part
                    one = found[order, pl.ds(start, share, stride=WIN), :]
                    if part:
                        one = pltpu.roll(one, part * WIN, 1)
                    total = jnp.where(lane == part, one, total)
                lanes = slice(tile * LANES, (tile + 1) * LANES)
                total = total * (1.0 / block)
                if order < vols:
                    keep_ref[order, :, lanes] = total
                else:
                    give_ref[turn, order - vols, :, lanes] = total


def lag_windows(
    place, codes, other_codes, frames, other_frames, template, more, other, planes, depth, own
):
    vols, rows, cols = frames.shape
    block = template.shape[-1]
    down, across = rows // block, cols // block
    tables = dft_constants(block)
    kept = -(-(block // 2 + 1) // 8) * 8
    smem = pl.BlockSpec(memory_space=pltpu.SMEM)
    vmem = pl.BlockSpec(memory_space=pltpu.VMEM)
    blocks = down * across
    many = 2 * vols * 2 * own
    found = jax.ShapeDtypeStruct((2 * vols, blocks * WIN, LANES), jnp.float32)
    if other:
        out = (vols, blocks // planes, WIN * WIN)
        out_shape = [jax.ShapeDtypeStruct(out, jnp.float32)] * planes
        out_shape.append(jax.ShapeDtypeStruct((planes, *out), jnp.float32))
        scratch_shapes = [pltpu.VMEM(found.shape, found.dtype)]
        last = vmem
    else:
        out_shape = [found]
        scratch_shapes = []
        last = pl.BlockSpec(memory_space=pl.ANY)
    return pl.pallas_call(
        functools.partial(spectrum_kernel, vols, across, block, own, planes, depth, other),
        out_shape=out_shape,
        in_specs=[smem] * 3 + [vmem] * (len(tables) + 3) + [last],
        out_specs=[vmem] * len(out_shape),
        scratch_shapes=scratch_shapes
        + [
            pltpu.VMEM((depth // 2, many, 3 * kept, LANES), jnp.float32),
            pltpu.VMEM((depth // 2, many, 1, LANES), jnp.float32),
        ],
        compiler_params=pltpu.CompilerParams(vmem_limit_bytes=VMEM_LIMIT),
        cost_estimate=pl.CostEstimate(
            flops=2 * 3 * rows * cols * block * (2 if other else 8),
            bytes_accessed=vols * rows * cols * 4 + rows * cols,
            transcendentals=0,
        ),
        name="lag_windows",
    )(place, codes, other_codes, *tables, frames, other_frames, template, more)


def exchange(value, axes, size, turn):
    return lax.ppermute(value, axes, [(at, at ^ turn) for at in range(size)])


def on_device(frames, template, shift_codes):
    vol_dev, pl_dev, img_rows, img_cols = frames.shape
    own, block = template.shape[0], template.shape[-1]
    depth = lax.axis_size("z")
    planes = lax.axis_size("plane")
    place = jnp.stack([lax.axis_index(axis) for axis in ("z", "y", "core", "plane")])
    other_codes = exchange(shift_codes, "core", 2, 1)
    other_frames = exchange(frames, "core", 2, 1)
    staged, *bands = stage([frames, *tap_constants(block)], template)
    pieces = [template] + [exchange(template, "z", depth, turn) for turn in range(1, depth)]
    averages, correlation = [], 0.0
    volumes = vol_dev * depth * 4
    for p in range(pl_dev):
        work = (place, shift_codes, other_codes, staged[:, p], other_frames[:, p])
        sizes = (depth, block, own)
        (far_sums,) = warp_sums(*work, bands, template, 1, *sizes)
        taken = exchange(far_sums, "y", 2, 1)
        near_sums = warp_sums(*work, bands, far_sums, 0, *sizes)
        pieces, near_sums = lax.optimization_barrier((pieces, near_sums))
        near = jnp.concatenate([piece[:, p] for piece in pieces], axis=0)
        far = exchange(near, "y", 2, 1)
        sums = [
            one.astype(jnp.float32) + taken[step * own : (step + 1) * own].astype(jnp.float32)
            for step, one in enumerate(near_sums)
        ]
        moved = [
            exchange(sums[turn].astype(jnp.bfloat16), "z", depth, turn) for turn in range(1, depth)
        ]
        sizes = (planes, depth, own)
        (part,) = lag_windows(*work, near, sums[0], 0, *sizes)
        *keep, give = lag_windows(*work, far, part, 1, *sizes)
        keep, moved = lax.optimization_barrier((keep, moved))
        total = sum((one.astype(jnp.float32) for one in moved), sums[0])
        averages.append(total * (1.0 / volumes))
        got = exchange(give, "core", 2, 1)
        for turn, one in enumerate(keep):
            one = one + got[turn]
            correlation += exchange(one, "plane", planes, turn) if turn else one
    return (correlation, jnp.stack(averages, axis=1))


def solution(mesh):
    devices = mesh.devices.reshape(-1, 2, 2, mesh.shape["plane"])
    split = jax.sharding.Mesh(devices, ("z", "y", "core", "plane"))
    vols = ("z", "y", "core")
    in_specs = (P(vols, "plane", None, None), P(vols, "plane", None, None), P(vols, None, None))
    out_specs = (P(vols, "plane", None), P(vols, "plane", None, None))
    return jax.shard_map(
        on_device, mesh=split, in_specs=in_specs, out_specs=out_specs, check_vma=False
    )
```

```python
import functools
import math

import jax
import jax.numpy as jnp
import numpy as np
from jax import lax
from jax.experimental import pallas as pl
from jax.experimental.pallas import tpu as pltpu
from jax.sharding import PartitionSpec as P

SHIFT = 8
WIN = 16
TAPS = 8
SUB = 16
EDGE = 16
LANES = 128
VMEM_LIMIT = 24 * 1024 * 1024

full_turn = 2.0 * math.pi


def dft_constants(block_size):
    positions = np.arange(block_size)
    angles = full_turn * (np.outer(positions, positions) % block_size) / block_size
    cosine = np.cos(angles)
    sine = -np.sin(angles)
    half = block_size // 2 + 1
    rows = -(-half // 16) * 16
    row_table = np.zeros((2 * rows, block_size))
    row_table[:half] = cosine[:half]
    row_table[rows : rows + half] = sine[:half]
    col_table = np.block([[cosine, sine], [-sine, cosine]])
    weights = np.full((half,), 2.0)
    weights[0] = weights[half - 1] = 1.0
    span = 2 * SHIFT + WIN
    lags = np.arange(span) - SHIFT - WIN // 2
    turns = full_turn * (np.outer(lags, positions) % block_size) / block_size
    lag_cos, lag_sin = np.cos(turns), np.sin(turns)
    lag_table = np.zeros((2 * span, 2 * rows))
    lag_table[:span, :half] = lag_cos[:, :half] * weights
    lag_table[:span, rows : rows + half] = -lag_sin[:, :half] * weights
    lag_table[span:, :half] = lag_sin[:, :half] * weights
    lag_table[span:, rows : rows + half] = lag_cos[:, :half] * weights
    span_table = np.zeros((2 * block_size, LANES))
    span_table[:block_size, :span] = lag_cos.T
    span_table[block_size:, :span] = -lag_sin.T
    return tuple(
        jnp.asarray(table, jnp.bfloat16) for table in (row_table, col_table, lag_table, span_table)
    )


def tap_constants(block_size):
    offsets = np.arange(TAPS) - (TAPS // 2 - 1)
    spots = offsets[None, :] - np.arange(SUB)[:, None] / SUB
    raw_taps = np.sinc(spots) * np.sinc(spots / (TAPS // 2))
    taps = raw_taps / raw_taps.sum(axis=-1, keepdims=True)

    def band(inputs, outputs):
        at = inputs - outputs + TAPS // 2 - 1
        return np.where((at >= 0) & (at < TAPS), taps[:, np.clip(at, 0, TAPS - 1)], 0.0)

    lanes = np.arange(block_size)[None, :]
    inputs = np.arange(block_size + 3 * EDGE)[:, None] - EDGE - SHIFT
    outputs = np.arange(2 * EDGE)[:, None] - SHIFT
    spare = np.arange(LANES)[None, :] % (2 * EDGE)
    first = band(spare - 2 * EDGE, outputs) * (spare >= EDGE)
    last = band(spare + EDGE, outputs) * (spare < EDGE)
    tables = band(inputs, lanes), np.stack([first, last], axis=1)
    return [jnp.asarray(table, jnp.float32) for table in tables]


def step_places(place_ref, step, across, own):
    z = place_ref[0] ^ step
    places = []
    for other in range(2):
        for one in range(own):
            index = ((2 * z + (place_ref[1] ^ other)) * 2 + place_ref[2]) * own + one
            places.append((index, index % across))
    return places


def step_band(place_ref, step, across, own):
    return (place_ref[0] ^ step) * (4 * own) // across


def stage_kernel(count, *refs):
    sources, targets, sems = refs[:count], refs[count + 1 : 2 * count + 1], refs[-1]
    copies = [
        pltpu.make_async_copy(source, target, sems.at[at])
        for at, (source, target) in enumerate(zip(sources, targets))
    ]
    for copy in copies:
        copy.start()
    refs[2 * count + 1][...] = jnp.zeros((8, LANES), jnp.float32)
    for copy in copies:
        copy.wait()


def stage(arrays, after):
    kept = [pltpu.with_memory_space_constraint(one, pltpu.HBM) for one in arrays]
    count = len(arrays)
    return pl.pallas_call(
        functools.partial(stage_kernel, count),
        out_shape=[jax.ShapeDtypeStruct(one.shape, one.dtype) for one in arrays]
        + [jax.ShapeDtypeStruct((8, LANES), jnp.float32)],
        in_specs=[pl.BlockSpec(memory_space=pltpu.HBM)] * count
        + [pl.BlockSpec(memory_space=pl.ANY)],
        out_specs=[pl.BlockSpec(memory_space=pltpu.VMEM)] * (count + 1),
        scratch_shapes=[pltpu.SemaphoreType.DMA((count,))],
        compiler_params=pltpu.CompilerParams(vmem_limit_bytes=VMEM_LIMIT),
        cost_estimate=pl.CostEstimate(
            flops=0, bytes_accessed=2 * sum(one.nbytes for one in arrays), transcendentals=0
        ),
        name="stage",
    )(*kept, pltpu.with_memory_space_constraint(after, pltpu.HBM))


def warp_step(place_ref, step, other, code_refs, frame_refs, band_refs, down, across, block, own):
    cols_ref, edges_ref = band_refs
    band = step_band(place_ref, step, across, own)
    row = pl.multiple_of(band * block, block)
    row_above = pl.multiple_of(jnp.maximum(row - EDGE, 0), EDGE)
    row_below = pl.multiple_of(jnp.minimum(row + block, down * block - EDGE), EDGE)
    zero = jnp.zeros((EDGE, LANES), jnp.bfloat16)
    gap = jnp.zeros((block - 2 * EDGE, LANES), jnp.bfloat16)
    no_tile = jnp.zeros((block + 2 * EDGE, block), jnp.bfloat16)
    volumes = [
        (codes, frames, v)
        for codes, frames in zip(code_refs, frame_refs)
        for v in range(frames.shape[0])
    ]
    many = len(volumes)
    per_tile = LANES // (2 * EDGE)
    lane = lax.broadcasted_iota(jnp.int32, (EDGE, LANES), 1) // (2 * EDGE)

    def tile(frames, v, at):
        lanes = pl.ds(pl.multiple_of(at * block, block), block)
        above = jnp.where(band > 0, frames[v, pl.ds(row_above, EDGE), lanes], zero)
        below = jnp.where(band < down - 1, frames[v, pl.ds(row_below, EDGE), lanes], zero)
        return jnp.concatenate([frames[v, pl.ds(row, block), lanes], below, above], axis=0)

    places = step_places(place_ref, step, across, own)[other * own : (other + 1) * own]
    start = places[0][1]
    tiles = []
    for _, frames, v in volumes:
        left = jnp.where(start > 0, tile(frames, v, jnp.maximum(start - 1, 0)), no_tile)
        right = jnp.where(
            start + own < across, tile(frames, v, jnp.minimum(start + own, across - 1)), no_tile
        )
        tiles.append([left] + [tile(frames, v, start + one) for one in range(own)] + [right])
    totals = []
    for one, (index, _) in enumerate(places):
        row_tiles, partials, edges = [], [], []
        firsts, lasts = [], []
        for order, (codes, _, v) in enumerate(volumes):
            row_code, col_code = codes[v, 0, index], codes[v, 1, index]
            left, middle, right = tiles[order][one : one + 3]
            sides = jnp.concatenate([right[:, : block // 2], left[:, block // 2 :]], axis=1)
            col_start = SHIFT - (col_code >> 4)
            cols = cols_ref[col_code & (SUB - 1), pl.ds(col_start, block + 2 * EDGE), :]
            cols = cols.astype(jnp.bfloat16)
            partial = jnp.dot(
                jnp.concatenate([middle, sides], axis=1),
                jnp.concatenate([cols[EDGE:], gap, cols[:EDGE]], axis=0),
                preferred_element_type=jnp.float32,
            ).astype(jnp.bfloat16)
            partials.append(partial[:block])
            edges.append(partial[block:])
            back = -row_code
            back_start = SHIFT + EDGE - (back >> 4)
            rows = cols_ref[back & (SUB - 1), pl.ds(back_start, block), :]
            row_tiles.append(rows.astype(jnp.bfloat16))
            row_start, step_at = SHIFT + (row_code >> 4), row_code & (SUB - 1)
            first = edges_ref[step_at, 0, pl.ds(row_start, EDGE), :]
            last = edges_ref[step_at, 1, pl.ds(row_start, EDGE), :]
            if order % per_tile:
                first = jnp.where(lane == order % per_tile, first, firsts.pop())
                last = jnp.where(lane == order % per_tile, last, lasts.pop())
            firsts.append(first)
            lasts.append(last)
        for first, last in zip(firsts, lasts):
            both = [first.astype(jnp.bfloat16), gap, last.astype(jnp.bfloat16)]
            row_tiles.append(jnp.concatenate(both, axis=0))
        deep = many * (block + 2 * EDGE)
        total = jnp.dot(
            jnp.concatenate(row_tiles, axis=1)[:, :deep],
            jnp.concatenate(partials + edges, axis=0),
            preferred_element_type=jnp.float32,
        )
        totals.append(total.astype(jnp.bfloat16))
    return totals


def warp_kernel(down, across, block, own, other, *refs):
    place_ref, *code_refs = refs[:3]
    frame_refs, band_refs, out_refs = refs[3:5], refs[5:7], refs[8:]
    depth = out_refs[0].shape[0] // own if other else len(out_refs)
    for step in range(depth):
        totals = warp_step(
            place_ref, step, other, code_refs, frame_refs, band_refs, down, across, block, own
        )
        for one, total in enumerate(totals):
            if other:
                out_refs[0][step * own + one] = total
            else:
                out_refs[step][one] = total


def warp_sums(
    place, codes, other_codes, frames, other_frames, bands, after, other, depth, block, own
):
    vols, rows, cols = frames.shape
    down, across = rows // block, cols // block
    smem = pl.BlockSpec(memory_space=pltpu.SMEM)
    vmem = pl.BlockSpec(memory_space=pltpu.VMEM)
    if other:
        out_shape = [jax.ShapeDtypeStruct((depth * own, block, block), jnp.bfloat16)]
    else:
        out_shape = [jax.ShapeDtypeStruct((own, block, block), jnp.bfloat16)] * depth
    return pl.pallas_call(
        functools.partial(warp_kernel, down, across, block, own, other),
        out_shape=out_shape,
        in_specs=[smem] * 3
        + [vmem] * (2 + len(bands))
        + [pl.BlockSpec(memory_space=pl.ANY)],
        out_specs=[vmem] * len(out_shape),
        compiler_params=pltpu.CompilerParams(vmem_limit_bytes=VMEM_LIMIT),
        cost_estimate=pl.CostEstimate(
            flops=2 * vols * rows * cols * block * 8,
            bytes_accessed=vols * rows * cols * 4 + rows * cols,
            transcendentals=0,
        ),
        name="warp",
    )(place, codes, other_codes, frames, other_frames, *bands, after)


def spectrum_kernel(vols, across, block, own, planes, depth, other, *refs):
    place_ref, codes_ref, other_codes_ref, row_ref, col_ref, lag_ref, span_ref = refs[:7]
    frames_ref, other_frames_ref, template_ref = refs[7:10]
    all_cross, all_sums = refs[-2:]
    if other:
        found_ref, out_refs, found = refs[10], refs[11:-3], refs[-3]
        found[...] = found_ref[...]
    else:
        found = refs[11]
        found[...] = jnp.zeros(found.shape, jnp.float32)

    row_table = row_ref[...]
    col_table = col_ref[...]
    lag_table = lag_ref[...]
    half = row_table.shape[0] // 2
    kept = -(-(block // 2 + 1) // 8) * 8
    span = lag_table.shape[0] // 2
    top = lax.broadcasted_iota(jnp.int32, (8, LANES), 0) == 0
    volumes = [(codes_ref, frames_ref, v) for v in range(vols)]
    volumes += [(other_codes_ref, other_frames_ref, v) for v in range(vols)]
    many = len(volumes)
    local = 2 * own
    no_rows = jnp.zeros((half - kept, LANES), jnp.float32)

    for half_step in range(depth // 2):
        cross, sums = all_cross.at[half_step], all_sums.at[half_step]
        places = []
        for step in (2 * half_step, 2 * half_step + 1):
            band = step_band(place_ref, step, across, own)
            band_rows = pl.ds(pl.multiple_of(band * block, block), block)
            chosen = step_places(place_ref, step, across, own)[other * own : (other + 1) * own]
            for one, (index, at) in enumerate(chosen):
                lanes = pl.ds(pl.multiple_of(at * block, block), block)
                places.append((index, band_rows, lanes, step * own + one))

        for pair in range(local // 2):
            pair_places = places[2 * pair : 2 * pair + 2]
            sources = [[template_ref[at] for _, _, _, at in pair_places]]
            for _, frames, v in volumes:
                sources.append([frames[v, rows, lanes] for _, rows, lanes, _ in pair_places])
            parts = []
            for source in sources:
                rows = jnp.dot(
                    row_table,
                    jnp.concatenate(source, axis=1),
                    preferred_element_type=jnp.float32,
                ).astype(jnp.bfloat16)
                for side in range(2):
                    lanes = slice(side * block, (side + 1) * block)
                    parts.append(jnp.concatenate([rows[:half, lanes], rows[half:, lanes]], axis=1))
            spectra = jnp.dot(
                jnp.concatenate(parts, axis=0), col_table, preferred_element_type=jnp.float32
            )
            temp = spectra[: 2 * half].astype(jnp.bfloat16).astype(jnp.float32)
            for order in range(many):
                for side in range(2):
                    one = (2 * pair + side) * many + order
                    base = (2 * (order + 1) + side) * half
                    total = jnp.zeros((8, LANES), jnp.float32)
                    for row in range(0, kept, 8):
                        at = side * half + row
                        temp_real = temp[at : at + 8, :block]
                        temp_imag = temp[at : at + 8, block:]
                        real = spectra[base + row : base + row + 8, :block]
                        imag = spectra[base + row : base + row + 8, block:]
                        cross_real = real * temp_real + imag * temp_imag
                        cross_imag = imag * temp_real - real * temp_imag
                        power = cross_real * cross_real + cross_imag * cross_imag
                        magnitude = power * lax.rsqrt(jnp.maximum(power, 1e-36))
                        cross[one, row : row + 8, :] = cross_real
                        cross[one, kept + row : kept + row + 8, :] = cross_imag
                        cross[one, 2 * kept + row : 2 * kept + row + 8, :] = magnitude
                        if row == 0:
                            total = jnp.where(top, magnitude, 2.0 * magnitude)
                        elif row == block // 2:
                            total += magnitude
                        else:
                            total += 2.0 * magnitude
                    sums[one] = jnp.sum(total, axis=0, keepdims=True)

        means = jnp.sum(sums[...], axis=2, keepdims=True) * (1.0 / (block * block)) + 1e-06
        lag_sums = []
        for pair in range(local // 2):
            for order in range(many):
                norms = []
                for side in range(2):
                    one = (2 * pair + side) * many + order
                    scale = pl.reciprocal(cross[one, 2 * kept :, :] + means[one], approx=True)
                    norms.append(
                        jnp.concatenate(
                            [
                                cross[one, :kept, :] * scale,
                                no_rows,
                                cross[one, kept : 2 * kept, :] * scale,
                                no_rows,
                            ],
                            axis=0,
                        ).astype(jnp.bfloat16)
                    )
                lag_rows = jnp.dot(
                    lag_table, jnp.concatenate(norms, axis=1), preferred_element_type=jnp.float32
                ).astype(jnp.bfloat16)
                for side in range(2):
                    lanes = slice(side * block, (side + 1) * block)
                    lag_sums.append(
                        jnp.concatenate([lag_rows[:span, lanes], lag_rows[span:, lanes]], axis=1)
                    )
        lags = jnp.dot(
            jnp.concatenate(lag_sums, axis=0), span_ref[...], preferred_element_type=jnp.float32
        )
        for pair in range(local // 2):
            for order, (codes, _, v) in enumerate(volumes):
                for side in range(2):
                    index = places[2 * pair + side][0]
                    row_shift = codes[v, 0, index] >> 4
                    col_shift = codes[v, 1, index] >> 4
                    at = (pair * many + order) * 2 + side
                    one = lags[at * span : (at + 1) * span]
                    one = pltpu.roll(one, span - SHIFT - row_shift, 0)[:WIN]
                    found[order, pl.ds(pl.multiple_of(index * WIN, WIN), WIN), :] = pltpu.roll(
                        one, LANES - SHIFT - col_shift, 1
                    )

    if not other:
        return

    keep_refs, give_ref = out_refs[:-1], out_refs[-1]
    share = found.shape[1] // WIN // planes
    per_tile = LANES // WIN
    lane = lax.broadcasted_iota(jnp.int32, (share, LANES), 1) // WIN
    for turn, keep_ref in enumerate(keep_refs):
        plane = place_ref[3] ^ turn
        for order in range(many):
            for tile in range(WIN // per_tile):
                total = jnp.zeros((share, LANES), jnp.float32)
                for part in range(per_tile):
                    start = plane * share * WIN + tile * per_tile + part
                    one = found[order, pl.ds(start, share, stride=WIN), :]
                    if part:
                        one = pltpu.roll(one, part * WIN, 1)
                    total = jnp.where(lane == part, one, total)
                lanes = slice(tile * LANES, (tile + 1) * LANES)
                total = total * (1.0 / block)
                if order < vols:
                    keep_ref[order, :, lanes] = total
                else:
                    give_ref[turn, order - vols, :, lanes] = total


def lag_windows(
    place, codes, other_codes, frames, other_frames, template, more, other, planes, depth, own
):
    vols, rows, cols = frames.shape
    block = template.shape[-1]
    down, across = rows // block, cols // block
    tables = dft_constants(block)
    kept = -(-(block // 2 + 1) // 8) * 8
    smem = pl.BlockSpec(memory_space=pltpu.SMEM)
    vmem = pl.BlockSpec(memory_space=pltpu.VMEM)
    blocks = down * across
    many = 2 * vols * 2 * own
    found = jax.ShapeDtypeStruct((2 * vols, blocks * WIN, LANES), jnp.float32)
    if other:
        out = (vols, blocks // planes, WIN * WIN)
        out_shape = [jax.ShapeDtypeStruct(out, jnp.float32)] * planes
        out_shape.append(jax.ShapeDtypeStruct((planes, *out), jnp.float32))
        scratch_shapes = [pltpu.VMEM(found.shape, found.dtype)]
        last = vmem
    else:
        out_shape = [found]
        scratch_shapes = []
        last = pl.BlockSpec(memory_space=pl.ANY)
    return pl.pallas_call(
        functools.partial(spectrum_kernel, vols, across, block, own, planes, depth, other),
        out_shape=out_shape,
        in_specs=[smem] * 3 + [vmem] * (len(tables) + 3) + [last],
        out_specs=[vmem] * len(out_shape),
        scratch_shapes=scratch_shapes
        + [
            pltpu.VMEM((depth // 2, many, 3 * kept, LANES), jnp.float32),
            pltpu.VMEM((depth // 2, many, 1, LANES), jnp.float32),
        ],
        compiler_params=pltpu.CompilerParams(vmem_limit_bytes=VMEM_LIMIT),
        cost_estimate=pl.CostEstimate(
            flops=2 * 3 * rows * cols * block * (2 if other else 8),
            bytes_accessed=vols * rows * cols * 4 + rows * cols,
            transcendentals=0,
        ),
        name="lag_windows",
    )(place, codes, other_codes, *tables, frames, other_frames, template, more)


def exchange(value, axes, size, turn):
    return lax.ppermute(value, axes, [(at, at ^ turn) for at in range(size)])


def on_device(frames, template, shift_codes):
    vol_dev, pl_dev, img_rows, img_cols = frames.shape
    own, block = template.shape[0], template.shape[-1]
    depth = lax.axis_size("z")
    planes = lax.axis_size("plane")
    place = jnp.stack([lax.axis_index(axis) for axis in ("z", "y", "core", "plane")])
    other_codes = exchange(shift_codes, "core", 2, 1)
    other_frames = exchange(frames, "core", 2, 1)
    staged, *bands, token = stage([frames, *tap_constants(block)], template)
    pieces, turn = [template], depth // 2
    while turn:
        held = pieces[0] if len(pieces) == 1 else jnp.concatenate(pieces, axis=0)
        fetched = exchange(held, "z", depth, turn)
        if turn > 1:
            fetched, token = lax.optimization_barrier((fetched, token))
            fetched = [fetched[at * own : (at + 1) * own] for at in range(len(pieces))]
            pieces = [piece for pair in zip(pieces, fetched) for piece in pair]
        turn //= 2
    averages, correlation = [], 0.0
    volumes = vol_dev * depth * 4
    for p in range(pl_dev):
        work = (place, shift_codes, other_codes, staged[:, p], other_frames[:, p])
        sizes = (depth, block, own)
        (far_sums,) = warp_sums(*work, bands, template, 1, *sizes)
        taken = exchange(far_sums, "y", 2, 1)
        near_sums = warp_sums(*work, bands, far_sums, 0, *sizes)
        kept, got, near_sums = lax.optimization_barrier((held, fetched, near_sums))
        near = jnp.stack(
            [one[:, p].reshape(depth // 2, own, block, block) for one in (kept, got)], axis=1
        ).reshape(depth * own, block, block)
        far = exchange(near, "y", 2, 1)
        sums = [
            one.astype(jnp.float32) + taken[step * own : (step + 1) * own].astype(jnp.float32)
            for step, one in enumerate(near_sums)
        ]
        moved = [
            exchange(sums[turn].astype(jnp.bfloat16), "z", depth, turn) for turn in range(1, depth)
        ]
        sizes = (planes, depth, own)
        (part,) = lag_windows(*work, near, near_sums[0], 0, *sizes)
        *keep, give = lag_windows(*work, far, part, 1, *sizes)
        keep, moved = lax.optimization_barrier((keep, moved))
        total = sum((one.astype(jnp.float32) for one in moved), sums[0])
        averages.append(total * (1.0 / volumes))
        got = exchange(give, "core", 2, 1)
        for turn, one in enumerate(keep):
            one = one + got[turn]
            correlation += exchange(one, "plane", planes, turn) if turn else one
    return (correlation, jnp.stack(averages, axis=1))


def solution(mesh):
    devices = mesh.devices.reshape(-1, 2, 2, mesh.shape["plane"])
    split = jax.sharding.Mesh(devices, ("z", "y", "core", "plane"))
    vols = ("z", "y", "core")
    in_specs = (P(vols, "plane", None, None), P(vols, "plane", None, None), P(vols, None, None))
    out_specs = (P(vols, "plane", None), P(vols, "plane", None, None))
    return jax.shard_map(
        on_device, mesh=split, in_specs=in_specs, out_specs=out_specs, check_vma=False
    )
```

```python
import functools
import math

import jax
import jax.numpy as jnp
import numpy as np
from jax import lax
from jax.experimental import pallas as pl
from jax.experimental.pallas import tpu as pltpu
from jax.sharding import PartitionSpec as P

SHIFT = 8
WIN = 16
TAPS = 8
SUB = 16
EDGE = 16
LANES = 128
VMEM_LIMIT = 24 * 1024 * 1024

full_turn = 2.0 * math.pi


def dft_constants(block_size):
    positions = np.arange(block_size)
    angles = full_turn * (np.outer(positions, positions) % block_size) / block_size
    cosine = np.cos(angles)
    sine = -np.sin(angles)
    half = block_size // 2 + 1
    rows = -(-half // 16) * 16
    row_table = np.zeros((2 * rows, block_size))
    row_table[:half] = cosine[:half]
    row_table[rows : rows + half] = sine[:half]
    col_table = np.block([[cosine, sine], [-sine, cosine]])
    weights = np.full((half,), 2.0)
    weights[0] = weights[half - 1] = 1.0
    span = 2 * SHIFT + WIN
    lags = np.arange(span) - SHIFT - WIN // 2
    turns = full_turn * (np.outer(lags, positions) % block_size) / block_size
    lag_cos, lag_sin = np.cos(turns), np.sin(turns)
    lag_table = np.zeros((2 * span, 2 * rows))
    lag_table[:span, :half] = lag_cos[:, :half] * weights
    lag_table[:span, rows : rows + half] = -lag_sin[:, :half] * weights
    lag_table[span:, :half] = lag_sin[:, :half] * weights
    lag_table[span:, rows : rows + half] = lag_cos[:, :half] * weights
    span_table = np.zeros((2 * block_size, LANES))
    span_table[:block_size, :span] = lag_cos.T
    span_table[block_size:, :span] = -lag_sin.T
    return tuple(
        jnp.asarray(table, jnp.bfloat16) for table in (row_table, col_table, lag_table, span_table)
    )


def tap_constants(block_size):
    offsets = np.arange(TAPS) - (TAPS // 2 - 1)
    spots = offsets[None, :] - np.arange(SUB)[:, None] / SUB
    raw_taps = np.sinc(spots) * np.sinc(spots / (TAPS // 2))
    taps = raw_taps / raw_taps.sum(axis=-1, keepdims=True)

    def band(inputs, outputs):
        at = inputs - outputs + TAPS // 2 - 1
        return np.where((at >= 0) & (at < TAPS), taps[:, np.clip(at, 0, TAPS - 1)], 0.0)

    lanes = np.arange(block_size)[None, :]
    inputs = np.arange(block_size + 3 * EDGE)[:, None] - EDGE - SHIFT
    outputs = np.arange(2 * EDGE)[:, None] - SHIFT
    spare = np.arange(LANES)[None, :] % (2 * EDGE)
    first = band(spare - 2 * EDGE, outputs) * (spare >= EDGE)
    last = band(spare + EDGE, outputs) * (spare < EDGE)
    tables = band(inputs, lanes), np.stack([first, last], axis=1)
    return [jnp.asarray(table, jnp.float32) for table in tables]


def step_places(place_ref, step, across, own):
    z = place_ref[0] ^ step
    places = []
    for other in range(2):
        for one in range(own):
            index = ((2 * z + (place_ref[1] ^ other)) * 2 + place_ref[2]) * own + one
            places.append((index, index % across))
    return places


def step_band(place_ref, step, across, own):
    return (place_ref[0] ^ step) * (4 * own) // across


def stage_kernel(count, *refs):
    sources, targets, sems = refs[:count], refs[count + 1 : 2 * count + 1], refs[-1]
    copies = [
        pltpu.make_async_copy(source, target, sems.at[at])
        for at, (source, target) in enumerate(zip(sources, targets))
    ]
    for copy in copies:
        copy.start()
    refs[2 * count + 1][...] = jnp.zeros((8, LANES), jnp.float32)
    for copy in copies:
        copy.wait()


def stage(arrays, after):
    kept = [pltpu.with_memory_space_constraint(one, pltpu.HBM) for one in arrays]
    count = len(arrays)
    return pl.pallas_call(
        functools.partial(stage_kernel, count),
        out_shape=[jax.ShapeDtypeStruct(one.shape, one.dtype) for one in arrays]
        + [jax.ShapeDtypeStruct((8, LANES), jnp.float32)],
        in_specs=[pl.BlockSpec(memory_space=pltpu.HBM)] * count
        + [pl.BlockSpec(memory_space=pl.ANY)],
        out_specs=[pl.BlockSpec(memory_space=pltpu.VMEM)] * (count + 1),
        scratch_shapes=[pltpu.SemaphoreType.DMA((count,))],
        compiler_params=pltpu.CompilerParams(vmem_limit_bytes=VMEM_LIMIT),
        cost_estimate=pl.CostEstimate(
            flops=0, bytes_accessed=2 * sum(one.nbytes for one in arrays), transcendentals=0
        ),
        name="stage",
    )(*kept, pltpu.with_memory_space_constraint(after, pltpu.HBM))


def warp_step(place_ref, step, other, code_refs, frame_refs, band_refs, down, across, block, own):
    cols_ref, edges_ref = band_refs
    band = step_band(place_ref, step, across, own)
    row = pl.multiple_of(band * block, block)
    row_above = pl.multiple_of(jnp.maximum(row - EDGE, 0), EDGE)
    row_below = pl.multiple_of(jnp.minimum(row + block, down * block - EDGE), EDGE)
    zero = jnp.zeros((EDGE, LANES), jnp.bfloat16)
    gap = jnp.zeros((block - 2 * EDGE, LANES), jnp.bfloat16)
    no_tile = jnp.zeros((block + 2 * EDGE, block), jnp.bfloat16)
    volumes = [
        (codes, frames, v)
        for codes, frames in zip(code_refs, frame_refs)
        for v in range(frames.shape[0])
    ]
    many = len(volumes)
    per_tile = LANES // (2 * EDGE)
    lane = lax.broadcasted_iota(jnp.int32, (EDGE, LANES), 1) // (2 * EDGE)

    def tile(frames, v, at):
        lanes = pl.ds(pl.multiple_of(at * block, block), block)
        above = jnp.where(band > 0, frames[v, pl.ds(row_above, EDGE), lanes], zero)
        below = jnp.where(band < down - 1, frames[v, pl.ds(row_below, EDGE), lanes], zero)
        return jnp.concatenate([frames[v, pl.ds(row, block), lanes], below, above], axis=0)

    places = step_places(place_ref, step, across, own)[other * own : (other + 1) * own]
    start = places[0][1]
    tiles = []
    for _, frames, v in volumes:
        left = jnp.where(start > 0, tile(frames, v, jnp.maximum(start - 1, 0)), no_tile)
        right = jnp.where(
            start + own < across, tile(frames, v, jnp.minimum(start + own, across - 1)), no_tile
        )
        tiles.append([left] + [tile(frames, v, start + one) for one in range(own)] + [right])
    totals = []
    for one, (index, _) in enumerate(places):
        row_tiles, partials, edges = [], [], []
        firsts, lasts = [], []
        for order, (codes, _, v) in enumerate(volumes):
            row_code, col_code = codes[v, 0, index], codes[v, 1, index]
            left, middle, right = tiles[order][one : one + 3]
            sides = jnp.concatenate([right[:, : block // 2], left[:, block // 2 :]], axis=1)
            col_start = SHIFT - (col_code >> 4)
            cols = cols_ref[col_code & (SUB - 1), pl.ds(col_start, block + 2 * EDGE), :]
            cols = cols.astype(jnp.bfloat16)
            partial = jnp.dot(
                jnp.concatenate([middle, sides], axis=1),
                jnp.concatenate([cols[EDGE:], gap, cols[:EDGE]], axis=0),
                preferred_element_type=jnp.float32,
            ).astype(jnp.bfloat16)
            partials.append(partial[:block])
            edges.append(partial[block:])
            back = -row_code
            back_start = SHIFT + EDGE - (back >> 4)
            rows = cols_ref[back & (SUB - 1), pl.ds(back_start, block), :]
            row_tiles.append(rows.astype(jnp.bfloat16))
            row_start, step_at = SHIFT + (row_code >> 4), row_code & (SUB - 1)
            first = edges_ref[step_at, 0, pl.ds(row_start, EDGE), :]
            last = edges_ref[step_at, 1, pl.ds(row_start, EDGE), :]
            if order % per_tile:
                first = jnp.where(lane == order % per_tile, first, firsts.pop())
                last = jnp.where(lane == order % per_tile, last, lasts.pop())
            firsts.append(first)
            lasts.append(last)
        for first, last in zip(firsts, lasts):
            both = [first.astype(jnp.bfloat16), gap, last.astype(jnp.bfloat16)]
            row_tiles.append(jnp.concatenate(both, axis=0))
        deep = many * (block + 2 * EDGE)
        total = jnp.dot(
            jnp.concatenate(row_tiles, axis=1)[:, :deep],
            jnp.concatenate(partials + edges, axis=0),
            preferred_element_type=jnp.float32,
        )
        totals.append(total.astype(jnp.bfloat16))
    return totals


def warp_kernel(down, across, block, own, other, *refs):
    place_ref, *code_refs = refs[:3]
    frame_refs, band_refs, out_refs = refs[3:5], refs[5:7], refs[8:]
    depth = out_refs[0].shape[0] // own if other else len(out_refs)
    for step in range(depth):
        totals = warp_step(
            place_ref, step, other, code_refs, frame_refs, band_refs, down, across, block, own
        )
        for one, total in enumerate(totals):
            if other:
                out_refs[0][step * own + one] = total
            else:
                out_refs[step][one] = total


def warp_sums(
    place, codes, other_codes, frames, other_frames, bands, after, other, depth, block, own
):
    vols, rows, cols = frames.shape
    down, across = rows // block, cols // block
    smem = pl.BlockSpec(memory_space=pltpu.SMEM)
    vmem = pl.BlockSpec(memory_space=pltpu.VMEM)
    if other:
        out_shape = [jax.ShapeDtypeStruct((depth * own, block, block), jnp.bfloat16)]
    else:
        out_shape = [jax.ShapeDtypeStruct((own, block, block), jnp.bfloat16)] * depth
    return pl.pallas_call(
        functools.partial(warp_kernel, down, across, block, own, other),
        out_shape=out_shape,
        in_specs=[smem] * 3
        + [vmem] * (2 + len(bands))
        + [pl.BlockSpec(memory_space=pl.ANY)],
        out_specs=[vmem] * len(out_shape),
        compiler_params=pltpu.CompilerParams(vmem_limit_bytes=VMEM_LIMIT),
        cost_estimate=pl.CostEstimate(
            flops=2 * vols * rows * cols * block * 8,
            bytes_accessed=vols * rows * cols * 4 + rows * cols,
            transcendentals=0,
        ),
        name="warp",
    )(place, codes, other_codes, frames, other_frames, *bands, after)


def spectrum_kernel(vols, across, block, own, planes, depth, other, *refs):
    place_ref, codes_ref, other_codes_ref, row_ref, col_ref, lag_ref, span_ref = refs[:7]
    frames_ref, other_frames_ref, template_ref = refs[7:10]
    all_cross, all_sums = refs[-2:]
    if other:
        found_ref, out_refs, found = refs[10], refs[11:-3], refs[-3]
        found[...] = found_ref[...]
    else:
        found = refs[11]
        found[...] = jnp.zeros(found.shape, jnp.float32)

    row_table = row_ref[...]
    col_table = col_ref[...]
    lag_table = lag_ref[...]
    half = row_table.shape[0] // 2
    kept = -(-(block // 2 + 1) // 8) * 8
    span = lag_table.shape[0] // 2
    top = lax.broadcasted_iota(jnp.int32, (8, LANES), 0) == 0
    volumes = [(codes_ref, frames_ref, v) for v in range(vols)]
    volumes += [(other_codes_ref, other_frames_ref, v) for v in range(vols)]
    many = len(volumes)
    local = 2 * own
    no_rows = jnp.zeros((half - kept, LANES), jnp.float32)

    for half_step in range(depth // 2):
        cross, sums = all_cross.at[half_step], all_sums.at[half_step]
        places = []
        for step in (2 * half_step, 2 * half_step + 1):
            band = step_band(place_ref, step, across, own)
            band_rows = pl.ds(pl.multiple_of(band * block, block), block)
            chosen = step_places(place_ref, step, across, own)[other * own : (other + 1) * own]
            for one, (index, at) in enumerate(chosen):
                lanes = pl.ds(pl.multiple_of(at * block, block), block)
                places.append((index, band_rows, lanes, step * own + one))

        for pair in range(local // 2):
            pair_places = places[2 * pair : 2 * pair + 2]
            sources = [[template_ref[at] for _, _, _, at in pair_places]]
            for _, frames, v in volumes:
                sources.append([frames[v, rows, lanes] for _, rows, lanes, _ in pair_places])
            parts = []
            for source in sources:
                rows = jnp.dot(
                    row_table,
                    jnp.concatenate(source, axis=1),
                    preferred_element_type=jnp.float32,
                ).astype(jnp.bfloat16)
                for side in range(2):
                    lanes = slice(side * block, (side + 1) * block)
                    parts.append(jnp.concatenate([rows[:half, lanes], rows[half:, lanes]], axis=1))
            spectra = jnp.dot(
                jnp.concatenate(parts, axis=0), col_table, preferred_element_type=jnp.float32
            )
            temp = spectra[: 2 * half].astype(jnp.bfloat16).astype(jnp.float32)
            for order in range(many):
                for side in range(2):
                    one = (2 * pair + side) * many + order
                    base = (2 * (order + 1) + side) * half
                    total = jnp.zeros((8, LANES), jnp.float32)
                    for row in range(0, kept, 8):
                        at = side * half + row
                        temp_real = temp[at : at + 8, :block]
                        temp_imag = temp[at : at + 8, block:]
                        real = spectra[base + row : base + row + 8, :block]
                        imag = spectra[base + row : base + row + 8, block:]
                        cross_real = real * temp_real + imag * temp_imag
                        cross_imag = imag * temp_real - real * temp_imag
                        power = cross_real * cross_real + cross_imag * cross_imag
                        magnitude = power * lax.rsqrt(jnp.maximum(power, 1e-36))
                        cross[one, row : row + 8, :] = cross_real
                        cross[one, kept + row : kept + row + 8, :] = cross_imag
                        cross[one, 2 * kept + row : 2 * kept + row + 8, :] = magnitude
                        if row == 0:
                            total = jnp.where(top, magnitude, 2.0 * magnitude)
                        elif row == block // 2:
                            total += magnitude
                        else:
                            total += 2.0 * magnitude
                    sums[one] = jnp.sum(total, axis=0, keepdims=True)

        means = jnp.sum(sums[...], axis=2, keepdims=True) * (1.0 / (block * block)) + 1e-06
        lag_sums = []
        for pair in range(local // 2):
            for order in range(many):
                norms = []
                for side in range(2):
                    one = (2 * pair + side) * many + order
                    scale = pl.reciprocal(cross[one, 2 * kept :, :] + means[one], approx=True)
                    norms.append(
                        jnp.concatenate(
                            [
                                cross[one, :kept, :] * scale,
                                no_rows,
                                cross[one, kept : 2 * kept, :] * scale,
                                no_rows,
                            ],
                            axis=0,
                        ).astype(jnp.bfloat16)
                    )
                lag_rows = jnp.dot(
                    lag_table, jnp.concatenate(norms, axis=1), preferred_element_type=jnp.float32
                ).astype(jnp.bfloat16)
                for side in range(2):
                    lanes = slice(side * block, (side + 1) * block)
                    lag_sums.append(
                        jnp.concatenate([lag_rows[:span, lanes], lag_rows[span:, lanes]], axis=1)
                    )
        lags = jnp.dot(
            jnp.concatenate(lag_sums, axis=0), span_ref[...], preferred_element_type=jnp.float32
        )
        for pair in range(local // 2):
            for order, (codes, _, v) in enumerate(volumes):
                for side in range(2):
                    index = places[2 * pair + side][0]
                    row_shift = codes[v, 0, index] >> 4
                    col_shift = codes[v, 1, index] >> 4
                    at = (pair * many + order) * 2 + side
                    one = lags[at * span : (at + 1) * span]
                    one = pltpu.roll(one, span - SHIFT - row_shift, 0)[:WIN]
                    found[order, pl.ds(pl.multiple_of(index * WIN, WIN), WIN), :] = pltpu.roll(
                        one, LANES - SHIFT - col_shift, 1
                    )

    if not other:
        return

    keep_refs, give_ref = out_refs[:-1], out_refs[-1]
    share = found.shape[1] // WIN // planes
    per_tile = LANES // WIN
    lane = lax.broadcasted_iota(jnp.int32, (share, LANES), 1) // WIN
    for turn, keep_ref in enumerate(keep_refs):
        plane = place_ref[3] ^ turn
        for order in range(many):
            for tile in range(WIN // per_tile):
                total = jnp.zeros((share, LANES), jnp.float32)
                for part in range(per_tile):
                    start = plane * share * WIN + tile * per_tile + part
                    one = found[order, pl.ds(start, share, stride=WIN), :]
                    if part:
                        one = pltpu.roll(one, part * WIN, 1)
                    total = jnp.where(lane == part, one, total)
                lanes = slice(tile * LANES, (tile + 1) * LANES)
                total = total * (1.0 / block)
                if order < vols:
                    keep_ref[order, :, lanes] = total
                else:
                    give_ref[turn, order - vols, :, lanes] = total


def lag_windows(
    place, codes, other_codes, frames, other_frames, template, more, other, planes, depth, own
):
    vols, rows, cols = frames.shape
    block = template.shape[-1]
    down, across = rows // block, cols // block
    tables = dft_constants(block)
    kept = -(-(block // 2 + 1) // 8) * 8
    smem = pl.BlockSpec(memory_space=pltpu.SMEM)
    vmem = pl.BlockSpec(memory_space=pltpu.VMEM)
    blocks = down * across
    many = 2 * vols * 2 * own
    found = jax.ShapeDtypeStruct((2 * vols, blocks * WIN, LANES), jnp.float32)
    if other:
        out = (vols, blocks // planes, WIN * WIN)
        out_shape = [jax.ShapeDtypeStruct(out, jnp.float32)] * planes
        out_shape.append(jax.ShapeDtypeStruct((planes, *out), jnp.float32))
        scratch_shapes = [pltpu.VMEM(found.shape, found.dtype)]
        last = vmem
    else:
        out_shape = [found]
        scratch_shapes = []
        last = pl.BlockSpec(memory_space=pl.ANY)
    return pl.pallas_call(
        functools.partial(spectrum_kernel, vols, across, block, own, planes, depth, other),
        out_shape=out_shape,
        in_specs=[smem] * 3 + [vmem] * (len(tables) + 3) + [last],
        out_specs=[vmem] * len(out_shape),
        scratch_shapes=scratch_shapes
        + [
            pltpu.VMEM((depth // 2, many, 3 * kept, LANES), jnp.float32),
            pltpu.VMEM((depth // 2, many, 1, LANES), jnp.float32),
        ],
        compiler_params=pltpu.CompilerParams(vmem_limit_bytes=VMEM_LIMIT),
        cost_estimate=pl.CostEstimate(
            flops=2 * 3 * rows * cols * block * (2 if other else 8),
            bytes_accessed=vols * rows * cols * 4 + rows * cols,
            transcendentals=0,
        ),
        name="lag_windows",
    )(place, codes, other_codes, *tables, frames, other_frames, template, more)


def exchange(value, axes, size, turn):
    return lax.ppermute(value, axes, [(at, at ^ turn) for at in range(size)])


def on_device(frames, template, shift_codes):
    vol_dev, pl_dev, img_rows, img_cols = frames.shape
    own, block = template.shape[0], template.shape[-1]
    depth = lax.axis_size("z")
    planes = lax.axis_size("plane")
    place = jnp.stack([lax.axis_index(axis) for axis in ("z", "y", "core", "plane")])
    other_codes = exchange(shift_codes, "core", 2, 1)
    other_frames = exchange(frames, "core", 2, 1)
    staged, *bands, token = stage([frames, *tap_constants(block)], template)
    later, token = lax.optimization_barrier((template, token))
    pieces = [template]
    for turn in range(1, depth):
        pieces.append(exchange(later if turn == depth - 1 else template, "z", depth, turn))
    averages, correlation = [], 0.0
    volumes = vol_dev * depth * 4
    for p in range(pl_dev):
        work = (place, shift_codes, other_codes, staged[:, p], other_frames[:, p])
        sizes = (depth, block, own)
        (far_sums,) = warp_sums(*work, bands, token, 1, *sizes)
        taken = exchange(far_sums, "y", 2, 1)
        near_sums = warp_sums(*work, bands, far_sums, 0, *sizes)
        pieces, near_sums = lax.optimization_barrier((pieces, near_sums))
        near = jnp.concatenate([piece[:, p] for piece in pieces], axis=0)
        far = exchange(near, "y", 2, 1)
        sums = [
            one.astype(jnp.float32) + taken[step * own : (step + 1) * own].astype(jnp.float32)
            for step, one in enumerate(near_sums)
        ]
        moved = [
            exchange(sums[turn].astype(jnp.bfloat16), "z", depth, turn) for turn in range(1, depth)
        ]
        sizes = (planes, depth, own)
        (part,) = lag_windows(*work, near, near_sums[0], 0, *sizes)
        *keep, give = lag_windows(*work, far, part, 1, *sizes)
        keep, moved = lax.optimization_barrier((keep, moved))
        total = sum((one.astype(jnp.float32) for one in moved), sums[0])
        averages.append(total * (1.0 / volumes))
        got = exchange(give, "core", 2, 1)
        for turn, one in enumerate(keep):
            one = one + got[turn]
            correlation += exchange(one, "plane", planes, turn) if turn else one
    return (correlation, jnp.stack(averages, axis=1))


def solution(mesh):
    devices = mesh.devices.reshape(-1, 2, 2, mesh.shape["plane"])
    split = jax.sharding.Mesh(devices, ("z", "y", "core", "plane"))
    vols = ("z", "y", "core")
    in_specs = (P(vols, "plane", None, None), P(vols, "plane", None, None), P(vols, None, None))
    out_specs = (P(vols, "plane", None), P(vols, "plane", None, None))
    return jax.shard_map(
        on_device, mesh=split, in_specs=in_specs, out_specs=out_specs, check_vma=False
    )
```

```python
import functools
import math

import jax
import jax.numpy as jnp
import numpy as np
from jax import lax
from jax.experimental import pallas as pl
from jax.experimental.pallas import tpu as pltpu
from jax.sharding import PartitionSpec as P

SHIFT = 8
WIN = 16
TAPS = 8
SUB = 16
EDGE = 16
LANES = 128
VMEM_LIMIT = 24 * 1024 * 1024

full_turn = 2.0 * math.pi


def dft_constants(block_size):
    positions = np.arange(block_size)
    angles = full_turn * (np.outer(positions, positions) % block_size) / block_size
    cosine = np.cos(angles)
    sine = -np.sin(angles)
    half = block_size // 2 + 1
    rows = -(-half // 16) * 16
    row_table = np.zeros((2 * rows, block_size))
    row_table[:half] = cosine[:half]
    row_table[rows : rows + half] = sine[:half]
    col_table = np.block([[cosine, sine], [-sine, cosine]])
    weights = np.full((half,), 2.0)
    weights[0] = weights[half - 1] = 1.0
    span = 2 * SHIFT + WIN
    lags = np.arange(span) - SHIFT - WIN // 2
    turns = full_turn * (np.outer(lags, positions) % block_size) / block_size
    lag_cos, lag_sin = np.cos(turns), np.sin(turns)
    lag_table = np.zeros((2 * span, 2 * rows))
    lag_table[:span, :half] = lag_cos[:, :half] * weights
    lag_table[:span, rows : rows + half] = -lag_sin[:, :half] * weights
    lag_table[span:, :half] = lag_sin[:, :half] * weights
    lag_table[span:, rows : rows + half] = lag_cos[:, :half] * weights
    span_table = np.zeros((2 * block_size, LANES))
    span_table[:block_size, :span] = lag_cos.T
    span_table[block_size:, :span] = -lag_sin.T
    return tuple(
        jnp.asarray(table, jnp.bfloat16) for table in (row_table, col_table, lag_table, span_table)
    )


def tap_constants(block_size):
    offsets = np.arange(TAPS) - (TAPS // 2 - 1)
    spots = offsets[None, :] - np.arange(SUB)[:, None] / SUB
    raw_taps = np.sinc(spots) * np.sinc(spots / (TAPS // 2))
    taps = raw_taps / raw_taps.sum(axis=-1, keepdims=True)

    def band(inputs, outputs):
        at = inputs - outputs + TAPS // 2 - 1
        return np.where((at >= 0) & (at < TAPS), taps[:, np.clip(at, 0, TAPS - 1)], 0.0)

    lanes = np.arange(block_size)[None, :]
    inputs = np.arange(block_size + 3 * EDGE)[:, None] - EDGE - SHIFT
    outputs = np.arange(2 * EDGE)[:, None] - SHIFT
    spare = np.arange(LANES)[None, :] % (2 * EDGE)
    first = band(spare - 2 * EDGE, outputs) * (spare >= EDGE)
    last = band(spare + EDGE, outputs) * (spare < EDGE)
    tables = band(inputs, lanes), np.stack([first, last], axis=1)
    return [jnp.asarray(table, jnp.float32) for table in tables]


def step_places(place_ref, step, across, own):
    z = place_ref[0] ^ step
    places = []
    for other in range(2):
        for one in range(own):
            index = ((2 * z + (place_ref[1] ^ other)) * 2 + place_ref[2]) * own + one
            places.append((index, index % across))
    return places


def step_band(place_ref, step, across, own):
    return (place_ref[0] ^ step) * (4 * own) // across


def stage_kernel(count, *refs):
    sources, targets, sems = refs[:count], refs[count + 1 : 2 * count + 1], refs[-1]
    copies = [
        pltpu.make_async_copy(source, target, sems.at[at])
        for at, (source, target) in enumerate(zip(sources, targets))
    ]
    for copy in copies:
        copy.start()
    for copy in copies:
        copy.wait()


def stage(arrays, after):
    kept = [pltpu.with_memory_space_constraint(one, pltpu.HBM) for one in arrays]
    count = len(arrays)
    return pl.pallas_call(
        functools.partial(stage_kernel, count),
        out_shape=[jax.ShapeDtypeStruct(one.shape, one.dtype) for one in arrays],
        in_specs=[pl.BlockSpec(memory_space=pltpu.HBM)] * count
        + [pl.BlockSpec(memory_space=pl.ANY)],
        out_specs=[pl.BlockSpec(memory_space=pltpu.VMEM)] * count,
        scratch_shapes=[pltpu.SemaphoreType.DMA((count,))],
        compiler_params=pltpu.CompilerParams(vmem_limit_bytes=VMEM_LIMIT),
        cost_estimate=pl.CostEstimate(
            flops=0, bytes_accessed=2 * sum(one.nbytes for one in arrays), transcendentals=0
        ),
        name="stage",
    )(*kept, pltpu.with_memory_space_constraint(after, pltpu.HBM))


def warp_step(place_ref, step, other, code_refs, frame_refs, band_refs, down, across, block, own):
    cols_ref, edges_ref = band_refs
    band = step_band(place_ref, step, across, own)
    row = pl.multiple_of(band * block, block)
    row_above = pl.multiple_of(jnp.maximum(row - EDGE, 0), EDGE)
    row_below = pl.multiple_of(jnp.minimum(row + block, down * block - EDGE), EDGE)
    zero = jnp.zeros((EDGE, LANES), jnp.bfloat16)
    gap = jnp.zeros((block - 2 * EDGE, LANES), jnp.bfloat16)
    no_tile = jnp.zeros((block + 2 * EDGE, block), jnp.bfloat16)
    volumes = [
        (codes, frames, v)
        for codes, frames in zip(code_refs, frame_refs)
        for v in range(frames.shape[0])
    ]
    many = len(volumes)
    per_tile = LANES // (2 * EDGE)
    lane = lax.broadcasted_iota(jnp.int32, (EDGE, LANES), 1) // (2 * EDGE)

    def tile(frames, v, at):
        lanes = pl.ds(pl.multiple_of(at * block, block), block)
        above = jnp.where(band > 0, frames[v, pl.ds(row_above, EDGE), lanes], zero)
        below = jnp.where(band < down - 1, frames[v, pl.ds(row_below, EDGE), lanes], zero)
        return jnp.concatenate([frames[v, pl.ds(row, block), lanes], below, above], axis=0)

    places = step_places(place_ref, step, across, own)[other * own : (other + 1) * own]
    start = places[0][1]
    tiles = []
    for _, frames, v in volumes:
        left = jnp.where(start > 0, tile(frames, v, jnp.maximum(start - 1, 0)), no_tile)
        right = jnp.where(
            start + own < across, tile(frames, v, jnp.minimum(start + own, across - 1)), no_tile
        )
        tiles.append([left] + [tile(frames, v, start + one) for one in range(own)] + [right])
    totals = []
    for one, (index, _) in enumerate(places):
        row_tiles, partials, edges = [], [], []
        firsts, lasts = [], []
        for order, (codes, _, v) in enumerate(volumes):
            row_code, col_code = codes[v, 0, index], codes[v, 1, index]
            left, middle, right = tiles[order][one : one + 3]
            sides = jnp.concatenate([right[:, : block // 2], left[:, block // 2 :]], axis=1)
            col_start = SHIFT - (col_code >> 4)
            cols = cols_ref[col_code & (SUB - 1), pl.ds(col_start, block + 2 * EDGE), :]
            cols = cols.astype(jnp.bfloat16)
            partial = jnp.dot(
                jnp.concatenate([middle, sides], axis=1),
                jnp.concatenate([cols[EDGE:], gap, cols[:EDGE]], axis=0),
                preferred_element_type=jnp.float32,
            ).astype(jnp.bfloat16)
            partials.append(partial[:block])
            edges.append(partial[block:])
            back = -row_code
            back_start = SHIFT + EDGE - (back >> 4)
            rows = cols_ref[back & (SUB - 1), pl.ds(back_start, block), :]
            row_tiles.append(rows.astype(jnp.bfloat16))
            row_start, step_at = SHIFT + (row_code >> 4), row_code & (SUB - 1)
            first = edges_ref[step_at, 0, pl.ds(row_start, EDGE), :]
            last = edges_ref[step_at, 1, pl.ds(row_start, EDGE), :]
            if order % per_tile:
                first = jnp.where(lane == order % per_tile, first, firsts.pop())
                last = jnp.where(lane == order % per_tile, last, lasts.pop())
            firsts.append(first)
            lasts.append(last)
        for first, last in zip(firsts, lasts):
            both = [first.astype(jnp.bfloat16), gap, last.astype(jnp.bfloat16)]
            row_tiles.append(jnp.concatenate(both, axis=0))
        deep = many * (block + 2 * EDGE)
        total = jnp.dot(
            jnp.concatenate(row_tiles, axis=1)[:, :deep],
            jnp.concatenate(partials + edges, axis=0),
            preferred_element_type=jnp.float32,
        )
        totals.append(total.astype(jnp.bfloat16))
    return totals


def warp_kernel(down, across, block, own, other, *refs):
    place_ref, *code_refs = refs[:3]
    frame_refs, band_refs, out_refs = refs[3:5], refs[5:7], refs[8:]
    depth = out_refs[0].shape[0] // own if other else len(out_refs)
    for step in range(depth):
        totals = warp_step(
            place_ref, step, other, code_refs, frame_refs, band_refs, down, across, block, own
        )
        for one, total in enumerate(totals):
            if other:
                out_refs[0][step * own + one] = total
            else:
                out_refs[step][one] = total


def warp_sums(
    place, codes, other_codes, frames, other_frames, bands, after, other, depth, block, own
):
    vols, rows, cols = frames.shape
    down, across = rows // block, cols // block
    smem = pl.BlockSpec(memory_space=pltpu.SMEM)
    vmem = pl.BlockSpec(memory_space=pltpu.VMEM)
    if other:
        out_shape = [jax.ShapeDtypeStruct((depth * own, block, block), jnp.bfloat16)]
    else:
        out_shape = [jax.ShapeDtypeStruct((own, block, block), jnp.bfloat16)] * depth
    return pl.pallas_call(
        functools.partial(warp_kernel, down, across, block, own, other),
        out_shape=out_shape,
        in_specs=[smem] * 3
        + [vmem] * (2 + len(bands))
        + [pl.BlockSpec(memory_space=pl.ANY)],
        out_specs=[vmem] * len(out_shape),
        compiler_params=pltpu.CompilerParams(vmem_limit_bytes=VMEM_LIMIT),
        cost_estimate=pl.CostEstimate(
            flops=2 * vols * rows * cols * block * 8,
            bytes_accessed=vols * rows * cols * 4 + rows * cols,
            transcendentals=0,
        ),
        name="warp",
    )(place, codes, other_codes, frames, other_frames, *bands, after)


def spectrum_kernel(vols, across, block, own, planes, depth, other, *refs):
    place_ref, codes_ref, other_codes_ref, row_ref, col_ref, lag_ref, span_ref = refs[:7]
    frames_ref, other_frames_ref, template_ref = refs[7:10]
    all_cross, all_sums = refs[-2:]
    if other:
        found_ref, out_refs, found = refs[10], refs[11:-3], refs[-3]
        found[...] = found_ref[...]
    else:
        found = refs[11]
        found[...] = jnp.zeros(found.shape, jnp.float32)

    row_table = row_ref[...]
    col_table = col_ref[...]
    lag_table = lag_ref[...]
    half = row_table.shape[0] // 2
    kept = -(-(block // 2 + 1) // 8) * 8
    span = lag_table.shape[0] // 2
    top = lax.broadcasted_iota(jnp.int32, (8, LANES), 0) == 0
    volumes = [(codes_ref, frames_ref, v) for v in range(vols)]
    volumes += [(other_codes_ref, other_frames_ref, v) for v in range(vols)]
    many = len(volumes)
    local = 2 * own
    no_rows = jnp.zeros((half - kept, LANES), jnp.float32)

    for half_step in range(depth // 2):
        cross, sums = all_cross.at[half_step], all_sums.at[half_step]
        places = []
        for step in (2 * half_step, 2 * half_step + 1):
            band = step_band(place_ref, step, across, own)
            band_rows = pl.ds(pl.multiple_of(band * block, block), block)
            chosen = step_places(place_ref, step, across, own)[other * own : (other + 1) * own]
            for one, (index, at) in enumerate(chosen):
                lanes = pl.ds(pl.multiple_of(at * block, block), block)
                places.append((index, band_rows, lanes, step * own + one))

        for pair in range(local // 2):
            pair_places = places[2 * pair : 2 * pair + 2]
            sources = [[template_ref[at] for _, _, _, at in pair_places]]
            for _, frames, v in volumes:
                sources.append([frames[v, rows, lanes] for _, rows, lanes, _ in pair_places])
            parts = []
            for source in sources:
                rows = jnp.dot(
                    row_table,
                    jnp.concatenate(source, axis=1),
                    preferred_element_type=jnp.float32,
                ).astype(jnp.bfloat16)
                for side in range(2):
                    lanes = slice(side * block, (side + 1) * block)
                    parts.append(jnp.concatenate([rows[:half, lanes], rows[half:, lanes]], axis=1))
            spectra = jnp.dot(
                jnp.concatenate(parts, axis=0), col_table, preferred_element_type=jnp.float32
            )
            temp = spectra[: 2 * half].astype(jnp.bfloat16).astype(jnp.float32)
            for order in range(many):
                for side in range(2):
                    one = (2 * pair + side) * many + order
                    base = (2 * (order + 1) + side) * half
                    total = jnp.zeros((8, LANES), jnp.float32)
                    for row in range(0, kept, 8):
                        at = side * half + row
                        temp_real = temp[at : at + 8, :block]
                        temp_imag = temp[at : at + 8, block:]
                        real = spectra[base + row : base + row + 8, :block]
                        imag = spectra[base + row : base + row + 8, block:]
                        cross_real = real * temp_real + imag * temp_imag
                        cross_imag = imag * temp_real - real * temp_imag
                        power = cross_real * cross_real + cross_imag * cross_imag
                        magnitude = power * lax.rsqrt(jnp.maximum(power, 1e-36))
                        cross[one, row : row + 8, :] = cross_real
                        cross[one, kept + row : kept + row + 8, :] = cross_imag
                        cross[one, 2 * kept + row : 2 * kept + row + 8, :] = magnitude
                        if row == 0:
                            total = jnp.where(top, magnitude, 2.0 * magnitude)
                        elif row == block // 2:
                            total += magnitude
                        else:
                            total += 2.0 * magnitude
                    sums[one] = jnp.sum(total, axis=0, keepdims=True)

        means = jnp.sum(sums[...], axis=2, keepdims=True) * (1.0 / (block * block)) + 1e-06
        lag_sums = []
        for pair in range(local // 2):
            for order in range(many):
                norms = []
                for side in range(2):
                    one = (2 * pair + side) * many + order
                    scale = pl.reciprocal(cross[one, 2 * kept :, :] + means[one], approx=True)
                    norms.append(
                        jnp.concatenate(
                            [
                                cross[one, :kept, :] * scale,
                                no_rows,
                                cross[one, kept : 2 * kept, :] * scale,
                                no_rows,
                            ],
                            axis=0,
                        ).astype(jnp.bfloat16)
                    )
                lag_rows = jnp.dot(
                    lag_table, jnp.concatenate(norms, axis=1), preferred_element_type=jnp.float32
                ).astype(jnp.bfloat16)
                for side in range(2):
                    lanes = slice(side * block, (side + 1) * block)
                    lag_sums.append(
                        jnp.concatenate([lag_rows[:span, lanes], lag_rows[span:, lanes]], axis=1)
                    )
        lags = jnp.dot(
            jnp.concatenate(lag_sums, axis=0), span_ref[...], preferred_element_type=jnp.float32
        )
        for pair in range(local // 2):
            for order, (codes, _, v) in enumerate(volumes):
                for side in range(2):
                    index = places[2 * pair + side][0]
                    row_shift = codes[v, 0, index] >> 4
                    col_shift = codes[v, 1, index] >> 4
                    at = (pair * many + order) * 2 + side
                    one = lags[at * span : (at + 1) * span]
                    one = pltpu.roll(one, span - SHIFT - row_shift, 0)[:WIN]
                    found[order, pl.ds(pl.multiple_of(index * WIN, WIN), WIN), :] = pltpu.roll(
                        one, LANES - SHIFT - col_shift, 1
                    )

    if not other:
        return

    keep_refs, give_ref = out_refs[:-1], out_refs[-1]
    share = found.shape[1] // WIN // planes
    per_tile = LANES // WIN
    lane = lax.broadcasted_iota(jnp.int32, (share, LANES), 1) // WIN
    for turn, keep_ref in enumerate(keep_refs):
        plane = place_ref[3] ^ turn
        for order in range(many):
            for tile in range(WIN // per_tile):
                total = jnp.zeros((share, LANES), jnp.float32)
                for part in range(per_tile):
                    start = plane * share * WIN + tile * per_tile + part
                    one = found[order, pl.ds(start, share, stride=WIN), :]
                    if part:
                        one = pltpu.roll(one, part * WIN, 1)
                    total = jnp.where(lane == part, one, total)
                lanes = slice(tile * LANES, (tile + 1) * LANES)
                total = total * (1.0 / block)
                if order < vols:
                    keep_ref[order, :, lanes] = total
                else:
                    give_ref[turn, order - vols, :, lanes] = total


def lag_windows(
    place, codes, other_codes, frames, other_frames, template, more, other, planes, depth, own
):
    vols, rows, cols = frames.shape
    block = template.shape[-1]
    down, across = rows // block, cols // block
    tables = dft_constants(block)
    kept = -(-(block // 2 + 1) // 8) * 8
    smem = pl.BlockSpec(memory_space=pltpu.SMEM)
    vmem = pl.BlockSpec(memory_space=pltpu.VMEM)
    blocks = down * across
    many = 2 * vols * 2 * own
    found = jax.ShapeDtypeStruct((2 * vols, blocks * WIN, LANES), jnp.float32)
    if other:
        out = (vols, blocks // planes, WIN * WIN)
        out_shape = [jax.ShapeDtypeStruct(out, jnp.float32)] * planes
        out_shape.append(jax.ShapeDtypeStruct((planes, *out), jnp.float32))
        scratch_shapes = [pltpu.VMEM(found.shape, found.dtype)]
        last = vmem
    else:
        out_shape = [found]
        scratch_shapes = []
        last = pl.BlockSpec(memory_space=pl.ANY)
    return pl.pallas_call(
        functools.partial(spectrum_kernel, vols, across, block, own, planes, depth, other),
        out_shape=out_shape,
        in_specs=[smem] * 3 + [vmem] * (len(tables) + 3) + [last],
        out_specs=[vmem] * len(out_shape),
        scratch_shapes=scratch_shapes
        + [
            pltpu.VMEM((depth // 2, many, 3 * kept, LANES), jnp.float32),
            pltpu.VMEM((depth // 2, many, 1, LANES), jnp.float32),
        ],
        compiler_params=pltpu.CompilerParams(vmem_limit_bytes=VMEM_LIMIT),
        cost_estimate=pl.CostEstimate(
            flops=2 * 3 * rows * cols * block * (2 if other else 8),
            bytes_accessed=vols * rows * cols * 4 + rows * cols,
            transcendentals=0,
        ),
        name="lag_windows",
    )(place, codes, other_codes, *tables, frames, other_frames, template, more)


def exchange(value, axes, size, turn):
    return lax.ppermute(value, axes, [(at, at ^ turn) for at in range(size)])


def on_device(frames, template, shift_codes):
    vol_dev, pl_dev, img_rows, img_cols = frames.shape
    own, block = template.shape[0], template.shape[-1]
    depth = lax.axis_size("z")
    planes = lax.axis_size("plane")
    place = jnp.stack([lax.axis_index(axis) for axis in ("z", "y", "core", "plane")])
    other_codes = exchange(shift_codes, "core", 2, 1)
    other_frames = exchange(frames, "core", 2, 1)
    staged, *bands = stage([frames, *tap_constants(block)], template)
    pieces = [template] + [exchange(template, "z", depth, turn) for turn in range(1, depth)]
    averages, correlation = [], 0.0
    volumes = vol_dev * depth * 4
    for p in range(pl_dev):
        work = (place, shift_codes, other_codes, staged[:, p], other_frames[:, p])
        sizes = (depth, block, own)
        (far_sums,) = warp_sums(*work, bands, template, 1, *sizes)
        taken = exchange(far_sums, "y", 2, 1)
        near_sums = warp_sums(*work, bands, far_sums, 0, *sizes)
        pieces, near_sums = lax.optimization_barrier((pieces, near_sums))
        near = jnp.concatenate([piece[:, p] for piece in pieces], axis=0)
        far = exchange(near, "y", 2, 1)
        sums = [
            one.astype(jnp.float32) + taken[step * own : (step + 1) * own].astype(jnp.float32)
            for step, one in enumerate(near_sums)
        ]
        moved = [
            exchange(sums[turn].astype(jnp.bfloat16), "z", depth, turn) for turn in range(1, depth)
        ]
        sizes = (planes, depth, own)
        (part,) = lag_windows(*work, near, near_sums[0], 0, *sizes)
        *keep, give = lag_windows(*work, far, part, 1, *sizes)
        keep, moved = lax.optimization_barrier((keep, moved))
        total = sum((one.astype(jnp.float32) for one in moved), sums[0])
        averages.append(total * (1.0 / volumes))
        got = exchange(give, "core", 2, 1)
        for turn, one in enumerate(keep):
            one = one + got[turn]
            correlation += exchange(one, "plane", planes, turn) if turn else one
    return (correlation, jnp.stack(averages, axis=1))


def solution(mesh):
    devices = mesh.devices.reshape(-1, 2, 2, mesh.shape["plane"])
    split = jax.sharding.Mesh(devices, ("z", "y", "core", "plane"))
    vols = ("z", "y", "core")
    in_specs = (P(vols, "plane", None, None), P(vols, "plane", None, None), P(vols, None, None))
    out_specs = (P(vols, "plane", None), P(vols, "plane", None, None))
    return jax.shard_map(
        on_device, mesh=split, in_specs=in_specs, out_specs=out_specs, check_vma=False
    )
```

```python
import functools
import math

import jax
import jax.numpy as jnp
import numpy as np
from jax import lax
from jax.experimental import pallas as pl
from jax.experimental.pallas import tpu as pltpu
from jax.sharding import PartitionSpec as P

SHIFT = 8
WIN = 16
TAPS = 8
SUB = 16
EDGE = 16
LANES = 128
VMEM_LIMIT = 24 * 1024 * 1024

full_turn = 2.0 * math.pi


def dft_constants(block_size):
    positions = np.arange(block_size)
    angles = full_turn * (np.outer(positions, positions) % block_size) / block_size
    cosine = np.cos(angles)
    sine = -np.sin(angles)
    half = block_size // 2 + 1
    rows = -(-half // 16) * 16
    row_table = np.zeros((2 * rows, block_size))
    row_table[:half] = cosine[:half]
    row_table[rows : rows + half] = sine[:half]
    col_table = np.block([[cosine, sine], [-sine, cosine]])
    weights = np.full((half,), 2.0)
    weights[0] = weights[half - 1] = 1.0
    span = 2 * SHIFT + WIN
    lags = np.arange(span) - SHIFT - WIN // 2
    turns = full_turn * (np.outer(lags, positions) % block_size) / block_size
    lag_cos, lag_sin = np.cos(turns), np.sin(turns)
    lag_table = np.zeros((2 * span, 2 * rows))
    lag_table[:span, :half] = lag_cos[:, :half] * weights
    lag_table[:span, rows : rows + half] = -lag_sin[:, :half] * weights
    lag_table[span:, :half] = lag_sin[:, :half] * weights
    lag_table[span:, rows : rows + half] = lag_cos[:, :half] * weights
    span_table = np.zeros((2 * block_size, LANES))
    span_table[:block_size, :span] = lag_cos.T
    span_table[block_size:, :span] = -lag_sin.T
    return tuple(
        jnp.asarray(table, jnp.bfloat16) for table in (row_table, col_table, lag_table, span_table)
    )


def tap_constants(block_size):
    offsets = np.arange(TAPS) - (TAPS // 2 - 1)
    spots = offsets[None, :] - np.arange(SUB)[:, None] / SUB
    raw_taps = np.sinc(spots) * np.sinc(spots / (TAPS // 2))
    taps = raw_taps / raw_taps.sum(axis=-1, keepdims=True)

    def band(inputs, outputs):
        at = inputs - outputs + TAPS // 2 - 1
        return np.where((at >= 0) & (at < TAPS), taps[:, np.clip(at, 0, TAPS - 1)], 0.0)

    lanes = np.arange(block_size)[None, :]
    inputs = np.arange(block_size + 3 * EDGE)[:, None] - EDGE - SHIFT
    outputs = np.arange(2 * EDGE)[:, None] - SHIFT
    spare = np.arange(LANES)[None, :] % (2 * EDGE)
    first = band(spare - 2 * EDGE, outputs) * (spare >= EDGE)
    last = band(spare + EDGE, outputs) * (spare < EDGE)
    tables = band(inputs, lanes), np.stack([first, last], axis=1)
    return [jnp.asarray(table, jnp.float32) for table in tables]


def step_places(place_ref, step, across, own):
    z = place_ref[0] ^ step
    places = []
    for other in range(2):
        for one in range(own):
            index = ((2 * z + (place_ref[1] ^ other)) * 2 + place_ref[2]) * own + one
            places.append((index, index % across))
    return places


def step_band(place_ref, step, across, own):
    return (place_ref[0] ^ step) * (4 * own) // across


def stage_kernel(count, *refs):
    sources, targets, sems = refs[:count], refs[count + 1 : 2 * count + 1], refs[-1]
    copies = [
        pltpu.make_async_copy(source, target, sems.at[at])
        for at, (source, target) in enumerate(zip(sources, targets))
    ]
    for copy in copies:
        copy.start()
    for copy in copies:
        copy.wait()


def stage(arrays, after):
    kept = [pltpu.with_memory_space_constraint(one, pltpu.HBM) for one in arrays]
    count = len(arrays)
    return pl.pallas_call(
        functools.partial(stage_kernel, count),
        out_shape=[jax.ShapeDtypeStruct(one.shape, one.dtype) for one in arrays],
        in_specs=[pl.BlockSpec(memory_space=pltpu.HBM)] * count
        + [pl.BlockSpec(memory_space=pl.ANY)],
        out_specs=[pl.BlockSpec(memory_space=pltpu.VMEM)] * count,
        scratch_shapes=[pltpu.SemaphoreType.DMA((count,))],
        compiler_params=pltpu.CompilerParams(vmem_limit_bytes=VMEM_LIMIT),
        cost_estimate=pl.CostEstimate(
            flops=0, bytes_accessed=2 * sum(one.nbytes for one in arrays), transcendentals=0
        ),
        name="stage",
    )(*kept, pltpu.with_memory_space_constraint(after, pltpu.HBM))


def warp_step(place_ref, step, other, code_refs, frame_refs, band_refs, down, across, block, own):
    cols_ref, edges_ref = band_refs
    band = step_band(place_ref, step, across, own)
    row = pl.multiple_of(band * block, block)
    row_above = pl.multiple_of(jnp.maximum(row - EDGE, 0), EDGE)
    row_below = pl.multiple_of(jnp.minimum(row + block, down * block - EDGE), EDGE)
    zero = jnp.zeros((EDGE, LANES), jnp.bfloat16)
    gap = jnp.zeros((block - 2 * EDGE, LANES), jnp.bfloat16)
    no_tile = jnp.zeros((block + 2 * EDGE, block), jnp.bfloat16)
    volumes = [
        (codes, frames, v)
        for codes, frames in zip(code_refs, frame_refs)
        for v in range(frames.shape[0])
    ]
    many = len(volumes)
    per_tile = LANES // (2 * EDGE)
    lane = lax.broadcasted_iota(jnp.int32, (EDGE, LANES), 1) // (2 * EDGE)

    def tile(frames, v, at):
        lanes = pl.ds(pl.multiple_of(at * block, block), block)
        above = jnp.where(band > 0, frames[v, pl.ds(row_above, EDGE), lanes], zero)
        below = jnp.where(band < down - 1, frames[v, pl.ds(row_below, EDGE), lanes], zero)
        return jnp.concatenate([frames[v, pl.ds(row, block), lanes], below, above], axis=0)

    places = step_places(place_ref, step, across, own)[other * own : (other + 1) * own]
    start = places[0][1]
    tiles = []
    for _, frames, v in volumes:
        left = jnp.where(start > 0, tile(frames, v, jnp.maximum(start - 1, 0)), no_tile)
        right = jnp.where(
            start + own < across, tile(frames, v, jnp.minimum(start + own, across - 1)), no_tile
        )
        tiles.append([left] + [tile(frames, v, start + one) for one in range(own)] + [right])
    totals = []
    for one, (index, _) in enumerate(places):
        row_tiles, partials, edges = [], [], []
        firsts, lasts = [], []
        for order, (codes, _, v) in enumerate(volumes):
            row_code, col_code = codes[v, 0, index], codes[v, 1, index]
            left, middle, right = tiles[order][one : one + 3]
            sides = jnp.concatenate([right[:, : block // 2], left[:, block // 2 :]], axis=1)
            col_start = SHIFT - (col_code >> 4)
            cols = cols_ref[col_code & (SUB - 1), pl.ds(col_start, block + 2 * EDGE), :]
            cols = cols.astype(jnp.bfloat16)
            partial = jnp.dot(
                jnp.concatenate([middle, sides], axis=1),
                jnp.concatenate([cols[EDGE:], gap, cols[:EDGE]], axis=0),
                preferred_element_type=jnp.float32,
            ).astype(jnp.bfloat16)
            partials.append(partial[:block])
            edges.append(partial[block:])
            back = -row_code
            back_start = SHIFT + EDGE - (back >> 4)
            rows = cols_ref[back & (SUB - 1), pl.ds(back_start, block), :]
            row_tiles.append(rows.astype(jnp.bfloat16))
            row_start, step_at = SHIFT + (row_code >> 4), row_code & (SUB - 1)
            first = edges_ref[step_at, 0, pl.ds(row_start, EDGE), :]
            last = edges_ref[step_at, 1, pl.ds(row_start, EDGE), :]
            if order % per_tile:
                first = jnp.where(lane == order % per_tile, first, firsts.pop())
                last = jnp.where(lane == order % per_tile, last, lasts.pop())
            firsts.append(first)
            lasts.append(last)
        for first, last in zip(firsts, lasts):
            both = [first.astype(jnp.bfloat16), gap, last.astype(jnp.bfloat16)]
            row_tiles.append(jnp.concatenate(both, axis=0))
        deep = many * (block + 2 * EDGE)
        total = jnp.dot(
            jnp.concatenate(row_tiles, axis=1)[:, :deep],
            jnp.concatenate(partials + edges, axis=0),
            preferred_element_type=jnp.float32,
        )
        totals.append(total.astype(jnp.bfloat16))
    return totals


def warp_kernel(down, across, block, own, other, *refs):
    place_ref, *code_refs = refs[:3]
    frame_refs, band_refs, out_refs = refs[3:5], refs[5:7], refs[8:]
    depth = out_refs[0].shape[0] // own if other else len(out_refs)
    for step in range(depth):
        totals = warp_step(
            place_ref, step, other, code_refs, frame_refs, band_refs, down, across, block, own
        )
        for one, total in enumerate(totals):
            if other:
                out_refs[0][step * own + one] = total
            else:
                out_refs[step][one] = total


def warp_sums(
    place, codes, other_codes, frames, other_frames, bands, after, other, depth, block, own
):
    vols, rows, cols = frames.shape
    down, across = rows // block, cols // block
    smem = pl.BlockSpec(memory_space=pltpu.SMEM)
    vmem = pl.BlockSpec(memory_space=pltpu.VMEM)
    if other:
        out_shape = [jax.ShapeDtypeStruct((depth * own, block, block), jnp.bfloat16)]
    else:
        out_shape = [jax.ShapeDtypeStruct((own, block, block), jnp.bfloat16)] * depth
    return pl.pallas_call(
        functools.partial(warp_kernel, down, across, block, own, other),
        out_shape=out_shape,
        in_specs=[smem] * 3
        + [vmem] * (2 + len(bands))
        + [pl.BlockSpec(memory_space=pl.ANY)],
        out_specs=[vmem] * len(out_shape),
        compiler_params=pltpu.CompilerParams(vmem_limit_bytes=VMEM_LIMIT),
        cost_estimate=pl.CostEstimate(
            flops=2 * vols * rows * cols * block * 8,
            bytes_accessed=vols * rows * cols * 4 + rows * cols,
            transcendentals=0,
        ),
        name="warp",
    )(place, codes, other_codes, frames, other_frames, *bands, after)


def spectrum_kernel(vols, across, block, own, planes, depth, other, *refs):
    place_ref, codes_ref, other_codes_ref, row_ref, col_ref, lag_ref, span_ref = refs[:7]
    frames_ref, other_frames_ref, template_ref = refs[7:10]
    all_cross, all_sums = refs[-2:]
    if other:
        found_ref, out_refs, found = refs[10], refs[11:-3], refs[-3]
        found[...] = found_ref[...]
    else:
        found = refs[11]
        found[...] = jnp.zeros(found.shape, jnp.float32)

    row_table = row_ref[...]
    col_table = col_ref[...]
    lag_table = lag_ref[...]
    half = row_table.shape[0] // 2
    kept = -(-(block // 2 + 1) // 8) * 8
    span = lag_table.shape[0] // 2
    top = lax.broadcasted_iota(jnp.int32, (8, LANES), 0) == 0
    volumes = [(codes_ref, frames_ref, v) for v in range(vols)]
    volumes += [(other_codes_ref, other_frames_ref, v) for v in range(vols)]
    many = len(volumes)
    local = 2 * own
    no_rows = jnp.zeros((half - kept, LANES), jnp.float32)

    for half_step in range(depth // 2):
        cross, sums = all_cross.at[half_step], all_sums.at[half_step]
        places = []
        for step in (2 * half_step, 2 * half_step + 1):
            band = step_band(place_ref, step, across, own)
            band_rows = pl.ds(pl.multiple_of(band * block, block), block)
            chosen = step_places(place_ref, step, across, own)[other * own : (other + 1) * own]
            for one, (index, at) in enumerate(chosen):
                lanes = pl.ds(pl.multiple_of(at * block, block), block)
                places.append((index, band_rows, lanes, step * own + one))

        for pair in range(local // 2):
            pair_places = places[2 * pair : 2 * pair + 2]
            sources = [[template_ref[at] for _, _, _, at in pair_places]]
            for _, frames, v in volumes:
                sources.append([frames[v, rows, lanes] for _, rows, lanes, _ in pair_places])
            parts = []
            for source in sources:
                rows = jnp.dot(
                    row_table,
                    jnp.concatenate(source, axis=1),
                    preferred_element_type=jnp.float32,
                ).astype(jnp.bfloat16)
                for side in range(2):
                    lanes = slice(side * block, (side + 1) * block)
                    parts.append(jnp.concatenate([rows[:half, lanes], rows[half:, lanes]], axis=1))
            spectra = jnp.dot(
                jnp.concatenate(parts, axis=0), col_table, preferred_element_type=jnp.float32
            )
            temp = spectra[: 2 * half].astype(jnp.bfloat16).astype(jnp.float32)
            for order in range(many):
                for side in range(2):
                    one = (2 * pair + side) * many + order
                    base = (2 * (order + 1) + side) * half
                    total = jnp.zeros((8, LANES), jnp.float32)
                    for row in range(0, kept, 8):
                        at = side * half + row
                        temp_real = temp[at : at + 8, :block]
                        temp_imag = temp[at : at + 8, block:]
                        real = spectra[base + row : base + row + 8, :block]
                        imag = spectra[base + row : base + row + 8, block:]
                        cross_real = real * temp_real + imag * temp_imag
                        cross_imag = imag * temp_real - real * temp_imag
                        power = cross_real * cross_real + cross_imag * cross_imag
                        magnitude = power * lax.rsqrt(jnp.maximum(power, 1e-36))
                        cross[one, row : row + 8, :] = cross_real
                        cross[one, kept + row : kept + row + 8, :] = cross_imag
                        cross[one, 2 * kept + row : 2 * kept + row + 8, :] = magnitude
                        if row == 0:
                            total = jnp.where(top, magnitude, 2.0 * magnitude)
                        elif row == block // 2:
                            total += magnitude
                        else:
                            total += 2.0 * magnitude
                    sums[one] = jnp.sum(total, axis=0, keepdims=True)

        means = jnp.sum(sums[...], axis=2, keepdims=True) * (1.0 / (block * block)) + 1e-06
        lag_sums = []
        for pair in range(local // 2):
            for order in range(many):
                norms = []
                for side in range(2):
                    one = (2 * pair + side) * many + order
                    scale = pl.reciprocal(cross[one, 2 * kept :, :] + means[one], approx=True)
                    norms.append(
                        jnp.concatenate(
                            [
                                cross[one, :kept, :] * scale,
                                no_rows,
                                cross[one, kept : 2 * kept, :] * scale,
                                no_rows,
                            ],
                            axis=0,
                        ).astype(jnp.bfloat16)
                    )
                lag_rows = jnp.dot(
                    lag_table, jnp.concatenate(norms, axis=1), preferred_element_type=jnp.float32
                ).astype(jnp.bfloat16)
                for side in range(2):
                    lanes = slice(side * block, (side + 1) * block)
                    lag_sums.append(
                        jnp.concatenate([lag_rows[:span, lanes], lag_rows[span:, lanes]], axis=1)
                    )
        lags = jnp.dot(
            jnp.concatenate(lag_sums, axis=0), span_ref[...], preferred_element_type=jnp.float32
        )
        for pair in range(local // 2):
            for order, (codes, _, v) in enumerate(volumes):
                for side in range(2):
                    index = places[2 * pair + side][0]
                    row_shift = codes[v, 0, index] >> 4
                    col_shift = codes[v, 1, index] >> 4
                    at = (pair * many + order) * 2 + side
                    one = lags[at * span : (at + 1) * span]
                    one = pltpu.roll(one, span - SHIFT - row_shift, 0)[:WIN]
                    found[order, pl.ds(pl.multiple_of(index * WIN, WIN), WIN), :] = pltpu.roll(
                        one, LANES - SHIFT - col_shift, 1
                    )

    if not other:
        return

    share = found.shape[1] // WIN // planes
    per_tile = LANES // WIN
    lane = lax.broadcasted_iota(jnp.int32, (share, LANES), 1) // WIN
    for turn, out_ref in enumerate(out_refs):
        plane = place_ref[3] ^ turn
        for order in range(many):
            for tile in range(WIN // per_tile):
                total = jnp.zeros((share, LANES), jnp.float32)
                for part in range(per_tile):
                    start = plane * share * WIN + tile * per_tile + part
                    one = found[order, pl.ds(start, share, stride=WIN), :]
                    if part:
                        one = pltpu.roll(one, part * WIN, 1)
                    total = jnp.where(lane == part, one, total)
                lanes = slice(tile * LANES, (tile + 1) * LANES)
                out_ref[order // vols, order % vols, :, lanes] = total * (1.0 / block)


def lag_windows(
    place, codes, other_codes, frames, other_frames, template, more, other, planes, depth, own
):
    vols, rows, cols = frames.shape
    block = template.shape[-1]
    down, across = rows // block, cols // block
    tables = dft_constants(block)
    kept = -(-(block // 2 + 1) // 8) * 8
    smem = pl.BlockSpec(memory_space=pltpu.SMEM)
    vmem = pl.BlockSpec(memory_space=pltpu.VMEM)
    blocks = down * across
    many = 2 * vols * 2 * own
    found = jax.ShapeDtypeStruct((2 * vols, blocks * WIN, LANES), jnp.float32)
    if other:
        out = (2, vols, blocks // planes, WIN * WIN)
        out_shape = [jax.ShapeDtypeStruct(out, jnp.float32)] * planes
        scratch_shapes = [pltpu.VMEM(found.shape, found.dtype)]
        last = vmem
    else:
        out_shape = [found]
        scratch_shapes = []
        last = pl.BlockSpec(memory_space=pl.ANY)
    return pl.pallas_call(
        functools.partial(spectrum_kernel, vols, across, block, own, planes, depth, other),
        out_shape=out_shape,
        in_specs=[smem] * 3 + [vmem] * (len(tables) + 3) + [last],
        out_specs=[vmem] * len(out_shape),
        scratch_shapes=scratch_shapes
        + [
            pltpu.VMEM((depth // 2, many, 3 * kept, LANES), jnp.float32),
            pltpu.VMEM((depth // 2, many, 1, LANES), jnp.float32),
        ],
        compiler_params=pltpu.CompilerParams(vmem_limit_bytes=VMEM_LIMIT),
        cost_estimate=pl.CostEstimate(
            flops=2 * 3 * rows * cols * block * (2 if other else 8),
            bytes_accessed=vols * rows * cols * 4 + rows * cols,
            transcendentals=0,
        ),
        name="lag_windows",
    )(place, codes, other_codes, *tables, frames, other_frames, template, more)


def exchange(value, axes, size, turn):
    return lax.ppermute(value, axes, [(at, at ^ turn) for at in range(size)])


def on_device(frames, template, shift_codes):
    vol_dev, pl_dev, img_rows, img_cols = frames.shape
    own, block = template.shape[0], template.shape[-1]
    depth = lax.axis_size("z")
    planes = lax.axis_size("plane")
    place = jnp.stack([lax.axis_index(axis) for axis in ("z", "y", "core", "plane")])
    other_codes = exchange(shift_codes, "core", 2, 1)
    other_frames = exchange(frames, "core", 2, 1)
    staged, *bands = stage([frames, *tap_constants(block)], template)
    turns = [depth - 1, *range(1, depth - 1)]
    fetched = {turn: exchange(template, "z", depth, turn) for turn in turns}
    pieces = [template] + [fetched[turn] for turn in range(1, depth)]
    averages, correlation = [], 0.0
    volumes = vol_dev * depth * 4
    for p in range(pl_dev):
        work = (place, shift_codes, other_codes, staged[:, p], other_frames[:, p])
        sizes = (depth, block, own)
        (far_sums,) = warp_sums(*work, bands, template, 1, *sizes)
        taken = exchange(far_sums, "y", 2, 1)
        near_sums = warp_sums(*work, bands, far_sums, 0, *sizes)
        pieces, near_sums = lax.optimization_barrier((pieces, near_sums))
        near = jnp.concatenate([piece[:, p] for piece in pieces], axis=0)
        far = exchange(near, "y", 2, 1)
        sums = [
            one.astype(jnp.float32) + taken[step * own : (step + 1) * own].astype(jnp.float32)
            for step, one in enumerate(near_sums)
        ]
        moved = [exchange(sums[turn].astype(jnp.bfloat16), "z", depth, turn) for turn in turns]
        sizes = (planes, depth, own)
        (part,) = lag_windows(*work, near, near_sums[0], 0, *sizes)
        found, *given = lag_windows(*work, far, part, 1, *sizes)
        found, moved = lax.optimization_barrier((found, moved))
        total = sum((one.astype(jnp.float32) for one in moved), sums[0])
        averages.append(total * (1.0 / volumes))
        for turn, one in enumerate(given):
            found = found + exchange(one, "plane", planes, turn + 1)
        correlation += found[0] + exchange(found[1], "core", 2, 1)
    return (correlation, jnp.stack(averages, axis=1))


def solution(mesh):
    devices = mesh.devices.reshape(-1, 2, 2, mesh.shape["plane"])
    split = jax.sharding.Mesh(devices, ("z", "y", "core", "plane"))
    vols = ("z", "y", "core")
    in_specs = (P(vols, "plane", None, None), P(vols, "plane", None, None), P(vols, None, None))
    out_specs = (P(vols, "plane", None), P(vols, "plane", None, None))
    return jax.shard_map(
        on_device, mesh=split, in_specs=in_specs, out_specs=out_specs, check_vma=False
    )
```

```python
import functools
import math

import jax
import jax.numpy as jnp
import numpy as np
from jax import lax
from jax.experimental import pallas as pl
from jax.experimental.pallas import tpu as pltpu
from jax.sharding import PartitionSpec as P

SHIFT = 8
WIN = 16
TAPS = 8
SUB = 16
EDGE = 16
LANES = 128
VMEM_LIMIT = 24 * 1024 * 1024

full_turn = 2.0 * math.pi


def dft_constants(block_size):
    positions = np.arange(block_size)
    angles = full_turn * (np.outer(positions, positions) % block_size) / block_size
    cosine = np.cos(angles)
    sine = -np.sin(angles)
    half = block_size // 2 + 1
    rows = -(-half // 16) * 16
    row_table = np.zeros((2 * rows, block_size))
    row_table[:half] = cosine[:half]
    row_table[rows : rows + half] = sine[:half]
    col_table = np.block([[cosine, sine], [-sine, cosine]])
    weights = np.full((half,), 2.0)
    weights[0] = weights[half - 1] = 1.0
    span = 2 * SHIFT + WIN
    lags = np.arange(span) - SHIFT - WIN // 2
    turns = full_turn * (np.outer(lags, positions) % block_size) / block_size
    lag_cos, lag_sin = np.cos(turns), np.sin(turns)
    lag_table = np.zeros((2 * span, 2 * rows))
    lag_table[:span, :half] = lag_cos[:, :half] * weights
    lag_table[:span, rows : rows + half] = -lag_sin[:, :half] * weights
    lag_table[span:, :half] = lag_sin[:, :half] * weights
    lag_table[span:, rows : rows + half] = lag_cos[:, :half] * weights
    span_table = np.zeros((2 * block_size, LANES))
    span_table[:block_size, :span] = lag_cos.T
    span_table[block_size:, :span] = -lag_sin.T
    return tuple(
        jnp.asarray(table, jnp.bfloat16) for table in (row_table, col_table, lag_table, span_table)
    )


def tap_constants(block_size):
    offsets = np.arange(TAPS) - (TAPS // 2 - 1)
    spots = offsets[None, :] - np.arange(SUB)[:, None] / SUB
    raw_taps = np.sinc(spots) * np.sinc(spots / (TAPS // 2))
    taps = raw_taps / raw_taps.sum(axis=-1, keepdims=True)

    def band(inputs, outputs):
        at = inputs - outputs + TAPS // 2 - 1
        return np.where((at >= 0) & (at < TAPS), taps[:, np.clip(at, 0, TAPS - 1)], 0.0)

    lanes = np.arange(block_size)[None, :]
    inputs = np.arange(block_size + 3 * EDGE)[:, None] - EDGE - SHIFT
    outputs = np.arange(2 * EDGE)[:, None] - SHIFT
    spare = np.arange(LANES)[None, :] % (2 * EDGE)
    first = band(spare - 2 * EDGE, outputs) * (spare >= EDGE)
    last = band(spare + EDGE, outputs) * (spare < EDGE)
    tables = band(inputs, lanes), np.stack([first, last], axis=1)
    return [jnp.asarray(table, jnp.float32) for table in tables]


def step_places(place_ref, step, across, own):
    z = place_ref[0] ^ step
    places = []
    for other in range(2):
        for one in range(own):
            index = ((2 * z + (place_ref[1] ^ other)) * 2 + place_ref[2]) * own + one
            places.append((index, index % across))
    return places


def step_band(place_ref, step, across, own):
    return (place_ref[0] ^ step) * (4 * own) // across


def warp_step(place_ref, step, other, code_refs, frame_refs, band_refs, down, across, block, own):
    cols_ref, edges_ref = band_refs
    band = step_band(place_ref, step, across, own)
    row = pl.multiple_of(band * block, block)
    row_above = pl.multiple_of(jnp.maximum(row - EDGE, 0), EDGE)
    row_below = pl.multiple_of(jnp.minimum(row + block, down * block - EDGE), EDGE)
    zero = jnp.zeros((EDGE, LANES), jnp.bfloat16)
    gap = jnp.zeros((block - 2 * EDGE, LANES), jnp.bfloat16)
    no_tile = jnp.zeros((block + 2 * EDGE, block), jnp.bfloat16)
    volumes = [
        (codes, frames, v)
        for codes, frames in zip(code_refs, frame_refs)
        for v in range(frames.shape[0])
    ]
    many = len(volumes)
    per_tile = LANES // (2 * EDGE)
    lane = lax.broadcasted_iota(jnp.int32, (EDGE, LANES), 1) // (2 * EDGE)

    def tile(frames, v, at):
        lanes = pl.ds(pl.multiple_of(at * block, block), block)
        above = jnp.where(band > 0, frames[v, pl.ds(row_above, EDGE), lanes], zero)
        below = jnp.where(band < down - 1, frames[v, pl.ds(row_below, EDGE), lanes], zero)
        return jnp.concatenate([frames[v, pl.ds(row, block), lanes], below, above], axis=0)

    places = step_places(place_ref, step, across, own)[other * own : (other + 1) * own]
    start = places[0][1]
    tiles = []
    for _, frames, v in volumes:
        left = jnp.where(start > 0, tile(frames, v, jnp.maximum(start - 1, 0)), no_tile)
        right = jnp.where(
            start + own < across, tile(frames, v, jnp.minimum(start + own, across - 1)), no_tile
        )
        tiles.append([left] + [tile(frames, v, start + one) for one in range(own)] + [right])
    totals = []
    for one, (index, _) in enumerate(places):
        row_tiles, partials, edges = [], [], []
        firsts, lasts = [], []
        for order, (codes, _, v) in enumerate(volumes):
            row_code, col_code = codes[v, 0, index], codes[v, 1, index]
            left, middle, right = tiles[order][one : one + 3]
            sides = jnp.concatenate([right[:, : block // 2], left[:, block // 2 :]], axis=1)
            col_start = SHIFT - (col_code >> 4)
            cols = cols_ref[col_code & (SUB - 1), pl.ds(col_start, block + 2 * EDGE), :]
            cols = cols.astype(jnp.bfloat16)
            partial = jnp.dot(
                jnp.concatenate([middle, sides], axis=1),
                jnp.concatenate([cols[EDGE:], gap, cols[:EDGE]], axis=0),
                preferred_element_type=jnp.float32,
            ).astype(jnp.bfloat16)
            partials.append(partial[:block])
            edges.append(partial[block:])
            back = -row_code
            back_start = SHIFT + EDGE - (back >> 4)
            rows = cols_ref[back & (SUB - 1), pl.ds(back_start, block), :]
            row_tiles.append(rows.astype(jnp.bfloat16))
            row_start, step_at = SHIFT + (row_code >> 4), row_code & (SUB - 1)
            first = edges_ref[step_at, 0, pl.ds(row_start, EDGE), :]
            last = edges_ref[step_at, 1, pl.ds(row_start, EDGE), :]
            if order % per_tile:
                first = jnp.where(lane == order % per_tile, first, firsts.pop())
                last = jnp.where(lane == order % per_tile, last, lasts.pop())
            firsts.append(first)
            lasts.append(last)
        for first, last in zip(firsts, lasts):
            both = [first.astype(jnp.bfloat16), gap, last.astype(jnp.bfloat16)]
            row_tiles.append(jnp.concatenate(both, axis=0))
        deep = many * (block + 2 * EDGE)
        total = jnp.dot(
            jnp.concatenate(row_tiles, axis=1)[:, :deep],
            jnp.concatenate(partials + edges, axis=0),
            preferred_element_type=jnp.float32,
        )
        totals.append(total)
    return totals


def first_kernel(down, across, block, own, place_ref, codes_ref, *refs):
    sources, (out_ref, token_ref) = refs[:3], refs[3:5]
    frames_ref, *band_refs = targets = refs[5:8]
    copies = [
        pltpu.make_async_copy(source, target, refs[8].at[at])
        for at, (source, target) in enumerate(zip(sources, targets))
    ]
    for copy in copies:
        copy.start()
    token_ref[...] = jnp.zeros(token_ref.shape, jnp.float32)
    for copy in copies:
        copy.wait()
    for step in range(out_ref.shape[0] // own):
        totals = warp_step(
            place_ref, step, 1, [codes_ref], [frames_ref], band_refs, down, across, block, own
        )
        for one, total in enumerate(totals):
            out_ref[step * own + one] = total


def first_sums(place, codes, frames, bands, depth, block, own):
    rows, cols = frames.shape[1:]
    down, across = rows // block, cols // block
    sources = [pltpu.with_memory_space_constraint(one, pltpu.HBM) for one in (frames, *bands)]
    smem = pl.BlockSpec(memory_space=pltpu.SMEM)
    return pl.pallas_call(
        functools.partial(first_kernel, down, across, block, own),
        out_shape=[
            jax.ShapeDtypeStruct((depth * own, block, block), jnp.float32),
            jax.ShapeDtypeStruct((8, LANES), jnp.float32),
        ],
        in_specs=[smem] * 2 + [pl.BlockSpec(memory_space=pltpu.HBM)] * len(sources),
        out_specs=[pl.BlockSpec(memory_space=pltpu.VMEM)] * 2,
        scratch_shapes=[pltpu.VMEM(one.shape, one.dtype) for one in sources]
        + [pltpu.SemaphoreType.DMA((len(sources),))],
        compiler_params=pltpu.CompilerParams(vmem_limit_bytes=VMEM_LIMIT),
        cost_estimate=pl.CostEstimate(
            flops=2 * frames.size * block * 8, bytes_accessed=frames.size * 4, transcendentals=0
        ),
        name="first_warp",
    )(place, codes, *sources)


def second_kernel(down, across, block, own, place_ref, codes_ref, frames_ref, *refs):
    band_refs, first_ref, out_ref = refs[:2], refs[2], refs[4]
    for step in range(out_ref.shape[0] // own):
        totals = warp_step(
            place_ref, step, 1, [codes_ref], [frames_ref], band_refs, down, across, block, own
        )
        for one, total in enumerate(totals):
            at = step * own + one
            out_ref[at] = (first_ref[at] + total).astype(jnp.bfloat16)


def second_sums(place, codes, frames, bands, first, after, block, own):
    rows, cols = frames.shape[1:]
    down, across = rows // block, cols // block
    smem = pl.BlockSpec(memory_space=pltpu.SMEM)
    vmem = pl.BlockSpec(memory_space=pltpu.VMEM)
    return pl.pallas_call(
        functools.partial(second_kernel, down, across, block, own),
        out_shape=jax.ShapeDtypeStruct(first.shape, jnp.bfloat16),
        in_specs=[smem] * 2 + [vmem] * (2 + len(bands)) + [pl.BlockSpec(memory_space=pl.ANY)],
        out_specs=vmem,
        compiler_params=pltpu.CompilerParams(vmem_limit_bytes=VMEM_LIMIT),
        cost_estimate=pl.CostEstimate(
            flops=2 * frames.size * block * 8, bytes_accessed=frames.size * 4, transcendentals=0
        ),
        name="second_warp",
    )(place, codes, frames, *bands, first, after)


def warp_kernel(down, across, block, own, place_ref, codes_ref, other_codes_ref, *refs):
    code_refs, frame_refs = (codes_ref, other_codes_ref), refs[:2]
    band_refs, out_refs = refs[2:4], refs[5:]
    for step, out_ref in enumerate(out_refs):
        totals = warp_step(
            place_ref, step, 0, code_refs, frame_refs, band_refs, down, across, block, own
        )
        for one, total in enumerate(totals):
            out_ref[one] = total.astype(jnp.bfloat16)


def warp_sums(place, codes, other_codes, frames, other_frames, bands, after, depth, block, own):
    vols, rows, cols = frames.shape
    down, across = rows // block, cols // block
    smem = pl.BlockSpec(memory_space=pltpu.SMEM)
    vmem = pl.BlockSpec(memory_space=pltpu.VMEM)
    return pl.pallas_call(
        functools.partial(warp_kernel, down, across, block, own),
        out_shape=[jax.ShapeDtypeStruct((own, block, block), jnp.bfloat16)] * depth,
        in_specs=[smem] * 3 + [vmem] * (2 + len(bands)) + [pl.BlockSpec(memory_space=pl.ANY)],
        out_specs=[vmem] * depth,
        compiler_params=pltpu.CompilerParams(vmem_limit_bytes=VMEM_LIMIT),
        cost_estimate=pl.CostEstimate(
            flops=2 * vols * rows * cols * block * 8,
            bytes_accessed=vols * rows * cols * 4 + rows * cols,
            transcendentals=0,
        ),
        name="warp",
    )(place, codes, other_codes, frames, other_frames, *bands, after)


def spectrum_kernel(vols, across, block, own, planes, depth, other, *refs):
    place_ref, codes_ref, other_codes_ref, row_ref, col_ref, lag_ref, span_ref = refs[:7]
    frames_ref, other_frames_ref, template_ref = refs[7:10]
    all_cross, all_sums = refs[-2:]
    if other:
        found_ref, out_refs, found = refs[10], refs[11:-3], refs[-3]
        found[...] = found_ref[...]
    else:
        found = refs[11]

    row_table = row_ref[...]
    col_table = col_ref[...]
    lag_table = lag_ref[...]
    half = row_table.shape[0] // 2
    kept = -(-(block // 2 + 1) // 8) * 8
    span = lag_table.shape[0] // 2
    top = lax.broadcasted_iota(jnp.int32, (8, LANES), 0) == 0
    volumes = [(codes_ref, frames_ref, v) for v in range(vols)]
    volumes += [(other_codes_ref, other_frames_ref, v) for v in range(vols)]
    many = len(volumes)
    local = 2 * own
    no_rows = jnp.zeros((half - kept, LANES), jnp.float32)

    for half_step in range(depth // 2):
        cross, sums = all_cross.at[half_step], all_sums.at[half_step]
        places = []
        for step in (2 * half_step, 2 * half_step + 1):
            band = step_band(place_ref, step, across, own)
            band_rows = pl.ds(pl.multiple_of(band * block, block), block)
            chosen = step_places(place_ref, step, across, own)[other * own : (other + 1) * own]
            for one, (index, at) in enumerate(chosen):
                lanes = pl.ds(pl.multiple_of(at * block, block), block)
                places.append((index, band_rows, lanes, step * own + one))

        for pair in range(local // 2):
            pair_places = places[2 * pair : 2 * pair + 2]
            sources = [[template_ref[at] for _, _, _, at in pair_places]]
            for _, frames, v in volumes:
                sources.append([frames[v, rows, lanes] for _, rows, lanes, _ in pair_places])
            parts = []
            for source in sources:
                rows = jnp.dot(
                    row_table,
                    jnp.concatenate(source, axis=1),
                    preferred_element_type=jnp.float32,
                ).astype(jnp.bfloat16)
                for side in range(2):
                    lanes = slice(side * block, (side + 1) * block)
                    parts.append(jnp.concatenate([rows[:half, lanes], rows[half:, lanes]], axis=1))
            spectra = jnp.dot(
                jnp.concatenate(parts, axis=0), col_table, preferred_element_type=jnp.float32
            )
            temp = spectra[: 2 * half].astype(jnp.bfloat16).astype(jnp.float32)
            for order in range(many):
                for side in range(2):
                    one = (2 * pair + side) * many + order
                    base = (2 * (order + 1) + side) * half
                    total = jnp.zeros((8, LANES), jnp.float32)
                    for row in range(0, kept, 8):
                        at = side * half + row
                        temp_real = temp[at : at + 8, :block]
                        temp_imag = temp[at : at + 8, block:]
                        real = spectra[base + row : base + row + 8, :block]
                        imag = spectra[base + row : base + row + 8, block:]
                        cross_real = real * temp_real + imag * temp_imag
                        cross_imag = imag * temp_real - real * temp_imag
                        power = cross_real * cross_real + cross_imag * cross_imag
                        magnitude = power * lax.rsqrt(jnp.maximum(power, 1e-36))
                        cross[one, row : row + 8, :] = cross_real
                        cross[one, kept + row : kept + row + 8, :] = cross_imag
                        cross[one, 2 * kept + row : 2 * kept + row + 8, :] = magnitude
                        if row == 0:
                            total = jnp.where(top, magnitude, 2.0 * magnitude)
                        elif row == block // 2:
                            total += magnitude
                        else:
                            total += 2.0 * magnitude
                    sums[one] = jnp.sum(total, axis=0, keepdims=True)

        means = jnp.sum(sums[...], axis=2, keepdims=True) * (1.0 / (block * block)) + 1e-06
        lag_sums = []
        for pair in range(local // 2):
            for order in range(many):
                norms = []
                for side in range(2):
                    one = (2 * pair + side) * many + order
                    scale = pl.reciprocal(cross[one, 2 * kept :, :] + means[one], approx=True)
                    norms.append(
                        jnp.concatenate(
                            [
                                cross[one, :kept, :] * scale,
                                no_rows,
                                cross[one, kept : 2 * kept, :] * scale,
                                no_rows,
                            ],
                            axis=0,
                        ).astype(jnp.bfloat16)
                    )
                lag_rows = jnp.dot(
                    lag_table, jnp.concatenate(norms, axis=1), preferred_element_type=jnp.float32
                ).astype(jnp.bfloat16)
                for side in range(2):
                    lanes = slice(side * block, (side + 1) * block)
                    lag_sums.append(
                        jnp.concatenate([lag_rows[:span, lanes], lag_rows[span:, lanes]], axis=1)
                    )
        lags = jnp.dot(
            jnp.concatenate(lag_sums, axis=0), span_ref[...], preferred_element_type=jnp.float32
        )
        for pair in range(local // 2):
            for order, (codes, _, v) in enumerate(volumes):
                for side in range(2):
                    index = places[2 * pair + side][0]
                    row_shift = codes[v, 0, index] >> 4
                    col_shift = codes[v, 1, index] >> 4
                    at = (pair * many + order) * 2 + side
                    one = lags[at * span : (at + 1) * span]
                    one = pltpu.roll(one, span - SHIFT - row_shift, 0)[:WIN]
                    at = index // (2 * own) * own + (2 * pair + side) % own
                    found[order, pl.ds(pl.multiple_of(at * WIN, WIN), WIN), :] = pltpu.roll(
                        one, LANES - SHIFT - col_shift, 1
                    )

    if not other:
        return

    share = found.shape[1] // WIN // planes
    per_tile = LANES // WIN
    lane = lax.broadcasted_iota(jnp.int32, (share, LANES), 1) // WIN
    for turn, out_ref in enumerate(out_refs):
        plane = place_ref[3] ^ turn
        for order in range(many):
            for tile in range(WIN // per_tile):
                total = jnp.zeros((share, LANES), jnp.float32)
                for part in range(per_tile):
                    start = plane * share * WIN + tile * per_tile + part
                    one = found[order, pl.ds(start, share, stride=WIN), :]
                    if part:
                        one = pltpu.roll(one, part * WIN, 1)
                    total = jnp.where(lane == part, one, total)
                lanes = slice(tile * LANES, (tile + 1) * LANES)
                out_ref[order // vols, order % vols, :, lanes] = total * (1.0 / block)


def lag_windows(
    place, codes, other_codes, frames, other_frames, template, more, other, planes, depth, own
):
    vols, rows, cols = frames.shape
    block = template.shape[-1]
    down, across = rows // block, cols // block
    tables = dft_constants(block)
    kept = -(-(block // 2 + 1) // 8) * 8
    smem = pl.BlockSpec(memory_space=pltpu.SMEM)
    vmem = pl.BlockSpec(memory_space=pltpu.VMEM)
    blocks = down * across // 2
    many = 2 * vols * 2 * own
    found = jax.ShapeDtypeStruct((2 * vols, blocks * WIN, LANES), jnp.float32)
    if other:
        out = (2, vols, blocks // planes, WIN * WIN)
        out_shape = [jax.ShapeDtypeStruct(out, jnp.float32)] * planes
        scratch_shapes = [pltpu.VMEM(found.shape, found.dtype)]
        last = vmem
    else:
        out_shape = [found]
        scratch_shapes = []
        last = pl.BlockSpec(memory_space=pl.ANY)
    return pl.pallas_call(
        functools.partial(spectrum_kernel, vols, across, block, own, planes, depth, other),
        out_shape=out_shape,
        in_specs=[smem] * 3 + [vmem] * (len(tables) + 3) + [last],
        out_specs=[vmem] * len(out_shape),
        scratch_shapes=scratch_shapes
        + [
            pltpu.VMEM((depth // 2, many, 3 * kept, LANES), jnp.float32),
            pltpu.VMEM((depth // 2, many, 1, LANES), jnp.float32),
        ],
        compiler_params=pltpu.CompilerParams(vmem_limit_bytes=VMEM_LIMIT),
        cost_estimate=pl.CostEstimate(
            flops=2 * 3 * rows * cols * block * (2 if other else 8),
            bytes_accessed=vols * rows * cols * 4 + rows * cols,
            transcendentals=0,
        ),
        name="lag_windows",
    )(place, codes, other_codes, *tables, frames, other_frames, template, more)


def exchange(value, axes, size, turn):
    return lax.ppermute(value, axes, [(at, at ^ turn) for at in range(size)])


def on_device(frames, template, shift_codes):
    vol_dev, pl_dev, img_rows, img_cols = frames.shape
    own, block = template.shape[0], template.shape[-1]
    depth = lax.axis_size("z")
    planes = lax.axis_size("plane")
    place = jnp.stack([lax.axis_index(axis) for axis in ("z", "y", "core", "plane")])
    core = place[2]
    other_codes = exchange(shift_codes, "core", 2, 1)
    other_frames = exchange(frames, "core", 2, 1)
    bands = tap_constants(block)
    sizes = (depth, block, own)
    first = [first_sums(place, shift_codes, frames[:, p], bands, *sizes) for p in range(pl_dev)]
    later, token = lax.optimization_barrier((template, first[0][1]))
    fetched = {depth - 1: exchange(template, "z", depth, depth - 1)}
    for turn in range(1, depth - 1):
        fetched[turn] = exchange(later, "z", depth, turn)
    pieces = [template] + [fetched[turn] for turn in range(1, depth)]
    averages, correlation = [], 0.0
    volumes = vol_dev * depth * 4
    for p in range(pl_dev):
        work = (place, shift_codes, other_codes, frames[:, p], other_frames[:, p])
        sizes = (depth, block, own)
        far_sums = second_sums(
            place, other_codes, other_frames[:, p], bands, first[p][0], token, block, own
        )
        taken = exchange(far_sums, "y", 2, 1)
        near_sums = warp_sums(*work, bands, far_sums, *sizes)
        pieces, near_sums = lax.optimization_barrier((pieces, near_sums))
        near = jnp.concatenate([piece[:, p] for piece in pieces], axis=0)
        far = exchange(near, "y", 2, 1)
        sums = [
            one.astype(jnp.float32) + taken[step * own : (step + 1) * own].astype(jnp.float32)
            for step, one in enumerate(near_sums)
        ]
        moved = [exchange(sums[turn].astype(jnp.bfloat16), "z", depth, turn) for turn in [depth - 1, *range(1, depth - 1)]]
        sizes = (planes, depth, own)
        (part,) = lag_windows(*work, near, near_sums[0], 0, *sizes)
        found, *given = lag_windows(*work, far, part, 1, *sizes)
        found, moved = lax.optimization_barrier((found, moved))
        total = sum((one.astype(jnp.float32) for one in moved), sums[0])
        averages.append(total * (1.0 / volumes))
        for turn, one in enumerate(given):
            found = found + exchange(one, "plane", planes, turn + 1)
        pair = (found[0], exchange(found[1], "core", 2, 1))
        pair = [jnp.where(core == at, *pair).reshape(vol_dev, -1, 1, own, WIN * WIN) for at in (0, 1)]
        correlation += jnp.concatenate(pair, axis=2).reshape(vol_dev, -1, WIN * WIN)
    return (correlation, jnp.stack(averages, axis=1))


def solution(mesh):
    devices = mesh.devices.reshape(-1, 2, 2, mesh.shape["plane"])
    split = jax.sharding.Mesh(devices, ("z", "y", "core", "plane"))
    vols = ("z", "y", "core")
    in_specs = (P(vols, "plane", None, None), P(vols, "plane", None, None), P(vols, None, None))
    out_specs = (P(vols, "plane", None), P(vols, "plane", None, None))
    return jax.shard_map(
        on_device, mesh=split, in_specs=in_specs, out_specs=out_specs, check_vma=False
    )
```

```python
import functools
import math

import jax
import jax.numpy as jnp
import numpy as np
from jax import lax
from jax.experimental import pallas as pl
from jax.experimental.pallas import tpu as pltpu
from jax.sharding import PartitionSpec as P

SHIFT = 8
WIN = 16
TAPS = 8
SUB = 16
EDGE = 16
LANES = 128
VMEM_LIMIT = 24 * 1024 * 1024

full_turn = 2.0 * math.pi


def dft_constants(block_size):
    positions = np.arange(block_size)
    angles = full_turn * (np.outer(positions, positions) % block_size) / block_size
    cosine = np.cos(angles)
    sine = -np.sin(angles)
    half = block_size // 2 + 1
    rows = -(-half // 16) * 16
    row_table = np.zeros((2 * rows, block_size))
    row_table[:half] = cosine[:half]
    row_table[rows : rows + half] = sine[:half]
    col_table = np.block([[cosine, sine], [-sine, cosine]])
    weights = np.full((half,), 2.0)
    weights[0] = weights[half - 1] = 1.0
    span = 2 * SHIFT + WIN
    lags = np.arange(span) - SHIFT - WIN // 2
    turns = full_turn * (np.outer(lags, positions) % block_size) / block_size
    lag_cos, lag_sin = np.cos(turns), np.sin(turns)
    lag_table = np.zeros((2 * span, 2 * rows))
    lag_table[:span, :half] = lag_cos[:, :half] * weights
    lag_table[:span, rows : rows + half] = -lag_sin[:, :half] * weights
    lag_table[span:, :half] = lag_sin[:, :half] * weights
    lag_table[span:, rows : rows + half] = lag_cos[:, :half] * weights
    span_table = np.zeros((2 * block_size, LANES))
    span_table[:block_size, :span] = lag_cos.T
    span_table[block_size:, :span] = -lag_sin.T
    return tuple(
        jnp.asarray(table, jnp.bfloat16) for table in (row_table, col_table, lag_table, span_table)
    )


def tap_constants(block_size):
    offsets = np.arange(TAPS) - (TAPS // 2 - 1)
    spots = offsets[None, :] - np.arange(SUB)[:, None] / SUB
    raw_taps = np.sinc(spots) * np.sinc(spots / (TAPS // 2))
    taps = raw_taps / raw_taps.sum(axis=-1, keepdims=True)

    def band(inputs, outputs):
        at = inputs - outputs + TAPS // 2 - 1
        return np.where((at >= 0) & (at < TAPS), taps[:, np.clip(at, 0, TAPS - 1)], 0.0)

    lanes = np.arange(block_size)[None, :]
    inputs = np.arange(block_size + 3 * EDGE)[:, None] - EDGE - SHIFT
    outputs = np.arange(2 * EDGE)[:, None] - SHIFT
    spare = np.arange(LANES)[None, :] % (2 * EDGE)
    first = band(spare - 2 * EDGE, outputs) * (spare >= EDGE)
    last = band(spare + EDGE, outputs) * (spare < EDGE)
    tables = band(inputs, lanes), np.stack([first, last], axis=1)
    return [jnp.asarray(table, jnp.float32) for table in tables]


def step_places(place_ref, step, across, own):
    z = place_ref[0] ^ step
    places = []
    for other in range(2):
        for one in range(own):
            index = ((2 * z + (place_ref[1] ^ other)) * 2 + place_ref[2]) * own + one
            places.append((index, index % across))
    return places


def step_band(place_ref, step, across, own):
    return (place_ref[0] ^ step) * (4 * own) // across


def stage_kernel(count, *refs):
    sources, targets, sems = refs[:count], refs[count + 1 : 2 * count + 1], refs[-1]
    copies = [
        pltpu.make_async_copy(source, target, sems.at[at])
        for at, (source, target) in enumerate(zip(sources, targets))
    ]
    for copy in copies:
        copy.start()
    for copy in copies:
        copy.wait()


def stage(arrays, after):
    kept = [pltpu.with_memory_space_constraint(one, pltpu.HBM) for one in arrays]
    count = len(arrays)
    return pl.pallas_call(
        functools.partial(stage_kernel, count),
        out_shape=[jax.ShapeDtypeStruct(one.shape, one.dtype) for one in arrays],
        in_specs=[pl.BlockSpec(memory_space=pltpu.HBM)] * count
        + [pl.BlockSpec(memory_space=pl.ANY)],
        out_specs=[pl.BlockSpec(memory_space=pltpu.VMEM)] * count,
        scratch_shapes=[pltpu.SemaphoreType.DMA((count,))],
        compiler_params=pltpu.CompilerParams(vmem_limit_bytes=VMEM_LIMIT),
        cost_estimate=pl.CostEstimate(
            flops=0, bytes_accessed=2 * sum(one.nbytes for one in arrays), transcendentals=0
        ),
        name="stage",
    )(*kept, pltpu.with_memory_space_constraint(after, pltpu.HBM))


def warp_step(place_ref, step, other, code_refs, frame_refs, band_refs, down, across, block, own):
    cols_ref, edges_ref = band_refs
    band = step_band(place_ref, step, across, own)
    row = pl.multiple_of(band * block, block)
    row_above = pl.multiple_of(jnp.maximum(row - EDGE, 0), EDGE)
    row_below = pl.multiple_of(jnp.minimum(row + block, down * block - EDGE), EDGE)
    zero = jnp.zeros((EDGE, LANES), jnp.bfloat16)
    gap = jnp.zeros((block - 2 * EDGE, LANES), jnp.bfloat16)
    no_tile = jnp.zeros((block + 2 * EDGE, block), jnp.bfloat16)
    volumes = [
        (codes, frames, v)
        for codes, frames in zip(code_refs, frame_refs)
        for v in range(frames.shape[0])
    ]
    many = len(volumes)
    per_tile = LANES // (2 * EDGE)
    lane = lax.broadcasted_iota(jnp.int32, (EDGE, LANES), 1) // (2 * EDGE)

    def tile(frames, v, at):
        lanes = pl.ds(pl.multiple_of(at * block, block), block)
        above = jnp.where(band > 0, frames[v, pl.ds(row_above, EDGE), lanes], zero)
        below = jnp.where(band < down - 1, frames[v, pl.ds(row_below, EDGE), lanes], zero)
        return jnp.concatenate([frames[v, pl.ds(row, block), lanes], below, above], axis=0)

    places = step_places(place_ref, step, across, own)[other * own : (other + 1) * own]
    start = places[0][1]
    tiles = []
    for _, frames, v in volumes:
        left = jnp.where(start > 0, tile(frames, v, jnp.maximum(start - 1, 0)), no_tile)
        right = jnp.where(
            start + own < across, tile(frames, v, jnp.minimum(start + own, across - 1)), no_tile
        )
        tiles.append([left] + [tile(frames, v, start + one) for one in range(own)] + [right])
    totals = []
    for one, (index, _) in enumerate(places):
        row_tiles, partials, edges = [], [], []
        firsts, lasts = [], []
        for order, (codes, _, v) in enumerate(volumes):
            row_code, col_code = codes[v, 0, index], codes[v, 1, index]
            left, middle, right = tiles[order][one : one + 3]
            sides = jnp.concatenate([right[:, : block // 2], left[:, block // 2 :]], axis=1)
            col_start = SHIFT - (col_code >> 4)
            cols = cols_ref[col_code & (SUB - 1), pl.ds(col_start, block + 2 * EDGE), :]
            cols = cols.astype(jnp.bfloat16)
            partial = jnp.dot(
                jnp.concatenate([middle, sides], axis=1),
                jnp.concatenate([cols[EDGE:], gap, cols[:EDGE]], axis=0),
                preferred_element_type=jnp.float32,
            ).astype(jnp.bfloat16)
            partials.append(partial[:block])
            edges.append(partial[block:])
            back = -row_code
            back_start = SHIFT + EDGE - (back >> 4)
            rows = cols_ref[back & (SUB - 1), pl.ds(back_start, block), :]
            row_tiles.append(rows.astype(jnp.bfloat16))
            row_start, step_at = SHIFT + (row_code >> 4), row_code & (SUB - 1)
            first = edges_ref[step_at, 0, pl.ds(row_start, EDGE), :]
            last = edges_ref[step_at, 1, pl.ds(row_start, EDGE), :]
            if order % per_tile:
                first = jnp.where(lane == order % per_tile, first, firsts.pop())
                last = jnp.where(lane == order % per_tile, last, lasts.pop())
            firsts.append(first)
            lasts.append(last)
        for first, last in zip(firsts, lasts):
            both = [first.astype(jnp.bfloat16), gap, last.astype(jnp.bfloat16)]
            row_tiles.append(jnp.concatenate(both, axis=0))
        deep = many * (block + 2 * EDGE)
        total = jnp.dot(
            jnp.concatenate(row_tiles, axis=1)[:, :deep],
            jnp.concatenate(partials + edges, axis=0),
            preferred_element_type=jnp.float32,
        )
        totals.append(total.astype(jnp.bfloat16))
    return totals


def warp_kernel(down, across, block, own, other, *refs):
    place_ref, *code_refs = refs[:3]
    frame_refs, band_refs, out_refs = refs[3:5], refs[5:7], refs[8:]
    depth = out_refs[0].shape[0] // own if other else len(out_refs)
    for step in range(depth):
        totals = warp_step(
            place_ref, step, other, code_refs, frame_refs, band_refs, down, across, block, own
        )
        for one, total in enumerate(totals):
            if other:
                out_refs[0][step * own + one] = total
            else:
                out_refs[step][one] = total


def warp_sums(
    place, codes, other_codes, frames, other_frames, bands, after, other, depth, block, own
):
    vols, rows, cols = frames.shape
    down, across = rows // block, cols // block
    smem = pl.BlockSpec(memory_space=pltpu.SMEM)
    vmem = pl.BlockSpec(memory_space=pltpu.VMEM)
    if other:
        out_shape = [jax.ShapeDtypeStruct((depth * own, block, block), jnp.bfloat16)]
    else:
        out_shape = [jax.ShapeDtypeStruct((own, block, block), jnp.bfloat16)] * depth
    return pl.pallas_call(
        functools.partial(warp_kernel, down, across, block, own, other),
        out_shape=out_shape,
        in_specs=[smem] * 3
        + [vmem] * (2 + len(bands))
        + [pl.BlockSpec(memory_space=pl.ANY)],
        out_specs=[vmem] * len(out_shape),
        compiler_params=pltpu.CompilerParams(vmem_limit_bytes=VMEM_LIMIT),
        cost_estimate=pl.CostEstimate(
            flops=2 * vols * rows * cols * block * 8,
            bytes_accessed=vols * rows * cols * 4 + rows * cols,
            transcendentals=0,
        ),
        name="warp",
    )(place, codes, other_codes, frames, other_frames, *bands, after)


def spectrum_kernel(vols, across, block, own, planes, depth, other, *refs):
    place_ref, codes_ref, other_codes_ref, row_ref, col_ref, lag_ref, span_ref = refs[:7]
    frames_ref, other_frames_ref, template_ref = refs[7:10]
    all_cross, all_sums = refs[-2:]
    if other:
        found_ref, out_refs, found = refs[10], refs[11:-3], refs[-3]
        found[...] = found_ref[...]
    else:
        found = refs[11]

    row_table = row_ref[...]
    col_table = col_ref[...]
    lag_table = lag_ref[...]
    half = row_table.shape[0] // 2
    kept = -(-(block // 2 + 1) // 8) * 8
    span = lag_table.shape[0] // 2
    top = lax.broadcasted_iota(jnp.int32, (8, LANES), 0) == 0
    volumes = [(codes_ref, frames_ref, v) for v in range(vols)]
    volumes += [(other_codes_ref, other_frames_ref, v) for v in range(vols)]
    many = len(volumes)
    local = 2 * own
    no_rows = jnp.zeros((half - kept, LANES), jnp.float32)

    for half_step in range(depth // 2):
        cross, sums = all_cross.at[half_step], all_sums.at[half_step]
        places = []
        for step in (2 * half_step, 2 * half_step + 1):
            band = step_band(place_ref, step, across, own)
            band_rows = pl.ds(pl.multiple_of(band * block, block), block)
            chosen = step_places(place_ref, step, across, own)[other * own : (other + 1) * own]
            for one, (index, at) in enumerate(chosen):
                lanes = pl.ds(pl.multiple_of(at * block, block), block)
                places.append((index, band_rows, lanes, step * own + one))

        for pair in range(local // 2):
            pair_places = places[2 * pair : 2 * pair + 2]
            sources = [[template_ref[at] for _, _, _, at in pair_places]]
            for _, frames, v in volumes:
                sources.append([frames[v, rows, lanes] for _, rows, lanes, _ in pair_places])
            parts = []
            for source in sources:
                rows = jnp.dot(
                    row_table,
                    jnp.concatenate(source, axis=1),
                    preferred_element_type=jnp.float32,
                ).astype(jnp.bfloat16)
                for side in range(2):
                    lanes = slice(side * block, (side + 1) * block)
                    parts.append(jnp.concatenate([rows[:half, lanes], rows[half:, lanes]], axis=1))
            spectra = jnp.dot(
                jnp.concatenate(parts, axis=0), col_table, preferred_element_type=jnp.float32
            )
            temp = spectra[: 2 * half].astype(jnp.bfloat16).astype(jnp.float32)
            for order in range(many):
                for side in range(2):
                    one = (2 * pair + side) * many + order
                    base = (2 * (order + 1) + side) * half
                    total = jnp.zeros((8, LANES), jnp.float32)
                    for row in range(0, kept, 8):
                        at = side * half + row
                        temp_real = temp[at : at + 8, :block]
                        temp_imag = temp[at : at + 8, block:]
                        real = spectra[base + row : base + row + 8, :block]
                        imag = spectra[base + row : base + row + 8, block:]
                        cross_real = real * temp_real + imag * temp_imag
                        cross_imag = imag * temp_real - real * temp_imag
                        power = cross_real * cross_real + cross_imag * cross_imag
                        magnitude = power * lax.rsqrt(jnp.maximum(power, 1e-36))
                        cross[one, row : row + 8, :] = cross_real
                        cross[one, kept + row : kept + row + 8, :] = cross_imag
                        cross[one, 2 * kept + row : 2 * kept + row + 8, :] = magnitude
                        if row == 0:
                            total = jnp.where(top, magnitude, 2.0 * magnitude)
                        elif row == block // 2:
                            total += magnitude
                        else:
                            total += 2.0 * magnitude
                    sums[one] = jnp.sum(total, axis=0, keepdims=True)

        means = jnp.sum(sums[...], axis=2, keepdims=True) * (1.0 / (block * block)) + 1e-06
        lag_sums = []
        for pair in range(local // 2):
            for order in range(many):
                norms = []
                for side in range(2):
                    one = (2 * pair + side) * many + order
                    scale = pl.reciprocal(cross[one, 2 * kept :, :] + means[one], approx=True)
                    norms.append(
                        jnp.concatenate(
                            [
                                cross[one, :kept, :] * scale,
                                no_rows,
                                cross[one, kept : 2 * kept, :] * scale,
                                no_rows,
                            ],
                            axis=0,
                        ).astype(jnp.bfloat16)
                    )
                lag_rows = jnp.dot(
                    lag_table, jnp.concatenate(norms, axis=1), preferred_element_type=jnp.float32
                ).astype(jnp.bfloat16)
                for side in range(2):
                    lanes = slice(side * block, (side + 1) * block)
                    lag_sums.append(
                        jnp.concatenate([lag_rows[:span, lanes], lag_rows[span:, lanes]], axis=1)
                    )
        lags = jnp.dot(
            jnp.concatenate(lag_sums, axis=0), span_ref[...], preferred_element_type=jnp.float32
        )
        for pair in range(local // 2):
            for order, (codes, _, v) in enumerate(volumes):
                for side in range(2):
                    index = places[2 * pair + side][0]
                    row_shift = codes[v, 0, index] >> 4
                    col_shift = codes[v, 1, index] >> 4
                    at = (pair * many + order) * 2 + side
                    one = lags[at * span : (at + 1) * span]
                    one = pltpu.roll(one, span - SHIFT - row_shift, 0)[:WIN]
                    at = index // (2 * own) * own + (2 * pair + side) % own
                    found[order, pl.ds(pl.multiple_of(at * WIN, WIN), WIN), :] = pltpu.roll(
                        one, LANES - SHIFT - col_shift, 1
                    )

    if not other:
        return

    share = found.shape[1] // WIN // planes
    per_tile = LANES // WIN
    lane = lax.broadcasted_iota(jnp.int32, (share, LANES), 1) // WIN
    for turn, out_ref in enumerate(out_refs):
        plane = place_ref[3] ^ turn
        for order in range(many):
            for tile in range(WIN // per_tile):
                total = jnp.zeros((share, LANES), jnp.float32)
                for part in range(per_tile):
                    start = plane * share * WIN + tile * per_tile + part
                    one = found[order, pl.ds(start, share, stride=WIN), :]
                    if part:
                        one = pltpu.roll(one, part * WIN, 1)
                    total = jnp.where(lane == part, one, total)
                lanes = slice(tile * LANES, (tile + 1) * LANES)
                out_ref[order // vols, order % vols, :, lanes] = total * (1.0 / block)


def lag_windows(
    place, codes, other_codes, frames, other_frames, template, more, other, planes, depth, own
):
    vols, rows, cols = frames.shape
    block = template.shape[-1]
    down, across = rows // block, cols // block
    tables = dft_constants(block)
    kept = -(-(block // 2 + 1) // 8) * 8
    smem = pl.BlockSpec(memory_space=pltpu.SMEM)
    vmem = pl.BlockSpec(memory_space=pltpu.VMEM)
    blocks = down * across // 2
    many = 2 * vols * 2 * own
    found = jax.ShapeDtypeStruct((2 * vols, blocks * WIN, LANES), jnp.float32)
    if other:
        out = (2, vols, blocks // planes, WIN * WIN)
        out_shape = [jax.ShapeDtypeStruct(out, jnp.float32)] * planes
        scratch_shapes = [pltpu.VMEM(found.shape, found.dtype)]
        last = vmem
    else:
        out_shape = [found]
        scratch_shapes = []
        last = pl.BlockSpec(memory_space=pl.ANY)
    return pl.pallas_call(
        functools.partial(spectrum_kernel, vols, across, block, own, planes, depth, other),
        out_shape=out_shape,
        in_specs=[smem] * 3 + [vmem] * (len(tables) + 3) + [last],
        out_specs=[vmem] * len(out_shape),
        scratch_shapes=scratch_shapes
        + [
            pltpu.VMEM((depth // 2, many, 3 * kept, LANES), jnp.float32),
            pltpu.VMEM((depth // 2, many, 1, LANES), jnp.float32),
        ],
        compiler_params=pltpu.CompilerParams(vmem_limit_bytes=VMEM_LIMIT),
        cost_estimate=pl.CostEstimate(
            flops=2 * 3 * rows * cols * block * (2 if other else 8),
            bytes_accessed=vols * rows * cols * 4 + rows * cols,
            transcendentals=0,
        ),
        name="lag_windows",
    )(place, codes, other_codes, *tables, frames, other_frames, template, more)


def exchange(value, axes, size, turn):
    return lax.ppermute(value, axes, [(at, at ^ turn) for at in range(size)])


def on_device(frames, template, shift_codes):
    vol_dev, pl_dev, img_rows, img_cols = frames.shape
    own, block = template.shape[0], template.shape[-1]
    depth = lax.axis_size("z")
    planes = lax.axis_size("plane")
    place = jnp.stack([lax.axis_index(axis) for axis in ("z", "y", "core", "plane")])
    core = place[2]
    other_codes = exchange(shift_codes, "core", 2, 1)
    other_frames = exchange(frames, "core", 2, 1)
    staged, *bands = stage([frames, *tap_constants(block)], template)
    turns = [depth - 1, *range(1, depth - 1)]
    fetched = {turn: exchange(template, "z", depth, turn) for turn in turns}
    pieces = [template] + [fetched[turn] for turn in range(1, depth)]
    averages, correlation = [], 0.0
    volumes = vol_dev * depth * 4
    for p in range(pl_dev):
        work = (place, shift_codes, other_codes, staged[:, p], other_frames[:, p])
        sizes = (depth, block, own)
        (far_sums,) = warp_sums(*work, bands, template, 1, *sizes)
        taken = exchange(far_sums, "y", 2, 1)
        near_sums = warp_sums(*work, bands, far_sums, 0, *sizes)
        pieces, near_sums = lax.optimization_barrier((pieces, near_sums))
        near = jnp.concatenate([piece[:, p] for piece in pieces], axis=0)
        far = exchange(near, "y", 2, 1)
        sums = [
            one.astype(jnp.float32) + taken[step * own : (step + 1) * own].astype(jnp.float32)
            for step, one in enumerate(near_sums)
        ]
        moved = [exchange(sums[turn].astype(jnp.bfloat16), "z", depth, turn) for turn in turns]
        sizes = (planes, depth, own)
        (part,) = lag_windows(*work, near, near_sums[0], 0, *sizes)
        found, *given = lag_windows(*work, far, part, 1, *sizes)
        found, moved = lax.optimization_barrier((found, moved))
        total = sum((one.astype(jnp.float32) for one in moved), sums[0])
        averages.append(total * (1.0 / volumes))
        for turn, one in enumerate(given):
            found = found + exchange(one, "plane", planes, turn + 1)
        pair = (found[0], exchange(found[1], "core", 2, 1))
        pair = [jnp.where(core == at, *pair).reshape(vol_dev, -1, 1, own, WIN * WIN) for at in (0, 1)]
        correlation += jnp.concatenate(pair, axis=2).reshape(vol_dev, -1, WIN * WIN)
    return (correlation, jnp.stack(averages, axis=1))


def solution(mesh):
    devices = mesh.devices.reshape(-1, 2, 2, mesh.shape["plane"])
    split = jax.sharding.Mesh(devices, ("z", "y", "core", "plane"))
    vols = ("z", "y", "core")
    in_specs = (P(vols, "plane", None, None), P(vols, "plane", None, None), P(vols, None, None))
    out_specs = (P(vols, "plane", None), P(vols, "plane", None, None))
    return jax.shard_map(
        on_device, mesh=split, in_specs=in_specs, out_specs=out_specs, check_vma=False
    )
```

```python
import functools
import math

import jax
import jax.numpy as jnp
import numpy as np
from jax import lax
from jax.experimental import pallas as pl
from jax.experimental.pallas import tpu as pltpu
from jax.sharding import PartitionSpec as P

SHIFT = 8
WIN = 16
TAPS = 8
SUB = 16
EDGE = 16
LANES = 128
VMEM_LIMIT = 24 * 1024 * 1024

full_turn = 2.0 * math.pi


def dft_constants(block_size):
    positions = np.arange(block_size)
    angles = full_turn * (np.outer(positions, positions) % block_size) / block_size
    cosine = np.cos(angles)
    sine = -np.sin(angles)
    half = block_size // 2 + 1
    rows = -(-half // 16) * 16
    row_table = np.zeros((2 * rows, block_size))
    row_table[:half] = cosine[:half]
    row_table[rows : rows + half] = sine[:half]
    col_table = np.block([[cosine, sine], [-sine, cosine]])
    weights = np.full((half,), 2.0)
    weights[0] = weights[half - 1] = 1.0
    span = 2 * SHIFT + WIN
    lags = np.arange(span) - SHIFT - WIN // 2
    turns = full_turn * (np.outer(lags, positions) % block_size) / block_size
    lag_cos, lag_sin = np.cos(turns), np.sin(turns)
    lag_table = np.zeros((2 * span, 2 * rows))
    lag_table[:span, :half] = lag_cos[:, :half] * weights
    lag_table[:span, rows : rows + half] = -lag_sin[:, :half] * weights
    lag_table[span:, :half] = lag_sin[:, :half] * weights
    lag_table[span:, rows : rows + half] = lag_cos[:, :half] * weights
    span_table = np.zeros((2 * block_size, LANES))
    span_table[:block_size, :span] = lag_cos.T
    span_table[block_size:, :span] = -lag_sin.T
    return tuple(
        jnp.asarray(table, jnp.bfloat16) for table in (row_table, col_table, lag_table, span_table)
    )


def tap_constants(block_size):
    offsets = np.arange(TAPS) - (TAPS // 2 - 1)
    spots = offsets[None, :] - np.arange(SUB)[:, None] / SUB
    raw_taps = np.sinc(spots) * np.sinc(spots / (TAPS // 2))
    taps = raw_taps / raw_taps.sum(axis=-1, keepdims=True)

    def band(inputs, outputs):
        at = inputs - outputs + TAPS // 2 - 1
        return np.where((at >= 0) & (at < TAPS), taps[:, np.clip(at, 0, TAPS - 1)], 0.0)

    lanes = np.arange(block_size)[None, :]
    inputs = np.arange(block_size + 3 * EDGE)[:, None] - EDGE - SHIFT
    outputs = np.arange(2 * EDGE)[:, None] - SHIFT
    spare = np.arange(LANES)[None, :] % (2 * EDGE)
    first = band(spare - 2 * EDGE, outputs) * (spare >= EDGE)
    last = band(spare + EDGE, outputs) * (spare < EDGE)
    tables = band(inputs, lanes), np.stack([first, last], axis=1)
    return [jnp.asarray(table, jnp.float32) for table in tables]


def step_places(place_ref, step, across, own):
    z = place_ref[0] ^ step
    places = []
    for other in range(2):
        for one in range(own):
            index = ((2 * z + (place_ref[1] ^ other)) * 2 + place_ref[2]) * own + one
            places.append((index, index % across))
    return places


def step_band(place_ref, step, across, own):
    return (place_ref[0] ^ step) * (4 * own) // across


def stage_kernel(count, chunks, *refs):
    sources, targets, sems = refs[:count], refs[count + 1 : 2 * count + 1], refs[-1]
    copies = []
    for source, target in zip(sources, targets):
        size = source.shape[0] // chunks
        for at in range(chunks):
            part = pl.ds(at * size, size)
            copies.append(
                pltpu.make_async_copy(source.at[part], target.at[part], sems.at[len(copies)])
            )
    for copy in copies:
        copy.start()
    for copy in copies:
        copy.wait()


def stage(arrays, after):
    chunks = 4
    kept = [pltpu.with_memory_space_constraint(one, pltpu.HBM) for one in arrays]
    count = len(arrays)
    return pl.pallas_call(
        functools.partial(stage_kernel, count, chunks),
        out_shape=[jax.ShapeDtypeStruct(one.shape, one.dtype) for one in arrays],
        in_specs=[pl.BlockSpec(memory_space=pltpu.HBM)] * count
        + [pl.BlockSpec(memory_space=pl.ANY)],
        out_specs=[pl.BlockSpec(memory_space=pltpu.VMEM)] * count,
        scratch_shapes=[pltpu.SemaphoreType.DMA((chunks * count,))],
        compiler_params=pltpu.CompilerParams(vmem_limit_bytes=VMEM_LIMIT),
        cost_estimate=pl.CostEstimate(
            flops=0, bytes_accessed=2 * sum(one.nbytes for one in arrays), transcendentals=0
        ),
        name="stage",
    )(*kept, pltpu.with_memory_space_constraint(after, pltpu.HBM))


def warp_step(place_ref, step, other, code_refs, frame_refs, band_refs, down, across, block, own):
    cols_ref, edges_ref = band_refs
    band = step_band(place_ref, step, across, own)
    row = pl.multiple_of(band * block, block)
    row_above = pl.multiple_of(jnp.maximum(row - EDGE, 0), EDGE)
    row_below = pl.multiple_of(jnp.minimum(row + block, down * block - EDGE), EDGE)
    zero = jnp.zeros((EDGE, LANES), jnp.bfloat16)
    gap = jnp.zeros((block - 2 * EDGE, LANES), jnp.bfloat16)
    no_tile = jnp.zeros((block + 2 * EDGE, block), jnp.bfloat16)
    volumes = [
        (codes, frames, v)
        for codes, frames in zip(code_refs, frame_refs)
        for v in range(frames.shape[0])
    ]
    many = len(volumes)
    per_tile = LANES // (2 * EDGE)
    lane = lax.broadcasted_iota(jnp.int32, (EDGE, LANES), 1) // (2 * EDGE)

    def tile(frames, v, at):
        lanes = pl.ds(pl.multiple_of(at * block, block), block)
        above = jnp.where(band > 0, frames[v, pl.ds(row_above, EDGE), lanes], zero)
        below = jnp.where(band < down - 1, frames[v, pl.ds(row_below, EDGE), lanes], zero)
        return jnp.concatenate([frames[v, pl.ds(row, block), lanes], below, above], axis=0)

    places = step_places(place_ref, step, across, own)[other * own : (other + 1) * own]
    start = places[0][1]
    tiles = []
    for _, frames, v in volumes:
        left = jnp.where(start > 0, tile(frames, v, jnp.maximum(start - 1, 0)), no_tile)
        right = jnp.where(
            start + own < across, tile(frames, v, jnp.minimum(start + own, across - 1)), no_tile
        )
        tiles.append([left] + [tile(frames, v, start + one) for one in range(own)] + [right])
    totals = []
    for one, (index, _) in enumerate(places):
        row_tiles, partials, edges = [], [], []
        firsts, lasts = [], []
        for order, (codes, _, v) in enumerate(volumes):
            row_code, col_code = codes[v, 0, index], codes[v, 1, index]
            left, middle, right = tiles[order][one : one + 3]
            sides = jnp.concatenate([right[:, : block // 2], left[:, block // 2 :]], axis=1)
            col_start = SHIFT - (col_code >> 4)
            cols = cols_ref[col_code & (SUB - 1), pl.ds(col_start, block + 2 * EDGE), :]
            cols = cols.astype(jnp.bfloat16)
            partial = jnp.dot(
                jnp.concatenate([middle, sides], axis=1),
                jnp.concatenate([cols[EDGE:], gap, cols[:EDGE]], axis=0),
                preferred_element_type=jnp.float32,
            ).astype(jnp.bfloat16)
            partials.append(partial[:block])
            edges.append(partial[block:])
            back = -row_code
            back_start = SHIFT + EDGE - (back >> 4)
            rows = cols_ref[back & (SUB - 1), pl.ds(back_start, block), :]
            row_tiles.append(rows.astype(jnp.bfloat16))
            row_start, step_at = SHIFT + (row_code >> 4), row_code & (SUB - 1)
            first = edges_ref[step_at, 0, pl.ds(row_start, EDGE), :]
            last = edges_ref[step_at, 1, pl.ds(row_start, EDGE), :]
            if order % per_tile:
                first = jnp.where(lane == order % per_tile, first, firsts.pop())
                last = jnp.where(lane == order % per_tile, last, lasts.pop())
            firsts.append(first)
            lasts.append(last)
        for first, last in zip(firsts, lasts):
            both = [first.astype(jnp.bfloat16), gap, last.astype(jnp.bfloat16)]
            row_tiles.append(jnp.concatenate(both, axis=0))
        deep = many * (block + 2 * EDGE)
        total = jnp.dot(
            jnp.concatenate(row_tiles, axis=1)[:, :deep],
            jnp.concatenate(partials + edges, axis=0),
            preferred_element_type=jnp.float32,
        )
        totals.append(total.astype(jnp.bfloat16))
    return totals


def warp_kernel(down, across, block, own, other, *refs):
    place_ref, *code_refs = refs[:3]
    frame_refs, band_refs, out_refs = refs[3:5], refs[5:7], refs[8:]
    depth = out_refs[0].shape[0] // own if other else len(out_refs)
    for step in range(depth):
        totals = warp_step(
            place_ref, step, other, code_refs, frame_refs, band_refs, down, across, block, own
        )
        for one, total in enumerate(totals):
            if other:
                out_refs[0][step * own + one] = total
            else:
                out_refs[step][one] = total


def warp_sums(
    place, codes, other_codes, frames, other_frames, bands, after, other, depth, block, own
):
    vols, rows, cols = frames.shape
    down, across = rows // block, cols // block
    smem = pl.BlockSpec(memory_space=pltpu.SMEM)
    vmem = pl.BlockSpec(memory_space=pltpu.VMEM)
    if other:
        out_shape = [jax.ShapeDtypeStruct((depth * own, block, block), jnp.bfloat16)]
    else:
        out_shape = [jax.ShapeDtypeStruct((own, block, block), jnp.bfloat16)] * depth
    return pl.pallas_call(
        functools.partial(warp_kernel, down, across, block, own, other),
        out_shape=out_shape,
        in_specs=[smem] * 3
        + [vmem] * (2 + len(bands))
        + [pl.BlockSpec(memory_space=pl.ANY)],
        out_specs=[vmem] * len(out_shape),
        compiler_params=pltpu.CompilerParams(vmem_limit_bytes=VMEM_LIMIT),
        cost_estimate=pl.CostEstimate(
            flops=2 * vols * rows * cols * block * 8,
            bytes_accessed=vols * rows * cols * 4 + rows * cols,
            transcendentals=0,
        ),
        name="warp",
    )(place, codes, other_codes, frames, other_frames, *bands, after)


def spectrum_kernel(vols, across, block, own, planes, depth, other, *refs):
    place_ref, codes_ref, other_codes_ref, row_ref, col_ref, lag_ref, span_ref = refs[:7]
    frames_ref, other_frames_ref, template_ref = refs[7:10]
    all_cross, all_sums = refs[-2:]
    if other:
        found_ref, out_refs, found = refs[10], refs[11:-3], refs[-3]
        found[...] = found_ref[...]
    else:
        found = refs[11]

    row_table = row_ref[...]
    col_table = col_ref[...]
    lag_table = lag_ref[...]
    half = row_table.shape[0] // 2
    kept = -(-(block // 2 + 1) // 8) * 8
    span = lag_table.shape[0] // 2
    top = lax.broadcasted_iota(jnp.int32, (8, LANES), 0) == 0
    volumes = [(codes_ref, frames_ref, v) for v in range(vols)]
    volumes += [(other_codes_ref, other_frames_ref, v) for v in range(vols)]
    many = len(volumes)
    local = 2 * own
    no_rows = jnp.zeros((half - kept, LANES), jnp.float32)

    for half_step in range(depth // 2):
        cross, sums = all_cross.at[half_step], all_sums.at[half_step]
        places = []
        for step in (2 * half_step, 2 * half_step + 1):
            band = step_band(place_ref, step, across, own)
            band_rows = pl.ds(pl.multiple_of(band * block, block), block)
            chosen = step_places(place_ref, step, across, own)[other * own : (other + 1) * own]
            for one, (index, at) in enumerate(chosen):
                lanes = pl.ds(pl.multiple_of(at * block, block), block)
                places.append((index, band_rows, lanes, step * own + one))

        for pair in range(local // 2):
            pair_places = places[2 * pair : 2 * pair + 2]
            sources = [[template_ref[at] for _, _, _, at in pair_places]]
            for _, frames, v in volumes:
                sources.append([frames[v, rows, lanes] for _, rows, lanes, _ in pair_places])
            parts = []
            for source in sources:
                rows = jnp.dot(
                    row_table,
                    jnp.concatenate(source, axis=1),
                    preferred_element_type=jnp.float32,
                ).astype(jnp.bfloat16)
                for side in range(2):
                    lanes = slice(side * block, (side + 1) * block)
                    parts.append(jnp.concatenate([rows[:half, lanes], rows[half:, lanes]], axis=1))
            spectra = jnp.dot(
                jnp.concatenate(parts, axis=0), col_table, preferred_element_type=jnp.float32
            )
            temp = spectra[: 2 * half].astype(jnp.bfloat16).astype(jnp.float32)
            for order in range(many):
                for side in range(2):
                    one = (2 * pair + side) * many + order
                    base = (2 * (order + 1) + side) * half
                    total = jnp.zeros((8, LANES), jnp.float32)
                    for row in range(0, kept, 8):
                        at = side * half + row
                        temp_real = temp[at : at + 8, :block]
                        temp_imag = temp[at : at + 8, block:]
                        real = spectra[base + row : base + row + 8, :block]
                        imag = spectra[base + row : base + row + 8, block:]
                        cross_real = real * temp_real + imag * temp_imag
                        cross_imag = imag * temp_real - real * temp_imag
                        power = cross_real * cross_real + cross_imag * cross_imag
                        magnitude = power * lax.rsqrt(jnp.maximum(power, 1e-36))
                        cross[one, row : row + 8, :] = cross_real
                        cross[one, kept + row : kept + row + 8, :] = cross_imag
                        cross[one, 2 * kept + row : 2 * kept + row + 8, :] = magnitude
                        if row == 0:
                            once = jnp.where(top, magnitude, 0.0)
                        elif row == block // 2:
                            once += magnitude
                        total += magnitude
                    sums[one] = jnp.sum(total + total - once, axis=0, keepdims=True)

        means = jnp.sum(sums[...], axis=2, keepdims=True) * (1.0 / (block * block)) + 1e-06
        lag_sums = []
        for pair in range(local // 2):
            for order in range(many):
                norms = []
                for side in range(2):
                    one = (2 * pair + side) * many + order
                    scale = pl.reciprocal(cross[one, 2 * kept :, :] + means[one], approx=True)
                    norms.append(
                        jnp.concatenate(
                            [
                                cross[one, :kept, :] * scale,
                                no_rows,
                                cross[one, kept : 2 * kept, :] * scale,
                                no_rows,
                            ],
                            axis=0,
                        ).astype(jnp.bfloat16)
                    )
                lag_rows = jnp.dot(
                    lag_table, jnp.concatenate(norms, axis=1), preferred_element_type=jnp.float32
                ).astype(jnp.bfloat16)
                for side in range(2):
                    lanes = slice(side * block, (side + 1) * block)
                    lag_sums.append(
                        jnp.concatenate([lag_rows[:span, lanes], lag_rows[span:, lanes]], axis=1)
                    )
        lags = jnp.dot(
            jnp.concatenate(lag_sums, axis=0), span_ref[...], preferred_element_type=jnp.float32
        )
        for pair in range(local // 2):
            for order, (codes, _, v) in enumerate(volumes):
                for side in range(2):
                    index = places[2 * pair + side][0]
                    row_shift = codes[v, 0, index] >> 4
                    col_shift = codes[v, 1, index] >> 4
                    at = (pair * many + order) * 2 + side
                    one = lags[at * span : (at + 1) * span]
                    one = pltpu.roll(one, span - SHIFT - row_shift, 0)[:WIN]
                    at = index // (2 * own) * own + (2 * pair + side) % own
                    found[order, pl.ds(pl.multiple_of(at * WIN, WIN), WIN), :] = pltpu.roll(
                        one, LANES - SHIFT - col_shift, 1
                    )

    if not other:
        return

    share = found.shape[1] // WIN // planes
    per_tile = LANES // WIN
    lane = lax.broadcasted_iota(jnp.int32, (share, LANES), 1) // WIN
    for turn, out_ref in enumerate(out_refs):
        plane = place_ref[3] ^ turn
        for order in range(many):
            for tile in range(WIN // per_tile):
                total = jnp.zeros((share, LANES), jnp.float32)
                for part in range(per_tile):
                    start = plane * share * WIN + tile * per_tile + part
                    one = found[order, pl.ds(start, share, stride=WIN), :]
                    if part:
                        one = pltpu.roll(one, part * WIN, 1)
                    total = jnp.where(lane == part, one, total)
                lanes = slice(tile * LANES, (tile + 1) * LANES)
                out_ref[order // vols, order % vols, :, lanes] = total * (1.0 / block)


def lag_windows(
    place, codes, other_codes, frames, other_frames, template, more, other, planes, depth, own
):
    vols, rows, cols = frames.shape
    block = template.shape[-1]
    down, across = rows // block, cols // block
    tables = dft_constants(block)
    kept = -(-(block // 2 + 1) // 8) * 8
    smem = pl.BlockSpec(memory_space=pltpu.SMEM)
    vmem = pl.BlockSpec(memory_space=pltpu.VMEM)
    blocks = down * across // 2
    many = 2 * vols * 2 * own
    found = jax.ShapeDtypeStruct((2 * vols, blocks * WIN, LANES), jnp.float32)
    if other:
        out = (2, vols, blocks // planes, WIN * WIN)
        out_shape = [jax.ShapeDtypeStruct(out, jnp.float32)] * planes
        scratch_shapes = [pltpu.VMEM(found.shape, found.dtype)]
        last = vmem
    else:
        out_shape = [found]
        scratch_shapes = []
        last = pl.BlockSpec(memory_space=pl.ANY)
    return pl.pallas_call(
        functools.partial(spectrum_kernel, vols, across, block, own, planes, depth, other),
        out_shape=out_shape,
        in_specs=[smem] * 3 + [vmem] * (len(tables) + 3) + [last],
        out_specs=[vmem] * len(out_shape),
        scratch_shapes=scratch_shapes
        + [
            pltpu.VMEM((depth // 2, many, 3 * kept, LANES), jnp.float32),
            pltpu.VMEM((depth // 2, many, 1, LANES), jnp.float32),
        ],
        compiler_params=pltpu.CompilerParams(vmem_limit_bytes=VMEM_LIMIT),
        cost_estimate=pl.CostEstimate(
            flops=2 * 3 * rows * cols * block * (2 if other else 8),
            bytes_accessed=vols * rows * cols * 4 + rows * cols,
            transcendentals=0,
        ),
        name="lag_windows",
    )(place, codes, other_codes, *tables, frames, other_frames, template, more)


def exchange(value, axes, size, turn):
    return lax.ppermute(value, axes, [(at, at ^ turn) for at in range(size)])


def on_device(frames, template, shift_codes):
    vol_dev, pl_dev, img_rows, img_cols = frames.shape
    own, block = template.shape[0], template.shape[-1]
    depth = lax.axis_size("z")
    planes = lax.axis_size("plane")
    place = jnp.stack([lax.axis_index(axis) for axis in ("z", "y", "core", "plane")])
    core = place[2]
    other_codes = exchange(shift_codes, "core", 2, 1)
    other_frames = exchange(frames, "core", 2, 1)
    halves = frames.reshape(4, pl_dev * vol_dev * img_rows // 4, img_cols)
    staged, *bands = stage([halves, *tap_constants(block)], template)
    staged = staged.reshape(frames.shape)
    turns = [depth - 1, *range(1, depth - 1)]
    fetched = {turn: exchange(template, "z", depth, turn) for turn in turns}
    pieces = [template] + [fetched[turn] for turn in range(1, depth)]
    averages, correlation = [], 0.0
    volumes = vol_dev * depth * 4
    for p in range(pl_dev):
        work = (place, shift_codes, other_codes, staged[:, p], other_frames[:, p])
        sizes = (depth, block, own)
        (far_sums,) = warp_sums(*work, bands, template, 1, *sizes)
        taken = exchange(far_sums, "y", 2, 1)
        near_sums = warp_sums(*work, bands, far_sums, 0, *sizes)
        pieces, near_sums = lax.optimization_barrier((pieces, near_sums))
        near = jnp.concatenate([piece[:, p] for piece in pieces], axis=0)
        far = exchange(near, "y", 2, 1)
        sums = [
            one.astype(jnp.float32) + taken[step * own : (step + 1) * own].astype(jnp.float32)
            for step, one in enumerate(near_sums)
        ]
        moved = [exchange(sums[turn].astype(jnp.bfloat16), "z", depth, turn) for turn in turns]
        sizes = (planes, depth, own)
        (part,) = lag_windows(*work, near, near_sums[0], 0, *sizes)
        found, *given = lag_windows(*work, far, part, 1, *sizes)
        found, moved = lax.optimization_barrier((found, moved))
        total = sum((one.astype(jnp.float32) for one in moved), sums[0])
        averages.append(total * (1.0 / volumes))
        for turn, one in enumerate(given):
            found = found + exchange(one, "plane", planes, turn + 1)
        pair = (found[0], exchange(found[1], "core", 2, 1))
        pair = [jnp.where(core == at, *pair).reshape(vol_dev, -1, 1, own, WIN * WIN) for at in (0, 1)]
        correlation += jnp.concatenate(pair, axis=2).reshape(vol_dev, -1, WIN * WIN)
    return (correlation, jnp.stack(averages, axis=1))


def solution(mesh):
    devices = mesh.devices.reshape(-1, 2, 2, mesh.shape["plane"])
    split = jax.sharding.Mesh(devices, ("z", "y", "core", "plane"))
    vols = ("z", "y", "core")
    in_specs = (P(vols, "plane", None, None), P(vols, "plane", None, None), P(vols, None, None))
    out_specs = (P(vols, "plane", None), P(vols, "plane", None, None))
    return jax.shard_map(
        on_device, mesh=split, in_specs=in_specs, out_specs=out_specs, check_vma=False
    )
```

```python
import functools
import math

import jax
import jax.numpy as jnp
import numpy as np
from jax import lax
from jax.experimental import pallas as pl
from jax.experimental.pallas import tpu as pltpu
from jax.sharding import PartitionSpec as P

SHIFT = 8
WIN = 16
TAPS = 8
SUB = 16
EDGE = 16
LANES = 128
VMEM_LIMIT = 24 * 1024 * 1024

full_turn = 2.0 * math.pi


def dft_constants(block_size):
    positions = np.arange(block_size)
    angles = full_turn * (np.outer(positions, positions) % block_size) / block_size
    cosine = np.cos(angles)
    sine = -np.sin(angles)
    half = block_size // 2 + 1
    rows = -(-half // 16) * 16
    row_table = np.zeros((2 * rows, block_size))
    row_table[:half] = cosine[:half]
    row_table[rows : rows + half] = sine[:half]
    col_table = np.block([[cosine, sine], [-sine, cosine]])
    weights = np.full((half,), 2.0)
    weights[0] = weights[half - 1] = 1.0
    span = 2 * SHIFT + WIN
    lags = np.arange(span) - SHIFT - WIN // 2
    turns = full_turn * (np.outer(lags, positions) % block_size) / block_size
    lag_cos, lag_sin = np.cos(turns), np.sin(turns)
    lag_table = np.zeros((2 * span, 2 * rows))
    lag_table[:span, :half] = lag_cos[:, :half] * weights
    lag_table[:span, rows : rows + half] = -lag_sin[:, :half] * weights
    lag_table[span:, :half] = lag_sin[:, :half] * weights
    lag_table[span:, rows : rows + half] = lag_cos[:, :half] * weights
    span_table = np.zeros((2 * block_size, LANES))
    span_table[:block_size, :span] = lag_cos.T
    span_table[block_size:, :span] = -lag_sin.T
    return tuple(
        jnp.asarray(table, jnp.bfloat16) for table in (row_table, col_table, lag_table, span_table)
    )


def tap_constants(block_size):
    offsets = np.arange(TAPS) - (TAPS // 2 - 1)
    spots = offsets[None, :] - np.arange(SUB)[:, None] / SUB
    raw_taps = np.sinc(spots) * np.sinc(spots / (TAPS // 2))
    taps = raw_taps / raw_taps.sum(axis=-1, keepdims=True)

    def band(inputs, outputs):
        at = inputs - outputs + TAPS // 2 - 1
        return np.where((at >= 0) & (at < TAPS), taps[:, np.clip(at, 0, TAPS - 1)], 0.0)

    lanes = np.arange(block_size)[None, :]
    inputs = np.arange(block_size + 3 * EDGE)[:, None] - EDGE - SHIFT
    outputs = np.arange(2 * EDGE)[:, None] - SHIFT
    spare = np.arange(LANES)[None, :] % (2 * EDGE)
    first = band(spare - 2 * EDGE, outputs) * (spare >= EDGE)
    last = band(spare + EDGE, outputs) * (spare < EDGE)
    tables = band(inputs, lanes), np.concatenate([first, last], axis=1)
    return [jnp.asarray(table, jnp.bfloat16) for table in tables]


def step_places(place_ref, step, across, own):
    z = place_ref[0] ^ step
    places = []
    for other in range(2):
        for one in range(own):
            index = ((2 * z + (place_ref[1] ^ other)) * 2 + place_ref[2]) * own + one
            places.append((index, index % across))
    return places


def step_band(place_ref, step, across, own):
    return (place_ref[0] ^ step) * (4 * own) // across


def stage_kernel(count, *refs):
    sources, targets = refs[:count], refs[count + 1 : 2 * count + 1]
    held, sems = refs[2 * count + 1 : 3 * count], refs[-1]
    copies = [
        pltpu.make_async_copy(source, target, sems.at[at])
        for at, (source, target) in enumerate(zip(sources, (*held, targets[-1])))
    ]
    for copy in copies:
        copy.start()
    for copy, one, target in zip(copies, held, targets):
        copy.wait()

        def widen(at, _):
            target[at] = one[at].astype(jnp.float32)
            return 0

        lax.fori_loop(0, one.shape[0], widen, 0)
    copies[-1].wait()


def stage(tables, frames, after):
    arrays = [
        pltpu.with_memory_space_constraint(one, pltpu.HBM) for one in (*tables, frames, after)
    ]
    count = len(tables) + 1
    vmem = pl.BlockSpec(memory_space=pltpu.VMEM)
    return pl.pallas_call(
        functools.partial(stage_kernel, count),
        out_shape=[jax.ShapeDtypeStruct(one.shape, jnp.float32) for one in tables]
        + [jax.ShapeDtypeStruct(frames.shape, frames.dtype)],
        in_specs=[pl.BlockSpec(memory_space=pltpu.HBM)] * count
        + [pl.BlockSpec(memory_space=pl.ANY)],
        out_specs=[vmem] * count,
        scratch_shapes=[pltpu.VMEM(one.shape, one.dtype) for one in tables]
        + [pltpu.SemaphoreType.DMA((count,))],
        compiler_params=pltpu.CompilerParams(vmem_limit_bytes=VMEM_LIMIT),
        cost_estimate=pl.CostEstimate(
            flops=0, bytes_accessed=2 * frames.nbytes, transcendentals=0
        ),
        name="stage",
    )(*arrays)


def warp_step(place_ref, step, other, code_refs, frame_refs, band_refs, down, across, block, own):
    cols_ref, edges_ref = band_refs
    band = step_band(place_ref, step, across, own)
    row = pl.multiple_of(band * block, block)
    row_above = pl.multiple_of(jnp.maximum(row - EDGE, 0), EDGE)
    row_below = pl.multiple_of(jnp.minimum(row + block, down * block - EDGE), EDGE)
    zero = jnp.zeros((EDGE, LANES), jnp.bfloat16)
    gap = jnp.zeros((block - 2 * EDGE, LANES), jnp.bfloat16)
    no_tile = jnp.zeros((block + 2 * EDGE, block), jnp.bfloat16)
    volumes = [
        (codes, frames, v)
        for codes, frames in zip(code_refs, frame_refs)
        for v in range(frames.shape[0])
    ]
    many = len(volumes)
    per_tile = LANES // (2 * EDGE)
    lane = lax.broadcasted_iota(jnp.int32, (EDGE, LANES), 1) // (2 * EDGE)

    def tile(frames, v, at):
        lanes = pl.ds(pl.multiple_of(at * block, block), block)
        above = jnp.where(band > 0, frames[v, pl.ds(row_above, EDGE), lanes], zero)
        below = jnp.where(band < down - 1, frames[v, pl.ds(row_below, EDGE), lanes], zero)
        return jnp.concatenate([frames[v, pl.ds(row, block), lanes], below, above], axis=0)

    places = step_places(place_ref, step, across, own)[other * own : (other + 1) * own]
    start = places[0][1]
    tiles = []
    for _, frames, v in volumes:
        left = jnp.where(start > 0, tile(frames, v, jnp.maximum(start - 1, 0)), no_tile)
        right = jnp.where(
            start + own < across, tile(frames, v, jnp.minimum(start + own, across - 1)), no_tile
        )
        tiles.append([left] + [tile(frames, v, start + one) for one in range(own)] + [right])
    totals = []
    for one, (index, _) in enumerate(places):
        row_tiles, partials, edges = [], [], []
        firsts, lasts = [], []
        for order, (codes, _, v) in enumerate(volumes):
            row_code, col_code = codes[v, 0, index], codes[v, 1, index]
            left, middle, right = tiles[order][one : one + 3]
            sides = jnp.concatenate([right[:, : block // 2], left[:, block // 2 :]], axis=1)
            col_start = SHIFT - (col_code >> 4)
            cols = cols_ref[col_code & (SUB - 1), pl.ds(col_start, block + 2 * EDGE), :]
            cols = cols.astype(jnp.bfloat16)
            partial = jnp.dot(
                jnp.concatenate([middle, sides], axis=1),
                jnp.concatenate([cols[EDGE:], gap, cols[:EDGE]], axis=0),
                preferred_element_type=jnp.float32,
            ).astype(jnp.bfloat16)
            partials.append(partial[:block])
            edges.append(partial[block:])
            back = -row_code
            back_start = SHIFT + EDGE - (back >> 4)
            rows = cols_ref[back & (SUB - 1), pl.ds(back_start, block), :]
            row_tiles.append(rows.astype(jnp.bfloat16))
            row_start, step_at = SHIFT + (row_code >> 4), row_code & (SUB - 1)
            first = edges_ref[step_at, pl.ds(row_start, EDGE), :]
            last = edges_ref[step_at, pl.ds(2 * EDGE + row_start, EDGE), :]
            if order % per_tile:
                first = jnp.where(lane == order % per_tile, first, firsts.pop())
                last = jnp.where(lane == order % per_tile, last, lasts.pop())
            firsts.append(first)
            lasts.append(last)
        for first, last in zip(firsts, lasts):
            both = [first.astype(jnp.bfloat16), gap, last.astype(jnp.bfloat16)]
            row_tiles.append(jnp.concatenate(both, axis=0))
        deep = many * (block + 2 * EDGE)
        total = jnp.dot(
            jnp.concatenate(row_tiles, axis=1)[:, :deep],
            jnp.concatenate(partials + edges, axis=0),
            preferred_element_type=jnp.float32,
        )
        totals.append(total.astype(jnp.bfloat16))
    return totals


def warp_kernel(down, across, block, own, other, *refs):
    place_ref, *code_refs = refs[:3]
    frame_refs, band_refs, out_refs = refs[3:5], refs[5:7], refs[8:]
    depth = out_refs[0].shape[0] // own if other else len(out_refs)
    for step in range(depth):
        totals = warp_step(
            place_ref, step, other, code_refs, frame_refs, band_refs, down, across, block, own
        )
        for one, total in enumerate(totals):
            if other:
                out_refs[0][step * own + one] = total
            else:
                out_refs[step][one] = total


def warp_sums(
    place, codes, other_codes, frames, other_frames, bands, after, other, depth, block, own
):
    vols, rows, cols = frames.shape
    down, across = rows // block, cols // block
    smem = pl.BlockSpec(memory_space=pltpu.SMEM)
    vmem = pl.BlockSpec(memory_space=pltpu.VMEM)
    if other:
        out_shape = [jax.ShapeDtypeStruct((depth * own, block, block), jnp.bfloat16)]
    else:
        out_shape = [jax.ShapeDtypeStruct((own, block, block), jnp.bfloat16)] * depth
    return pl.pallas_call(
        functools.partial(warp_kernel, down, across, block, own, other),
        out_shape=out_shape,
        in_specs=[smem] * 3
        + [vmem] * (2 + len(bands))
        + [pl.BlockSpec(memory_space=pl.ANY)],
        out_specs=[vmem] * len(out_shape),
        compiler_params=pltpu.CompilerParams(vmem_limit_bytes=VMEM_LIMIT),
        cost_estimate=pl.CostEstimate(
            flops=2 * vols * rows * cols * block * 8,
            bytes_accessed=vols * rows * cols * 4 + rows * cols,
            transcendentals=0,
        ),
        name="warp",
    )(place, codes, other_codes, frames, other_frames, *bands, after)


def spectrum_kernel(vols, across, block, own, planes, depth, other, *refs):
    place_ref, codes_ref, other_codes_ref, row_ref, col_ref, lag_ref, span_ref = refs[:7]
    frames_ref, other_frames_ref, template_ref = refs[7:10]
    all_cross, all_sums = refs[-2:]
    if other:
        found_ref, out_refs, found = refs[10], refs[11:-3], refs[-3]
        found[...] = found_ref[...]
    else:
        found = refs[11]

    row_table = row_ref[...]
    col_table = col_ref[...]
    lag_table = lag_ref[...]
    half = row_table.shape[0] // 2
    kept = -(-(block // 2 + 1) // 8) * 8
    span = lag_table.shape[0] // 2
    top = lax.broadcasted_iota(jnp.int32, (8, LANES), 0) == 0
    volumes = [(codes_ref, frames_ref, v) for v in range(vols)]
    volumes += [(other_codes_ref, other_frames_ref, v) for v in range(vols)]
    many = len(volumes)
    local = 2 * own
    no_rows = jnp.zeros((half - kept, LANES), jnp.float32)

    for half_step in range(depth // 2):
        cross, sums = all_cross.at[half_step], all_sums.at[half_step]
        places = []
        for step in (2 * half_step, 2 * half_step + 1):
            band = step_band(place_ref, step, across, own)
            band_rows = pl.ds(pl.multiple_of(band * block, block), block)
            chosen = step_places(place_ref, step, across, own)[other * own : (other + 1) * own]
            for one, (index, at) in enumerate(chosen):
                lanes = pl.ds(pl.multiple_of(at * block, block), block)
                places.append((index, band_rows, lanes, step * own + one))

        for pair in range(local // 2):
            pair_places = places[2 * pair : 2 * pair + 2]
            sources = [[template_ref[at] for _, _, _, at in pair_places]]
            for _, frames, v in volumes:
                sources.append([frames[v, rows, lanes] for _, rows, lanes, _ in pair_places])
            parts = []
            for source in sources:
                rows = jnp.dot(
                    row_table,
                    jnp.concatenate(source, axis=1),
                    preferred_element_type=jnp.float32,
                ).astype(jnp.bfloat16)
                for side in range(2):
                    lanes = slice(side * block, (side + 1) * block)
                    parts.append(jnp.concatenate([rows[:half, lanes], rows[half:, lanes]], axis=1))
            spectra = jnp.dot(
                jnp.concatenate(parts, axis=0), col_table, preferred_element_type=jnp.float32
            )
            temp = spectra[: 2 * half].astype(jnp.bfloat16).astype(jnp.float32)
            for order in range(many):
                for side in range(2):
                    one = (2 * pair + side) * many + order
                    base = (2 * (order + 1) + side) * half
                    total = jnp.zeros((8, LANES), jnp.float32)
                    for row in range(0, kept, 8):
                        at = side * half + row
                        temp_real = temp[at : at + 8, :block]
                        temp_imag = temp[at : at + 8, block:]
                        real = spectra[base + row : base + row + 8, :block]
                        imag = spectra[base + row : base + row + 8, block:]
                        cross_real = real * temp_real + imag * temp_imag
                        cross_imag = imag * temp_real - real * temp_imag
                        power = cross_real * cross_real + cross_imag * cross_imag
                        magnitude = power * lax.rsqrt(jnp.maximum(power, 1e-36))
                        cross[one, row : row + 8, :] = cross_real
                        cross[one, kept + row : kept + row + 8, :] = cross_imag
                        cross[one, 2 * kept + row : 2 * kept + row + 8, :] = magnitude
                        if row == 0:
                            once = jnp.where(top, magnitude, 0.0)
                        elif row == block // 2:
                            once += magnitude
                        total += magnitude
                    sums[one] = jnp.sum(total + total - once, axis=0, keepdims=True)

        means = jnp.sum(sums[...], axis=2, keepdims=True) * (1.0 / (block * block)) + 1e-06
        lag_sums = []
        for pair in range(local // 2):
            for order in range(many):
                norms = []
                for side in range(2):
                    one = (2 * pair + side) * many + order
                    scale = pl.reciprocal(cross[one, 2 * kept :, :] + means[one], approx=True)
                    norms.append(
                        jnp.concatenate(
                            [
                                cross[one, :kept, :] * scale,
                                no_rows,
                                cross[one, kept : 2 * kept, :] * scale,
                                no_rows,
                            ],
                            axis=0,
                        ).astype(jnp.bfloat16)
                    )
                lag_rows = jnp.dot(
                    lag_table, jnp.concatenate(norms, axis=1), preferred_element_type=jnp.float32
                ).astype(jnp.bfloat16)
                for side in range(2):
                    lanes = slice(side * block, (side + 1) * block)
                    lag_sums.append(
                        jnp.concatenate([lag_rows[:span, lanes], lag_rows[span:, lanes]], axis=1)
                    )
        lags = jnp.dot(
            jnp.concatenate(lag_sums, axis=0), span_ref[...], preferred_element_type=jnp.float32
        )
        for pair in range(local // 2):
            for order, (codes, _, v) in enumerate(volumes):
                for side in range(2):
                    index = places[2 * pair + side][0]
                    row_shift = codes[v, 0, index] >> 4
                    col_shift = codes[v, 1, index] >> 4
                    at = (pair * many + order) * 2 + side
                    one = lags[at * span : (at + 1) * span]
                    one = pltpu.roll(one, span - SHIFT - row_shift, 0)[:WIN]
                    at = index // (2 * own) * own + (2 * pair + side) % own
                    found[order, pl.ds(pl.multiple_of(at * WIN, WIN), WIN), :] = pltpu.roll(
                        one, LANES - SHIFT - col_shift, 1
                    )

    if not other:
        return

    share = found.shape[1] // WIN // planes
    per_tile = LANES // WIN
    lane = lax.broadcasted_iota(jnp.int32, (share, LANES), 1) // WIN
    for turn, out_ref in enumerate(out_refs):
        plane = place_ref[3] ^ turn
        for order in range(many):
            for tile in range(WIN // per_tile):
                total = jnp.zeros((share, LANES), jnp.float32)
                for part in range(per_tile):
                    start = plane * share * WIN + tile * per_tile + part
                    one = found[order, pl.ds(start, share, stride=WIN), :]
                    if part:
                        one = pltpu.roll(one, part * WIN, 1)
                    total = jnp.where(lane == part, one, total)
                lanes = slice(tile * LANES, (tile + 1) * LANES)
                total = (total * (1.0 / block)).astype(out_ref.dtype)
                out_ref[order // vols, order % vols, :, lanes] = total


def lag_windows(
    place, codes, other_codes, frames, other_frames, template, more, other, planes, depth, own
):
    vols, rows, cols = frames.shape
    block = template.shape[-1]
    down, across = rows // block, cols // block
    tables = dft_constants(block)
    kept = -(-(block // 2 + 1) // 8) * 8
    smem = pl.BlockSpec(memory_space=pltpu.SMEM)
    vmem = pl.BlockSpec(memory_space=pltpu.VMEM)
    blocks = down * across // 2
    many = 2 * vols * 2 * own
    found = jax.ShapeDtypeStruct((2 * vols, blocks * WIN, LANES), jnp.float32)
    if other:
        out = (2, vols, blocks // planes, WIN * WIN)
        out_shape = [jax.ShapeDtypeStruct(out, jnp.float32)]
        out_shape += [jax.ShapeDtypeStruct(out, jnp.bfloat16)] * (planes - 1)
        scratch_shapes = [pltpu.VMEM(found.shape, found.dtype)]
        last = vmem
    else:
        out_shape = [found]
        scratch_shapes = []
        last = pl.BlockSpec(memory_space=pl.ANY)
    return pl.pallas_call(
        functools.partial(spectrum_kernel, vols, across, block, own, planes, depth, other),
        out_shape=out_shape,
        in_specs=[smem] * 3 + [vmem] * (len(tables) + 3) + [last],
        out_specs=[vmem] * len(out_shape),
        scratch_shapes=scratch_shapes
        + [
            pltpu.VMEM((depth // 2, many, 3 * kept, LANES), jnp.float32),
            pltpu.VMEM((depth // 2, many, 1, LANES), jnp.float32),
        ],
        compiler_params=pltpu.CompilerParams(vmem_limit_bytes=VMEM_LIMIT),
        cost_estimate=pl.CostEstimate(
            flops=2 * 3 * rows * cols * block * (2 if other else 8),
            bytes_accessed=vols * rows * cols * 4 + rows * cols,
            transcendentals=0,
        ),
        name="lag_windows",
    )(place, codes, other_codes, *tables, frames, other_frames, template, more)


def exchange(value, axes, size, turn):
    return lax.ppermute(value, axes, [(at, at ^ turn) for at in range(size)])


def on_device(frames, template, shift_codes):
    vol_dev, pl_dev, img_rows, img_cols = frames.shape
    own, block = template.shape[0], template.shape[-1]
    depth = lax.axis_size("z")
    planes = lax.axis_size("plane")
    place = jnp.stack([lax.axis_index(axis) for axis in ("z", "y", "core", "plane")])
    core = place[2]
    other_codes = exchange(shift_codes, "core", 2, 1)
    other_frames = exchange(frames, "core", 2, 1)
    *bands, staged = stage(tap_constants(block), frames, template)
    turns = [depth - 1, *range(1, depth - 1)]
    fetched = {turn: exchange(template, "z", depth, turn) for turn in turns}
    pieces = [template] + [fetched[turn] for turn in range(1, depth)]
    averages, correlation = [], 0.0
    volumes = vol_dev * depth * 4
    for p in range(pl_dev):
        work = (place, shift_codes, other_codes, staged[:, p], other_frames[:, p])
        sizes = (depth, block, own)
        (far_sums,) = warp_sums(*work, bands, template, 1, *sizes)
        taken = exchange(far_sums, "y", 2, 1)
        near_sums = warp_sums(*work, bands, far_sums, 0, *sizes)
        pieces, near_sums = lax.optimization_barrier((pieces, near_sums))
        near = jnp.concatenate([piece[:, p] for piece in pieces], axis=0)
        far = exchange(near, "y", 2, 1)
        sums = [
            one.astype(jnp.float32) + taken[step * own : (step + 1) * own].astype(jnp.float32)
            for step, one in enumerate(near_sums)
        ]
        moved = [exchange(sums[turn].astype(jnp.bfloat16), "z", depth, turn) for turn in turns]
        sizes = (planes, depth, own)
        (part,) = lag_windows(*work, near, near_sums[0], 0, *sizes)
        found, *given = lag_windows(*work, far, part, 1, *sizes)
        found, moved = lax.optimization_barrier((found, moved))
        total = sum((one.astype(jnp.float32) for one in moved), sums[0])
        averages.append(total * (1.0 / volumes))
        for turn, one in enumerate(given):
            found = found + exchange(one, "plane", planes, turn + 1).astype(jnp.float32)
        given = exchange(found[1].astype(jnp.bfloat16), "core", 2, 1)
        pair = (found[0], given.astype(jnp.float32))
        pair = [jnp.where(core == at, *pair).reshape(vol_dev, -1, 1, own, WIN * WIN) for at in (0, 1)]
        correlation += jnp.concatenate(pair, axis=2).reshape(vol_dev, -1, WIN * WIN)
    return (correlation, jnp.stack(averages, axis=1))


def solution(mesh):
    devices = mesh.devices.reshape(-1, 2, 2, mesh.shape["plane"])
    split = jax.sharding.Mesh(devices, ("z", "y", "core", "plane"))
    vols = ("z", "y", "core")
    in_specs = (P(vols, "plane", None, None), P(vols, "plane", None, None), P(vols, None, None))
    out_specs = (P(vols, "plane", None), P(vols, "plane", None, None))
    return jax.shard_map(
        on_device, mesh=split, in_specs=in_specs, out_specs=out_specs, check_vma=False
    )
```

```python
import functools
import math

import jax
import jax.numpy as jnp
import numpy as np
from jax import lax
from jax.experimental import pallas as pl
from jax.experimental.pallas import tpu as pltpu
from jax.sharding import PartitionSpec as P

SHIFT = 8
WIN = 16
TAPS = 8
SUB = 16
EDGE = 16
LANES = 128
VMEM_LIMIT = 24 * 1024 * 1024

full_turn = 2.0 * math.pi


def dft_constants(block_size):
    positions = np.arange(block_size)
    angles = full_turn * (np.outer(positions, positions) % block_size) / block_size
    cosine = np.cos(angles)
    sine = -np.sin(angles)
    half = block_size // 2 + 1
    rows = -(-half // 16) * 16
    row_table = np.zeros((2 * rows, block_size))
    row_table[:half] = cosine[:half]
    row_table[rows : rows + half] = sine[:half]
    col_table = np.block([[cosine, sine], [-sine, cosine]])
    weights = np.full((half,), 2.0)
    weights[0] = weights[half - 1] = 1.0
    span = 2 * SHIFT + WIN
    lags = np.arange(span) - SHIFT - WIN // 2
    turns = full_turn * (np.outer(lags, positions) % block_size) / block_size
    lag_cos, lag_sin = np.cos(turns), np.sin(turns)
    lag_table = np.zeros((2 * span, 2 * rows))
    lag_table[:span, :half] = lag_cos[:, :half] * weights
    lag_table[:span, rows : rows + half] = -lag_sin[:, :half] * weights
    lag_table[span:, :half] = lag_sin[:, :half] * weights
    lag_table[span:, rows : rows + half] = lag_cos[:, :half] * weights
    span_table = np.zeros((2 * block_size, LANES))
    span_table[:block_size, :span] = lag_cos.T
    span_table[block_size:, :span] = -lag_sin.T
    return tuple(
        jnp.asarray(table, jnp.bfloat16) for table in (row_table, col_table, lag_table, span_table)
    )


def tap_constants(block_size):
    offsets = np.arange(TAPS) - (TAPS // 2 - 1)
    spots = offsets[None, :] - np.arange(SUB)[:, None] / SUB
    raw_taps = np.sinc(spots) * np.sinc(spots / (TAPS // 2))
    taps = raw_taps / raw_taps.sum(axis=-1, keepdims=True)

    def band(inputs, outputs):
        at = inputs - outputs + TAPS // 2 - 1
        return np.where((at >= 0) & (at < TAPS), taps[:, np.clip(at, 0, TAPS - 1)], 0.0)

    lanes = np.arange(block_size)[None, :]
    inputs = np.arange(block_size + 3 * EDGE)[:, None] - EDGE - SHIFT
    outputs = np.arange(2 * EDGE)[:, None] - SHIFT
    spare = np.arange(LANES)[None, :] % (2 * EDGE)
    first = band(spare - 2 * EDGE, outputs) * (spare >= EDGE)
    last = band(spare + EDGE, outputs) * (spare < EDGE)
    tables = band(inputs, lanes), np.concatenate([first, last], axis=1)
    return [jnp.asarray(table, jnp.bfloat16) for table in tables]


def step_places(place_ref, step, across, own):
    z = place_ref[0] ^ step
    places = []
    for other in range(2):
        for one in range(own):
            index = ((2 * z + (place_ref[1] ^ other)) * 2 + place_ref[2]) * own + one
            places.append((index, index % across))
    return places


def step_band(place_ref, step, across, own):
    return (place_ref[0] ^ step) * (4 * own) // across


def stage_kernel(count, *refs):
    sources, targets = refs[:count], refs[count + 1 : 2 * count + 1]
    held, sems = refs[2 * count + 1 : 3 * count], refs[-1]
    copies = [
        pltpu.make_async_copy(source, target, sems.at[at])
        for at, (source, target) in enumerate(zip(sources, (*held, targets[-1])))
    ]
    for copy in copies:
        copy.start()
    for copy, one, target in zip(copies, held, targets):
        copy.wait()

        def widen(at, _):
            target[at] = one[at].astype(jnp.float32)
            return 0

        lax.fori_loop(0, one.shape[0], widen, 0)
    copies[-1].wait()


def stage(tables, frames, after):
    arrays = [
        pltpu.with_memory_space_constraint(one, pltpu.HBM) for one in (*tables, frames, after)
    ]
    count = len(tables) + 1
    vmem = pl.BlockSpec(memory_space=pltpu.VMEM)
    return pl.pallas_call(
        functools.partial(stage_kernel, count),
        out_shape=[jax.ShapeDtypeStruct(one.shape, jnp.float32) for one in tables]
        + [jax.ShapeDtypeStruct(frames.shape, frames.dtype)],
        in_specs=[pl.BlockSpec(memory_space=pltpu.HBM)] * count
        + [pl.BlockSpec(memory_space=pl.ANY)],
        out_specs=[vmem] * count,
        scratch_shapes=[pltpu.VMEM(one.shape, one.dtype) for one in tables]
        + [pltpu.SemaphoreType.DMA((count,))],
        compiler_params=pltpu.CompilerParams(vmem_limit_bytes=VMEM_LIMIT),
        cost_estimate=pl.CostEstimate(
            flops=0, bytes_accessed=2 * frames.nbytes, transcendentals=0
        ),
        name="stage",
    )(*arrays)


def warp_step(place_ref, step, other, code_refs, frame_refs, band_refs, down, across, block, own):
    cols_ref, edges_ref = band_refs
    band = step_band(place_ref, step, across, own)
    row = pl.multiple_of(band * block, block)
    row_above = pl.multiple_of(jnp.maximum(row - EDGE, 0), EDGE)
    row_below = pl.multiple_of(jnp.minimum(row + block, down * block - EDGE), EDGE)
    zero = jnp.zeros((EDGE, LANES), jnp.bfloat16)
    gap = jnp.zeros((block - 2 * EDGE, LANES), jnp.bfloat16)
    no_tile = jnp.zeros((block + 2 * EDGE, block), jnp.bfloat16)
    volumes = [
        (codes, frames, v)
        for codes, frames in zip(code_refs, frame_refs)
        for v in range(frames.shape[0])
    ]
    many = len(volumes)
    per_tile = LANES // (2 * EDGE)
    lane = lax.broadcasted_iota(jnp.int32, (EDGE, LANES), 1) // (2 * EDGE)

    def tile(frames, v, at):
        lanes = pl.ds(pl.multiple_of(at * block, block), block)
        above = jnp.where(band > 0, frames[v, pl.ds(row_above, EDGE), lanes], zero)
        below = jnp.where(band < down - 1, frames[v, pl.ds(row_below, EDGE), lanes], zero)
        return jnp.concatenate([frames[v, pl.ds(row, block), lanes], below, above], axis=0)

    places = step_places(place_ref, step, across, own)[other * own : (other + 1) * own]
    start = places[0][1]
    tiles = []
    for _, frames, v in volumes:
        left = jnp.where(start > 0, tile(frames, v, jnp.maximum(start - 1, 0)), no_tile)
        right = jnp.where(
            start + own < across, tile(frames, v, jnp.minimum(start + own, across - 1)), no_tile
        )
        tiles.append([left] + [tile(frames, v, start + one) for one in range(own)] + [right])
    totals = []
    for one, (index, _) in enumerate(places):
        row_tiles, partials, edges = [], [], []
        firsts, lasts = [], []
        for order, (codes, _, v) in enumerate(volumes):
            row_code, col_code = codes[v, 0, index], codes[v, 1, index]
            left, middle, right = tiles[order][one : one + 3]
            sides = jnp.concatenate([right[:, : block // 2], left[:, block // 2 :]], axis=1)
            col_start = SHIFT - (col_code >> 4)
            cols = cols_ref[col_code & (SUB - 1), pl.ds(col_start, block + 2 * EDGE), :]
            cols = cols.astype(jnp.bfloat16)
            partial = jnp.dot(
                jnp.concatenate([middle, sides], axis=1),
                jnp.concatenate([cols[EDGE:], gap, cols[:EDGE]], axis=0),
                preferred_element_type=jnp.float32,
            ).astype(jnp.bfloat16)
            partials.append(partial[:block])
            edges.append(partial[block:])
            back = -row_code
            back_start = SHIFT + EDGE - (back >> 4)
            rows = cols_ref[back & (SUB - 1), pl.ds(back_start, block), :]
            row_tiles.append(rows.astype(jnp.bfloat16))
            row_start, step_at = SHIFT + (row_code >> 4), row_code & (SUB - 1)
            first = edges_ref[step_at, pl.ds(row_start, EDGE), :]
            last = edges_ref[step_at, pl.ds(2 * EDGE + row_start, EDGE), :]
            if order % per_tile:
                first = jnp.where(lane == order % per_tile, first, firsts.pop())
                last = jnp.where(lane == order % per_tile, last, lasts.pop())
            firsts.append(first)
            lasts.append(last)
        for first, last in zip(firsts, lasts):
            both = [first.astype(jnp.bfloat16), gap, last.astype(jnp.bfloat16)]
            row_tiles.append(jnp.concatenate(both, axis=0))
        deep = many * (block + 2 * EDGE)
        total = jnp.dot(
            jnp.concatenate(row_tiles, axis=1)[:, :deep],
            jnp.concatenate(partials + edges, axis=0),
            preferred_element_type=jnp.float32,
        )
        totals.append(total.astype(jnp.bfloat16))
    return totals


def warp_kernel(down, across, block, own, other, *refs):
    place_ref, *code_refs = refs[:3]
    frame_refs, band_refs, out_refs = refs[3:5], refs[5:7], refs[8:]
    depth = out_refs[0].shape[0] // own if other else len(out_refs)
    for step in range(depth):
        totals = warp_step(
            place_ref, step, other, code_refs, frame_refs, band_refs, down, across, block, own
        )
        for one, total in enumerate(totals):
            if other:
                out_refs[0][step * own + one] = total
            else:
                out_refs[step][one] = total


def warp_sums(
    place, codes, other_codes, frames, other_frames, bands, after, other, depth, block, own
):
    vols, rows, cols = frames.shape
    down, across = rows // block, cols // block
    smem = pl.BlockSpec(memory_space=pltpu.SMEM)
    vmem = pl.BlockSpec(memory_space=pltpu.VMEM)
    if other:
        out_shape = [jax.ShapeDtypeStruct((depth * own, block, block), jnp.bfloat16)]
    else:
        out_shape = [jax.ShapeDtypeStruct((own, block, block), jnp.bfloat16)] * depth
    return pl.pallas_call(
        functools.partial(warp_kernel, down, across, block, own, other),
        out_shape=out_shape,
        in_specs=[smem] * 3
        + [vmem] * (2 + len(bands))
        + [pl.BlockSpec(memory_space=pl.ANY)],
        out_specs=[vmem] * len(out_shape),
        compiler_params=pltpu.CompilerParams(vmem_limit_bytes=VMEM_LIMIT),
        cost_estimate=pl.CostEstimate(
            flops=2 * vols * rows * cols * block * 8,
            bytes_accessed=vols * rows * cols * 4 + rows * cols,
            transcendentals=0,
        ),
        name="warp",
    )(place, codes, other_codes, frames, other_frames, *bands, after)


def spectrum_kernel(vols, across, block, own, planes, depth, other, *refs):
    place_ref, codes_ref, other_codes_ref, row_ref, col_ref, lag_ref, span_ref = refs[:7]
    frames_ref, other_frames_ref, template_ref = refs[7:10]
    all_cross, all_sums = refs[-2:]
    if other:
        found_ref, out_refs, found = refs[10], refs[11:-3], refs[-3]
        found[...] = found_ref[...]
    else:
        found = refs[11]

    row_table = row_ref[...]
    col_table = col_ref[...]
    lag_table = lag_ref[...]
    half = row_table.shape[0] // 2
    kept = -(-(block // 2 + 1) // 8) * 8
    span = lag_table.shape[0] // 2
    top = lax.broadcasted_iota(jnp.int32, (8, LANES), 0) == 0
    volumes = [(codes_ref, frames_ref, v) for v in range(vols)]
    volumes += [(other_codes_ref, other_frames_ref, v) for v in range(vols)]
    many = len(volumes)
    local = 2 * own
    no_rows = jnp.zeros((half - kept, LANES), jnp.float32)

    for half_step in range(depth // 2):
        cross, sums = all_cross.at[half_step], all_sums.at[half_step]
        places = []
        for step in (2 * half_step, 2 * half_step + 1):
            band = step_band(place_ref, step, across, own)
            band_rows = pl.ds(pl.multiple_of(band * block, block), block)
            chosen = step_places(place_ref, step, across, own)[other * own : (other + 1) * own]
            for one, (index, at) in enumerate(chosen):
                lanes = pl.ds(pl.multiple_of(at * block, block), block)
                places.append((index, band_rows, lanes, step * own + one))

        for pair in range(local // 2):
            pair_places = places[2 * pair : 2 * pair + 2]
            sources = [[template_ref[at] for _, _, _, at in pair_places]]
            for _, frames, v in volumes:
                sources.append([frames[v, rows, lanes] for _, rows, lanes, _ in pair_places])
            parts = []
            for source in sources:
                rows = jnp.dot(
                    row_table,
                    jnp.concatenate(source, axis=1),
                    preferred_element_type=jnp.float32,
                ).astype(jnp.bfloat16)
                for side in range(2):
                    lanes = slice(side * block, (side + 1) * block)
                    parts.append(jnp.concatenate([rows[:half, lanes], rows[half:, lanes]], axis=1))
            spectra = jnp.dot(
                jnp.concatenate(parts, axis=0), col_table, preferred_element_type=jnp.float32
            )
            temp = spectra[: 2 * half].astype(jnp.bfloat16).astype(jnp.float32)
            for order in range(many):
                for side in range(2):
                    one = (2 * pair + side) * many + order
                    base = (2 * (order + 1) + side) * half
                    total = jnp.zeros((8, LANES), jnp.float32)
                    for row in range(0, kept, 8):
                        at = side * half + row
                        temp_real = temp[at : at + 8, :block]
                        temp_imag = temp[at : at + 8, block:]
                        real = spectra[base + row : base + row + 8, :block]
                        imag = spectra[base + row : base + row + 8, block:]
                        cross_real = real * temp_real + imag * temp_imag
                        cross_imag = imag * temp_real - real * temp_imag
                        power = cross_real * cross_real + cross_imag * cross_imag
                        magnitude = power * lax.rsqrt(jnp.maximum(power, 1e-36))
                        cross[one, row : row + 8, :] = cross_real
                        cross[one, kept + row : kept + row + 8, :] = cross_imag
                        cross[one, 2 * kept + row : 2 * kept + row + 8, :] = magnitude
                        if row == 0:
                            once = jnp.where(top, magnitude, 0.0)
                        elif row == block // 2:
                            once += magnitude
                        total += magnitude
                    sums[one] = jnp.sum(total + total - once, axis=0, keepdims=True)

        means = jnp.sum(sums[...], axis=2, keepdims=True) * (1.0 / (block * block)) + 1e-06
        lag_sums = []
        for pair in range(local // 2):
            for order in range(many):
                norms = []
                for side in range(2):
                    one = (2 * pair + side) * many + order
                    scale = pl.reciprocal(cross[one, 2 * kept :, :] + means[one], approx=True)
                    norms.append(
                        jnp.concatenate(
                            [
                                cross[one, :kept, :] * scale,
                                no_rows,
                                cross[one, kept : 2 * kept, :] * scale,
                                no_rows,
                            ],
                            axis=0,
                        ).astype(jnp.bfloat16)
                    )
                lag_rows = jnp.dot(
                    lag_table, jnp.concatenate(norms, axis=1), preferred_element_type=jnp.float32
                ).astype(jnp.bfloat16)
                for side in range(2):
                    lanes = slice(side * block, (side + 1) * block)
                    lag_sums.append(
                        jnp.concatenate([lag_rows[:span, lanes], lag_rows[span:, lanes]], axis=1)
                    )
        lags = jnp.dot(
            jnp.concatenate(lag_sums, axis=0), span_ref[...], preferred_element_type=jnp.float32
        )
        for pair in range(local // 2):
            for order, (codes, _, v) in enumerate(volumes):
                for side in range(2):
                    index = places[2 * pair + side][0]
                    row_shift = codes[v, 0, index] >> 4
                    col_shift = codes[v, 1, index] >> 4
                    at = (pair * many + order) * 2 + side
                    one = lags[at * span : (at + 1) * span]
                    one = pltpu.roll(one, span - SHIFT - row_shift, 0)[:WIN]
                    at = index // (2 * own) * own + (2 * pair + side) % own
                    found[order, pl.ds(pl.multiple_of(at * WIN, WIN), WIN), :] = pltpu.roll(
                        one, LANES - SHIFT - col_shift, 1
                    )

    if not other:
        return

    share = found.shape[1] // WIN // planes
    per_tile = LANES // WIN
    lane = lax.broadcasted_iota(jnp.int32, (share, LANES), 1) // WIN
    for turn, out_ref in enumerate(out_refs):
        plane = place_ref[3] ^ turn
        for order in range(many):
            for tile in range(WIN // per_tile):
                total = jnp.zeros((share, LANES), jnp.float32)
                for part in range(per_tile):
                    start = plane * share * WIN + tile * per_tile + part
                    one = found[order, pl.ds(start, share, stride=WIN), :]
                    if part:
                        one = pltpu.roll(one, part * WIN, 1)
                    total = jnp.where(lane == part, one, total)
                lanes = slice(tile * LANES, (tile + 1) * LANES)
                total = (total * (1.0 / block)).astype(out_ref.dtype)
                out_ref[order // vols, order % vols, :, lanes] = total


def lag_windows(
    place, codes, other_codes, frames, other_frames, template, more, other, planes, depth, own
):
    vols, rows, cols = frames.shape
    block = template.shape[-1]
    down, across = rows // block, cols // block
    tables = dft_constants(block)
    kept = -(-(block // 2 + 1) // 8) * 8
    smem = pl.BlockSpec(memory_space=pltpu.SMEM)
    vmem = pl.BlockSpec(memory_space=pltpu.VMEM)
    blocks = down * across // 2
    many = 2 * vols * 2 * own
    found = jax.ShapeDtypeStruct((2 * vols, blocks * WIN, LANES), jnp.float32)
    if other:
        out = (2, vols, blocks // planes, WIN * WIN)
        out_shape = [jax.ShapeDtypeStruct(out, jnp.float32)]
        out_shape += [jax.ShapeDtypeStruct(out, jnp.bfloat16)] * (planes - 1)
        scratch_shapes = [pltpu.VMEM(found.shape, found.dtype)]
        last = vmem
    else:
        out_shape = [found]
        scratch_shapes = []
        last = pl.BlockSpec(memory_space=pl.ANY)
    return pl.pallas_call(
        functools.partial(spectrum_kernel, vols, across, block, own, planes, depth, other),
        out_shape=out_shape,
        in_specs=[smem] * 3 + [vmem] * (len(tables) + 3) + [last],
        out_specs=[vmem] * len(out_shape),
        scratch_shapes=scratch_shapes
        + [
            pltpu.VMEM((depth // 2, many, 3 * kept, LANES), jnp.float32),
            pltpu.VMEM((depth // 2, many, 1, LANES), jnp.float32),
        ],
        compiler_params=pltpu.CompilerParams(vmem_limit_bytes=VMEM_LIMIT),
        cost_estimate=pl.CostEstimate(
            flops=2 * 3 * rows * cols * block * (2 if other else 2),
            bytes_accessed=vols * rows * cols * 4 + rows * cols,
            transcendentals=0,
        ),
        name="lag_windows",
    )(place, codes, other_codes, *tables, frames, other_frames, template, more)


def exchange(value, axes, size, turn):
    return lax.ppermute(value, axes, [(at, at ^ turn) for at in range(size)])


def on_device(frames, template, shift_codes):
    vol_dev, pl_dev, img_rows, img_cols = frames.shape
    own, block = template.shape[0], template.shape[-1]
    depth = lax.axis_size("z")
    planes = lax.axis_size("plane")
    place = jnp.stack([lax.axis_index(axis) for axis in ("z", "y", "core", "plane")])
    core = place[2]
    other_codes = exchange(shift_codes, "core", 2, 1)
    other_frames = exchange(frames, "core", 2, 1)
    *bands, staged = stage(tap_constants(block), frames, template)
    turns = [depth - 1, *range(1, depth - 1)]
    later, other_codes = lax.optimization_barrier((template, other_codes))
    fetched = {
        turn: exchange(later if turn == depth - 1 else template, "z", depth, turn) for turn in turns
    }
    pieces = [template] + [fetched[turn] for turn in range(1, depth)]
    averages, correlation = [], 0.0
    volumes = vol_dev * depth * 4
    for p in range(pl_dev):
        work = (place, shift_codes, other_codes, staged[:, p], other_frames[:, p])
        sizes = (depth, block, own)
        (far_sums,) = warp_sums(*work, bands, template, 1, *sizes)
        taken = exchange(far_sums, "y", 2, 1)
        near_sums = warp_sums(*work, bands, far_sums, 0, *sizes)
        pieces, near_sums = lax.optimization_barrier((pieces, near_sums))
        near = jnp.concatenate([piece[:, p] for piece in pieces], axis=0)
        far = exchange(near, "y", 2, 1)
        sums = [
            one.astype(jnp.float32) + taken[step * own : (step + 1) * own].astype(jnp.float32)
            for step, one in enumerate(near_sums)
        ]
        moved = [exchange(sums[turn].astype(jnp.bfloat16), "z", depth, turn) for turn in turns]
        sizes = (planes, depth, own)
        (part,) = lag_windows(*work, near, near_sums[0], 0, *sizes)
        found, *given = lag_windows(*work, far, part, 1, *sizes)
        found, moved = lax.optimization_barrier((found, moved))
        total = sum((one.astype(jnp.float32) for one in moved), sums[0])
        averages.append(total * (1.0 / volumes))
        for turn, one in enumerate(given):
            found = found + exchange(one, "plane", planes, turn + 1).astype(jnp.float32)
        given = exchange(found[1].astype(jnp.bfloat16), "core", 2, 1)
        pair = (found[0], given.astype(jnp.float32))
        pair = [jnp.where(core == at, *pair).reshape(vol_dev, -1, 1, own, WIN * WIN) for at in (0, 1)]
        correlation += jnp.concatenate(pair, axis=2).reshape(vol_dev, -1, WIN * WIN)
    return (correlation, jnp.stack(averages, axis=1))


def solution(mesh):
    devices = mesh.devices.reshape(-1, 2, 2, mesh.shape["plane"])
    split = jax.sharding.Mesh(devices, ("z", "y", "core", "plane"))
    vols = ("z", "y", "core")
    in_specs = (P(vols, "plane", None, None), P(vols, "plane", None, None), P(vols, None, None))
    out_specs = (P(vols, "plane", None), P(vols, "plane", None, None))
    return jax.shard_map(
        on_device, mesh=split, in_specs=in_specs, out_specs=out_specs, check_vma=False
    )
```

```python
import functools
import math

import jax
import jax.numpy as jnp
import numpy as np
from jax import lax
from jax.experimental import pallas as pl
from jax.experimental.pallas import tpu as pltpu
from jax.sharding import PartitionSpec as P

SHIFT = 8
WIN = 16
TAPS = 8
SUB = 16
EDGE = 16
LANES = 128
VMEM_LIMIT = 24 * 1024 * 1024

full_turn = 2.0 * math.pi


def dft_constants(block_size):
    positions = np.arange(block_size)
    angles = full_turn * (np.outer(positions, positions) % block_size) / block_size
    cosine = np.cos(angles)
    sine = -np.sin(angles)
    half = block_size // 2 + 1
    rows = -(-half // 16) * 16
    row_table = np.zeros((2 * rows, block_size))
    row_table[:half] = cosine[:half]
    row_table[rows : rows + half] = sine[:half]
    col_table = np.block([[cosine, sine], [-sine, cosine]])
    weights = np.full((half,), 2.0)
    weights[0] = weights[half - 1] = 1.0
    span = 2 * SHIFT + WIN
    lags = np.arange(span) - SHIFT - WIN // 2
    turns = full_turn * (np.outer(lags, positions) % block_size) / block_size
    lag_cos, lag_sin = np.cos(turns), np.sin(turns)
    lag_table = np.zeros((2 * span, 2 * rows))
    lag_table[:span, :half] = lag_cos[:, :half] * weights
    lag_table[:span, rows : rows + half] = -lag_sin[:, :half] * weights
    lag_table[span:, :half] = lag_sin[:, :half] * weights
    lag_table[span:, rows : rows + half] = lag_cos[:, :half] * weights
    span_table = np.zeros((2 * block_size, LANES))
    span_table[:block_size, :span] = lag_cos.T
    span_table[block_size:, :span] = -lag_sin.T
    return tuple(
        jnp.asarray(table, jnp.bfloat16) for table in (row_table, col_table, lag_table, span_table)
    )


def tap_constants(block_size):
    offsets = np.arange(TAPS) - (TAPS // 2 - 1)
    spots = offsets[None, :] - np.arange(SUB)[:, None] / SUB
    raw_taps = np.sinc(spots) * np.sinc(spots / (TAPS // 2))
    taps = raw_taps / raw_taps.sum(axis=-1, keepdims=True)

    def band(inputs, outputs):
        at = inputs - outputs + TAPS // 2 - 1
        return np.where((at >= 0) & (at < TAPS), taps[:, np.clip(at, 0, TAPS - 1)], 0.0)

    lanes = np.arange(block_size)[None, :]
    inputs = np.arange(block_size + 3 * EDGE)[:, None] - EDGE - SHIFT
    outputs = np.arange(2 * EDGE)[:, None] - SHIFT
    spare = np.arange(LANES)[None, :] % (2 * EDGE)
    first = band(spare - 2 * EDGE, outputs) * (spare >= EDGE)
    last = band(spare + EDGE, outputs) * (spare < EDGE)
    tables = band(inputs, lanes), np.concatenate([first, last], axis=1)
    return [jnp.asarray(table, jnp.bfloat16) for table in tables]


def step_places(place_ref, step, across, own):
    z = place_ref[0] ^ step
    places = []
    for other in range(2):
        for one in range(own):
            index = ((2 * z + (place_ref[1] ^ other)) * 2 + place_ref[2]) * own + one
            places.append((index, index % across))
    return places


def step_band(place_ref, step, across, own):
    return (place_ref[0] ^ step) * (4 * own) // across


def stage_kernel(count, *refs):
    sources, targets = refs[:count], refs[count + 1 : 2 * count + 1]
    held, sems = refs[2 * count + 1 : 3 * count], refs[-1]
    copies = [
        pltpu.make_async_copy(source, target, sems.at[at])
        for at, (source, target) in enumerate(zip(sources, (*held, targets[-1])))
    ]
    for copy in copies:
        copy.start()
    for copy, one, target in zip(copies, held, targets):
        copy.wait()

        def widen(at, _):
            target[at] = one[at].astype(jnp.float32)
            return 0

        lax.fori_loop(0, one.shape[0], widen, 0)
    copies[-1].wait()


def stage(tables, frames, after):
    arrays = [
        pltpu.with_memory_space_constraint(one, pltpu.HBM) for one in (*tables, frames, after)
    ]
    count = len(tables) + 1
    vmem = pl.BlockSpec(memory_space=pltpu.VMEM)
    return pl.pallas_call(
        functools.partial(stage_kernel, count),
        out_shape=[jax.ShapeDtypeStruct(one.shape, jnp.float32) for one in tables]
        + [jax.ShapeDtypeStruct(frames.shape, frames.dtype)],
        in_specs=[pl.BlockSpec(memory_space=pltpu.HBM)] * count
        + [pl.BlockSpec(memory_space=pl.ANY)],
        out_specs=[vmem] * count,
        scratch_shapes=[pltpu.VMEM(one.shape, one.dtype) for one in tables]
        + [pltpu.SemaphoreType.DMA((count,))],
        compiler_params=pltpu.CompilerParams(vmem_limit_bytes=VMEM_LIMIT),
        cost_estimate=pl.CostEstimate(
            flops=0, bytes_accessed=2 * frames.nbytes, transcendentals=0
        ),
        name="stage",
    )(*arrays)


def warp_step(place_ref, step, other, code_refs, frame_refs, band_refs, down, across, block, own):
    cols_ref, edges_ref = band_refs
    band = step_band(place_ref, step, across, own)
    row = pl.multiple_of(band * block, block)
    row_above = pl.multiple_of(jnp.maximum(row - EDGE, 0), EDGE)
    row_below = pl.multiple_of(jnp.minimum(row + block, down * block - EDGE), EDGE)
    zero = jnp.zeros((EDGE, LANES), jnp.bfloat16)
    gap = jnp.zeros((block - 2 * EDGE, LANES), jnp.bfloat16)
    no_tile = jnp.zeros((block + 2 * EDGE, block), jnp.bfloat16)
    volumes = [
        (codes, frames, v)
        for codes, frames in zip(code_refs, frame_refs)
        for v in range(frames.shape[0])
    ]
    many = len(volumes)
    per_tile = LANES // (2 * EDGE)
    lane = lax.broadcasted_iota(jnp.int32, (EDGE, LANES), 1) // (2 * EDGE)

    def tile(frames, v, at):
        lanes = pl.ds(pl.multiple_of(at * block, block), block)
        above = jnp.where(band > 0, frames[v, pl.ds(row_above, EDGE), lanes], zero)
        below = jnp.where(band < down - 1, frames[v, pl.ds(row_below, EDGE), lanes], zero)
        return jnp.concatenate([frames[v, pl.ds(row, block), lanes], below, above], axis=0)

    places = step_places(place_ref, step, across, own)[other * own : (other + 1) * own]
    start = places[0][1]
    tiles = []
    for _, frames, v in volumes:
        left = jnp.where(start > 0, tile(frames, v, jnp.maximum(start - 1, 0)), no_tile)
        right = jnp.where(
            start + own < across, tile(frames, v, jnp.minimum(start + own, across - 1)), no_tile
        )
        tiles.append([left] + [tile(frames, v, start + one) for one in range(own)] + [right])
    totals = []
    for one, (index, _) in enumerate(places):
        row_tiles, partials, edges = [], [], []
        firsts, lasts = [], []
        for order, (codes, _, v) in enumerate(volumes):
            row_code, col_code = codes[v, 0, index], codes[v, 1, index]
            left, middle, right = tiles[order][one : one + 3]
            sides = jnp.concatenate([right[:, : block // 2], left[:, block // 2 :]], axis=1)
            col_start = SHIFT - (col_code >> 4)
            cols = cols_ref[col_code & (SUB - 1), pl.ds(col_start, block + 2 * EDGE), :]
            cols = cols.astype(jnp.bfloat16)
            partial = jnp.dot(
                jnp.concatenate([middle, sides], axis=1),
                jnp.concatenate([cols[EDGE:], gap, cols[:EDGE]], axis=0),
                preferred_element_type=jnp.float32,
            ).astype(jnp.bfloat16)
            partials.append(partial[:block])
            edges.append(partial[block:])
            back = -row_code
            back_start = SHIFT + EDGE - (back >> 4)
            rows = cols_ref[back & (SUB - 1), pl.ds(back_start, block), :]
            row_tiles.append(rows.astype(jnp.bfloat16))
            row_start, step_at = SHIFT + (row_code >> 4), row_code & (SUB - 1)
            first = edges_ref[step_at, pl.ds(row_start, EDGE), :]
            last = edges_ref[step_at, pl.ds(2 * EDGE + row_start, EDGE), :]
            if order % per_tile:
                first = jnp.where(lane == order % per_tile, first, firsts.pop())
                last = jnp.where(lane == order % per_tile, last, lasts.pop())
            firsts.append(first)
            lasts.append(last)
        for first, last in zip(firsts, lasts):
            both = [first.astype(jnp.bfloat16), gap, last.astype(jnp.bfloat16)]
            row_tiles.append(jnp.concatenate(both, axis=0))
        deep = many * (block + 2 * EDGE)
        total = jnp.dot(
            jnp.concatenate(row_tiles, axis=1)[:, :deep],
            jnp.concatenate(partials + edges, axis=0),
            preferred_element_type=jnp.float32,
        )
        totals.append(total.astype(jnp.bfloat16))
    return totals


def warp_kernel(down, across, block, own, other, *refs):
    place_ref, *code_refs = refs[:3]
    frame_refs, band_refs, out_refs = refs[3:5], refs[5:7], refs[8:]
    depth = out_refs[0].shape[0] // own if other else len(out_refs)
    for step in range(depth):
        totals = warp_step(
            place_ref, step, other, code_refs, frame_refs, band_refs, down, across, block, own
        )
        for one, total in enumerate(totals):
            if other:
                out_refs[0][step * own + one] = total
            else:
                out_refs[step][one] = total


def warp_sums(
    place, codes, other_codes, frames, other_frames, bands, after, other, depth, block, own
):
    vols, rows, cols = frames.shape
    down, across = rows // block, cols // block
    smem = pl.BlockSpec(memory_space=pltpu.SMEM)
    vmem = pl.BlockSpec(memory_space=pltpu.VMEM)
    if other:
        out_shape = [jax.ShapeDtypeStruct((depth * own, block, block), jnp.bfloat16)]
    else:
        out_shape = [jax.ShapeDtypeStruct((own, block, block), jnp.bfloat16)] * depth
    return pl.pallas_call(
        functools.partial(warp_kernel, down, across, block, own, other),
        out_shape=out_shape,
        in_specs=[smem] * 3
        + [vmem] * (2 + len(bands))
        + [pl.BlockSpec(memory_space=pl.ANY)],
        out_specs=[vmem] * len(out_shape),
        compiler_params=pltpu.CompilerParams(vmem_limit_bytes=VMEM_LIMIT),
        cost_estimate=pl.CostEstimate(
            flops=2 * vols * rows * cols * block * 8,
            bytes_accessed=vols * rows * cols * 4 + rows * cols,
            transcendentals=0,
        ),
        name="warp",
    )(place, codes, other_codes, frames, other_frames, *bands, after)


def spectrum_kernel(vols, across, block, own, planes, depth, other, *refs):
    place_ref, codes_ref, other_codes_ref, row_ref, col_ref, lag_ref, span_ref = refs[:7]
    frames_ref, other_frames_ref, template_ref = refs[7:10]
    all_cross, all_sums = refs[-2:]
    ready = []
    if other:
        found_ref, spectra_ref, out_refs, found = refs[10], refs[11], refs[12:-3], refs[-3]
        found[...] = found_ref[...]
        ready.append(spectra_ref)
    else:
        found, spectra_ref = refs[11:13]

    row_table = row_ref[...]
    col_table = col_ref[...]
    lag_table = lag_ref[...]
    half = row_table.shape[0] // 2
    kept = -(-(block // 2 + 1) // 8) * 8
    span = lag_table.shape[0] // 2
    top = lax.broadcasted_iota(jnp.int32, (8, LANES), 0) == 0
    volumes = [(codes_ref, frames_ref, v) for v in range(vols)]
    volumes += [(other_codes_ref, other_frames_ref, v) for v in range(vols)]
    many = len(volumes)
    local = 2 * own
    no_rows = jnp.zeros((half - kept, LANES), jnp.float32)

    def find_places(half_step, row):
        places = []
        for step in (2 * half_step, 2 * half_step + 1):
            band = step_band(place_ref, step, across, own)
            band_rows = pl.ds(pl.multiple_of(band * block, block), block)
            chosen = step_places(place_ref, step, across, own)[row * own : (row + 1) * own]
            for one, (index, at) in enumerate(chosen):
                lanes = pl.ds(pl.multiple_of(at * block, block), block)
                places.append((index, band_rows, lanes, step * own + one))
        return places

    def frame_sources(pair_places):
        return [
            [frames[v, rows, lanes] for _, rows, lanes, _ in pair_places]
            for _, frames, v in volumes
        ]

    def transform(sources):
        parts = []
        for source in sources:
            rows = jnp.dot(
                row_table, jnp.concatenate(source, axis=1), preferred_element_type=jnp.float32
            ).astype(jnp.bfloat16)
            for side in range(2):
                lanes = slice(side * block, (side + 1) * block)
                parts.append(jnp.concatenate([rows[:half, lanes], rows[half:, lanes]], axis=1))
        return jnp.dot(
            jnp.concatenate(parts, axis=0), col_table, preferred_element_type=jnp.float32
        )

    for half_step in range(depth // 2):
        cross, sums = all_cross.at[half_step], all_sums.at[half_step]
        places = find_places(half_step, other)
        for pair in range(local // 2):
            pair_places = places[2 * pair : 2 * pair + 2]
            sources = [[template_ref[at] for _, _, _, at in pair_places]]
            sources += frame_sources(pair_places)
            if ready and half_step == 0:
                spectra = jnp.concatenate([transform(sources[:1]), ready[0][pair]], axis=0)
            else:
                spectra = transform(sources)
            temp = spectra[: 2 * half].astype(jnp.bfloat16).astype(jnp.float32)
            for order in range(many):
                for side in range(2):
                    one = (2 * pair + side) * many + order
                    base = (2 * (order + 1) + side) * half
                    total = jnp.zeros((8, LANES), jnp.float32)
                    for row in range(0, kept, 8):
                        at = side * half + row
                        temp_real = temp[at : at + 8, :block]
                        temp_imag = temp[at : at + 8, block:]
                        real = spectra[base + row : base + row + 8, :block]
                        imag = spectra[base + row : base + row + 8, block:]
                        cross_real = real * temp_real + imag * temp_imag
                        cross_imag = imag * temp_real - real * temp_imag
                        power = cross_real * cross_real + cross_imag * cross_imag
                        magnitude = power * lax.rsqrt(jnp.maximum(power, 1e-36))
                        cross[one, row : row + 8, :] = cross_real
                        cross[one, kept + row : kept + row + 8, :] = cross_imag
                        cross[one, 2 * kept + row : 2 * kept + row + 8, :] = magnitude
                        if row == 0:
                            once = jnp.where(top, magnitude, 0.0)
                        elif row == block // 2:
                            once += magnitude
                        total += magnitude
                    sums[one] = jnp.sum(total + total - once, axis=0, keepdims=True)

        means = jnp.sum(sums[...], axis=2, keepdims=True) * (1.0 / (block * block)) + 1e-06
        lag_sums = []
        for pair in range(local // 2):
            for order in range(many):
                norms = []
                for side in range(2):
                    one = (2 * pair + side) * many + order
                    scale = pl.reciprocal(cross[one, 2 * kept :, :] + means[one], approx=True)
                    norms.append(
                        jnp.concatenate(
                            [
                                cross[one, :kept, :] * scale,
                                no_rows,
                                cross[one, kept : 2 * kept, :] * scale,
                                no_rows,
                            ],
                            axis=0,
                        ).astype(jnp.bfloat16)
                    )
                lag_rows = jnp.dot(
                    lag_table, jnp.concatenate(norms, axis=1), preferred_element_type=jnp.float32
                ).astype(jnp.bfloat16)
                for side in range(2):
                    lanes = slice(side * block, (side + 1) * block)
                    lag_sums.append(
                        jnp.concatenate([lag_rows[:span, lanes], lag_rows[span:, lanes]], axis=1)
                    )
        lags = jnp.dot(
            jnp.concatenate(lag_sums, axis=0), span_ref[...], preferred_element_type=jnp.float32
        )
        for pair in range(local // 2):
            for order, (codes, _, v) in enumerate(volumes):
                for side in range(2):
                    index = places[2 * pair + side][0]
                    row_shift = codes[v, 0, index] >> 4
                    col_shift = codes[v, 1, index] >> 4
                    at = (pair * many + order) * 2 + side
                    one = lags[at * span : (at + 1) * span]
                    one = pltpu.roll(one, span - SHIFT - row_shift, 0)[:WIN]
                    at = index // (2 * own) * own + (2 * pair + side) % own
                    found[order, pl.ds(pl.multiple_of(at * WIN, WIN), WIN), :] = pltpu.roll(
                        one, LANES - SHIFT - col_shift, 1
                    )

    if not other:
        places = find_places(0, 1)
        for pair in range(local // 2):
            spectra_ref[pair] = transform(frame_sources(places[2 * pair : 2 * pair + 2]))
        return

    share = found.shape[1] // WIN // planes
    per_tile = LANES // WIN
    lane = lax.broadcasted_iota(jnp.int32, (share, LANES), 1) // WIN
    for turn, out_ref in enumerate(out_refs):
        plane = place_ref[3] ^ turn
        for order in range(many):
            for tile in range(WIN // per_tile):
                total = jnp.zeros((share, LANES), jnp.float32)
                for part in range(per_tile):
                    start = plane * share * WIN + tile * per_tile + part
                    one = found[order, pl.ds(start, share, stride=WIN), :]
                    if part:
                        one = pltpu.roll(one, part * WIN, 1)
                    total = jnp.where(lane == part, one, total)
                lanes = slice(tile * LANES, (tile + 1) * LANES)
                total = (total * (1.0 / block)).astype(out_ref.dtype)
                out_ref[order // vols, order % vols, :, lanes] = total


def lag_windows(
    place, codes, other_codes, frames, other_frames, template, more, other, planes, depth, own
):
    vols, rows, cols = frames.shape
    block = template.shape[-1]
    down, across = rows // block, cols // block
    tables = dft_constants(block)
    kept = -(-(block // 2 + 1) // 8) * 8
    smem = pl.BlockSpec(memory_space=pltpu.SMEM)
    vmem = pl.BlockSpec(memory_space=pltpu.VMEM)
    blocks = down * across // 2
    many = 2 * vols * 2 * own
    found = jax.ShapeDtypeStruct((2 * vols, blocks * WIN, LANES), jnp.float32)
    if other:
        out = (2, vols, blocks // planes, WIN * WIN)
        out_shape = [jax.ShapeDtypeStruct(out, jnp.float32)]
        out_shape += [jax.ShapeDtypeStruct(out, jnp.bfloat16)] * (planes - 1)
        scratch_shapes = [pltpu.VMEM(found.shape, found.dtype)]
        last = [vmem, vmem]
    else:
        half = tables[0].shape[0] // 2
        spectra = (own, 2 * vols * 2 * half, 2 * block)
        out_shape = [found, jax.ShapeDtypeStruct(spectra, jnp.float32)]
        scratch_shapes = []
        last = [pl.BlockSpec(memory_space=pl.ANY)]
    return pl.pallas_call(
        functools.partial(spectrum_kernel, vols, across, block, own, planes, depth, other),
        out_shape=out_shape,
        in_specs=[smem] * 3 + [vmem] * (len(tables) + 3) + last,
        out_specs=[vmem] * len(out_shape),
        scratch_shapes=scratch_shapes
        + [
            pltpu.VMEM((depth // 2, many, 3 * kept, LANES), jnp.float32),
            pltpu.VMEM((depth // 2, many, 1, LANES), jnp.float32),
        ],
        compiler_params=pltpu.CompilerParams(vmem_limit_bytes=VMEM_LIMIT),
        cost_estimate=pl.CostEstimate(
            flops=2 * 3 * rows * cols * block * (2 if other else 8),
            bytes_accessed=vols * rows * cols * 4 + rows * cols,
            transcendentals=0,
        ),
        name="lag_windows",
    )(place, codes, other_codes, *tables, frames, other_frames, template, *more)


def exchange(value, axes, size, turn):
    return lax.ppermute(value, axes, [(at, at ^ turn) for at in range(size)])


def on_device(frames, template, shift_codes):
    vol_dev, pl_dev, img_rows, img_cols = frames.shape
    own, block = template.shape[0], template.shape[-1]
    depth = lax.axis_size("z")
    planes = lax.axis_size("plane")
    place = jnp.stack([lax.axis_index(axis) for axis in ("z", "y", "core", "plane")])
    core = place[2]
    other_codes = exchange(shift_codes, "core", 2, 1)
    other_frames = exchange(frames, "core", 2, 1)
    *bands, staged = stage(tap_constants(block), frames, template)
    turns = [depth - 1, *range(1, depth - 1)]
    fetched = {turn: exchange(template, "z", depth, turn) for turn in turns}
    pieces = [template] + [fetched[turn] for turn in range(1, depth)]
    averages, correlation = [], 0.0
    volumes = vol_dev * depth * 4
    for p in range(pl_dev):
        work = (place, shift_codes, other_codes, staged[:, p], other_frames[:, p])
        sizes = (depth, block, own)
        (far_sums,) = warp_sums(*work, bands, template, 1, *sizes)
        taken = exchange(far_sums, "y", 2, 1)
        near_sums = warp_sums(*work, bands, far_sums, 0, *sizes)
        pieces, near_sums = lax.optimization_barrier((pieces, near_sums))
        near = jnp.concatenate([piece[:, p] for piece in pieces], axis=0)
        far = exchange(near, "y", 2, 1)
        sums = [
            one.astype(jnp.float32) + taken[step * own : (step + 1) * own].astype(jnp.float32)
            for step, one in enumerate(near_sums)
        ]
        moved = [exchange(sums[turn].astype(jnp.bfloat16), "z", depth, turn) for turn in turns]
        sizes = (planes, depth, own)
        part = lag_windows(*work, near, near_sums[:1], 0, *sizes)
        found, *given = lag_windows(*work, far, part, 1, *sizes)
        found, moved = lax.optimization_barrier((found, moved))
        total = sum((one.astype(jnp.float32) for one in moved), sums[0])
        averages.append(total * (1.0 / volumes))
        for turn, one in enumerate(given):
            found = found + exchange(one, "plane", planes, turn + 1).astype(jnp.float32)
        given = exchange(found[1].astype(jnp.bfloat16), "core", 2, 1)
        pair = (found[0], given.astype(jnp.float32))
        pair = [jnp.where(core == at, *pair).reshape(vol_dev, -1, 1, own, WIN * WIN) for at in (0, 1)]
        correlation += jnp.concatenate(pair, axis=2).reshape(vol_dev, -1, WIN * WIN)
    return (correlation, jnp.stack(averages, axis=1))


def solution(mesh):
    devices = mesh.devices.reshape(-1, 2, 2, mesh.shape["plane"])
    split = jax.sharding.Mesh(devices, ("z", "y", "core", "plane"))
    vols = ("z", "y", "core")
    in_specs = (P(vols, "plane", None, None), P(vols, "plane", None, None), P(vols, None, None))
    out_specs = (P(vols, "plane", None), P(vols, "plane", None, None))
    return jax.shard_map(
        on_device, mesh=split, in_specs=in_specs, out_specs=out_specs, check_vma=False
    )
```

```python
import functools
import math

import jax
import jax.numpy as jnp
import numpy as np
from jax import lax
from jax.experimental import pallas as pl
from jax.experimental.pallas import tpu as pltpu
from jax.sharding import PartitionSpec as P

SHIFT = 8
WIN = 16
TAPS = 8
SUB = 16
EDGE = 16
LANES = 128
VMEM_LIMIT = 24 * 1024 * 1024

full_turn = 2.0 * math.pi


def dft_constants(block_size):
    positions = np.arange(block_size)
    angles = full_turn * (np.outer(positions, positions) % block_size) / block_size
    cosine = np.cos(angles)
    sine = -np.sin(angles)
    half = block_size // 2 + 1
    rows = -(-half // 16) * 16
    row_table = np.zeros((2 * rows, block_size))
    row_table[:half] = cosine[:half]
    row_table[rows : rows + half] = sine[:half]
    col_table = np.block([[cosine, sine], [-sine, cosine]])
    weights = np.full((half,), 2.0)
    weights[0] = weights[half - 1] = 1.0
    span = 2 * SHIFT + WIN
    lags = np.arange(span) - SHIFT - WIN // 2
    turns = full_turn * (np.outer(lags, positions) % block_size) / block_size
    lag_cos, lag_sin = np.cos(turns), np.sin(turns)
    lag_table = np.zeros((2 * span, 2 * rows))
    lag_table[:span, :half] = lag_cos[:, :half] * weights
    lag_table[:span, rows : rows + half] = -lag_sin[:, :half] * weights
    lag_table[span:, :half] = lag_sin[:, :half] * weights
    lag_table[span:, rows : rows + half] = lag_cos[:, :half] * weights
    span_table = np.zeros((2 * block_size, LANES))
    span_table[:block_size, :span] = lag_cos.T
    span_table[block_size:, :span] = -lag_sin.T
    return tuple(
        jnp.asarray(table, jnp.bfloat16) for table in (row_table, col_table, lag_table, span_table)
    )


def tap_constants(block_size):
    offsets = np.arange(TAPS) - (TAPS // 2 - 1)
    spots = offsets[None, :] - np.arange(SUB)[:, None] / SUB
    raw_taps = np.sinc(spots) * np.sinc(spots / (TAPS // 2))
    taps = raw_taps / raw_taps.sum(axis=-1, keepdims=True)

    def band(inputs, outputs):
        at = inputs - outputs + TAPS // 2 - 1
        return np.where((at >= 0) & (at < TAPS), taps[:, np.clip(at, 0, TAPS - 1)], 0.0)

    lanes = np.arange(block_size)[None, :]
    inputs = np.arange(block_size + 3 * EDGE)[:, None] - EDGE - SHIFT
    outputs = np.arange(2 * EDGE)[:, None] - SHIFT
    spare = np.arange(LANES)[None, :] % (2 * EDGE)
    first = band(spare - 2 * EDGE, outputs) * (spare >= EDGE)
    last = band(spare + EDGE, outputs) * (spare < EDGE)
    tables = band(inputs, lanes), np.concatenate([first, last], axis=1)
    return [jnp.asarray(table, jnp.bfloat16) for table in tables]


def step_places(place_ref, step, across, own):
    z = place_ref[0] ^ step
    places = []
    for other in range(2):
        for one in range(own):
            index = ((2 * z + (place_ref[1] ^ other)) * 2 + place_ref[2]) * own + one
            places.append((index, index % across))
    return places


def step_band(place_ref, step, across, own):
    return (place_ref[0] ^ step) * (4 * own) // across


def stage_kernel(count, *refs):
    sources, targets = refs[:count], refs[count + 1 : 2 * count + 1]
    held, sems = refs[2 * count + 1 : 3 * count], refs[-1]
    copies = [
        pltpu.make_async_copy(source, target, sems.at[at])
        for at, (source, target) in enumerate(zip(sources, (*held, targets[-1])))
    ]
    for copy in copies:
        copy.start()
    for copy, one, target in zip(copies, held, targets):
        copy.wait()

        def widen(at, _):
            target[at] = one[at].astype(jnp.float32)
            return 0

        lax.fori_loop(0, one.shape[0], widen, 0)
    copies[-1].wait()


def stage(tables, frames, after):
    arrays = [
        pltpu.with_memory_space_constraint(one, pltpu.HBM) for one in (*tables, frames, after)
    ]
    count = len(tables) + 1
    vmem = pl.BlockSpec(memory_space=pltpu.VMEM)
    return pl.pallas_call(
        functools.partial(stage_kernel, count),
        out_shape=[jax.ShapeDtypeStruct(one.shape, jnp.float32) for one in tables]
        + [jax.ShapeDtypeStruct(frames.shape, frames.dtype)],
        in_specs=[pl.BlockSpec(memory_space=pltpu.HBM)] * count
        + [pl.BlockSpec(memory_space=pl.ANY)],
        out_specs=[vmem] * count,
        scratch_shapes=[pltpu.VMEM(one.shape, one.dtype) for one in tables]
        + [pltpu.SemaphoreType.DMA((count,))],
        compiler_params=pltpu.CompilerParams(vmem_limit_bytes=VMEM_LIMIT),
        cost_estimate=pl.CostEstimate(
            flops=0, bytes_accessed=2 * frames.nbytes, transcendentals=0
        ),
        name="stage",
    )(*arrays)


def warp_step(place_ref, step, other, code_refs, frame_refs, band_refs, down, across, block, own):
    cols_ref, edges_ref = band_refs
    band = step_band(place_ref, step, across, own)
    row = pl.multiple_of(band * block, block)
    row_above = pl.multiple_of(jnp.maximum(row - EDGE, 0), EDGE)
    row_below = pl.multiple_of(jnp.minimum(row + block, down * block - EDGE), EDGE)
    zero = jnp.zeros((EDGE, LANES), jnp.bfloat16)
    gap = jnp.zeros((block - 2 * EDGE, LANES), jnp.bfloat16)
    no_tile = jnp.zeros((block + 2 * EDGE, block), jnp.bfloat16)
    volumes = [
        (codes, frames, v)
        for codes, frames in zip(code_refs, frame_refs)
        for v in range(frames.shape[0])
    ]
    many = len(volumes)
    per_tile = LANES // (2 * EDGE)
    lane = lax.broadcasted_iota(jnp.int32, (EDGE, LANES), 1) // (2 * EDGE)

    def tile(frames, v, at):
        lanes = pl.ds(pl.multiple_of(at * block, block), block)
        above = jnp.where(band > 0, frames[v, pl.ds(row_above, EDGE), lanes], zero)
        below = jnp.where(band < down - 1, frames[v, pl.ds(row_below, EDGE), lanes], zero)
        return jnp.concatenate([frames[v, pl.ds(row, block), lanes], below, above], axis=0)

    places = step_places(place_ref, step, across, own)[other * own : (other + 1) * own]
    start = places[0][1]
    tiles = []
    for _, frames, v in volumes:
        left = jnp.where(start > 0, tile(frames, v, jnp.maximum(start - 1, 0)), no_tile)
        right = jnp.where(
            start + own < across, tile(frames, v, jnp.minimum(start + own, across - 1)), no_tile
        )
        tiles.append([left] + [tile(frames, v, start + one) for one in range(own)] + [right])
    totals = []
    for one, (index, _) in enumerate(places):
        row_tiles, partials, edges = [], [], []
        firsts, lasts = [], []
        for order, (codes, _, v) in enumerate(volumes):
            row_code, col_code = codes[v, 0, index], codes[v, 1, index]
            left, middle, right = tiles[order][one : one + 3]
            sides = jnp.concatenate([right[:, : block // 2], left[:, block // 2 :]], axis=1)
            col_start = SHIFT - (col_code >> 4)
            cols = cols_ref[col_code & (SUB - 1), pl.ds(col_start, block + 2 * EDGE), :]
            cols = cols.astype(jnp.bfloat16)
            partial = jnp.dot(
                jnp.concatenate([middle, sides], axis=1),
                jnp.concatenate([cols[EDGE:], gap, cols[:EDGE]], axis=0),
                preferred_element_type=jnp.float32,
            ).astype(jnp.bfloat16)
            partials.append(partial[:block])
            edges.append(partial[block:])
            back = -row_code
            back_start = SHIFT + EDGE - (back >> 4)
            rows = cols_ref[back & (SUB - 1), pl.ds(back_start, block), :]
            row_tiles.append(rows.astype(jnp.bfloat16))
            row_start, step_at = SHIFT + (row_code >> 4), row_code & (SUB - 1)
            first = edges_ref[step_at, pl.ds(row_start, EDGE), :]
            last = edges_ref[step_at, pl.ds(2 * EDGE + row_start, EDGE), :]
            if order % per_tile:
                first = jnp.where(lane == order % per_tile, first, firsts.pop())
                last = jnp.where(lane == order % per_tile, last, lasts.pop())
            firsts.append(first)
            lasts.append(last)
        for first, last in zip(firsts, lasts):
            both = [first.astype(jnp.bfloat16), gap, last.astype(jnp.bfloat16)]
            row_tiles.append(jnp.concatenate(both, axis=0))
        deep = many * (block + 2 * EDGE)
        total = jnp.dot(
            jnp.concatenate(row_tiles, axis=1)[:, :deep],
            jnp.concatenate(partials + edges, axis=0),
            preferred_element_type=jnp.float32,
        )
        totals.append(total.astype(jnp.bfloat16))
    return totals


def warp_kernel(down, across, block, own, other, *refs):
    place_ref, *code_refs = refs[:3]
    frame_refs, band_refs, out_refs = refs[3:5], refs[5:7], refs[8:]
    depth = out_refs[0].shape[0] // own if other else len(out_refs)
    for step in range(depth):
        totals = warp_step(
            place_ref, step, other, code_refs, frame_refs, band_refs, down, across, block, own
        )
        for one, total in enumerate(totals):
            if other:
                out_refs[0][step * own + one] = total
            else:
                out_refs[step][one] = total


def warp_sums(
    place, codes, other_codes, frames, other_frames, bands, after, other, depth, block, own
):
    vols, rows, cols = frames.shape
    down, across = rows // block, cols // block
    smem = pl.BlockSpec(memory_space=pltpu.SMEM)
    vmem = pl.BlockSpec(memory_space=pltpu.VMEM)
    if other:
        out_shape = [jax.ShapeDtypeStruct((depth * own, block, block), jnp.bfloat16)]
    else:
        out_shape = [jax.ShapeDtypeStruct((own, block, block), jnp.bfloat16)] * depth
    return pl.pallas_call(
        functools.partial(warp_kernel, down, across, block, own, other),
        out_shape=out_shape,
        in_specs=[smem] * 3
        + [vmem] * (2 + len(bands))
        + [pl.BlockSpec(memory_space=pl.ANY)],
        out_specs=[vmem] * len(out_shape),
        compiler_params=pltpu.CompilerParams(vmem_limit_bytes=VMEM_LIMIT),
        cost_estimate=pl.CostEstimate(
            flops=2 * vols * rows * cols * block * 8,
            bytes_accessed=vols * rows * cols * 4 + rows * cols,
            transcendentals=0,
        ),
        name="warp",
    )(place, codes, other_codes, frames, other_frames, *bands, after)


def spectrum_kernel(vols, across, block, own, planes, depth, other, *refs):
    place_ref, codes_ref, other_codes_ref, row_ref, col_ref, lag_ref, span_ref = refs[:7]
    frames_ref, other_frames_ref, template_ref = refs[7:10]
    all_cross, all_sums = refs[-2:]
    ready = []
    if other:
        found_ref, spectra_ref, out_refs, found = refs[10], refs[11], refs[12:-3], refs[-3]
        found[...] = found_ref[...]
        ready.append(spectra_ref)
    else:
        found, spectra_ref = refs[11:13]

    row_table = row_ref[...]
    col_table = col_ref[...]
    lag_table = lag_ref[...]
    half = row_table.shape[0] // 2
    kept = -(-(block // 2 + 1) // 8) * 8
    span = lag_table.shape[0] // 2
    top = lax.broadcasted_iota(jnp.int32, (8, LANES), 0) == 0
    volumes = [(codes_ref, frames_ref, v) for v in range(vols)]
    volumes += [(other_codes_ref, other_frames_ref, v) for v in range(vols)]
    many = len(volumes)
    local = 2 * own
    no_rows = jnp.zeros((half - kept, LANES), jnp.float32)

    def find_places(half_step, row):
        places = []
        for step in (2 * half_step, 2 * half_step + 1):
            band = step_band(place_ref, step, across, own)
            band_rows = pl.ds(pl.multiple_of(band * block, block), block)
            chosen = step_places(place_ref, step, across, own)[row * own : (row + 1) * own]
            for one, (index, at) in enumerate(chosen):
                lanes = pl.ds(pl.multiple_of(at * block, block), block)
                places.append((index, band_rows, lanes, step * own + one))
        return places

    def frame_sources(pair_places):
        return [
            [frames[v, rows, lanes] for _, rows, lanes, _ in pair_places]
            for _, frames, v in volumes
        ]

    def transform(sources):
        parts = []
        for source in sources:
            rows = jnp.dot(
                row_table, jnp.concatenate(source, axis=1), preferred_element_type=jnp.float32
            ).astype(jnp.bfloat16)
            for side in range(2):
                lanes = slice(side * block, (side + 1) * block)
                parts.append(jnp.concatenate([rows[:half, lanes], rows[half:, lanes]], axis=1))
        return jnp.dot(
            jnp.concatenate(parts, axis=0), col_table, preferred_element_type=jnp.float32
        )

    for half_step in range(depth // 2):
        cross, sums = all_cross.at[half_step], all_sums.at[half_step]
        places = find_places(half_step, other)
        for pair in range(local // 2):
            pair_places = places[2 * pair : 2 * pair + 2]
            sources = [[template_ref[at] for _, _, _, at in pair_places]]
            sources += frame_sources(pair_places)
            if ready and half_step == 0:
                spectra = jnp.concatenate([transform(sources[:1]), ready[0][pair]], axis=0)
            else:
                spectra = transform(sources)
            temp = spectra[: 2 * half].astype(jnp.bfloat16).astype(jnp.float32)
            for order in range(many):
                for side in range(2):
                    one = (2 * pair + side) * many + order
                    base = (2 * (order + 1) + side) * half
                    total = jnp.zeros((8, LANES), jnp.float32)
                    for row in range(0, kept, 8):
                        at = side * half + row
                        temp_real = temp[at : at + 8, :block]
                        temp_imag = temp[at : at + 8, block:]
                        real = spectra[base + row : base + row + 8, :block]
                        imag = spectra[base + row : base + row + 8, block:]
                        cross_real = real * temp_real + imag * temp_imag
                        cross_imag = imag * temp_real - real * temp_imag
                        power = cross_real * cross_real + cross_imag * cross_imag
                        magnitude = power * lax.rsqrt(jnp.maximum(power, 1e-36))
                        cross[one, row : row + 8, :] = cross_real
                        cross[one, kept + row : kept + row + 8, :] = cross_imag
                        cross[one, 2 * kept + row : 2 * kept + row + 8, :] = magnitude
                        if row == 0:
                            once = jnp.where(top, magnitude, 0.0)
                        elif row == block // 2:
                            once += magnitude
                        total += magnitude
                    sums[one] = jnp.sum(total + total - once, axis=0, keepdims=True)

        means = jnp.sum(sums[...], axis=2, keepdims=True) * (1.0 / (block * block)) + 1e-06
        lag_sums = []
        for pair in range(local // 2):
            for order in range(many):
                norms = []
                for side in range(2):
                    one = (2 * pair + side) * many + order
                    scale = pl.reciprocal(cross[one, 2 * kept :, :] + means[one], approx=True)
                    norms.append(
                        jnp.concatenate(
                            [
                                cross[one, :kept, :] * scale,
                                no_rows,
                                cross[one, kept : 2 * kept, :] * scale,
                                no_rows,
                            ],
                            axis=0,
                        ).astype(jnp.bfloat16)
                    )
                lag_rows = jnp.dot(
                    lag_table, jnp.concatenate(norms, axis=1), preferred_element_type=jnp.float32
                ).astype(jnp.bfloat16)
                for side in range(2):
                    lanes = slice(side * block, (side + 1) * block)
                    lag_sums.append(
                        jnp.concatenate([lag_rows[:span, lanes], lag_rows[span:, lanes]], axis=1)
                    )
        lags = jnp.dot(
            jnp.concatenate(lag_sums, axis=0), span_ref[...], preferred_element_type=jnp.float32
        )
        for pair in range(local // 2):
            for order, (codes, _, v) in enumerate(volumes):
                for side in range(2):
                    index = places[2 * pair + side][0]
                    row_shift = codes[v, 0, index] >> 4
                    col_shift = codes[v, 1, index] >> 4
                    at = (pair * many + order) * 2 + side
                    one = lags[at * span : (at + 1) * span]
                    one = pltpu.roll(one, span - SHIFT - row_shift, 0)[:WIN]
                    at = index // (2 * own) * own + (2 * pair + side) % own
                    found[order, pl.ds(pl.multiple_of(at * WIN, WIN), WIN), :] = pltpu.roll(
                        one, LANES - SHIFT - col_shift, 1
                    )

    if not other:
        places = find_places(0, 1)
        for pair in range(local // 2):
            spectra_ref[pair] = transform(frame_sources(places[2 * pair : 2 * pair + 2]))
        return

    share = (found.shape[1] // WIN - 1) // planes
    per_tile = LANES // WIN
    lane = lax.broadcasted_iota(jnp.int32, (share, LANES), 1) // WIN
    for turn, out_ref in enumerate(out_refs):
        plane = place_ref[3] ^ turn
        for order in range(many):
            for tile in range(WIN // per_tile):
                total = jnp.zeros((share, LANES), jnp.float32)
                for part in range(per_tile):
                    start = plane * share * WIN + tile * per_tile + part
                    one = found[order, pl.ds(start, share, stride=WIN), :]
                    if part:
                        one = pltpu.roll(one, part * WIN, 1)
                    total = jnp.where(lane == part, one, total)
                lanes = slice(tile * LANES, (tile + 1) * LANES)
                total = (total * (1.0 / block)).astype(out_ref.dtype)
                out_ref[order // vols, order % vols, :, lanes] = total


def lag_windows(
    place, codes, other_codes, frames, other_frames, template, more, other, planes, depth, own
):
    vols, rows, cols = frames.shape
    block = template.shape[-1]
    down, across = rows // block, cols // block
    tables = dft_constants(block)
    kept = -(-(block // 2 + 1) // 8) * 8
    smem = pl.BlockSpec(memory_space=pltpu.SMEM)
    vmem = pl.BlockSpec(memory_space=pltpu.VMEM)
    blocks = down * across // 2
    many = 2 * vols * 2 * own
    found = jax.ShapeDtypeStruct((2 * vols, (blocks + 1) * WIN, LANES), jnp.float32)
    if other:
        out = (2, vols, blocks // planes, WIN * WIN)
        out_shape = [jax.ShapeDtypeStruct(out, jnp.float32)]
        out_shape += [jax.ShapeDtypeStruct(out, jnp.bfloat16)] * (planes - 1)
        scratch_shapes = [pltpu.VMEM(found.shape, found.dtype)]
        last = [vmem, vmem]
    else:
        half = tables[0].shape[0] // 2
        spectra = (own, 2 * vols * 2 * half, 2 * block)
        out_shape = [found, jax.ShapeDtypeStruct(spectra, jnp.float32)]
        scratch_shapes = []
        last = [pl.BlockSpec(memory_space=pl.ANY)]
    return pl.pallas_call(
        functools.partial(spectrum_kernel, vols, across, block, own, planes, depth, other),
        out_shape=out_shape,
        in_specs=[smem] * 3 + [vmem] * (len(tables) + 3) + last,
        out_specs=[vmem] * len(out_shape),
        scratch_shapes=scratch_shapes
        + [
            pltpu.VMEM((depth // 2, many, 3 * kept, LANES), jnp.float32),
            pltpu.VMEM((depth // 2, many, 1, LANES), jnp.float32),
        ],
        compiler_params=pltpu.CompilerParams(vmem_limit_bytes=VMEM_LIMIT),
        cost_estimate=pl.CostEstimate(
            flops=2 * 3 * rows * cols * block * (2 if other else 8),
            bytes_accessed=vols * rows * cols * 4 + rows * cols,
            transcendentals=0,
        ),
        name="lag_windows",
    )(place, codes, other_codes, *tables, frames, other_frames, template, *more)


def exchange(value, axes, size, turn):
    return lax.ppermute(value, axes, [(at, at ^ turn) for at in range(size)])


def on_device(frames, template, shift_codes):
    vol_dev, pl_dev, img_rows, img_cols = frames.shape
    own, block = template.shape[0], template.shape[-1]
    depth = lax.axis_size("z")
    planes = lax.axis_size("plane")
    place = jnp.stack([lax.axis_index(axis) for axis in ("z", "y", "core", "plane")])
    core = place[2]
    other_codes = exchange(shift_codes, "core", 2, 1)
    other_frames = exchange(frames, "core", 2, 1)
    *bands, staged = stage(tap_constants(block), frames, template)
    turns = [depth - 1, *range(1, depth - 1)]
    fetched = {turn: exchange(template, "z", depth, turn) for turn in turns}
    pieces = [template] + [fetched[turn] for turn in range(1, depth)]
    averages, correlation = [], 0.0
    volumes = vol_dev * depth * 4
    for p in range(pl_dev):
        work = (place, shift_codes, other_codes, staged[:, p], other_frames[:, p])
        sizes = (depth, block, own)
        (far_sums,) = warp_sums(*work, bands, template, 1, *sizes)
        taken = exchange(far_sums, "y", 2, 1)
        near_sums = warp_sums(*work, bands, far_sums, 0, *sizes)
        pieces, near_sums = lax.optimization_barrier((pieces, near_sums))
        near = jnp.concatenate([piece[:, p] for piece in pieces], axis=0)
        far = exchange(near, "y", 2, 1)
        sums = [
            one.astype(jnp.float32) + taken[step * own : (step + 1) * own].astype(jnp.float32)
            for step, one in enumerate(near_sums)
        ]
        moved = [exchange(sums[turn].astype(jnp.bfloat16), "z", depth, turn) for turn in turns]
        sizes = (planes, depth, own)
        part = lag_windows(*work, near, near_sums[:1], 0, *sizes)
        found, *given = lag_windows(*work, far, part, 1, *sizes)
        found, moved = lax.optimization_barrier((found, moved))
        total = sum((one.astype(jnp.float32) for one in moved), sums[0])
        averages.append(total * (1.0 / volumes))
        for turn, one in enumerate(given):
            found = found + exchange(one, "plane", planes, turn + 1).astype(jnp.float32)
        given = exchange(found[1].astype(jnp.bfloat16), "core", 2, 1)
        pair = (found[0], given.astype(jnp.float32))
        pair = [jnp.where(core == at, *pair).reshape(vol_dev, -1, 1, own, WIN * WIN) for at in (0, 1)]
        correlation += jnp.concatenate(pair, axis=2).reshape(vol_dev, -1, WIN * WIN)
    return (correlation, jnp.stack(averages, axis=1))


def solution(mesh):
    devices = mesh.devices.reshape(-1, 2, 2, mesh.shape["plane"])
    split = jax.sharding.Mesh(devices, ("z", "y", "core", "plane"))
    vols = ("z", "y", "core")
    in_specs = (P(vols, "plane", None, None), P(vols, "plane", None, None), P(vols, None, None))
    out_specs = (P(vols, "plane", None), P(vols, "plane", None, None))
    return jax.shard_map(
        on_device, mesh=split, in_specs=in_specs, out_specs=out_specs, check_vma=False
    )
```

```python
import functools
import math

import jax
import jax.numpy as jnp
import numpy as np
from jax import lax
from jax.experimental import pallas as pl
from jax.experimental.pallas import tpu as pltpu
from jax.sharding import PartitionSpec as P

SHIFT = 8
WIN = 16
TAPS = 8
SUB = 16
EDGE = 16
LANES = 128
VMEM_LIMIT = 24 * 1024 * 1024

full_turn = 2.0 * math.pi


def dft_constants(block_size):
    positions = np.arange(block_size)
    angles = full_turn * (np.outer(positions, positions) % block_size) / block_size
    cosine = np.cos(angles)
    sine = -np.sin(angles)
    half = block_size // 2 + 1
    rows = -(-half // 16) * 16
    row_table = np.zeros((2 * rows, block_size))
    row_table[:half] = cosine[:half]
    row_table[rows : rows + half] = sine[:half]
    col_table = np.block([[cosine, sine], [-sine, cosine]])
    weights = np.full((half,), 2.0)
    weights[0] = weights[half - 1] = 1.0
    span = 2 * SHIFT + WIN
    lags = np.arange(span) - SHIFT - WIN // 2
    turns = full_turn * (np.outer(lags, positions) % block_size) / block_size
    lag_cos, lag_sin = np.cos(turns), np.sin(turns)
    lag_table = np.zeros((2 * span, 2 * rows))
    lag_table[:span, :half] = lag_cos[:, :half] * weights
    lag_table[:span, rows : rows + half] = -lag_sin[:, :half] * weights
    lag_table[span:, :half] = lag_sin[:, :half] * weights
    lag_table[span:, rows : rows + half] = lag_cos[:, :half] * weights
    span_table = np.zeros((2 * block_size, LANES))
    span_table[:block_size, :span] = lag_cos.T
    span_table[block_size:, :span] = -lag_sin.T
    return tuple(
        jnp.asarray(table, jnp.bfloat16) for table in (row_table, col_table, lag_table, span_table)
    )


def tap_constants(block_size):
    offsets = np.arange(TAPS) - (TAPS // 2 - 1)
    spots = offsets[None, :] - np.arange(SUB)[:, None] / SUB
    raw_taps = np.sinc(spots) * np.sinc(spots / (TAPS // 2))
    taps = raw_taps / raw_taps.sum(axis=-1, keepdims=True)

    def band(inputs, outputs):
        at = inputs - outputs + TAPS // 2 - 1
        return np.where((at >= 0) & (at < TAPS), taps[:, np.clip(at, 0, TAPS - 1)], 0.0)

    lanes = np.arange(block_size)[None, :]
    inputs = np.arange(block_size + 3 * EDGE)[:, None] - EDGE - SHIFT
    outputs = np.arange(2 * EDGE)[:, None] - SHIFT
    spare = np.arange(LANES)[None, :] % (2 * EDGE)
    first = band(spare - 2 * EDGE, outputs) * (spare >= EDGE)
    last = band(spare + EDGE, outputs) * (spare < EDGE)
    tables = band(inputs, lanes), np.concatenate([first, last], axis=1)
    return [jnp.asarray(table, jnp.bfloat16) for table in tables]


def step_places(place_ref, step, across, own):
    z = place_ref[0] ^ step
    places = []
    for other in range(2):
        for one in range(own):
            index = ((2 * z + (place_ref[1] ^ other)) * 2 + place_ref[2]) * own + one
            places.append((index, index % across))
    return places


def step_band(place_ref, step, across, own):
    return (place_ref[0] ^ step) * (4 * own) // across


def stage_kernel(count, *refs):
    sources, targets = refs[:count], refs[count + 1 : 2 * count + 1]
    held, sems = refs[2 * count + 1 : 3 * count], refs[-1]
    copies = [
        pltpu.make_async_copy(source, target, sems.at[at])
        for at, (source, target) in enumerate(zip(sources, (*held, targets[-1])))
    ]
    for copy in copies:
        copy.start()
    for copy, one, target in zip(copies, held, targets):
        copy.wait()

        def widen(at, _):
            target[at] = one[at].astype(jnp.float32)
            return 0

        lax.fori_loop(0, one.shape[0], widen, 0)
    copies[-1].wait()


def stage(tables, frames, after):
    arrays = [
        pltpu.with_memory_space_constraint(one, pltpu.HBM) for one in (*tables, frames, after)
    ]
    count = len(tables) + 1
    vmem = pl.BlockSpec(memory_space=pltpu.VMEM)
    return pl.pallas_call(
        functools.partial(stage_kernel, count),
        out_shape=[jax.ShapeDtypeStruct(one.shape, jnp.float32) for one in tables]
        + [jax.ShapeDtypeStruct(frames.shape, frames.dtype)],
        in_specs=[pl.BlockSpec(memory_space=pltpu.HBM)] * count
        + [pl.BlockSpec(memory_space=pl.ANY)],
        out_specs=[vmem] * count,
        scratch_shapes=[pltpu.VMEM(one.shape, one.dtype) for one in tables]
        + [pltpu.SemaphoreType.DMA((count,))],
        compiler_params=pltpu.CompilerParams(vmem_limit_bytes=VMEM_LIMIT),
        cost_estimate=pl.CostEstimate(
            flops=0, bytes_accessed=2 * frames.nbytes, transcendentals=0
        ),
        name="stage",
    )(*arrays)


def warp_step(place_ref, step, other, code_refs, frame_refs, band_refs, down, across, block, own):
    cols_ref, edges_ref = band_refs
    band = step_band(place_ref, step, across, own)
    row = pl.multiple_of(band * block, block)
    row_above = pl.multiple_of(jnp.maximum(row - EDGE, 0), EDGE)
    row_below = pl.multiple_of(jnp.minimum(row + block, down * block - EDGE), EDGE)
    zero = jnp.zeros((EDGE, LANES), jnp.bfloat16)
    gap = jnp.zeros((block - 2 * EDGE, LANES), jnp.bfloat16)
    no_tile = jnp.zeros((block + 2 * EDGE, block), jnp.bfloat16)
    volumes = [
        (codes, frames, v)
        for codes, frames in zip(code_refs, frame_refs)
        for v in range(frames.shape[0])
    ]
    many = len(volumes)
    per_tile = LANES // (2 * EDGE)
    lane = lax.broadcasted_iota(jnp.int32, (EDGE, LANES), 1) // (2 * EDGE)

    def tile(frames, v, at):
        lanes = pl.ds(pl.multiple_of(at * block, block), block)
        above = jnp.where(band > 0, frames[v, pl.ds(row_above, EDGE), lanes], zero)
        below = jnp.where(band < down - 1, frames[v, pl.ds(row_below, EDGE), lanes], zero)
        return jnp.concatenate([frames[v, pl.ds(row, block), lanes], below, above], axis=0)

    places = step_places(place_ref, step, across, own)[other * own : (other + 1) * own]
    start = places[0][1]
    tiles = []
    for _, frames, v in volumes:
        left = jnp.where(start > 0, tile(frames, v, jnp.maximum(start - 1, 0)), no_tile)
        right = jnp.where(
            start + own < across, tile(frames, v, jnp.minimum(start + own, across - 1)), no_tile
        )
        tiles.append([left] + [tile(frames, v, start + one) for one in range(own)] + [right])
    totals = []
    for one, (index, _) in enumerate(places):
        row_tiles, partials, edges = [], [], []
        firsts, lasts = [], []
        for order, (codes, _, v) in enumerate(volumes):
            row_code, col_code = codes[v, 0, index], codes[v, 1, index]
            left, middle, right = tiles[order][one : one + 3]
            sides = jnp.concatenate([right[:, : block // 2], left[:, block // 2 :]], axis=1)
            col_start = SHIFT - (col_code >> 4)
            cols = cols_ref[col_code & (SUB - 1), pl.ds(col_start, block + 2 * EDGE), :]
            cols = cols.astype(jnp.bfloat16)
            partial = jnp.dot(
                jnp.concatenate([middle, sides], axis=1),
                jnp.concatenate([cols[EDGE:], gap, cols[:EDGE]], axis=0),
                preferred_element_type=jnp.float32,
            ).astype(jnp.bfloat16)
            partials.append(partial[:block])
            edges.append(partial[block:])
            back = -row_code
            back_start = SHIFT + EDGE - (back >> 4)
            rows = cols_ref[back & (SUB - 1), pl.ds(back_start, block), :]
            row_tiles.append(rows.astype(jnp.bfloat16))
            row_start, step_at = SHIFT + (row_code >> 4), row_code & (SUB - 1)
            first = edges_ref[step_at, pl.ds(row_start, EDGE), :]
            last = edges_ref[step_at, pl.ds(2 * EDGE + row_start, EDGE), :]
            if order % per_tile:
                first = jnp.where(lane == order % per_tile, first, firsts.pop())
                last = jnp.where(lane == order % per_tile, last, lasts.pop())
            firsts.append(first)
            lasts.append(last)
        for first, last in zip(firsts, lasts):
            both = [first.astype(jnp.bfloat16), gap, last.astype(jnp.bfloat16)]
            row_tiles.append(jnp.concatenate(both, axis=0))
        deep = many * (block + 2 * EDGE)
        total = jnp.dot(
            jnp.concatenate(row_tiles, axis=1)[:, :deep],
            jnp.concatenate(partials + edges, axis=0),
            preferred_element_type=jnp.float32,
        )
        totals.append(total.astype(jnp.bfloat16))
    return totals


def warp_kernel(down, across, block, own, other, *refs):
    place_ref, *code_refs = refs[:3]
    frame_refs, band_refs, out_refs = refs[3:5], refs[5:7], refs[8:]
    depth = out_refs[0].shape[0] // own if other else len(out_refs)
    for step in range(depth):
        totals = warp_step(
            place_ref, step, other, code_refs, frame_refs, band_refs, down, across, block, own
        )
        for one, total in enumerate(totals):
            if other:
                out_refs[0][step * own + one] = total
            else:
                out_refs[step][one] = total


def warp_sums(
    place, codes, other_codes, frames, other_frames, bands, after, other, depth, block, own
):
    vols, rows, cols = frames.shape
    down, across = rows // block, cols // block
    smem = pl.BlockSpec(memory_space=pltpu.SMEM)
    vmem = pl.BlockSpec(memory_space=pltpu.VMEM)
    if other:
        out_shape = [jax.ShapeDtypeStruct((depth * own, block, block), jnp.bfloat16)]
    else:
        out_shape = [jax.ShapeDtypeStruct((own, block, block), jnp.bfloat16)] * depth
    return pl.pallas_call(
        functools.partial(warp_kernel, down, across, block, own, other),
        out_shape=out_shape,
        in_specs=[smem] * 3
        + [vmem] * (2 + len(bands))
        + [pl.BlockSpec(memory_space=pl.ANY)],
        out_specs=[vmem] * len(out_shape),
        compiler_params=pltpu.CompilerParams(vmem_limit_bytes=VMEM_LIMIT),
        cost_estimate=pl.CostEstimate(
            flops=2 * vols * rows * cols * block * 8,
            bytes_accessed=vols * rows * cols * 4 + rows * cols,
            transcendentals=0,
        ),
        name="warp",
    )(place, codes, other_codes, frames, other_frames, *bands, after)


def spectrum_kernel(vols, across, block, own, planes, depth, other, *refs):
    place_ref, codes_ref, other_codes_ref, row_ref, col_ref, lag_ref, span_ref = refs[:7]
    frames_ref, other_frames_ref, template_ref = refs[7:10]
    all_cross, all_sums = refs[-2:]
    ready = []
    if other:
        found_ref, spectra_ref, out_refs, found = refs[10], refs[11], refs[12:-3], refs[-3]
        found[...] = found_ref[...]
        ready.append(spectra_ref)
    else:
        found, spectra_ref = refs[11:13]

    row_table = row_ref[...]
    col_table = col_ref[...]
    lag_table = lag_ref[...]
    half = row_table.shape[0] // 2
    kept = -(-(block // 2 + 1) // 8) * 8
    span = lag_table.shape[0] // 2
    top = lax.broadcasted_iota(jnp.int32, (8, LANES), 0) == 0
    volumes = [(codes_ref, frames_ref, v) for v in range(vols)]
    volumes += [(other_codes_ref, other_frames_ref, v) for v in range(vols)]
    many = len(volumes)
    local = 2 * own
    no_rows = jnp.zeros((half - kept, LANES), jnp.float32)

    def find_places(half_step, row):
        places = []
        for step in (2 * half_step, 2 * half_step + 1):
            band = step_band(place_ref, step, across, own)
            band_rows = pl.ds(pl.multiple_of(band * block, block), block)
            chosen = step_places(place_ref, step, across, own)[row * own : (row + 1) * own]
            for one, (index, at) in enumerate(chosen):
                lanes = pl.ds(pl.multiple_of(at * block, block), block)
                places.append((index, band_rows, lanes, step * own + one))
        return places

    def frame_sources(pair_places):
        return [
            [frames[v, rows, lanes] for _, rows, lanes, _ in pair_places]
            for _, frames, v in volumes
        ]

    def transform(sources):
        parts = []
        for source in sources:
            rows = jnp.dot(
                row_table, jnp.concatenate(source, axis=1), preferred_element_type=jnp.float32
            ).astype(jnp.bfloat16)
            for side in range(2):
                lanes = slice(side * block, (side + 1) * block)
                parts.append(jnp.concatenate([rows[:half, lanes], rows[half:, lanes]], axis=1))
        return jnp.dot(
            jnp.concatenate(parts, axis=0), col_table, preferred_element_type=jnp.float32
        )

    for half_step in range(depth // 2):
        cross, sums = all_cross.at[half_step], all_sums.at[half_step]
        places = find_places(half_step, other)
        for pair in range(local // 2):
            pair_places = places[2 * pair : 2 * pair + 2]
            sources = [[template_ref[at] for _, _, _, at in pair_places]]
            sources += frame_sources(pair_places)
            if ready and half_step == 0:
                spectra = jnp.concatenate([transform(sources[:1]), ready[0][pair]], axis=0)
            else:
                spectra = transform(sources)
            temp = spectra[: 2 * half].astype(jnp.bfloat16).astype(jnp.float32)
            for order in range(many):
                for side in range(2):
                    one = (2 * pair + side) * many + order
                    base = (2 * (order + 1) + side) * half
                    total = jnp.zeros((8, LANES), jnp.float32)
                    for row in range(0, kept, 8):
                        at = side * half + row
                        temp_real = temp[at : at + 8, :block]
                        temp_imag = temp[at : at + 8, block:]
                        real = spectra[base + row : base + row + 8, :block]
                        imag = spectra[base + row : base + row + 8, block:]
                        cross_real = real * temp_real + imag * temp_imag
                        cross_imag = imag * temp_real - real * temp_imag
                        power = cross_real * cross_real + cross_imag * cross_imag
                        magnitude = power * lax.rsqrt(jnp.maximum(power, 1e-36))
                        cross[one, row : row + 8, :] = cross_real
                        cross[one, kept + row : kept + row + 8, :] = cross_imag
                        cross[one, 2 * kept + row : 2 * kept + row + 8, :] = magnitude
                        if row == 0:
                            once = jnp.where(top, magnitude, 0.0)
                        elif row == block // 2:
                            once += magnitude
                        total += magnitude
                    sums[one] = jnp.sum(total + total - once, axis=0, keepdims=True)

        lag_sums = []
        for pair in range(local // 2):
            first = 2 * pair * many
            magnitudes = jnp.sum(sums[first : first + 2 * many], axis=2, keepdims=True)
            means = magnitudes * (1.0 / (block * block)) + 1e-06
            for order in range(many):
                norms = []
                for side in range(2):
                    one = (2 * pair + side) * many + order
                    scale = pl.reciprocal(cross[one, 2 * kept :, :] + means[one - first], approx=True)
                    norms.append(
                        jnp.concatenate(
                            [
                                cross[one, :kept, :] * scale,
                                no_rows,
                                cross[one, kept : 2 * kept, :] * scale,
                                no_rows,
                            ],
                            axis=0,
                        ).astype(jnp.bfloat16)
                    )
                lag_rows = jnp.dot(
                    lag_table, jnp.concatenate(norms, axis=1), preferred_element_type=jnp.float32
                ).astype(jnp.bfloat16)
                for side in range(2):
                    lanes = slice(side * block, (side + 1) * block)
                    lag_sums.append(
                        jnp.concatenate([lag_rows[:span, lanes], lag_rows[span:, lanes]], axis=1)
                    )
        lags = jnp.dot(
            jnp.concatenate(lag_sums, axis=0), span_ref[...], preferred_element_type=jnp.float32
        )
        for pair in range(local // 2):
            for order, (codes, _, v) in enumerate(volumes):
                for side in range(2):
                    index = places[2 * pair + side][0]
                    row_shift = codes[v, 0, index] >> 4
                    col_shift = codes[v, 1, index] >> 4
                    at = (pair * many + order) * 2 + side
                    one = lags[at * span : (at + 1) * span]
                    one = pltpu.roll(one, span - SHIFT - row_shift, 0)[:WIN]
                    at = index // (2 * own) * own + (2 * pair + side) % own
                    found[order, pl.ds(pl.multiple_of(at * WIN, WIN), WIN), :] = pltpu.roll(
                        one, LANES - SHIFT - col_shift, 1
                    )

    if not other:
        places = find_places(0, 1)
        for pair in range(local // 2):
            spectra_ref[pair] = transform(frame_sources(places[2 * pair : 2 * pair + 2]))
        return

    share = (found.shape[1] // WIN - 1) // planes
    per_tile = LANES // WIN
    lane = lax.broadcasted_iota(jnp.int32, (share, LANES), 1) // WIN
    for turn, out_ref in enumerate(out_refs):
        plane = place_ref[3] ^ turn
        for order in range(many):
            for tile in range(WIN // per_tile):
                total = jnp.zeros((share, LANES), jnp.float32)
                for part in range(per_tile):
                    start = plane * share * WIN + tile * per_tile + part
                    one = found[order, pl.ds(start, share, stride=WIN), :]
                    if part:
                        one = pltpu.roll(one, part * WIN, 1)
                    total = jnp.where(lane == part, one, total)
                lanes = slice(tile * LANES, (tile + 1) * LANES)
                total = (total * (1.0 / block)).astype(out_ref.dtype)
                out_ref[order // vols, order % vols, :, lanes] = total


def lag_windows(
    place, codes, other_codes, frames, other_frames, template, more, other, planes, depth, own
):
    vols, rows, cols = frames.shape
    block = template.shape[-1]
    down, across = rows // block, cols // block
    tables = dft_constants(block)
    kept = -(-(block // 2 + 1) // 8) * 8
    smem = pl.BlockSpec(memory_space=pltpu.SMEM)
    vmem = pl.BlockSpec(memory_space=pltpu.VMEM)
    blocks = down * across // 2
    many = 2 * vols * 2 * own
    found = jax.ShapeDtypeStruct((2 * vols, (blocks + 1) * WIN, LANES), jnp.float32)
    if other:
        out = (2, vols, blocks // planes, WIN * WIN)
        out_shape = [jax.ShapeDtypeStruct(out, jnp.float32)]
        out_shape += [jax.ShapeDtypeStruct(out, jnp.bfloat16)] * (planes - 1)
        scratch_shapes = [pltpu.VMEM(found.shape, found.dtype)]
        last = [vmem, vmem]
    else:
        half = tables[0].shape[0] // 2
        spectra = (own, 2 * vols * 2 * half, 2 * block)
        out_shape = [found, jax.ShapeDtypeStruct(spectra, jnp.float32)]
        scratch_shapes = []
        last = [pl.BlockSpec(memory_space=pl.ANY)]
    return pl.pallas_call(
        functools.partial(spectrum_kernel, vols, across, block, own, planes, depth, other),
        out_shape=out_shape,
        in_specs=[smem] * 3 + [vmem] * (len(tables) + 3) + last,
        out_specs=[vmem] * len(out_shape),
        scratch_shapes=scratch_shapes
        + [
            pltpu.VMEM((depth // 2, many, 3 * kept, LANES), jnp.float32),
            pltpu.VMEM((depth // 2, many, 1, LANES), jnp.float32),
        ],
        compiler_params=pltpu.CompilerParams(vmem_limit_bytes=VMEM_LIMIT),
        cost_estimate=pl.CostEstimate(
            flops=2 * 3 * rows * cols * block * (2 if other else 8),
            bytes_accessed=vols * rows * cols * 4 + rows * cols,
            transcendentals=0,
        ),
        name="lag_windows",
    )(place, codes, other_codes, *tables, frames, other_frames, template, *more)


def exchange(value, axes, size, turn):
    return lax.ppermute(value, axes, [(at, at ^ turn) for at in range(size)])


def on_device(frames, template, shift_codes):
    vol_dev, pl_dev, img_rows, img_cols = frames.shape
    own, block = template.shape[0], template.shape[-1]
    depth = lax.axis_size("z")
    planes = lax.axis_size("plane")
    place = jnp.stack([lax.axis_index(axis) for axis in ("z", "y", "core", "plane")])
    core = place[2]
    other_codes = exchange(shift_codes, "core", 2, 1)
    other_frames = exchange(frames, "core", 2, 1)
    *bands, staged = stage(tap_constants(block), frames, template)
    turns = [depth - 1, *range(1, depth - 1)]
    fetched = {turn: exchange(template, "z", depth, turn) for turn in turns}
    pieces = [template] + [fetched[turn] for turn in range(1, depth)]
    averages, correlation = [], 0.0
    volumes = vol_dev * depth * 4
    for p in range(pl_dev):
        work = (place, shift_codes, other_codes, staged[:, p], other_frames[:, p])
        sizes = (depth, block, own)
        (far_sums,) = warp_sums(*work, bands, template, 1, *sizes)
        taken = exchange(far_sums, "y", 2, 1)
        near_sums = warp_sums(*work, bands, far_sums, 0, *sizes)
        pieces, near_sums = lax.optimization_barrier((pieces, near_sums))
        near = jnp.concatenate([piece[:, p] for piece in pieces], axis=0)
        far = exchange(near, "y", 2, 1)
        sums = [
            one.astype(jnp.float32) + taken[step * own : (step + 1) * own].astype(jnp.float32)
            for step, one in enumerate(near_sums)
        ]
        moved = [exchange(sums[turn].astype(jnp.bfloat16), "z", depth, turn) for turn in turns]
        sizes = (planes, depth, own)
        part = lag_windows(*work, near, near_sums[:1], 0, *sizes)
        found, *given = lag_windows(*work, far, part, 1, *sizes)
        found, moved = lax.optimization_barrier((found, moved))
        total = sum((one.astype(jnp.float32) for one in moved), sums[0])
        averages.append(total * (1.0 / volumes))
        for turn, one in enumerate(given):
            found = found + exchange(one, "plane", planes, turn + 1).astype(jnp.float32)
        given = exchange(found[1].astype(jnp.bfloat16), "core", 2, 1)
        pair = (found[0], given.astype(jnp.float32))
        pair = [jnp.where(core == at, *pair).reshape(vol_dev, -1, 1, own, WIN * WIN) for at in (0, 1)]
        correlation += jnp.concatenate(pair, axis=2).reshape(vol_dev, -1, WIN * WIN)
    return (correlation, jnp.stack(averages, axis=1))


def solution(mesh):
    devices = mesh.devices.reshape(-1, 2, 2, mesh.shape["plane"])
    split = jax.sharding.Mesh(devices, ("z", "y", "core", "plane"))
    vols = ("z", "y", "core")
    in_specs = (P(vols, "plane", None, None), P(vols, "plane", None, None), P(vols, None, None))
    out_specs = (P(vols, "plane", None), P(vols, "plane", None, None))
    return jax.shard_map(
        on_device, mesh=split, in_specs=in_specs, out_specs=out_specs, check_vma=False
    )
```

```python
import functools
import math

import jax
import jax.numpy as jnp
import numpy as np
from jax import lax
from jax.experimental import pallas as pl
from jax.experimental.pallas import tpu as pltpu
from jax.sharding import PartitionSpec as P

SHIFT = 8
WIN = 16
TAPS = 8
SUB = 16
EDGE = 16
LANES = 128
VMEM_LIMIT = 24 * 1024 * 1024

full_turn = 2.0 * math.pi


def dft_constants(block_size):
    positions = np.arange(block_size)
    angles = full_turn * (np.outer(positions, positions) % block_size) / block_size
    cosine = np.cos(angles)
    sine = -np.sin(angles)
    half = block_size // 2 + 1
    rows = -(-half // 16) * 16
    row_table = np.zeros((2 * rows, block_size))
    row_table[:half] = cosine[:half]
    row_table[rows : rows + half] = sine[:half]
    col_table = np.block([[cosine, sine], [-sine, cosine]])
    weights = np.full((half,), 2.0)
    weights[0] = weights[half - 1] = 1.0
    span = 2 * SHIFT + WIN
    lags = np.arange(span) - SHIFT - WIN // 2
    turns = full_turn * (np.outer(lags, positions) % block_size) / block_size
    lag_cos, lag_sin = np.cos(turns), np.sin(turns)
    lag_table = np.zeros((2 * span, 2 * rows))
    lag_table[:span, :half] = lag_cos[:, :half] * weights
    lag_table[:span, rows : rows + half] = -lag_sin[:, :half] * weights
    lag_table[span:, :half] = lag_sin[:, :half] * weights
    lag_table[span:, rows : rows + half] = lag_cos[:, :half] * weights
    span_table = np.zeros((2 * block_size, LANES))
    span_table[:block_size, :span] = lag_cos.T
    span_table[block_size:, :span] = -lag_sin.T
    return tuple(
        jnp.asarray(table, jnp.bfloat16) for table in (row_table, col_table, lag_table, span_table)
    )


def tap_constants(block_size):
    offsets = np.arange(TAPS) - (TAPS // 2 - 1)
    spots = offsets[None, :] - np.arange(SUB)[:, None] / SUB
    raw_taps = np.sinc(spots) * np.sinc(spots / (TAPS // 2))
    taps = raw_taps / raw_taps.sum(axis=-1, keepdims=True)

    def band(inputs, outputs):
        at = inputs - outputs + TAPS // 2 - 1
        return np.where((at >= 0) & (at < TAPS), taps[:, np.clip(at, 0, TAPS - 1)], 0.0)

    lanes = np.arange(block_size)[None, :]
    inputs = np.arange(block_size + 3 * EDGE)[:, None] - EDGE - SHIFT
    outputs = np.arange(2 * EDGE)[:, None] - SHIFT
    spare = np.arange(LANES)[None, :] % (2 * EDGE)
    first = band(spare - 2 * EDGE, outputs) * (spare >= EDGE)
    last = band(spare + EDGE, outputs) * (spare < EDGE)
    tables = band(inputs, lanes), np.concatenate([first, last], axis=1)
    return [jnp.asarray(table, jnp.bfloat16) for table in tables]


def step_places(place_ref, step, across, own):
    z = place_ref[0] ^ step
    places = []
    for other in range(2):
        for one in range(own):
            index = ((2 * z + (place_ref[1] ^ other)) * 2 + place_ref[2]) * own + one
            places.append((index, index % across))
    return places


def step_band(place_ref, step, across, own):
    return (place_ref[0] ^ step) * (4 * own) // across


def stage_kernel(count, *refs):
    sources, targets = refs[:count], refs[count + 1 : 2 * count + 1]
    held, sems = refs[2 * count + 1 : 3 * count], refs[-1]
    copies = [
        pltpu.make_async_copy(source, target, sems.at[at])
        for at, (source, target) in enumerate(zip(sources, (*held, targets[-1])))
    ]
    for copy in copies:
        copy.start()
    for copy, one, target in zip(copies, held, targets):
        copy.wait()

        def widen(at, _):
            target[at] = one[at].astype(jnp.float32)
            return 0

        lax.fori_loop(0, one.shape[0], widen, 0)
    copies[-1].wait()


def stage(tables, frames, after):
    arrays = [
        pltpu.with_memory_space_constraint(one, pltpu.HBM) for one in (*tables, frames, after)
    ]
    count = len(tables) + 1
    vmem = pl.BlockSpec(memory_space=pltpu.VMEM)
    return pl.pallas_call(
        functools.partial(stage_kernel, count),
        out_shape=[jax.ShapeDtypeStruct(one.shape, jnp.float32) for one in tables]
        + [jax.ShapeDtypeStruct(frames.shape, frames.dtype)],
        in_specs=[pl.BlockSpec(memory_space=pltpu.HBM)] * count
        + [pl.BlockSpec(memory_space=pl.ANY)],
        out_specs=[vmem] * count,
        scratch_shapes=[pltpu.VMEM(one.shape, one.dtype) for one in tables]
        + [pltpu.SemaphoreType.DMA((count,))],
        compiler_params=pltpu.CompilerParams(vmem_limit_bytes=VMEM_LIMIT),
        cost_estimate=pl.CostEstimate(
            flops=0, bytes_accessed=2 * frames.nbytes, transcendentals=0
        ),
        name="stage",
    )(*arrays)


def warp_step(place_ref, step, other, code_refs, frame_refs, band_refs, down, across, block, own):
    cols_ref, edges_ref = band_refs
    band = step_band(place_ref, step, across, own)
    row = pl.multiple_of(band * block, block)
    row_above = pl.multiple_of(jnp.maximum(row - EDGE, 0), EDGE)
    row_below = pl.multiple_of(jnp.minimum(row + block, down * block - EDGE), EDGE)
    zero = jnp.zeros((EDGE, LANES), jnp.bfloat16)
    gap = jnp.zeros((block - 2 * EDGE, LANES), jnp.bfloat16)
    no_tile = jnp.zeros((block + 2 * EDGE, block), jnp.bfloat16)
    volumes = [
        (codes, frames, v)
        for codes, frames in zip(code_refs, frame_refs)
        for v in range(frames.shape[0])
    ]
    many = len(volumes)
    per_tile = LANES // (2 * EDGE)
    lane = lax.broadcasted_iota(jnp.int32, (EDGE, LANES), 1) // (2 * EDGE)

    def tile(frames, v, at):
        lanes = pl.ds(pl.multiple_of(at * block, block), block)
        above = jnp.where(band > 0, frames[v, pl.ds(row_above, EDGE), lanes], zero)
        below = jnp.where(band < down - 1, frames[v, pl.ds(row_below, EDGE), lanes], zero)
        return jnp.concatenate([frames[v, pl.ds(row, block), lanes], below, above], axis=0)

    places = step_places(place_ref, step, across, own)[other * own : (other + 1) * own]
    start = places[0][1]
    tiles = []
    for _, frames, v in volumes:
        left = jnp.where(start > 0, tile(frames, v, jnp.maximum(start - 1, 0)), no_tile)
        right = jnp.where(
            start + own < across, tile(frames, v, jnp.minimum(start + own, across - 1)), no_tile
        )
        tiles.append([left] + [tile(frames, v, start + one) for one in range(own)] + [right])
    totals = []
    for one, (index, _) in enumerate(places):
        row_tiles, partials, edges = [], [], []
        firsts, lasts = [], []
        for order, (codes, _, v) in enumerate(volumes):
            row_code, col_code = codes[v, 0, index], codes[v, 1, index]
            left, middle, right = tiles[order][one : one + 3]
            sides = jnp.concatenate([right[:, : block // 2], left[:, block // 2 :]], axis=1)
            col_start = SHIFT - (col_code >> 4)
            cols = cols_ref[col_code & (SUB - 1), pl.ds(col_start, block + 2 * EDGE), :]
            cols = cols.astype(jnp.bfloat16)
            partial = jnp.dot(
                jnp.concatenate([middle, sides], axis=1),
                jnp.concatenate([cols[EDGE:], gap, cols[:EDGE]], axis=0),
                preferred_element_type=jnp.float32,
            ).astype(jnp.bfloat16)
            partials.append(partial[:block])
            edges.append(partial[block:])
            back = -row_code
            back_start = SHIFT + EDGE - (back >> 4)
            rows = cols_ref[back & (SUB - 1), pl.ds(back_start, block), :]
            row_tiles.append(rows.astype(jnp.bfloat16))
            row_start, step_at = SHIFT + (row_code >> 4), row_code & (SUB - 1)
            first = edges_ref[step_at, pl.ds(row_start, EDGE), :]
            last = edges_ref[step_at, pl.ds(2 * EDGE + row_start, EDGE), :]
            if order % per_tile:
                first = jnp.where(lane == order % per_tile, first, firsts.pop())
                last = jnp.where(lane == order % per_tile, last, lasts.pop())
            firsts.append(first)
            lasts.append(last)
        for first, last in zip(firsts, lasts):
            both = [first.astype(jnp.bfloat16), gap, last.astype(jnp.bfloat16)]
            row_tiles.append(jnp.concatenate(both, axis=0))
        deep = many * (block + 2 * EDGE)
        total = jnp.dot(
            jnp.concatenate(row_tiles, axis=1)[:, :deep],
            jnp.concatenate(partials + edges, axis=0),
            preferred_element_type=jnp.float32,
        )
        totals.append(total.astype(jnp.bfloat16))
    return totals


def warp_kernel(down, across, block, own, other, *refs):
    place_ref, *code_refs = refs[:3]
    frame_refs, band_refs, out_refs = refs[3:5], refs[5:7], refs[8:]
    depth = out_refs[0].shape[0] // own if other else len(out_refs)
    for step in range(depth):
        totals = warp_step(
            place_ref, step, other, code_refs, frame_refs, band_refs, down, across, block, own
        )
        for one, total in enumerate(totals):
            if other:
                out_refs[0][step * own + one] = total
            else:
                out_refs[step][one] = total


def warp_sums(
    place, codes, other_codes, frames, other_frames, bands, after, other, depth, block, own
):
    vols, rows, cols = frames.shape
    down, across = rows // block, cols // block
    smem = pl.BlockSpec(memory_space=pltpu.SMEM)
    vmem = pl.BlockSpec(memory_space=pltpu.VMEM)
    if other:
        out_shape = [jax.ShapeDtypeStruct((depth * own, block, block), jnp.bfloat16)]
    else:
        out_shape = [jax.ShapeDtypeStruct((own, block, block), jnp.bfloat16)] * depth
    return pl.pallas_call(
        functools.partial(warp_kernel, down, across, block, own, other),
        out_shape=out_shape,
        in_specs=[smem] * 3
        + [vmem] * (2 + len(bands))
        + [pl.BlockSpec(memory_space=pl.ANY)],
        out_specs=[vmem] * len(out_shape),
        compiler_params=pltpu.CompilerParams(vmem_limit_bytes=VMEM_LIMIT),
        cost_estimate=pl.CostEstimate(
            flops=2 * vols * rows * cols * block * 8,
            bytes_accessed=vols * rows * cols * 4 + rows * cols,
            transcendentals=0,
        ),
        name="warp",
    )(place, codes, other_codes, frames, other_frames, *bands, after)


def spectrum_kernel(vols, across, block, own, planes, depth, other, *refs):
    place_ref, codes_ref, other_codes_ref, row_ref, col_ref, lag_ref, span_ref = refs[:7]
    frames_ref, other_frames_ref, template_ref = refs[7:10]
    all_cross, all_sums = refs[-2:]
    ready = []
    if other:
        found_ref, spectra_ref, out_refs, found = refs[10], refs[11], refs[12:-3], refs[-3]
        found[...] = found_ref[...]
        ready.append(spectra_ref)
    else:
        found, spectra_ref = refs[11:13]

    row_table = row_ref[...]
    col_table = col_ref[...]
    lag_table = lag_ref[...]
    half = row_table.shape[0] // 2
    kept = -(-(block // 2 + 1) // 8) * 8
    span = lag_table.shape[0] // 2
    top = lax.broadcasted_iota(jnp.int32, (8, LANES), 0) == 0
    volumes = [(codes_ref, frames_ref, v) for v in range(vols)]
    volumes += [(other_codes_ref, other_frames_ref, v) for v in range(vols)]
    many = len(volumes)
    local = 2 * own
    no_rows = jnp.zeros((half - kept, LANES), jnp.float32)

    def find_places(half_step, row):
        places = []
        for step in (2 * half_step, 2 * half_step + 1):
            band = step_band(place_ref, step, across, own)
            band_rows = pl.ds(pl.multiple_of(band * block, block), block)
            chosen = step_places(place_ref, step, across, own)[row * own : (row + 1) * own]
            for one, (index, at) in enumerate(chosen):
                lanes = pl.ds(pl.multiple_of(at * block, block), block)
                places.append((index, band_rows, lanes, step * own + one))
        return places

    def frame_sources(pair_places):
        return [
            [frames[v, rows, lanes] for _, rows, lanes, _ in pair_places]
            for _, frames, v in volumes
        ]

    def transform(sources):
        parts = []
        for source in sources:
            rows = jnp.dot(
                row_table, jnp.concatenate(source, axis=1), preferred_element_type=jnp.float32
            ).astype(jnp.bfloat16)
            for side in range(2):
                lanes = slice(side * block, (side + 1) * block)
                parts.append(jnp.concatenate([rows[:half, lanes], rows[half:, lanes]], axis=1))
        return jnp.dot(
            jnp.concatenate(parts, axis=0), col_table, preferred_element_type=jnp.float32
        )

    def first_pass(half_step, pair):
        cross, sums = all_cross.at[half_step], all_sums.at[half_step]
        places = find_places(half_step, other)
        pair_places = places[2 * pair : 2 * pair + 2]
        sources = [[template_ref[at] for _, _, _, at in pair_places]]
        sources += frame_sources(pair_places)
        if ready and half_step == 0:
            spectra = jnp.concatenate([transform(sources[:1]), ready[0][pair]], axis=0)
        else:
            spectra = transform(sources)
        temp = spectra[: 2 * half].astype(jnp.bfloat16).astype(jnp.float32)
        for order in range(many):
            for side in range(2):
                one = (2 * pair + side) * many + order
                base = (2 * (order + 1) + side) * half
                total = jnp.zeros((8, LANES), jnp.float32)
                for row in range(0, kept, 8):
                    at = side * half + row
                    temp_real = temp[at : at + 8, :block]
                    temp_imag = temp[at : at + 8, block:]
                    real = spectra[base + row : base + row + 8, :block]
                    imag = spectra[base + row : base + row + 8, block:]
                    cross_real = real * temp_real + imag * temp_imag
                    cross_imag = imag * temp_real - real * temp_imag
                    power = cross_real * cross_real + cross_imag * cross_imag
                    magnitude = power * lax.rsqrt(jnp.maximum(power, 1e-36))
                    cross[one, row : row + 8, :] = cross_real
                    cross[one, kept + row : kept + row + 8, :] = cross_imag
                    cross[one, 2 * kept + row : 2 * kept + row + 8, :] = magnitude
                    if row == 0:
                        once = jnp.where(top, magnitude, 0.0)
                    elif row == block // 2:
                        once += magnitude
                    total += magnitude
                sums[one] = jnp.sum(total + total - once, axis=0, keepdims=True)


    def second_pass(half_step, pair):
        cross, sums = all_cross.at[half_step], all_sums.at[half_step]
        places = find_places(half_step, other)
        lag_sums = []
        first = 2 * pair * many
        magnitudes = jnp.sum(sums[first : first + 2 * many], axis=2, keepdims=True)
        means = magnitudes * (1.0 / (block * block)) + 1e-06
        for order in range(many):
            norms = []
            for side in range(2):
                one = (2 * pair + side) * many + order
                scale = pl.reciprocal(cross[one, 2 * kept :, :] + means[one - first], approx=True)
                norms.append(
                    jnp.concatenate(
                        [
                            cross[one, :kept, :] * scale,
                            no_rows,
                            cross[one, kept : 2 * kept, :] * scale,
                            no_rows,
                        ],
                        axis=0,
                    ).astype(jnp.bfloat16)
                )
            lag_rows = jnp.dot(
                lag_table, jnp.concatenate(norms, axis=1), preferred_element_type=jnp.float32
            ).astype(jnp.bfloat16)
            for side in range(2):
                lanes = slice(side * block, (side + 1) * block)
                lag_sums.append(
                    jnp.concatenate([lag_rows[:span, lanes], lag_rows[span:, lanes]], axis=1)
                )
        lags = jnp.dot(
            jnp.concatenate(lag_sums, axis=0), span_ref[...], preferred_element_type=jnp.float32
        )
        for order, (codes, _, v) in enumerate(volumes):
            for side in range(2):
                index = places[2 * pair + side][0]
                row_shift = codes[v, 0, index] >> 4
                col_shift = codes[v, 1, index] >> 4
                at = order * 2 + side
                one = lags[at * span : (at + 1) * span]
                one = pltpu.roll(one, span - SHIFT - row_shift, 0)[:WIN]
                at = index // (2 * own) * own + (2 * pair + side) % own
                found[order, pl.ds(pl.multiple_of(at * WIN, WIN), WIN), :] = pltpu.roll(
                    one, LANES - SHIFT - col_shift, 1
                )

    units = [(at, pair) for at in range(depth // 2) for pair in range(local // 2)]
    first_pass(*units[0])
    for before, unit in zip(units, units[1:]):
        first_pass(*unit)
        second_pass(*before)
    second_pass(*units[-1])

    if not other:
        places = find_places(0, 1)
        for pair in range(local // 2):
            spectra_ref[pair] = transform(frame_sources(places[2 * pair : 2 * pair + 2]))
        return

    share = (found.shape[1] // WIN - 1) // planes
    per_tile = LANES // WIN
    lane = lax.broadcasted_iota(jnp.int32, (share, LANES), 1) // WIN
    for turn, out_ref in enumerate(out_refs):
        plane = place_ref[3] ^ turn
        for order in range(many):
            for tile in range(WIN // per_tile):
                total = jnp.zeros((share, LANES), jnp.float32)
                for part in range(per_tile):
                    start = plane * share * WIN + tile * per_tile + part
                    one = found[order, pl.ds(start, share, stride=WIN), :]
                    if part:
                        one = pltpu.roll(one, part * WIN, 1)
                    total = jnp.where(lane == part, one, total)
                lanes = slice(tile * LANES, (tile + 1) * LANES)
                total = (total * (1.0 / block)).astype(out_ref.dtype)
                out_ref[order // vols, order % vols, :, lanes] = total


def lag_windows(
    place, codes, other_codes, frames, other_frames, template, more, other, planes, depth, own
):
    vols, rows, cols = frames.shape
    block = template.shape[-1]
    down, across = rows // block, cols // block
    tables = dft_constants(block)
    kept = -(-(block // 2 + 1) // 8) * 8
    smem = pl.BlockSpec(memory_space=pltpu.SMEM)
    vmem = pl.BlockSpec(memory_space=pltpu.VMEM)
    blocks = down * across // 2
    many = 2 * vols * 2 * own
    found = jax.ShapeDtypeStruct((2 * vols, (blocks + 1) * WIN, LANES), jnp.float32)
    if other:
        out = (2, vols, blocks // planes, WIN * WIN)
        out_shape = [jax.ShapeDtypeStruct(out, jnp.float32)]
        out_shape += [jax.ShapeDtypeStruct(out, jnp.bfloat16)] * (planes - 1)
        scratch_shapes = [pltpu.VMEM(found.shape, found.dtype)]
        last = [vmem, vmem]
    else:
        half = tables[0].shape[0] // 2
        spectra = (own, 2 * vols * 2 * half, 2 * block)
        out_shape = [found, jax.ShapeDtypeStruct(spectra, jnp.float32)]
        scratch_shapes = []
        last = [pl.BlockSpec(memory_space=pl.ANY)]
    return pl.pallas_call(
        functools.partial(spectrum_kernel, vols, across, block, own, planes, depth, other),
        out_shape=out_shape,
        in_specs=[smem] * 3 + [vmem] * (len(tables) + 3) + last,
        out_specs=[vmem] * len(out_shape),
        scratch_shapes=scratch_shapes
        + [
            pltpu.VMEM((depth // 2, many, 3 * kept, LANES), jnp.float32),
            pltpu.VMEM((depth // 2, many, 1, LANES), jnp.float32),
        ],
        compiler_params=pltpu.CompilerParams(vmem_limit_bytes=VMEM_LIMIT),
        cost_estimate=pl.CostEstimate(
            flops=2 * 3 * rows * cols * block * (2 if other else 8),
            bytes_accessed=vols * rows * cols * 4 + rows * cols,
            transcendentals=0,
        ),
        name="lag_windows",
    )(place, codes, other_codes, *tables, frames, other_frames, template, *more)


def exchange(value, axes, size, turn):
    return lax.ppermute(value, axes, [(at, at ^ turn) for at in range(size)])


def on_device(frames, template, shift_codes):
    vol_dev, pl_dev, img_rows, img_cols = frames.shape
    own, block = template.shape[0], template.shape[-1]
    depth = lax.axis_size("z")
    planes = lax.axis_size("plane")
    place = jnp.stack([lax.axis_index(axis) for axis in ("z", "y", "core", "plane")])
    core = place[2]
    other_codes = exchange(shift_codes, "core", 2, 1)
    other_frames = exchange(frames, "core", 2, 1)
    *bands, staged = stage(tap_constants(block), frames, template)
    turns = [depth - 1, *range(1, depth - 1)]
    fetched = {turn: exchange(template, "z", depth, turn) for turn in turns}
    pieces = [template] + [fetched[turn] for turn in range(1, depth)]
    averages, correlation = [], 0.0
    volumes = vol_dev * depth * 4
    for p in range(pl_dev):
        work = (place, shift_codes, other_codes, staged[:, p], other_frames[:, p])
        sizes = (depth, block, own)
        (far_sums,) = warp_sums(*work, bands, template, 1, *sizes)
        taken = exchange(far_sums, "y", 2, 1)
        near_sums = warp_sums(*work, bands, far_sums, 0, *sizes)
        pieces, near_sums = lax.optimization_barrier((pieces, near_sums))
        near = jnp.concatenate([piece[:, p] for piece in pieces], axis=0)
        far = exchange(near, "y", 2, 1)
        sums = [
            one.astype(jnp.float32) + taken[step * own : (step + 1) * own].astype(jnp.float32)
            for step, one in enumerate(near_sums)
        ]
        moved = [exchange(sums[turn].astype(jnp.bfloat16), "z", depth, turn) for turn in turns]
        sizes = (planes, depth, own)
        part = lag_windows(*work, near, near_sums[:1], 0, *sizes)
        found, *given = lag_windows(*work, far, part, 1, *sizes)
        found, moved = lax.optimization_barrier((found, moved))
        total = sum((one.astype(jnp.float32) for one in moved), sums[0])
        averages.append(total * (1.0 / volumes))
        for turn, one in enumerate(given):
            found = found + exchange(one, "plane", planes, turn + 1).astype(jnp.float32)
        given = exchange(found[1].astype(jnp.bfloat16), "core", 2, 1)
        pair = (found[0], given.astype(jnp.float32))
        pair = [jnp.where(core == at, *pair).reshape(vol_dev, -1, 1, own, WIN * WIN) for at in (0, 1)]
        correlation += jnp.concatenate(pair, axis=2).reshape(vol_dev, -1, WIN * WIN)
    return (correlation, jnp.stack(averages, axis=1))


def solution(mesh):
    devices = mesh.devices.reshape(-1, 2, 2, mesh.shape["plane"])
    split = jax.sharding.Mesh(devices, ("z", "y", "core", "plane"))
    vols = ("z", "y", "core")
    in_specs = (P(vols, "plane", None, None), P(vols, "plane", None, None), P(vols, None, None))
    out_specs = (P(vols, "plane", None), P(vols, "plane", None, None))
    return jax.shard_map(
        on_device, mesh=split, in_specs=in_specs, out_specs=out_specs, check_vma=False
    )
```

```python
import functools
import math

import jax
import jax.numpy as jnp
import numpy as np
from jax import lax
from jax.experimental import pallas as pl
from jax.experimental.pallas import tpu as pltpu
from jax.sharding import PartitionSpec as P

SHIFT = 8
WIN = 16
TAPS = 8
SUB = 16
EDGE = 16
LANES = 128
VMEM_LIMIT = 24 * 1024 * 1024

full_turn = 2.0 * math.pi


def dft_constants(block_size):
    positions = np.arange(block_size)
    angles = full_turn * (np.outer(positions, positions) % block_size) / block_size
    cosine = np.cos(angles)
    sine = -np.sin(angles)
    half = block_size // 2 + 1
    rows = -(-half // 16) * 16
    row_table = np.zeros((2 * rows, block_size))
    row_table[:half] = cosine[:half]
    row_table[rows : rows + half] = sine[:half]
    col_table = np.block([[cosine, sine], [-sine, cosine]])
    weights = np.full((half,), 2.0)
    weights[0] = weights[half - 1] = 1.0
    span = 2 * SHIFT + WIN
    lags = np.arange(span) - SHIFT - WIN // 2
    turns = full_turn * (np.outer(lags, positions) % block_size) / block_size
    lag_cos, lag_sin = np.cos(turns), np.sin(turns)
    lag_table = np.zeros((2 * span, 2 * rows))
    lag_table[:span, :half] = lag_cos[:, :half] * weights
    lag_table[:span, rows : rows + half] = -lag_sin[:, :half] * weights
    lag_table[span:, :half] = lag_sin[:, :half] * weights
    lag_table[span:, rows : rows + half] = lag_cos[:, :half] * weights
    span_table = np.zeros((2 * block_size, LANES))
    span_table[:block_size, :span] = lag_cos.T
    span_table[block_size:, :span] = -lag_sin.T
    return tuple(
        jnp.asarray(table, jnp.bfloat16) for table in (row_table, col_table, lag_table, span_table)
    )


def tap_constants(block_size):
    offsets = np.arange(TAPS) - (TAPS // 2 - 1)
    spots = offsets[None, :] - np.arange(SUB)[:, None] / SUB
    raw_taps = np.sinc(spots) * np.sinc(spots / (TAPS // 2))
    taps = raw_taps / raw_taps.sum(axis=-1, keepdims=True)

    def band(inputs, outputs):
        at = inputs - outputs + TAPS // 2 - 1
        return np.where((at >= 0) & (at < TAPS), taps[:, np.clip(at, 0, TAPS - 1)], 0.0)

    lanes = np.arange(block_size)[None, :]
    inputs = np.arange(block_size + 3 * EDGE)[:, None] - EDGE - SHIFT
    outputs = np.arange(2 * EDGE)[:, None] - SHIFT
    spare = np.arange(LANES)[None, :] % (2 * EDGE)
    first = band(spare - 2 * EDGE, outputs) * (spare >= EDGE)
    last = band(spare + EDGE, outputs) * (spare < EDGE)
    tables = band(inputs, lanes), np.concatenate([first, last], axis=1)
    return [jnp.asarray(table, jnp.bfloat16) for table in tables]


def step_places(place_ref, step, across, own):
    z = place_ref[0] ^ step
    places = []
    for other in range(2):
        for one in range(own):
            index = ((2 * z + (place_ref[1] ^ other)) * 2 + place_ref[2]) * own + one
            places.append((index, index % across))
    return places


def step_band(place_ref, step, across, own):
    return (place_ref[0] ^ step) * (4 * own) // across


def stage_kernel(count, *refs):
    sources, targets = refs[:count], refs[count + 1 : 2 * count + 1]
    held, sems = refs[2 * count + 1 : 3 * count], refs[-1]
    copies = [
        pltpu.make_async_copy(source, target, sems.at[at])
        for at, (source, target) in enumerate(zip(sources, (*held, targets[-1])))
    ]
    for copy in copies:
        copy.start()
    for copy, one, target in zip(copies, held, targets):
        copy.wait()

        def widen(at, _):
            target[at] = one[at].astype(jnp.float32)
            return 0

        lax.fori_loop(0, one.shape[0], widen, 0)
    copies[-1].wait()


def stage(tables, frames, after):
    arrays = [
        pltpu.with_memory_space_constraint(one, pltpu.HBM) for one in (*tables, frames, after)
    ]
    count = len(tables) + 1
    vmem = pl.BlockSpec(memory_space=pltpu.VMEM)
    return pl.pallas_call(
        functools.partial(stage_kernel, count),
        out_shape=[jax.ShapeDtypeStruct(one.shape, jnp.float32) for one in tables]
        + [jax.ShapeDtypeStruct(frames.shape, frames.dtype)],
        in_specs=[pl.BlockSpec(memory_space=pltpu.HBM)] * count
        + [pl.BlockSpec(memory_space=pl.ANY)],
        out_specs=[vmem] * count,
        scratch_shapes=[pltpu.VMEM(one.shape, one.dtype) for one in tables]
        + [pltpu.SemaphoreType.DMA((count,))],
        compiler_params=pltpu.CompilerParams(vmem_limit_bytes=VMEM_LIMIT),
        cost_estimate=pl.CostEstimate(
            flops=0, bytes_accessed=2 * frames.nbytes, transcendentals=0
        ),
        name="stage",
    )(*arrays)


def warp_step(place_ref, step, other, code_refs, frame_refs, band_refs, down, across, block, own):
    cols_ref, edges_ref = band_refs
    band = step_band(place_ref, step, across, own)
    row = pl.multiple_of(band * block, block)
    row_above = pl.multiple_of(jnp.maximum(row - EDGE, 0), EDGE)
    row_below = pl.multiple_of(jnp.minimum(row + block, down * block - EDGE), EDGE)
    zero = jnp.zeros((EDGE, LANES), jnp.bfloat16)
    gap = jnp.zeros((block - 2 * EDGE, LANES), jnp.bfloat16)
    no_tile = jnp.zeros((block + 2 * EDGE, block), jnp.bfloat16)
    volumes = [
        (codes, frames, v)
        for codes, frames in zip(code_refs, frame_refs)
        for v in range(frames.shape[0])
    ]
    many = len(volumes)
    per_tile = LANES // (2 * EDGE)
    lane = lax.broadcasted_iota(jnp.int32, (EDGE, LANES), 1) // (2 * EDGE)

    def tile(frames, v, at):
        lanes = pl.ds(pl.multiple_of(at * block, block), block)
        above = jnp.where(band > 0, frames[v, pl.ds(row_above, EDGE), lanes], zero)
        below = jnp.where(band < down - 1, frames[v, pl.ds(row_below, EDGE), lanes], zero)
        return jnp.concatenate([frames[v, pl.ds(row, block), lanes], below, above], axis=0)

    places = step_places(place_ref, step, across, own)[other * own : (other + 1) * own]
    start = places[0][1]
    tiles = []
    for _, frames, v in volumes:
        left = jnp.where(start > 0, tile(frames, v, jnp.maximum(start - 1, 0)), no_tile)
        right = jnp.where(
            start + own < across, tile(frames, v, jnp.minimum(start + own, across - 1)), no_tile
        )
        tiles.append([left] + [tile(frames, v, start + one) for one in range(own)] + [right])
    totals = []
    for one, (index, _) in enumerate(places):
        row_tiles, partials, edges = [], [], []
        firsts, lasts = [], []
        for order, (codes, _, v) in enumerate(volumes):
            row_code, col_code = codes[v, 0, index], codes[v, 1, index]
            left, middle, right = tiles[order][one : one + 3]
            sides = jnp.concatenate([right[:, : block // 2], left[:, block // 2 :]], axis=1)
            col_start = SHIFT - (col_code >> 4)
            cols = cols_ref[col_code & (SUB - 1), pl.ds(col_start, block + 2 * EDGE), :]
            cols = cols.astype(jnp.bfloat16)
            partial = jnp.dot(
                jnp.concatenate([middle, sides], axis=1),
                jnp.concatenate([cols[EDGE:], gap, cols[:EDGE]], axis=0),
                preferred_element_type=jnp.float32,
            ).astype(jnp.bfloat16)
            partials.append(partial[:block])
            edges.append(partial[block:])
            back = -row_code
            back_start = SHIFT + EDGE - (back >> 4)
            rows = cols_ref[back & (SUB - 1), pl.ds(back_start, block), :]
            row_tiles.append(rows.astype(jnp.bfloat16))
            row_start, step_at = SHIFT + (row_code >> 4), row_code & (SUB - 1)
            first = edges_ref[step_at, pl.ds(row_start, EDGE), :]
            last = edges_ref[step_at, pl.ds(2 * EDGE + row_start, EDGE), :]
            if order % per_tile:
                first = jnp.where(lane == order % per_tile, first, firsts.pop())
                last = jnp.where(lane == order % per_tile, last, lasts.pop())
            firsts.append(first)
            lasts.append(last)
        for first, last in zip(firsts, lasts):
            both = [first.astype(jnp.bfloat16), gap, last.astype(jnp.bfloat16)]
            row_tiles.append(jnp.concatenate(both, axis=0))
        deep = many * (block + 2 * EDGE)
        total = jnp.dot(
            jnp.concatenate(row_tiles, axis=1)[:, :deep],
            jnp.concatenate(partials + edges, axis=0),
            preferred_element_type=jnp.float32,
        )
        totals.append(total.astype(jnp.bfloat16))
    return totals


def warp_kernel(down, across, block, own, other, *refs):
    place_ref, *code_refs = refs[:3]
    frame_refs, band_refs, out_refs = refs[3:5], refs[5:7], refs[8:]
    depth = out_refs[0].shape[0] // own if other else len(out_refs)
    for step in range(depth):
        totals = warp_step(
            place_ref, step, other, code_refs, frame_refs, band_refs, down, across, block, own
        )
        for one, total in enumerate(totals):
            if other:
                out_refs[0][step * own + one] = total
            else:
                out_refs[step][one] = total


def warp_sums(
    place, codes, other_codes, frames, other_frames, bands, after, other, depth, block, own
):
    vols, rows, cols = frames.shape
    down, across = rows // block, cols // block
    smem = pl.BlockSpec(memory_space=pltpu.SMEM)
    vmem = pl.BlockSpec(memory_space=pltpu.VMEM)
    if other:
        out_shape = [jax.ShapeDtypeStruct((depth * own, block, block), jnp.bfloat16)]
    else:
        out_shape = [jax.ShapeDtypeStruct((own, block, block), jnp.bfloat16)] * depth
    return pl.pallas_call(
        functools.partial(warp_kernel, down, across, block, own, other),
        out_shape=out_shape,
        in_specs=[smem] * 3
        + [vmem] * (2 + len(bands))
        + [pl.BlockSpec(memory_space=pl.ANY)],
        out_specs=[vmem] * len(out_shape),
        compiler_params=pltpu.CompilerParams(vmem_limit_bytes=VMEM_LIMIT),
        cost_estimate=pl.CostEstimate(
            flops=2 * vols * rows * cols * block * 8,
            bytes_accessed=vols * rows * cols * 4 + rows * cols,
            transcendentals=0,
        ),
        name="warp",
    )(place, codes, other_codes, frames, other_frames, *bands, after)


def spectrum_kernel(vols, across, block, own, planes, depth, other, *refs):
    place_ref, codes_ref, other_codes_ref, row_ref, col_ref, lag_ref, span_ref = refs[:7]
    frames_ref, other_frames_ref, template_ref = refs[7:10]
    all_cross, all_sums = refs[-2:]
    ready = []
    if other:
        found_ref, spectra_ref, out_refs, found = refs[10], refs[11], refs[12:-3], refs[-3]
        found[...] = found_ref[...]
        ready.append(spectra_ref)
    else:
        found, spectra_ref = refs[11:13]

    row_table = row_ref[...]
    col_table = col_ref[...]
    lag_table = lag_ref[...]
    half = row_table.shape[0] // 2
    kept = -(-(block // 2 + 1) // 8) * 8
    span = lag_table.shape[0] // 2
    top = lax.broadcasted_iota(jnp.int32, (8, LANES), 0) == 0
    volumes = [(codes_ref, frames_ref, v) for v in range(vols)]
    volumes += [(other_codes_ref, other_frames_ref, v) for v in range(vols)]
    many = len(volumes)
    local = 2 * own
    no_rows = jnp.zeros((half - kept, LANES), jnp.float32)

    def find_places(half_step, row):
        places = []
        for step in (2 * half_step, 2 * half_step + 1):
            band = step_band(place_ref, step, across, own)
            band_rows = pl.ds(pl.multiple_of(band * block, block), block)
            chosen = step_places(place_ref, step, across, own)[row * own : (row + 1) * own]
            for one, (index, at) in enumerate(chosen):
                lanes = pl.ds(pl.multiple_of(at * block, block), block)
                places.append((index, band_rows, lanes, step * own + one))
        return places

    def frame_sources(pair_places):
        return [
            [frames[v, rows, lanes] for _, rows, lanes, _ in pair_places]
            for _, frames, v in volumes
        ]

    def transform(sources):
        parts = []
        for source in sources:
            rows = jnp.dot(
                row_table, jnp.concatenate(source, axis=1), preferred_element_type=jnp.float32
            ).astype(jnp.bfloat16)
            for side in range(2):
                lanes = slice(side * block, (side + 1) * block)
                parts.append(jnp.concatenate([rows[:half, lanes], rows[half:, lanes]], axis=1))
        return jnp.dot(
            jnp.concatenate(parts, axis=0), col_table, preferred_element_type=jnp.float32
        )

    def first_pass(half_step, pair):
        cross, sums = all_cross.at[half_step], all_sums.at[half_step]
        places = find_places(half_step, other)
        pair_places = places[2 * pair : 2 * pair + 2]
        sources = [[template_ref[at] for _, _, _, at in pair_places]]
        sources += frame_sources(pair_places)
        if ready and half_step == 0:
            spectra = jnp.concatenate([transform(sources[:1]), ready[0][pair]], axis=0)
        else:
            spectra = transform(sources)
        temp = spectra[: 2 * half].astype(jnp.bfloat16).astype(jnp.float32)
        for order in range(many):
            for side in range(2):
                one = (2 * pair + side) * many + order
                base = (2 * (order + 1) + side) * half
                total = jnp.zeros((8, LANES), jnp.float32)
                for row in range(0, kept, 8):
                    at = side * half + row
                    temp_real = temp[at : at + 8, :block]
                    temp_imag = temp[at : at + 8, block:]
                    real = spectra[base + row : base + row + 8, :block]
                    imag = spectra[base + row : base + row + 8, block:]
                    cross_real = real * temp_real + imag * temp_imag
                    cross_imag = imag * temp_real - real * temp_imag
                    power = cross_real * cross_real + cross_imag * cross_imag
                    magnitude = power * lax.rsqrt(jnp.maximum(power, 1e-36))
                    cross[one, row : row + 8, :] = cross_real
                    cross[one, kept + row : kept + row + 8, :] = cross_imag
                    cross[one, 2 * kept + row : 2 * kept + row + 8, :] = magnitude
                    if row == 0:
                        once = jnp.where(top, magnitude, 0.0)
                    elif row == block // 2:
                        once += magnitude
                    total += magnitude
                sums[one] = jnp.sum(total + total - once, axis=0, keepdims=True)


    def second_pass(half_step, pair):
        cross, sums = all_cross.at[half_step], all_sums.at[half_step]
        places = find_places(half_step, other)
        lag_sums = []
        first = 2 * pair * many
        magnitudes = jnp.sum(sums[first : first + 2 * many], axis=2, keepdims=True)
        means = magnitudes * (1.0 / (block * block)) + 1e-06
        for order in range(many):
            norms = []
            for side in range(2):
                one = (2 * pair + side) * many + order
                scale = pl.reciprocal(cross[one, 2 * kept :, :] + means[one - first], approx=True)
                norms.append(
                    jnp.concatenate(
                        [
                            cross[one, :kept, :] * scale,
                            no_rows,
                            cross[one, kept : 2 * kept, :] * scale,
                            no_rows,
                        ],
                        axis=0,
                    ).astype(jnp.bfloat16)
                )
            lag_rows = jnp.dot(
                lag_table, jnp.concatenate(norms, axis=1), preferred_element_type=jnp.float32
            ).astype(jnp.bfloat16)
            for side in range(2):
                lanes = slice(side * block, (side + 1) * block)
                lag_sums.append(
                    jnp.concatenate([lag_rows[:span, lanes], lag_rows[span:, lanes]], axis=1)
                )
        lags = jnp.dot(
            jnp.concatenate(lag_sums, axis=0), span_ref[...], preferred_element_type=jnp.float32
        )
        for order, (codes, _, v) in enumerate(volumes):
            for side in range(2):
                index = places[2 * pair + side][0]
                row_shift = codes[v, 0, index] >> 4
                col_shift = codes[v, 1, index] >> 4
                at = order * 2 + side
                one = lags[at * span : (at + 1) * span]
                one = pltpu.roll(one, span - SHIFT - row_shift, 0)[:WIN]
                at = index // (2 * own) * own + (2 * pair + side) % own
                found[order, pl.ds(pl.multiple_of(at * WIN, WIN), WIN), :] = pltpu.roll(
                    one, LANES - SHIFT - col_shift, 1
                )

    units = [(at, pair) for at in range(depth // 2) for pair in range(local // 2)]
    lead = local // 2 if other else 1
    for at in range(0, len(units), lead):
        for unit in units[at : at + lead]:
            first_pass(*unit)
        for unit in units[at : at + lead] if other else units[max(at - 1, 0) : at]:
            second_pass(*unit)
    if not other:
        second_pass(*units[-1])

    if not other:
        places = find_places(0, 1)
        for pair in range(local // 2):
            spectra_ref[pair] = transform(frame_sources(places[2 * pair : 2 * pair + 2]))
        return

    share = (found.shape[1] // WIN - 1) // planes
    per_tile = LANES // WIN
    lane = lax.broadcasted_iota(jnp.int32, (share, LANES), 1) // WIN
    for turn, out_ref in enumerate(out_refs):
        plane = place_ref[3] ^ turn
        for order in range(many):
            for tile in range(WIN // per_tile):
                total = jnp.zeros((share, LANES), jnp.float32)
                for part in range(per_tile):
                    start = plane * share * WIN + tile * per_tile + part
                    one = found[order, pl.ds(start, share, stride=WIN), :]
                    if part:
                        one = pltpu.roll(one, part * WIN, 1)
                    total = jnp.where(lane == part, one, total)
                lanes = slice(tile * LANES, (tile + 1) * LANES)
                total = (total * (1.0 / block)).astype(out_ref.dtype)
                out_ref[order // vols, order % vols, :, lanes] = total


def lag_windows(
    place, codes, other_codes, frames, other_frames, template, more, other, planes, depth, own
):
    vols, rows, cols = frames.shape
    block = template.shape[-1]
    down, across = rows // block, cols // block
    tables = dft_constants(block)
    kept = -(-(block // 2 + 1) // 8) * 8
    smem = pl.BlockSpec(memory_space=pltpu.SMEM)
    vmem = pl.BlockSpec(memory_space=pltpu.VMEM)
    blocks = down * across // 2
    many = 2 * vols * 2 * own
    found = jax.ShapeDtypeStruct((2 * vols, (blocks + 1) * WIN, LANES), jnp.float32)
    if other:
        out = (2, vols, blocks // planes, WIN * WIN)
        out_shape = [jax.ShapeDtypeStruct(out, jnp.float32)]
        out_shape += [jax.ShapeDtypeStruct(out, jnp.bfloat16)] * (planes - 1)
        scratch_shapes = [pltpu.VMEM(found.shape, found.dtype)]
        last = [vmem, vmem]
    else:
        half = tables[0].shape[0] // 2
        spectra = (own, 2 * vols * 2 * half, 2 * block)
        out_shape = [found, jax.ShapeDtypeStruct(spectra, jnp.float32)]
        scratch_shapes = []
        last = [pl.BlockSpec(memory_space=pl.ANY)]
    return pl.pallas_call(
        functools.partial(spectrum_kernel, vols, across, block, own, planes, depth, other),
        out_shape=out_shape,
        in_specs=[smem] * 3 + [vmem] * (len(tables) + 3) + last,
        out_specs=[vmem] * len(out_shape),
        scratch_shapes=scratch_shapes
        + [
            pltpu.VMEM((depth // 2, many, 3 * kept, LANES), jnp.float32),
            pltpu.VMEM((depth // 2, many, 1, LANES), jnp.float32),
        ],
        compiler_params=pltpu.CompilerParams(vmem_limit_bytes=VMEM_LIMIT),
        cost_estimate=pl.CostEstimate(
            flops=2 * 3 * rows * cols * block * (2 if other else 8),
            bytes_accessed=vols * rows * cols * 4 + rows * cols,
            transcendentals=0,
        ),
        name="lag_windows",
    )(place, codes, other_codes, *tables, frames, other_frames, template, *more)


def exchange(value, axes, size, turn):
    return lax.ppermute(value, axes, [(at, at ^ turn) for at in range(size)])


def on_device(frames, template, shift_codes):
    vol_dev, pl_dev, img_rows, img_cols = frames.shape
    own, block = template.shape[0], template.shape[-1]
    depth = lax.axis_size("z")
    planes = lax.axis_size("plane")
    place = jnp.stack([lax.axis_index(axis) for axis in ("z", "y", "core", "plane")])
    core = place[2]
    other_codes = exchange(shift_codes, "core", 2, 1)
    other_frames = exchange(frames, "core", 2, 1)
    *bands, staged = stage(tap_constants(block), frames, template)
    turns = [depth - 1, *range(1, depth - 1)]
    fetched = {turn: exchange(template, "z", depth, turn) for turn in turns}
    pieces = [template] + [fetched[turn] for turn in range(1, depth)]
    averages, correlation = [], 0.0
    volumes = vol_dev * depth * 4
    for p in range(pl_dev):
        work = (place, shift_codes, other_codes, staged[:, p], other_frames[:, p])
        sizes = (depth, block, own)
        (far_sums,) = warp_sums(*work, bands, template, 1, *sizes)
        taken = exchange(far_sums, "y", 2, 1)
        near_sums = warp_sums(*work, bands, far_sums, 0, *sizes)
        pieces, near_sums = lax.optimization_barrier((pieces, near_sums))
        near = jnp.concatenate([piece[:, p] for piece in pieces], axis=0)
        far = exchange(near, "y", 2, 1)
        sums = [
            one.astype(jnp.float32) + taken[step * own : (step + 1) * own].astype(jnp.float32)
            for step, one in enumerate(near_sums)
        ]
        moved = [exchange(sums[turn].astype(jnp.bfloat16), "z", depth, turn) for turn in turns]
        sizes = (planes, depth, own)
        part = lag_windows(*work, near, near_sums[:1], 0, *sizes)
        found, *given = lag_windows(*work, far, part, 1, *sizes)
        found, moved = lax.optimization_barrier((found, moved))
        total = sum((one.astype(jnp.float32) for one in moved), sums[0])
        averages.append(total * (1.0 / volumes))
        for turn, one in enumerate(given):
            found = found + exchange(one, "plane", planes, turn + 1).astype(jnp.float32)
        given = exchange(found[1].astype(jnp.bfloat16), "core", 2, 1)
        pair = (found[0], given.astype(jnp.float32))
        pair = [jnp.where(core == at, *pair).reshape(vol_dev, -1, 1, own, WIN * WIN) for at in (0, 1)]
        correlation += jnp.concatenate(pair, axis=2).reshape(vol_dev, -1, WIN * WIN)
    return (correlation, jnp.stack(averages, axis=1))


def solution(mesh):
    devices = mesh.devices.reshape(-1, 2, 2, mesh.shape["plane"])
    split = jax.sharding.Mesh(devices, ("z", "y", "core", "plane"))
    vols = ("z", "y", "core")
    in_specs = (P(vols, "plane", None, None), P(vols, "plane", None, None), P(vols, None, None))
    out_specs = (P(vols, "plane", None), P(vols, "plane", None, None))
    return jax.shard_map(
        on_device, mesh=split, in_specs=in_specs, out_specs=out_specs, check_vma=False
    )
```
